32 devices in a mesh: dp: 4 (over y, x), table: 8 (over z, core).
Axes of the slice: x: 2, y: 2, z: 4, core: 2. Of those that a mesh axis runs over, the one named last changes fastest.
Arguments:
- item_ids: int32 [8192], P('dp'), may hold values from 0 to 32767
- user_len: int32 [32], P('dp'), may hold values from 32 to 256
- emb_table: bfloat16 [512, 32768], P('table'), may hold values from -6 to 6
- cotangent: bfloat16 [512, 8192], P('table', 'dp'), may hold values from -6 to 6
- w_uvqk: bfloat16 [512, 2048], replicated, may hold values from -0.25 to 0.25
- w_out: bfloat16 [512, 512], replicated, may hold values from -0.25 to 0.25
- gain_in: float32 [512], replicated, may hold values from 0.25 to 1.75
- gain_mid: float32 [512], replicated, may hold values from 0.25 to 1.75
Outputs:
- layer_out: bfloat16 [512, 8192], P('table', 'dp')
- table_grad: float32 [512, 32768], P('table', 'dp')
The draws below stay inside these ranges and needn't reach their ends.
All inputs are finite; a program needn't handle non-finite values.
Results may differ from the reference program's by a relative error of at most 0.012.
Values may be sent and summed in bfloat16 or wider, within the bound.
No kernel may reach another device: no remote copies, remote signals or barrier semaphores. Data moves between devices by JAX's collectives and lax.ppermute only.
A program may use at most 128 MiB of HBM per device.

```python
import math
import jax
import jax.numpy as jnp
import numpy as np
from jax import lax

D = 512
HEADS = 8
SLOT = 256
VOCAB = 32768
SLOTS_DEV = 1
USERS = 32
ROWS = 8192


def plant(drawn, rng, least, top_value):
    spot = [jax.random.randint(jax.random.fold_in(rng, axis), (), 0, length) for axis, length in enumerate(drawn.shape)]
    widest = drawn.shape.index(max(drawn.shape))
    neighbour = spot[:widest] + [(spot[widest] + 1) % drawn.shape[widest]] + spot[widest + 1:]
    return drawn.at[tuple(spot)].set(least).at[tuple(neighbour)].set(top_value)


def level_of(own_key, shape, cuts, least, largest):
    level = 1.0
    for position, shards_of in cuts:
        heights = jax.random.uniform(jax.random.fold_in(jax.random.fold_in(own_key, 6), position), (shards_of,), jnp.float32, least / len(cuts), largest / len(cuts))
        level = level * jnp.repeat(jnp.exp(heights), shape[position] // shards_of).reshape((-1,) + (1,) * (len(shape) - 1 - position))
    return level


def cumulative_ranks(number_of, skew):
    loads = [(1 << 20) // math.isqrt(standing ** skew) + 1 for standing in range(1, number_of + 1)]
    scale = 1 + sum(loads) // (1 << 30)
    return np.cumsum(np.array([max(1, weight // scale) for weight in loads]))


def skewed_ids(rng, dims, amount, slope):
    grid = cumulative_ranks(amount, slope)
    pick = jax.random.randint(jax.random.fold_in(rng, 1), dims, 0, int(grid[amount - 1]))
    rank = jnp.searchsorted(jnp.asarray(grid, jnp.int32), pick, side="right")
    return jax.random.permutation(jax.random.fold_in(rng, 2), amount)[rank].astype(jnp.int32)


def gaussian(own_key, dims, scale, most, split=(), kind=jnp.bfloat16):
    result = scale * jax.random.normal(own_key, dims, jnp.float32)
    if split:
        result = result * level_of(own_key, dims, split, -0.22, 0.18)
    return jnp.clip(result, -most, most).astype(kind)


def setup_inputs(seed: int = 0) -> dict:
    key_list = jax.random.split(jax.random.key(seed), 9)
    item_ids = plant(skewed_ids(key_list[0], (ROWS,), VOCAB, 2), jax.random.fold_in(key_list[0], 3), 0, VOCAB - 1).astype(jnp.int32)
    user_len = plant(jax.random.randint(key_list[1], (USERS,), SLOT // 8, SLOT + 1), jax.random.fold_in(key_list[1], 1), SLOT // 8, SLOT).astype(jnp.int32)
    emb_table = gaussian(key_list[2], (D, VOCAB), 1.0, 6.0, ((0, 8),))
    cotangent = gaussian(key_list[3], (D, ROWS), 1.0, 6.0, ((0, 8), (1, 4)))
    w_uvqk = gaussian(key_list[4], (D, 4 * D), D ** -0.5, 0.25)
    w_out = gaussian(key_list[5], (D, D), D ** -0.5, 0.25)
    gain_in = jnp.clip(1.0 + 0.15 * jax.random.normal(key_list[6], (D,), jnp.float32), 0.25, 1.75)
    gain_mid = jnp.clip(1.0 + 0.15 * jax.random.normal(key_list[7], (D,), jnp.float32), 0.25, 1.75)
    return {"item_ids": item_ids, "user_len": user_len, "emb_table": emb_table, "cotangent": cotangent, "w_uvqk": w_uvqk, "w_out": w_out, "gain_in": gain_in, "gain_mid": gain_mid}


norm_eps = 1e-05

def row_norm(values, gain):
    centred = values - lax.optimization_barrier(jnp.mean(values, axis=-1, keepdims=True))
    spread_sq = lax.optimization_barrier(jnp.mean(centred * centred, axis=-1, keepdims=True))
    return centred * lax.rsqrt(spread_sq + norm_eps) * gain

def hstu_layer(embedded, lengths, w_uvqk, w_out, gain_in, gain_mid):
    slots, positions, width = embedded.shape
    head_dim = width // HEADS
    widened = embedded.astype(jnp.float32)
    normed = row_norm(widened, gain_in).astype(jnp.bfloat16)
    projected = jnp.dot(normed.reshape(-1, width), w_uvqk, preferred_element_type=jnp.float32)
    projected = jax.nn.silu(projected).astype(jnp.bfloat16).reshape(slots, positions, 4, HEADS, head_dim)
    gate_rows = projected[:, :, 0].reshape(slots, positions, width)
    value_rows = projected[:, :, 1].astype(jnp.float32)
    queries = projected[:, :, 2].astype(jnp.float32)
    key_rows = projected[:, :, 3].astype(jnp.float32)
    scores = jnp.einsum('sqhd,skhd->shqk', queries, key_rows) * head_dim ** (-0.5)
    order = jnp.arange(positions, dtype=jnp.int32)
    causal = order[None, :] <= order[:, None]
    key_mask = causal[None, :, :] & (order[None, None, :] < lengths[:, None, None])
    divisor = lengths.astype(jnp.float32)[:, None, None, None]
    weights = jnp.where(key_mask[:, None], jax.nn.silu(scores), 0.0) / divisor
    weights = weights.astype(jnp.bfloat16).astype(jnp.float32)
    attended = jnp.einsum('shqk,skhd->sqhd', weights, value_rows).reshape(slots, positions, width)
    mixed = (row_norm(attended, gain_mid) * gate_rows.astype(jnp.float32)).astype(jnp.bfloat16)
    update = jnp.dot(mixed.reshape(-1, width), w_out, preferred_element_type=jnp.float32)
    return (widened + update.reshape(slots, positions, width)).astype(jnp.bfloat16)

def reference(item_ids, user_len, emb_table, cotangent, w_uvqk, w_out, gain_in, gain_mid):
    user_count = user_len.shape[0]
    groups = user_count // SLOTS_DEV
    embedded = emb_table.T[item_ids].reshape(groups, SLOTS_DEV, SLOT, D)
    cot_rows = cotangent.T.reshape(groups, SLOTS_DEV, SLOT, D)
    lengths = user_len.reshape(groups, SLOTS_DEV)

    def one_group(packed):
        rows_in, cot_in, lens_in = packed
        order = jnp.arange(SLOT, dtype=jnp.int32)
        valid_rows = order[None, :] < lens_in[:, None]
        masked = jnp.where(valid_rows[:, :, None], cot_in, jnp.zeros_like(cot_in))

        def forward(values):
            return hstu_layer(values, lens_in, w_uvqk, w_out, gain_in, gain_mid)
        layer_rows, pullback = jax.vjp(forward, rows_in)
        return (layer_rows, pullback(masked)[0])
    layer_rows, row_grad = lax.map(one_group, (embedded, cot_rows, lengths))
    layer_out = layer_rows.reshape(-1, D).T
    table_grad = jax.ops.segment_sum(row_grad.reshape(-1, D).astype(jnp.float32), item_ids, num_segments=VOCAB)
    return (layer_out, table_grad.T)
```

```python
import jax
import jax.numpy as jnp
from jax import lax
from jax.experimental import pallas as pl
from jax.experimental.pallas import tpu as pltpu
from jax.sharding import PartitionSpec as P

HEADS = 8
NORM_EPS = 1e-05
LANES = 128
VMEM_BYTES = 48 * 1024 * 1024

F32 = jnp.float32
BF16 = jnp.bfloat16


def dot_nn(left, right):
    return jnp.dot(left, right, preferred_element_type=F32)


def dot_nt(left, right):
    return lax.dot_general(left, right, (((1,), (1,)), ((), ())), preferred_element_type=F32)


def dot_tn(left, right):
    return lax.dot_general(left, right, (((0,), (0,)), ((), ())), preferred_element_type=F32)


def gather_kernel(ids_ref, table_ref, out_ref):
    users, features, positions = out_ref.shape
    lane = lax.broadcasted_iota(jnp.int32, (features, LANES), 1)
    blocks = positions // LANES

    def one_block(step, carry):
        user = step // blocks
        part = step % blocks
        gathered = jnp.zeros((features, LANES), F32)
        for slot in range(LANES):
            item = ids_ref[step * LANES + slot]
            start = pl.multiple_of((item // LANES) * LANES, LANES)
            source = item % LANES
            tile = table_ref[:, pl.ds(start, LANES)].astype(F32)
            moved = pltpu.roll(tile, (slot + LANES - source) % LANES, 1)
            gathered = jnp.where(lane == slot, moved, gathered)
        out_ref[user, :, pl.ds(pl.multiple_of(part * LANES, LANES), LANES)] = gathered.astype(BF16)
        return carry

    lax.fori_loop(0, users * blocks, one_block, 0)


def gather_columns(item_ids, table, users, positions):
    features = table.shape[0]
    return pl.pallas_call(
        gather_kernel,
        out_shape=jax.ShapeDtypeStruct((users, features, positions), table.dtype),
        in_specs=[
            pl.BlockSpec(memory_space=pltpu.SMEM),
            pl.BlockSpec(memory_space=pltpu.VMEM),
        ],
        out_specs=pl.BlockSpec(memory_space=pltpu.VMEM),
        compiler_params=pltpu.CompilerParams(vmem_limit_bytes=VMEM_BYTES),
        name="gather_columns",
    )(item_ids, table)


def norm_forward(values):
    centred = values - jnp.mean(values, axis=0, keepdims=True)
    inverse = lax.rsqrt(jnp.mean(centred * centred, axis=0, keepdims=True) + NORM_EPS)
    return centred * inverse, inverse


def norm_backward(grad, normal, inverse):
    shift = jnp.mean(grad, axis=0, keepdims=True)
    slope = jnp.mean(grad * normal, axis=0, keepdims=True)
    return (grad - shift - normal * slope) * inverse


def silu_pair(z):
    gate = 0.5 + 0.5 * jnp.tanh(0.5 * z)
    value = z * gate
    return value, gate + value * (1.0 - gate)


def layer_kernel(
    len_ref,
    emb_ref,
    cot_ref,
    w_in_ref,
    w_in_t_ref,
    w_out_ref,
    w_out_t_ref,
    gain_in_ref,
    gain_mid_ref,
    out_ref,
    grad_ref,
    proj_ref,
    slope_ref,
    weight_ref,
    score_slope_ref,
    att_ref,
    dproj_ref,
):
    width, positions = emb_ref.shape
    head_dim = width // HEADS
    half = positions // 2
    length = len_ref[0]
    share = 1.0 / length.astype(F32)

    embedded = emb_ref[...].astype(F32)
    normal_in, inverse_in = norm_forward(embedded)
    normed = (normal_in * gain_in_ref[...]).astype(BF16)
    for part in range(4):
        rows = pl.ds(part * width, width)
        value, slope = silu_pair(dot_nn(w_in_t_ref[rows, :], normed))
        proj_ref[rows, :] = value.astype(BF16)
        slope_ref[rows, :] = slope

    def mask(key_start, query_start, shape):
        key = lax.broadcasted_iota(jnp.int32, shape, 0) + key_start
        query = lax.broadcasted_iota(jnp.int32, shape, 1) + query_start
        return (key <= query) & (key < length)

    low = mask(0, 0, (half, positions))
    high = mask(half, half, (half, half))
    scale = head_dim ** (-0.5)
    for head in range(HEADS):
        at = head * head_dim
        values = proj_ref[pl.ds(width + at, head_dim), :]
        queries = proj_ref[pl.ds(2 * width + at, head_dim), :]
        keys = proj_ref[pl.ds(3 * width + at, head_dim), :]
        for start, allowed in ((0, low), (half, high)):
            scores = dot_tn(keys[:, start : start + half], queries[:, start:]) * scale
            value, slope = silu_pair(scores)
            weight_ref[head, pl.ds(start, half), pl.ds(start, positions - start)] = jnp.where(
                allowed, value * share, 0.0
            ).astype(BF16)
            score_slope_ref[head, pl.ds(start, half), pl.ds(start, positions - start)] = jnp.where(
                allowed, slope * (share * scale), 0.0
            )
        weight_ref[head, pl.ds(half, half), pl.ds(0, half)] = jnp.zeros((half, half), BF16)
        att_ref[pl.ds(at, head_dim), :] = dot_nn(values, weight_ref[head])

    normal_mid, inverse_mid = norm_forward(att_ref[...])
    gate_rows = proj_ref[pl.ds(0, width), :].astype(F32)
    scaled = normal_mid * gain_mid_ref[...]
    mixed = (scaled * gate_rows).astype(BF16)
    out_ref[...] = (embedded + dot_nn(w_out_t_ref[...], mixed)).astype(BF16)

    valid = lax.broadcasted_iota(jnp.int32, (width, positions), 1) < length
    cotangent = jnp.where(valid, cot_ref[...].astype(F32), 0.0)
    d_mixed = dot_nn(w_out_ref[...], cotangent.astype(BF16))
    dproj_ref[pl.ds(0, width), :] = (d_mixed * scaled * slope_ref[pl.ds(0, width), :]).astype(BF16)
    d_att = norm_backward(d_mixed * gate_rows * gain_mid_ref[...], normal_mid, inverse_mid)
    att_ref[...] = d_att
    for head in range(HEADS):
        at = head * head_dim
        v_rows = pl.ds(width + at, head_dim)
        q_rows = pl.ds(2 * width + at, head_dim)
        k_rows = pl.ds(3 * width + at, head_dim)
        values, queries, keys = proj_ref[v_rows, :], proj_ref[q_rows, :], proj_ref[k_rows, :]
        d_head = att_ref[pl.ds(at, head_dim), :].astype(BF16)
        low_scores = (
            dot_tn(values[:, :half], d_head) * score_slope_ref[head, pl.ds(0, half), :]
        ).astype(BF16)
        high_scores = (
            dot_tn(values[:, half:], d_head[:, half:])
            * score_slope_ref[head, pl.ds(half, half), pl.ds(half, half)]
        ).astype(BF16)
        d_scores = jnp.concatenate(
            [
                low_scores,
                jnp.concatenate([jnp.zeros((half, half), BF16), high_scores], axis=1),
            ],
            axis=0,
        )
        d_values = dot_nt(d_head, weight_ref[head])
        d_queries = dot_nn(keys, d_scores)
        d_keys = dot_nt(queries, d_scores)
        dproj_ref[v_rows, :] = (d_values * slope_ref[v_rows, :]).astype(BF16)
        dproj_ref[q_rows, :] = (d_queries * slope_ref[q_rows, :]).astype(BF16)
        dproj_ref[k_rows, :] = (d_keys * slope_ref[k_rows, :]).astype(BF16)
    d_normed = dot_nn(w_in_ref[...], dproj_ref[...])
    d_embedded = norm_backward(d_normed * gain_in_ref[...], normal_in, inverse_in)
    grad_ref[...] = (cotangent + d_embedded).astype(BF16)


def run_layer(length, embedded, cotangent, w_in, w_out, gain_in, gain_mid):
    width, positions = embedded.shape
    vmem = pl.BlockSpec(memory_space=pltpu.VMEM)
    shape = jax.ShapeDtypeStruct((width, positions), BF16)
    return pl.pallas_call(
        layer_kernel,
        out_shape=(shape, shape),
        in_specs=[pl.BlockSpec(memory_space=pltpu.SMEM)] + [vmem] * 8,
        out_specs=(vmem, vmem),
        scratch_shapes=[
            pltpu.VMEM((4 * width, positions), BF16),
            pltpu.VMEM((4 * width, positions), F32),
            pltpu.VMEM((HEADS, positions, positions), BF16),
            pltpu.VMEM((HEADS, positions, positions), F32),
            pltpu.VMEM((width, positions), F32),
            pltpu.VMEM((4 * width, positions), BF16),
        ],
        compiler_params=pltpu.CompilerParams(vmem_limit_bytes=VMEM_BYTES),
        name="layer",
    )(
        length,
        embedded,
        cotangent,
        w_in,
        w_in.T,
        w_out,
        w_out.T,
        gain_in.reshape(width, 1),
        gain_mid.reshape(width, 1),
    )


LOW = 256
STACK = 4


def scatter_kernel(ids_ref, grad_ref, out_ref, spread_ref, low_ref):
    _, users, features, positions = grad_ref.shape
    own = out_ref.shape[1]
    for user in range(users):
        columns = pl.ds(user * positions, positions)
        item = ids_ref[0, pl.ds(user, 1), :]
        row = lax.broadcasted_iota(jnp.int32, (LOW, positions), 0)
        low_ref[:, columns] = jnp.where(row == item % LOW, 1.0, 0.0).astype(BF16)

    @pl.when(pl.program_id(0) == 0)
    def _():
        out_ref[...] = jnp.zeros_like(out_ref)

    def one_stack(step, carry):
        for user in range(users):
            columns = pl.ds(user * positions, positions)
            high = lax.shift_right_arithmetic(ids_ref[0, pl.ds(user, 1), :], LOW.bit_length() - 1)
            for place in range(STACK):
                chosen = jnp.where(high == step * STACK + place, 1.0, 0.0).astype(BF16)
                spread_ref[pl.ds(place * features, features), columns] = grad_ref[0, user] * chosen
        sums = dot_nt(spread_ref[...], low_ref[...])
        for place in range(STACK):
            columns = pl.ds(pl.multiple_of((step * STACK + place) * LOW, LOW), LOW)
            out_ref[:, columns] += sums[place * features : (place + 1) * features]
        return carry

    lax.fori_loop(0, own // (LOW * STACK), one_stack, 0)


def scatter_columns(item_ids, grads, own):
    groups, users, features, positions = grads.shape
    return pl.pallas_call(
        scatter_kernel,
        grid=(groups,),
        out_shape=jax.ShapeDtypeStruct((features, own), F32),
        in_specs=[
            pl.BlockSpec((1, users, positions), lambda g: (g, 0, 0)),
            pl.BlockSpec((1, users, features, positions), lambda g: (g, 0, 0, 0)),
        ],
        out_specs=pl.BlockSpec((features, own), lambda g: (0, 0)),
        scratch_shapes=[
            pltpu.VMEM((STACK * features, users * positions), BF16),
            pltpu.VMEM((LOW, users * positions), BF16),
        ],
        compiler_params=pltpu.CompilerParams(vmem_limit_bytes=VMEM_BYTES),
        name="scatter_columns",
    )(item_ids, grads)


def on_device(item_ids, user_len, emb_table, cotangent, w_uvqk, w_out, gain_in, gain_mid):
    dp_size = lax.axis_size("dp")
    table_size = lax.axis_size("table")
    users = user_len.shape[0]
    assert users == table_size
    features, vocab = emb_table.shape
    rows = item_ids.shape[0]
    positions = rows // users
    width = features * table_size
    own = vocab // dp_size

    all_ids = lax.all_gather(item_ids, "dp", axis=0, tiled=False)
    cot_send = jnp.transpose(cotangent.reshape(features, users, positions), (1, 0, 2))
    cot_cols = lax.all_to_all(cot_send, "table", split_axis=0, concat_axis=0, tiled=True)
    emb_send = gather_columns(item_ids, emb_table, users, positions)
    emb_cols = lax.all_to_all(emb_send, "table", split_axis=0, concat_axis=0, tiled=True)
    length = lax.dynamic_slice_in_dim(user_len, lax.axis_index("table"), 1)
    out_cols, grad_cols = run_layer(
        length,
        emb_cols.reshape(width, positions),
        cot_cols.reshape(width, positions),
        w_uvqk,
        w_out,
        gain_in,
        gain_mid,
    )
    per_peer = (table_size, features, positions)
    grad_home = lax.all_to_all(
        grad_cols.reshape(per_peer), "table", split_axis=0, concat_axis=0, tiled=True
    )
    out_home = lax.all_to_all(
        out_cols.reshape(per_peer), "table", split_axis=0, concat_axis=0, tiled=True
    )
    all_grads = lax.all_gather(grad_home, "dp", axis=0, tiled=False)
    own_ids = all_ids.reshape(dp_size, users, positions) - lax.axis_index("dp") * own
    table_grad = scatter_columns(own_ids, all_grads, own)
    layer_out = jnp.transpose(out_home, (1, 0, 2)).reshape(features, rows)
    return (layer_out, table_grad)


def solution(mesh):
    return jax.shard_map(
        on_device,
        mesh=mesh,
        in_specs=(P("dp"), P("dp"), P("table", None), P("table", "dp"), P(), P(), P(), P()),
        out_specs=(P("table", "dp"), P("table", "dp")),
        check_vma=False,
    )
```

```python
import functools

import jax
import jax.numpy as jnp
from jax import lax
from jax.experimental import pallas as pl
from jax.experimental.pallas import tpu as pltpu
from jax.sharding import PartitionSpec as P

HEADS = 8
NORM_EPS = 1e-05
LANES = 128
VMEM_BYTES = 48 * 1024 * 1024

F32 = jnp.float32
BF16 = jnp.bfloat16


def dot_nn(left, right):
    return jnp.dot(left, right, preferred_element_type=F32)


def dot_nt(left, right):
    return lax.dot_general(left, right, (((1,), (1,)), ((), ())), preferred_element_type=F32)


def dot_tn(left, right):
    return lax.dot_general(left, right, (((0,), (0,)), ((), ())), preferred_element_type=F32)


BLOCK = 256


def gather_kernel(me_ref, row_ref, group_ref, table_ref, *refs):
    users, positions = group_ref.shape
    out_refs, (rows_ref, picked_ref) = refs[:users], refs[users:]
    features, wide = table_ref.shape
    pack = LANES // features
    step = pl.program_id(0)
    for part in range(wide // (BLOCK * pack)):
        first = part * BLOCK * pack
        stack = jnp.concatenate(
            [table_ref[:, first + s * BLOCK : first + (s + 1) * BLOCK] for s in range(pack)], axis=0
        )
        at = pl.multiple_of((step * (wide // (BLOCK * pack)) + part) * BLOCK, BLOCK)
        rows_ref[pl.ds(at, BLOCK), :] = stack.astype(F32).T

    @pl.when(step == pl.num_programs(0) - 1)
    def _():
        row = lax.broadcasted_iota(jnp.int32, (LANES, LANES), 0)
        column = lax.broadcasted_iota(jnp.int32, (LANES, LANES), 1)
        same = jnp.where(row == column, 1.0, 0.0).astype(BF16)
        for place in range(users):
            user = me_ref[0] ^ place

            def some(part, carry):
                for slot in range(UNROLL):
                    position = part * UNROLL + slot
                    picked_ref[pl.ds(position, 1), :] = rows_ref[
                        pl.ds(row_ref[user * positions + position], 1), :
                    ]
                return carry

            lax.fori_loop(0, positions // UNROLL, some, 0)
            turned = dot_nt(same, picked_ref[...].astype(BF16))
            group = group_ref[pl.ds(user, 1), :]
            total = jnp.zeros((features, positions), F32)
            for s in range(pack):
                total += jnp.where(group == s, turned[s * features : (s + 1) * features], 0.0)
            out_refs[place][...] = total.astype(BF16)


UNROLL = 32


def gather_columns(me, item_ids, table):
    users, positions = item_ids.shape
    features, vocab = table.shape
    pack = LANES // features
    wide = 8 * BLOCK * pack
    row = item_ids // (BLOCK * pack) * BLOCK + item_ids % BLOCK
    group = item_ids // BLOCK % pack
    smem = pl.BlockSpec(memory_space=pltpu.SMEM)
    block = pl.BlockSpec((features, positions), lambda i: (0, 0))
    return pl.pallas_call(
        gather_kernel,
        grid=(vocab // wide,),
        out_shape=[jax.ShapeDtypeStruct((features, positions), table.dtype)] * users,
        in_specs=[
            smem,
            smem,
            pl.BlockSpec((users, positions), lambda i: (0, 0)),
            pl.BlockSpec((features, wide), lambda i: (0, i)),
        ],
        out_specs=[block] * users,
        scratch_shapes=[
            pltpu.VMEM((vocab // pack, LANES), F32),
            pltpu.VMEM((positions, LANES), F32),
        ],
        compiler_params=pltpu.CompilerParams(vmem_limit_bytes=VMEM_BYTES),
        name="gather_columns",
    )(me, row.reshape(-1), group, table)


def split_kernel(me_ref, wide_ref, *out_refs):
    positions = out_refs[0].shape[1]
    for place, out_ref in enumerate(out_refs):
        start = pl.multiple_of((me_ref[0] ^ place) * positions, positions)
        out_ref[...] = wide_ref[:, pl.ds(start, positions)]


def split_columns(me, wide, users):
    features, rows = wide.shape
    vmem = pl.BlockSpec(memory_space=pltpu.VMEM)
    return pl.pallas_call(
        split_kernel,
        out_shape=[jax.ShapeDtypeStruct((features, rows // users), wide.dtype)] * users,
        in_specs=[pl.BlockSpec(memory_space=pltpu.SMEM), vmem],
        out_specs=[vmem] * users,
        name="split_columns",
    )(me, wide)


def norm_forward(values):
    centred = values - jnp.mean(values, axis=0, keepdims=True)
    inverse = lax.rsqrt(jnp.mean(centred * centred, axis=0, keepdims=True) + NORM_EPS)
    return centred * inverse, inverse


def norm_backward(grad, normal, inverse):
    shift = jnp.mean(grad, axis=0, keepdims=True)
    slope = jnp.mean(grad * normal, axis=0, keepdims=True)
    return (grad - shift - normal * slope) * inverse


def silu_pair(z):
    gate = 0.5 + 0.5 * jnp.tanh(0.5 * z)
    value = z * gate
    return value, gate + value * (1.0 - gate)


def layer_kernel(peers, me_ref, len_ref, *refs):
    emb_parts, cot_parts, refs = refs[:peers], refs[peers : 2 * peers], refs[2 * peers :]
    w_in_ref, w_in_t_ref, w_out_ref, w_out_t_ref, gain_in_ref, gain_mid_ref, *refs = refs
    out_parts, grad_parts, refs = refs[:peers], refs[peers : 2 * peers], refs[2 * peers :]
    emb_ref, cot_ref, proj_ref, slope_ref, weight_ref, score_slope_ref, att_ref, dproj_ref = refs
    width, positions = emb_ref.shape
    features = width // peers

    def rows_of(place):
        return pl.ds(pl.multiple_of((me_ref[0] ^ place) * features, features), features)

    for place in range(peers):
        emb_ref[rows_of(place), :] = emb_parts[place][...]
        cot_ref[rows_of(place), :] = cot_parts[place][...]
    head_dim = width // HEADS
    half = positions // 2
    length = len_ref[me_ref[0]]
    share = 1.0 / length.astype(F32)

    embedded = emb_ref[...].astype(F32)
    normal_in, inverse_in = norm_forward(embedded)
    normed = (normal_in * gain_in_ref[...]).astype(BF16)
    for part in range(4):
        rows = pl.ds(part * width, width)
        value, slope = silu_pair(dot_nn(w_in_t_ref[rows, :], normed))
        proj_ref[rows, :] = value.astype(BF16)
        slope_ref[rows, :] = slope

    def mask(key_start, query_start, shape):
        key = lax.broadcasted_iota(jnp.int32, shape, 0) + key_start
        query = lax.broadcasted_iota(jnp.int32, shape, 1) + query_start
        return (key <= query) & (key < length)

    low = mask(0, 0, (half, positions))
    high = mask(half, half, (half, half))
    scale = head_dim ** (-0.5)
    for head in range(HEADS):
        at = head * head_dim
        values = proj_ref[pl.ds(width + at, head_dim), :]
        queries = proj_ref[pl.ds(2 * width + at, head_dim), :]
        keys = proj_ref[pl.ds(3 * width + at, head_dim), :]
        for start, allowed in ((0, low), (half, high)):
            scores = dot_tn(keys[:, start : start + half], queries[:, start:]) * scale
            value, slope = silu_pair(scores)
            weight_ref[head, pl.ds(start, half), pl.ds(start, positions - start)] = jnp.where(
                allowed, value * share, 0.0
            ).astype(BF16)
            score_slope_ref[head, pl.ds(start, half), pl.ds(start, positions - start)] = jnp.where(
                allowed, slope * (share * scale), 0.0
            )
        weight_ref[head, pl.ds(half, half), pl.ds(0, half)] = jnp.zeros((half, half), BF16)
        att_ref[pl.ds(at, head_dim), :] = dot_nn(values, weight_ref[head])

    normal_mid, inverse_mid = norm_forward(att_ref[...])
    gate_rows = proj_ref[pl.ds(0, width), :].astype(F32)
    scaled = normal_mid * gain_mid_ref[...]
    mixed = (scaled * gate_rows).astype(BF16)
    emb_ref[...] = (embedded + dot_nn(w_out_t_ref[...], mixed)).astype(BF16)
    for place in range(peers):
        out_parts[place][...] = emb_ref[rows_of(place), :]

    valid = lax.broadcasted_iota(jnp.int32, (width, positions), 1) < length
    cotangent = jnp.where(valid, cot_ref[...].astype(F32), 0.0)
    d_mixed = dot_nn(w_out_ref[...], cotangent.astype(BF16))
    dproj_ref[pl.ds(0, width), :] = (d_mixed * scaled * slope_ref[pl.ds(0, width), :]).astype(BF16)
    d_att = norm_backward(d_mixed * gate_rows * gain_mid_ref[...], normal_mid, inverse_mid)
    att_ref[...] = d_att
    for head in range(HEADS):
        at = head * head_dim
        v_rows = pl.ds(width + at, head_dim)
        q_rows = pl.ds(2 * width + at, head_dim)
        k_rows = pl.ds(3 * width + at, head_dim)
        values, queries, keys = proj_ref[v_rows, :], proj_ref[q_rows, :], proj_ref[k_rows, :]
        d_head = att_ref[pl.ds(at, head_dim), :].astype(BF16)
        low_scores = (
            dot_tn(values[:, :half], d_head) * score_slope_ref[head, pl.ds(0, half), :]
        ).astype(BF16)
        high_scores = (
            dot_tn(values[:, half:], d_head[:, half:])
            * score_slope_ref[head, pl.ds(half, half), pl.ds(half, half)]
        ).astype(BF16)
        d_scores = jnp.concatenate(
            [
                low_scores,
                jnp.concatenate([jnp.zeros((half, half), BF16), high_scores], axis=1),
            ],
            axis=0,
        )
        d_values = dot_nt(d_head, weight_ref[head])
        d_queries = dot_nn(keys, d_scores)
        d_keys = dot_nt(queries, d_scores)
        dproj_ref[v_rows, :] = (d_values * slope_ref[v_rows, :]).astype(BF16)
        dproj_ref[q_rows, :] = (d_queries * slope_ref[q_rows, :]).astype(BF16)
        dproj_ref[k_rows, :] = (d_keys * slope_ref[k_rows, :]).astype(BF16)
    d_normed = dot_nn(w_in_ref[...], dproj_ref[...])
    d_embedded = norm_backward(d_normed * gain_in_ref[...], normal_in, inverse_in)
    cot_ref[...] = (cotangent + d_embedded).astype(BF16)
    for place in range(peers):
        grad_parts[place][...] = cot_ref[rows_of(place), :]


def run_layer(me, lengths, embedded, cotangent, w_in, w_out, gain_in, gain_mid):
    peers = len(embedded)
    width, positions = w_out.shape[0], embedded[0].shape[1]
    smem, vmem = pl.BlockSpec(memory_space=pltpu.SMEM), pl.BlockSpec(memory_space=pltpu.VMEM)
    shape = jax.ShapeDtypeStruct((width // peers, positions), BF16)
    results = pl.pallas_call(
        functools.partial(layer_kernel, peers),
        out_shape=[shape] * (2 * peers),
        in_specs=[smem] * 2 + [vmem] * (2 * peers + 6),
        out_specs=[vmem] * (2 * peers),
        scratch_shapes=[
            pltpu.VMEM((width, positions), BF16),
            pltpu.VMEM((width, positions), BF16),
            pltpu.VMEM((4 * width, positions), BF16),
            pltpu.VMEM((4 * width, positions), F32),
            pltpu.VMEM((HEADS, positions, positions), BF16),
            pltpu.VMEM((HEADS, positions, positions), F32),
            pltpu.VMEM((width, positions), F32),
            pltpu.VMEM((4 * width, positions), BF16),
        ],
        compiler_params=pltpu.CompilerParams(vmem_limit_bytes=VMEM_BYTES),
        name="layer",
    )(
        me,
        lengths,
        *embedded,
        *cotangent,
        w_in,
        w_in.T,
        w_out,
        w_out.T,
        gain_in.reshape(width, 1),
        gain_mid.reshape(width, 1),
    )
    return results[:peers], results[peers:]


LOW = 256
STACK = 4


def scatter_kernel(groups, me_ref, base_ref, *refs):
    id_refs, grad_refs, refs = refs[:groups], refs[groups : 2 * groups], refs[2 * groups :]
    out_ref, spread_ref, low_ref = refs
    users, features, positions = grad_refs[0].shape
    own = out_ref.shape[1]
    row = lax.broadcasted_iota(jnp.int32, (LOW, positions), 0)
    for group in range(groups):
        def items(place):
            return id_refs[group][pl.ds(me_ref[0] ^ place, 1), :] - base_ref[0]

        for place in range(users):
            columns = pl.ds(place * positions, positions)
            low_ref[:, columns] = jnp.where(row == items(place) % LOW, 1.0, 0.0).astype(BF16)

        def one_stack(step, carry):
            for place in range(users):
                columns = pl.ds(place * positions, positions)
                high = lax.shift_right_arithmetic(items(place), LOW.bit_length() - 1)
                for part in range(STACK):
                    chosen = jnp.where(high == step * STACK + part, 1.0, 0.0).astype(BF16)
                    spread_ref[pl.ds(part * features, features), columns] = (
                        grad_refs[group][place] * chosen
                    )
            sums = dot_nt(spread_ref[...], low_ref[...])
            for part in range(STACK):
                columns = pl.ds(pl.multiple_of((step * STACK + part) * LOW, LOW), LOW)
                term = sums[part * features : (part + 1) * features]
                out_ref[:, columns] = term if group == 0 else out_ref[:, columns] + term
            return carry

        lax.fori_loop(0, own // (LOW * STACK), one_stack, 0)


def scatter_columns(me, base, item_ids, grads, own):
    groups = len(grads)
    users, features, positions = grads[0].shape
    smem, vmem = pl.BlockSpec(memory_space=pltpu.SMEM), pl.BlockSpec(memory_space=pltpu.VMEM)
    return pl.pallas_call(
        functools.partial(scatter_kernel, groups),
        out_shape=jax.ShapeDtypeStruct((features, own), F32),
        in_specs=[smem] * 2 + [vmem] * (2 * groups),
        out_specs=vmem,
        scratch_shapes=[
            pltpu.VMEM((STACK * features, users * positions), BF16),
            pltpu.VMEM((LOW, users * positions), BF16),
        ],
        compiler_params=pltpu.CompilerParams(vmem_limit_bytes=VMEM_BYTES),
        name="scatter_columns",
    )(me, base, *item_ids, *grads)


def join_kernel(me_ref, *refs):
    part_refs, out_ref = refs[:-1], refs[-1]
    positions = part_refs[0].shape[1]
    for place, part_ref in enumerate(part_refs):
        start = pl.multiple_of((me_ref[0] ^ place) * positions, positions)
        out_ref[:, pl.ds(start, positions)] = part_ref[...]


def join_columns(me, parts):
    features, positions = parts[0].shape
    vmem = pl.BlockSpec(memory_space=pltpu.VMEM)
    return pl.pallas_call(
        join_kernel,
        out_shape=jax.ShapeDtypeStruct((features, positions * len(parts)), parts[0].dtype),
        in_specs=[pl.BlockSpec(memory_space=pltpu.SMEM)] + [vmem] * len(parts),
        out_specs=vmem,
        name="join_columns",
    )(me, *parts)


def swap(value, axis, distance):
    size = lax.axis_size(axis)
    return lax.ppermute(value, axis, [(i, i ^ distance) for i in range(size)])


def swap_blocks(blocks, axis):
    received = {k: swap(blocks[k], axis, k) for k in reversed(range(1, len(blocks)))}
    return [blocks[0]] + [received[k] for k in range(1, len(blocks))]


def on_device(item_ids, user_len, emb_table, cotangent, w_uvqk, w_out, gain_in, gain_mid):
    dp_size = lax.axis_size("dp")
    table_size = lax.axis_size("table")
    users = user_len.shape[0]
    assert users == table_size
    assert dp_size & (dp_size - 1) == 0 and table_size & (table_size - 1) == 0
    vocab = emb_table.shape[1]
    positions = item_ids.shape[0] // users
    own = vocab // dp_size
    me = lax.axis_index("table").astype(jnp.int32).reshape(1)
    base = (lax.axis_index("dp").astype(jnp.int32) * own).reshape(1)

    ids = item_ids.reshape(users, positions)
    cot_parts = swap_blocks(split_columns(me, cotangent, users), "table")
    all_ids = [ids] + [swap(ids, "dp", k) for k in range(1, dp_size)]
    emb_parts = swap_blocks(gather_columns(me, ids, emb_table), "table")
    out_parts, grad_parts = run_layer(
        me, user_len, emb_parts, cot_parts, w_uvqk, w_out, gain_in, gain_mid
    )
    grad_home = jnp.stack(swap_blocks(grad_parts, "table"))
    all_grads = [grad_home] + [swap(grad_home, "dp", k) for k in range(1, dp_size)]
    out_home = swap_blocks(out_parts, "table")
    table_grad = scatter_columns(me, base, all_ids, all_grads, own)
    layer_out = join_columns(me, out_home)
    return (layer_out, table_grad)


def solution(mesh):
    return jax.shard_map(
        on_device,
        mesh=mesh,
        in_specs=(P("dp"), P("dp"), P("table", None), P("table", "dp"), P(), P(), P(), P()),
        out_specs=(P("table", "dp"), P("table", "dp")),
        check_vma=False,
    )
```

```python
import functools

import jax
import jax.numpy as jnp
from jax import lax
from jax.experimental import pallas as pl
from jax.experimental.pallas import tpu as pltpu
from jax.sharding import PartitionSpec as P

HEADS = 8
NORM_EPS = 1e-05
LANES = 128
VMEM_BYTES = 48 * 1024 * 1024

F32 = jnp.float32
BF16 = jnp.bfloat16


def dot_nn(left, right):
    return jnp.dot(left, right, preferred_element_type=F32)


def dot_nt(left, right):
    return lax.dot_general(left, right, (((1,), (1,)), ((), ())), preferred_element_type=F32)


def dot_tn(left, right):
    return lax.dot_general(left, right, (((0,), (0,)), ((), ())), preferred_element_type=F32)


BLOCK = 256
UNROLL = 32
CAPACITY = 128


def gather_kernel(ids_ref, wide_ids_ref, cot_ref, table_ref, out_ref, rows_ref, picked_ref):
    users, positions = wide_ids_ref.shape
    features, wide = table_ref.shape
    pack = LANES // features
    span = BLOCK * pack
    step = pl.program_id(0)
    for part in range(wide // span):
        stack = jnp.concatenate(
            [
                table_ref[:, part * span + s * BLOCK : part * span + (s + 1) * BLOCK]
                for s in range(pack)
            ],
            axis=0,
        )
        at = pl.multiple_of((step * (wide // span) + part) * BLOCK, BLOCK)
        rows_ref[pl.ds(at, BLOCK), :] = stack.astype(F32).T

    @pl.when(step == pl.num_programs(0) - 1)
    def _():
        row = lax.broadcasted_iota(jnp.int32, (LANES, LANES), 0)
        column = lax.broadcasted_iota(jnp.int32, (LANES, LANES), 1)
        same = jnp.where(row == column, 1.0, 0.0).astype(BF16)
        for user in range(users):

            def some(part, carry):
                for slot in range(UNROLL):
                    position = part * UNROLL + slot
                    item = ids_ref[user * positions + position]
                    item_row = (item // span) * BLOCK + item % BLOCK
                    picked_ref[pl.ds(position, 1), :] = rows_ref[pl.ds(item_row, 1), :]
                return carry

            lax.fori_loop(0, positions // UNROLL, some, 0)
            turned = dot_nt(same, picked_ref[...].astype(BF16))
            group = wide_ids_ref[pl.ds(user, 1), :] // BLOCK % pack
            total = jnp.zeros((features, positions), F32)
            for s in range(pack):
                total += jnp.where(group == s, turned[s * features : (s + 1) * features], 0.0)
            out_ref[user, pl.ds(0, features), :] = total.astype(BF16)
            out_ref[user, pl.ds(features, features), :] = cot_ref[
                :, user * positions : (user + 1) * positions
            ]


def gather_columns(item_ids, wide_ids, cotangent, table):
    users, positions = wide_ids.shape
    features, vocab = table.shape
    pack = LANES // features
    wide = 8 * BLOCK * pack
    shape = (users, 2 * features, positions)
    return pl.pallas_call(
        gather_kernel,
        grid=(vocab // wide,),
        out_shape=jax.ShapeDtypeStruct(shape, table.dtype),
        in_specs=[
            pl.BlockSpec(memory_space=pltpu.SMEM),
            pl.BlockSpec(wide_ids.shape, lambda i: (0, 0)),
            pl.BlockSpec(cotangent.shape, lambda i: (0, 0)),
            pl.BlockSpec((features, wide), lambda i: (0, i)),
        ],
        out_specs=pl.BlockSpec(shape, lambda i: (0, 0, 0)),
        scratch_shapes=[
            pltpu.VMEM((vocab // pack, LANES), F32),
            pltpu.VMEM((positions, LANES), F32),
        ],
        compiler_params=pltpu.CompilerParams(vmem_limit_bytes=VMEM_BYTES),
        name="gather_columns",
    )(item_ids, wide_ids, cotangent, table)


def ranks(member):
    positions = member.shape[1]
    row = lax.broadcasted_iota(jnp.int32, (positions, positions), 0)
    column = lax.broadcasted_iota(jnp.int32, (positions, positions), 1)
    before = jnp.where(row < column, 1.0, 0.0).astype(BF16)
    return dot_nn(member.astype(BF16), before).astype(jnp.int32)


def pack_grads(grads, items, turn, owners, own):
    positions = items.shape[1]
    owner = lax.broadcasted_iota(jnp.int32, (max(owners, 16), positions), 0)
    belongs = items // own == owner
    rank = jnp.sum(
        jnp.where(belongs, ranks(jnp.where(belongs, 1.0, 0.0)), 0), axis=0, keepdims=True
    ) - turn * CAPACITY
    fits = (rank >= 0) & (rank < CAPACITY) & (items < own * owners)
    slot = jnp.where(fits, items // own * CAPACITY + rank, -1)
    row = lax.broadcasted_iota(jnp.int32, (owners * CAPACITY, positions), 0)
    chosen = jnp.where(row == slot, 1.0, 0.0).astype(BF16)
    return dot_nt(grads, chosen).astype(BF16)


def store_packed(packed, out_ref):
    owners, peers, features, _ = out_ref.shape
    for owner in range(owners):
        for peer in range(peers):
            out_ref[owner, peer] = packed[
                peer * features : (peer + 1) * features,
                owner * CAPACITY : (owner + 1) * CAPACITY,
            ]


def norm_forward(values):
    centred = values - jnp.mean(values, axis=0, keepdims=True)
    inverse = lax.rsqrt(jnp.mean(centred * centred, axis=0, keepdims=True) + NORM_EPS)
    return centred * inverse, inverse


def norm_backward(grad, normal, inverse):
    shift = jnp.mean(grad, axis=0, keepdims=True)
    slope = jnp.mean(grad * normal, axis=0, keepdims=True)
    return (grad - shift - normal * slope) * inverse


def silu_pair(z):
    gate = 0.5 + 0.5 * jnp.tanh(0.5 * z)
    value = z * gate
    return value, gate + value * (1.0 - gate)


def layer_kernel(
    own,
    me_ref,
    len_ref,
    ids_ref,
    recv_ref,
    w_in_ref,
    w_in_t_ref,
    w_out_ref,
    w_out_t_ref,
    gain_in_ref,
    gain_mid_ref,
    out_ref,
    grad_ref,
    packed_ref,
    emb_ref,
    cot_ref,
    proj_ref,
    slope_ref,
    weight_ref,
    score_slope_ref,
    att_ref,
    dproj_ref,
):
    peers, both, positions = recv_ref.shape
    features = both // 2
    width = peers * features
    head_dim = width // HEADS
    half = positions // 2
    length = len_ref[me_ref[0]]
    share = 1.0 / length.astype(F32)
    for peer in range(peers):
        emb_ref[pl.ds(peer * features, features), :] = recv_ref[peer, pl.ds(0, features), :]
        cot_ref[pl.ds(peer * features, features), :] = recv_ref[peer, pl.ds(features, features), :]

    embedded = emb_ref[...].astype(F32)
    normal_in, inverse_in = norm_forward(embedded)
    normed = (normal_in * gain_in_ref[...]).astype(BF16)
    for part in range(4):
        rows = pl.ds(part * width, width)
        value, slope = silu_pair(dot_nn(w_in_t_ref[rows, :], normed))
        proj_ref[rows, :] = value.astype(BF16)
        slope_ref[rows, :] = slope

    def mask(key_start, query_start, shape):
        key = lax.broadcasted_iota(jnp.int32, shape, 0) + key_start
        query = lax.broadcasted_iota(jnp.int32, shape, 1) + query_start
        return (key <= query) & (key < length)

    low = mask(0, 0, (half, positions))
    high = mask(half, half, (half, half))
    scale = head_dim ** (-0.5)
    for head in range(HEADS):
        at = head * head_dim
        values = proj_ref[pl.ds(width + at, head_dim), :]
        queries = proj_ref[pl.ds(2 * width + at, head_dim), :]
        keys = proj_ref[pl.ds(3 * width + at, head_dim), :]
        for start, allowed in ((0, low), (half, high)):
            scores = dot_tn(keys[:, start : start + half], queries[:, start:]) * scale
            value, slope = silu_pair(scores)
            weight_ref[head, pl.ds(start, half), pl.ds(start, positions - start)] = jnp.where(
                allowed, value * share, 0.0
            ).astype(BF16)
            score_slope_ref[head, pl.ds(start, half), pl.ds(start, positions - start)] = jnp.where(
                allowed, slope * (share * scale), 0.0
            )
        weight_ref[head, pl.ds(half, half), pl.ds(0, half)] = jnp.zeros((half, half), BF16)
        att_ref[pl.ds(at, head_dim), :] = dot_nn(values, weight_ref[head])

    normal_mid, inverse_mid = norm_forward(att_ref[...])
    gate_rows = proj_ref[pl.ds(0, width), :].astype(F32)
    scaled = normal_mid * gain_mid_ref[...]
    mixed = (scaled * gate_rows).astype(BF16)
    out_ref[...] = (embedded + dot_nn(w_out_t_ref[...], mixed)).astype(BF16)

    valid = lax.broadcasted_iota(jnp.int32, (width, positions), 1) < length
    cotangent = jnp.where(valid, cot_ref[...].astype(F32), 0.0)
    d_mixed = dot_nn(w_out_ref[...], cotangent.astype(BF16))
    dproj_ref[pl.ds(0, width), :] = (d_mixed * scaled * slope_ref[pl.ds(0, width), :]).astype(BF16)
    d_att = norm_backward(d_mixed * gate_rows * gain_mid_ref[...], normal_mid, inverse_mid)
    att_ref[...] = d_att
    for head in range(HEADS):
        at = head * head_dim
        v_rows = pl.ds(width + at, head_dim)
        q_rows = pl.ds(2 * width + at, head_dim)
        k_rows = pl.ds(3 * width + at, head_dim)
        values, queries, keys = proj_ref[v_rows, :], proj_ref[q_rows, :], proj_ref[k_rows, :]
        d_head = att_ref[pl.ds(at, head_dim), :].astype(BF16)
        low_scores = (
            dot_tn(values[:, :half], d_head) * score_slope_ref[head, pl.ds(0, half), :]
        ).astype(BF16)
        high_scores = (
            dot_tn(values[:, half:], d_head[:, half:])
            * score_slope_ref[head, pl.ds(half, half), pl.ds(half, half)]
        ).astype(BF16)
        d_scores = jnp.concatenate(
            [
                low_scores,
                jnp.concatenate([jnp.zeros((half, half), BF16), high_scores], axis=1),
            ],
            axis=0,
        )
        d_values = dot_nt(d_head, weight_ref[head])
        d_queries = dot_nn(keys, d_scores)
        d_keys = dot_nt(queries, d_scores)
        dproj_ref[v_rows, :] = (d_values * slope_ref[v_rows, :]).astype(BF16)
        dproj_ref[q_rows, :] = (d_queries * slope_ref[q_rows, :]).astype(BF16)
        dproj_ref[k_rows, :] = (d_keys * slope_ref[k_rows, :]).astype(BF16)
    d_normed = dot_nn(w_in_ref[...], dproj_ref[...])
    d_embedded = norm_backward(d_normed * gain_in_ref[...], normal_in, inverse_in)
    grads = (cotangent + d_embedded).astype(BF16)
    grad_ref[...] = grads
    owners = packed_ref.shape[0]
    store_packed(pack_grads(grads, ids_ref[pl.ds(me_ref[0], 1), :], 0, owners, own), packed_ref)


def run_layer(me, lengths, valid_ids, received, w_in, w_out, gain_in, gain_mid, owners, own):
    peers, both, positions = received.shape
    features, width = both // 2, w_out.shape[0]
    smem, vmem = pl.BlockSpec(memory_space=pltpu.SMEM), pl.BlockSpec(memory_space=pltpu.VMEM)
    shape = jax.ShapeDtypeStruct((width, positions), BF16)
    return pl.pallas_call(
        functools.partial(layer_kernel, own),
        out_shape=[
            shape,
            shape,
            jax.ShapeDtypeStruct((owners, peers, features, CAPACITY), BF16),
        ],
        in_specs=[smem] * 2 + [vmem] * 8,
        out_specs=[vmem] * 3,
        scratch_shapes=[
            pltpu.VMEM((width, positions), BF16),
            pltpu.VMEM((width, positions), BF16),
            pltpu.VMEM((4 * width, positions), BF16),
            pltpu.VMEM((4 * width, positions), F32),
            pltpu.VMEM((HEADS, positions, positions), BF16),
            pltpu.VMEM((HEADS, positions, positions), F32),
            pltpu.VMEM((width, positions), F32),
            pltpu.VMEM((4 * width, positions), BF16),
        ],
        compiler_params=pltpu.CompilerParams(vmem_limit_bytes=VMEM_BYTES),
        cost_estimate=pl.CostEstimate(flops=3 * 10**9, bytes_accessed=10**7, transcendentals=10**6),
        name="layer",
    )(
        me,
        lengths,
        valid_ids,
        received,
        w_in,
        w_in.T,
        w_out,
        w_out.T,
        gain_in.reshape(width, 1),
        gain_mid.reshape(width, 1),
    )


def pack_kernel(own, me_ref, turn_ref, ids_ref, grad_ref, packed_ref):
    owners = packed_ref.shape[0]
    items = ids_ref[pl.ds(me_ref[0], 1), :]
    store_packed(pack_grads(grad_ref[...], items, turn_ref[0], owners, own), packed_ref)


def pack_turn(me, turn, valid_ids, grads, owners, own):
    peers = valid_ids.shape[0]
    smem, vmem = pl.BlockSpec(memory_space=pltpu.SMEM), pl.BlockSpec(memory_space=pltpu.VMEM)
    return pl.pallas_call(
        functools.partial(pack_kernel, own),
        out_shape=jax.ShapeDtypeStruct((owners, peers, grads.shape[0] // peers, CAPACITY), BF16),
        in_specs=[smem, smem, vmem, vmem],
        out_specs=vmem,
        compiler_params=pltpu.CompilerParams(vmem_limit_bytes=VMEM_BYTES),
        name="pack_turn",
    )(me, turn, valid_ids, grads)


LOW = 256
STACK = 8


def plan_kernel(own, home_ref, turn_ref, *refs):
    groups = len(refs) - 3
    id_refs, (low_ref, high_ref, most_ref) = refs[:groups], refs[groups:]
    users, positions = id_refs[0].shape
    digit = lax.broadcasted_iota(jnp.int32, (LOW, positions), 0)
    place = lax.broadcasted_iota(jnp.int32, (CAPACITY, positions), 0)
    most = jnp.zeros((users, 1), F32)
    for group in range(groups):
        source = home_ref[0] ^ group
        items = id_refs[group][...]
        for owner in range(groups):
            count = jnp.sum(jnp.where(items // own == owner, 1.0, 0.0), axis=1, keepdims=True)
            most = jnp.maximum(most, count)
        local = items - home_ref[0] * own
        mine = (local >= 0) & (local < own)
        rank = ranks(jnp.where(mine, 1.0, 0.0)) - turn_ref[0] * CAPACITY
        slot = jnp.where(mine, rank, -1)
        low = local % LOW
        high = jnp.where(mine, local // LOW + 1, 0).astype(F32)
        for user in range(users):
            chosen = jnp.where(place == slot[user : user + 1], 1.0, 0.0).astype(BF16)
            digits = jnp.where(digit == low[user : user + 1], 1.0, 0.0).astype(BF16)
            low_ref[source * users + user] = dot_nt(chosen, digits).astype(BF16)
            wide_high = jnp.broadcast_to(high[user : user + 1], (16, positions)).astype(BF16)
            high_ref[pl.ds(source * users + user, 1), :] = dot_nt(wide_high, chosen)[:1]
    most_ref[0] = jnp.max(most).astype(jnp.int32)


def plan_turn(home, turn, all_ids, own):
    groups = len(all_ids)
    users = all_ids[0].shape[0]
    smem, vmem = pl.BlockSpec(memory_space=pltpu.SMEM), pl.BlockSpec(memory_space=pltpu.VMEM)
    return pl.pallas_call(
        functools.partial(plan_kernel, own),
        out_shape=[
            jax.ShapeDtypeStruct((groups * users, CAPACITY, LOW), BF16),
            jax.ShapeDtypeStruct((groups * users, CAPACITY), F32),
            jax.ShapeDtypeStruct((1,), jnp.int32),
        ],
        in_specs=[smem, smem] + [vmem] * groups,
        out_specs=[vmem, vmem, smem],
        compiler_params=pltpu.CompilerParams(vmem_limit_bytes=VMEM_BYTES),
        cost_estimate=pl.CostEstimate(flops=10**9, bytes_accessed=10**7, transcendentals=0),
        name="plan_turn",
    )(home, turn, *all_ids)


def scatter_kernel(stack, low_ref, high_ref, recv_ref, *refs):
    *before_ref, out_ref, spread_ref = refs
    users, features, capacity = recv_ref.shape
    step = pl.program_id(0)
    for user in range(users):
        high = high_ref[pl.ds(user, 1), :]
        for part in range(stack):
            wanted = (step * stack + part + 1).astype(F32)
            chosen = jnp.where(high == wanted, 1.0, 0.0).astype(BF16)
            spread_ref[pl.ds(part * features, features), pl.ds(user * capacity, capacity)] = (
                recv_ref[user] * chosen
            )
    sums = dot_nn(spread_ref[...], low_ref[...])
    for part in range(stack):
        columns = pl.ds(part * LOW, LOW)
        term = sums[part * features : (part + 1) * features]
        out_ref[:, columns] = term + before_ref[0][:, columns] if before_ref else term


def scatter_slots(low, high, received, own, before=None):
    users, features, capacity = received.shape
    stack = min(STACK, own // LOW)
    block = pl.BlockSpec((features, stack * LOW), lambda i: (0, i))
    extra = [] if before is None else [before]
    return pl.pallas_call(
        functools.partial(scatter_kernel, stack),
        grid=(own // (LOW * stack),),
        out_shape=jax.ShapeDtypeStruct((features, own), F32),
        in_specs=[
            pl.BlockSpec((users * capacity, LOW), lambda i: (0, 0)),
            pl.BlockSpec(high.shape, lambda i: (0, 0)),
            pl.BlockSpec(received.shape, lambda i: (0, 0, 0)),
        ]
        + [block] * len(extra),
        out_specs=block,
        scratch_shapes=[pltpu.VMEM((stack * features, users * capacity), BF16)],
        input_output_aliases={3: 0} if extra else {},
        compiler_params=pltpu.CompilerParams(vmem_limit_bytes=VMEM_BYTES),
        cost_estimate=pl.CostEstimate(flops=4 * 10**9, bytes_accessed=10**7, transcendentals=0),
        name="scatter_slots",
    )(low.reshape(users * capacity, LOW), high, received, *extra)


def join_kernel(parts_ref, out_ref):
    peers, _, positions = parts_ref.shape
    for peer in range(peers):
        out_ref[:, pl.ds(peer * positions, positions)] = parts_ref[peer]


def join_columns(parts):
    peers, features, positions = parts.shape
    vmem = pl.BlockSpec(memory_space=pltpu.VMEM)
    return pl.pallas_call(
        join_kernel,
        out_shape=jax.ShapeDtypeStruct((features, positions * peers), parts.dtype),
        in_specs=[vmem],
        out_specs=vmem,
        name="join_columns",
    )(parts)


def swap(value, axis, distance):
    size = lax.axis_size(axis)
    return lax.ppermute(value, axis, [(i, i ^ distance) for i in range(size)])


def exchange(value, axis):
    return lax.all_to_all(value, axis, split_axis=0, concat_axis=0, tiled=True)


def on_device(item_ids, user_len, emb_table, cotangent, w_uvqk, w_out, gain_in, gain_mid):
    dp_size = lax.axis_size("dp")
    table_size = lax.axis_size("table")
    users = user_len.shape[0]
    features, vocab = emb_table.shape
    positions = item_ids.shape[0] // users
    own = vocab // dp_size
    assert users == table_size and positions <= 256 and own // LOW <= 255
    assert dp_size & (dp_size - 1) == 0
    me = lax.axis_index("table").astype(jnp.int32).reshape(1)
    home = lax.axis_index("dp").astype(jnp.int32).reshape(1)

    ids = item_ids.reshape(users, positions)
    order = jnp.arange(positions, dtype=jnp.int32)
    valid_ids = jnp.where(order[None, :] < user_len[:, None], ids, vocab)
    all_ids = [valid_ids] + [swap(valid_ids, "dp", k) for k in range(1, dp_size)]
    received = exchange(gather_columns(item_ids, ids, cotangent, emb_table), "table")
    first = jnp.zeros((1,), jnp.int32)
    low, high, most = plan_turn(home, first, all_ids, own)
    out_cols, grads, packed = run_layer(
        me, user_len, valid_ids, received, w_uvqk, w_out, gain_in, gain_mid, dp_size, own
    )
    flat = (dp_size * table_size, features, CAPACITY)
    slots = exchange(packed.reshape(flat), ("dp", "table"))
    out_home = exchange(out_cols.reshape(table_size, features, positions), "table")
    table_grad = scatter_slots(low, high, slots, own)
    layer_out = join_columns(out_home)

    turns = (most[0] + CAPACITY - 1) // CAPACITY

    def another(state):
        turn, sums = state
        at = turn.reshape(1)
        more = pack_turn(me, at, valid_ids, grads, dp_size, own)
        more_low, more_high, _ = plan_turn(home, at, all_ids, own)
        arrived = exchange(more.reshape(flat), ("dp", "table"))
        return turn + 1, scatter_slots(more_low, more_high, arrived, own, sums)

    _, table_grad = lax.while_loop(
        lambda state: state[0] < turns, another, (jnp.int32(1), table_grad)
    )
    return (layer_out, table_grad)


def solution(mesh):
    return jax.shard_map(
        on_device,
        mesh=mesh,
        in_specs=(P("dp"), P("dp"), P("table", None), P("table", "dp"), P(), P(), P(), P()),
        out_specs=(P("table", "dp"), P("table", "dp")),
        check_vma=False,
    )
```

```python
import functools

import jax
import jax.numpy as jnp
from jax import lax
from jax.experimental import pallas as pl
from jax.experimental.pallas import tpu as pltpu
from jax.sharding import PartitionSpec as P

HEADS = 8
NORM_EPS = 1e-05
LANES = 128
VMEM_BYTES = 48 * 1024 * 1024

F32 = jnp.float32
BF16 = jnp.bfloat16


def dot_nn(left, right):
    return jnp.dot(left, right, preferred_element_type=F32)


def dot_nt(left, right):
    return lax.dot_general(left, right, (((1,), (1,)), ((), ())), preferred_element_type=F32)


def dot_tn(left, right):
    return lax.dot_general(left, right, (((0,), (0,)), ((), ())), preferred_element_type=F32)


BLOCK = 256
UNROLL = 32


def gather_kernel(ids_ref, wide_ids_ref, table_ref, out_ref, rows_ref, picked_ref):
    users, positions = wide_ids_ref.shape
    features, wide = table_ref.shape
    pack = LANES // features
    span = BLOCK * pack
    span_bits, block_bits = span.bit_length() - 1, BLOCK.bit_length() - 1
    step = pl.program_id(0)
    for part in range(wide // span):
        stack = jnp.concatenate(
            [
                table_ref[:, part * span + s * BLOCK : part * span + (s + 1) * BLOCK]
                for s in range(pack)
            ],
            axis=0,
        )
        at = pl.multiple_of((step * (wide // span) + part) * BLOCK, BLOCK)
        rows_ref[pl.ds(at, BLOCK), :] = stack.astype(F32).T

    @pl.when(step == pl.num_programs(0) - 1)
    def _():
        row = lax.broadcasted_iota(jnp.int32, (LANES, LANES), 0)
        column = lax.broadcasted_iota(jnp.int32, (LANES, LANES), 1)
        same = jnp.where(row == column, 1.0, 0.0).astype(BF16)
        for user in range(users):

            def some(part, carry):
                for slot in range(UNROLL):
                    position = part * UNROLL + slot
                    item = ids_ref[user * positions + position]
                    item_row = ((item >> span_bits) << block_bits) | (item & (BLOCK - 1))
                    picked_ref[pl.ds(position, 1), :] = rows_ref[pl.ds(item_row, 1), :]
                return carry

            lax.fori_loop(0, positions // UNROLL, some, 0)
            turned = dot_nt(same, picked_ref[...].astype(BF16))
            group = (wide_ids_ref[pl.ds(user, 1), :] >> block_bits) & (pack - 1)
            total = jnp.zeros((features, positions), F32)
            for s in range(pack):
                total += jnp.where(group == s, turned[s * features : (s + 1) * features], 0.0)
            out_ref[user] = total.astype(BF16)


def gather_columns(item_ids, wide_ids, table):
    users, positions = wide_ids.shape
    features, vocab = table.shape
    pack = LANES // features
    wide = 8 * BLOCK * pack
    shape = (users, features, positions)
    return pl.pallas_call(
        gather_kernel,
        grid=(vocab // wide,),
        out_shape=jax.ShapeDtypeStruct(shape, table.dtype),
        in_specs=[
            pl.BlockSpec(memory_space=pltpu.SMEM),
            pl.BlockSpec(wide_ids.shape, lambda i: (0, 0)),
            pl.BlockSpec((features, wide), lambda i: (0, i)),
        ],
        out_specs=pl.BlockSpec(shape, lambda i: (0, 0, 0)),
        scratch_shapes=[
            pltpu.VMEM((vocab // pack, LANES), F32),
            pltpu.VMEM((positions, LANES), F32),
        ],
        compiler_params=pltpu.CompilerParams(vmem_limit_bytes=VMEM_BYTES),
        cost_estimate=pl.CostEstimate(flops=8 * 10**9, bytes_accessed=5 * 10**6, transcendentals=0),
        name="gather_columns",
    )(item_ids, wide_ids, table)


def norm_forward(values):
    centred = values - jnp.mean(values, axis=0, keepdims=True)
    inverse = lax.rsqrt(jnp.mean(centred * centred, axis=0, keepdims=True) + NORM_EPS)
    return centred * inverse, inverse


def norm_backward(grad, normal, inverse):
    shift = jnp.mean(grad, axis=0, keepdims=True)
    slope = jnp.mean(grad * normal, axis=0, keepdims=True)
    return (grad - shift - normal * slope) * inverse


def silu_pair(z):
    gate = 0.5 + 0.5 * jnp.tanh(0.5 * z)
    value = z * gate
    return value, gate + value * (1.0 - gate)


def layer_kernel(
    me_ref,
    len_ref,
    emb_ref,
    cot_ref,
    w_in_ref,
    w_in_t_ref,
    w_out_ref,
    w_out_t_ref,
    gain_in_ref,
    gain_mid_ref,
    out_ref,
    grad_ref,
    proj_ref,
    slope_ref,
    weight_ref,
    score_slope_ref,
    att_ref,
    dproj_ref,
):
    width, positions = emb_ref.shape
    head_dim = width // HEADS
    half = positions // 2
    length = len_ref[me_ref[0]]
    share = 1.0 / length.astype(F32)

    embedded = emb_ref[...].astype(F32)
    normal_in, inverse_in = norm_forward(embedded)
    normed = (normal_in * gain_in_ref[...]).astype(BF16)
    for part in range(4):
        rows = pl.ds(part * width, width)
        value, slope = silu_pair(dot_nn(w_in_t_ref[rows, :], normed))
        proj_ref[rows, :] = value.astype(BF16)
        slope_ref[rows, :] = slope

    def mask(key_start, query_start, shape):
        key = lax.broadcasted_iota(jnp.int32, shape, 0) + key_start
        query = lax.broadcasted_iota(jnp.int32, shape, 1) + query_start
        return (key <= query) & (key < length)

    low = mask(0, 0, (half, positions))
    high = mask(half, half, (half, half))
    scale = head_dim ** (-0.5)
    for head in range(HEADS):
        at = head * head_dim
        values = proj_ref[pl.ds(width + at, head_dim), :]
        queries = proj_ref[pl.ds(2 * width + at, head_dim), :]
        keys = proj_ref[pl.ds(3 * width + at, head_dim), :]
        for start, allowed in ((0, low), (half, high)):
            scores = dot_tn(keys[:, start : start + half], queries[:, start:]) * scale
            value, slope = silu_pair(scores)
            weight_ref[head, pl.ds(start, half), pl.ds(start, positions - start)] = jnp.where(
                allowed, value * share, 0.0
            ).astype(BF16)
            score_slope_ref[head, pl.ds(start, half), pl.ds(start, positions - start)] = jnp.where(
                allowed, slope * (share * scale), 0.0
            )
        weight_ref[head, pl.ds(half, half), pl.ds(0, half)] = jnp.zeros((half, half), BF16)
        att_ref[pl.ds(at, head_dim), :] = dot_nn(values, weight_ref[head])

    normal_mid, inverse_mid = norm_forward(att_ref[...])
    gate_rows = proj_ref[pl.ds(0, width), :].astype(F32)
    scaled = normal_mid * gain_mid_ref[...]
    mixed = (scaled * gate_rows).astype(BF16)
    out_ref[...] = (embedded + dot_nn(w_out_t_ref[...], mixed)).astype(BF16)

    valid = lax.broadcasted_iota(jnp.int32, (width, positions), 1) < length
    cotangent = jnp.where(valid, cot_ref[...].astype(F32), 0.0)
    d_mixed = dot_nn(w_out_ref[...], cotangent.astype(BF16))
    dproj_ref[pl.ds(0, width), :] = (d_mixed * scaled * slope_ref[pl.ds(0, width), :]).astype(BF16)
    d_att = norm_backward(d_mixed * gate_rows * gain_mid_ref[...], normal_mid, inverse_mid)
    att_ref[...] = d_att
    for head in range(HEADS):
        at = head * head_dim
        v_rows = pl.ds(width + at, head_dim)
        q_rows = pl.ds(2 * width + at, head_dim)
        k_rows = pl.ds(3 * width + at, head_dim)
        values, queries, keys = proj_ref[v_rows, :], proj_ref[q_rows, :], proj_ref[k_rows, :]
        d_head = att_ref[pl.ds(at, head_dim), :].astype(BF16)
        low_scores = (
            dot_tn(values[:, :half], d_head) * score_slope_ref[head, pl.ds(0, half), :]
        ).astype(BF16)
        high_scores = (
            dot_tn(values[:, half:], d_head[:, half:])
            * score_slope_ref[head, pl.ds(half, half), pl.ds(half, half)]
        ).astype(BF16)
        d_scores = jnp.concatenate(
            [
                low_scores,
                jnp.concatenate([jnp.zeros((half, half), BF16), high_scores], axis=1),
            ],
            axis=0,
        )
        d_values = dot_nt(d_head, weight_ref[head])
        d_queries = dot_nn(keys, d_scores)
        d_keys = dot_nt(queries, d_scores)
        dproj_ref[v_rows, :] = (d_values * slope_ref[v_rows, :]).astype(BF16)
        dproj_ref[q_rows, :] = (d_queries * slope_ref[q_rows, :]).astype(BF16)
        dproj_ref[k_rows, :] = (d_keys * slope_ref[k_rows, :]).astype(BF16)
    d_normed = dot_nn(w_in_ref[...], dproj_ref[...])
    d_embedded = norm_backward(d_normed * gain_in_ref[...], normal_in, inverse_in)
    grad_ref[...] = (cotangent + d_embedded).astype(BF16)


def run_layer(me, lengths, embedded, cotangent, w_in, w_out, gain_in, gain_mid):
    width, positions = embedded.shape
    smem, vmem = pl.BlockSpec(memory_space=pltpu.SMEM), pl.BlockSpec(memory_space=pltpu.VMEM)
    shape = jax.ShapeDtypeStruct((width, positions), BF16)
    return pl.pallas_call(
        layer_kernel,
        out_shape=[shape, shape],
        in_specs=[smem] * 2 + [vmem] * 8,
        out_specs=[vmem] * 2,
        scratch_shapes=[
            pltpu.VMEM((4 * width, positions), BF16),
            pltpu.VMEM((4 * width, positions), F32),
            pltpu.VMEM((HEADS, positions, positions), BF16),
            pltpu.VMEM((HEADS, positions, positions), F32),
            pltpu.VMEM((width, positions), F32),
            pltpu.VMEM((4 * width, positions), BF16),
        ],
        compiler_params=pltpu.CompilerParams(vmem_limit_bytes=VMEM_BYTES),
        cost_estimate=pl.CostEstimate(flops=10**10, bytes_accessed=10**7, transcendentals=10**6),
        name="layer",
    )(
        me,
        lengths,
        embedded,
        cotangent,
        w_in,
        w_in.T,
        w_out,
        w_out.T,
        gain_in.reshape(width, 1),
        gain_mid.reshape(width, 1),
    )


LOW = 256
STACK = 8


def ranks(member):
    users, positions = member.shape
    ones = jnp.where(member, 1.0, 0.0)
    row = lax.broadcasted_iota(jnp.int32, (positions, positions), 0)
    column = lax.broadcasted_iota(jnp.int32, (positions, positions), 1)
    before = jnp.where(row < column, 1.0, 0.0).astype(BF16)
    totals = jnp.sum(ones, axis=1, keepdims=True)
    user = lax.broadcasted_iota(jnp.int32, (users, 1), 0)
    earlier = jnp.zeros((users, 1), F32)
    for other in range(users - 1):
        earlier += jnp.where(user > other, totals[other : other + 1], 0.0)
    rank = dot_nn(ones.astype(BF16), before) + earlier
    return rank.astype(jnp.int32), jnp.sum(totals)


def plan_kernel(own, home_ref, turn_ref, ids_ref, low_ref, high_ref, slot_ref, most_ref, *scratch):
    chosen_ref, digit_ref, wide_ref = scratch
    groups, users, positions = ids_ref.shape
    capacity = low_ref.shape[1]
    home = home_ref[0]
    first = turn_ref[0] * capacity
    digit = lax.broadcasted_iota(jnp.int32, (LOW, positions), 0)
    place = lax.broadcasted_iota(jnp.int32, (capacity, positions), 0)

    def one_group(group, most):
        items = ids_ref[group]
        for owner in range(groups):
            count = jnp.sum(jnp.where(items // own == owner, 1.0, 0.0))
            most = jnp.maximum(most, count)
        local = items - home * own
        mine = (local >= 0) & (local < own)
        rank, _ = ranks(mine)
        slot = jnp.where(mine, rank - first, -1)
        low = local & (LOW - 1)
        high = jnp.where(mine, (local >> (LOW.bit_length() - 1)) + 1, 0).astype(F32)
        for user in range(users):
            columns = pl.ds(user * positions, positions)
            chosen_ref[:, columns] = jnp.where(place == slot[user : user + 1], 1.0, 0.0).astype(BF16)
            digit_ref[:, columns] = jnp.where(digit == low[user : user + 1], 1.0, 0.0).astype(BF16)
            wide_ref[:, columns] = jnp.broadcast_to(high[user : user + 1], (16, positions)).astype(BF16)
        source = home ^ group
        low_ref[source] = dot_nt(chosen_ref[...], digit_ref[...]).astype(BF16)
        high_ref[pl.ds(source, 1), :] = dot_nt(wide_ref[...], chosen_ref[...])[:1]
        return most

    most_ref[0] = lax.fori_loop(0, groups, one_group, jnp.float32(0)).astype(jnp.int32)

    items = ids_ref[0]
    slot = jnp.full(items.shape, -1, jnp.int32)
    for owner in range(groups):
        belongs = items // own == owner
        rank = ranks(belongs)[0] - first
        fits = belongs & (rank >= 0) & (rank < capacity)
        slot = jnp.where(fits, rank + owner * capacity, slot)
    padded = jnp.concatenate(
        [slot.astype(F32), jnp.zeros((LANES - users, positions), F32)], axis=0
    )
    slot_ref[...] = padded.T.astype(jnp.int32)


def plan_turn(home, turn, all_ids, own, capacity):
    groups, users, positions = all_ids.shape
    smem, vmem = pl.BlockSpec(memory_space=pltpu.SMEM), pl.BlockSpec(memory_space=pltpu.VMEM)
    return pl.pallas_call(
        functools.partial(plan_kernel, own),
        out_shape=[
            jax.ShapeDtypeStruct((groups, capacity, LOW), BF16),
            jax.ShapeDtypeStruct((groups, capacity), F32),
            jax.ShapeDtypeStruct((positions, LANES), jnp.int32),
            jax.ShapeDtypeStruct((1,), jnp.int32),
        ],
        in_specs=[smem, smem, vmem],
        out_specs=[vmem, vmem, vmem, smem],
        scratch_shapes=[
            pltpu.VMEM((capacity, users * positions), BF16),
            pltpu.VMEM((LOW, users * positions), BF16),
            pltpu.VMEM((16, users * positions), BF16),
        ],
        compiler_params=pltpu.CompilerParams(vmem_limit_bytes=VMEM_BYTES),
        cost_estimate=pl.CostEstimate(flops=4 * 10**9, bytes_accessed=5 * 10**6, transcendentals=0),
        name="plan_turn",
    )(home, turn, all_ids)


def pack_kernel(slot_ref, grad_ref, packed_ref, wide_ref, chosen_ref):
    users, _, positions = grad_ref.shape
    capacity = packed_ref.shape[2]
    owner = pl.program_id(0)
    place = lax.broadcasted_iota(jnp.int32, (positions, capacity), 1) + owner * capacity
    for user in range(users):
        rows = pl.ds(user * positions, positions)
        wide_ref[:, rows] = grad_ref[user]
        slot = slot_ref[:, user : user + 1]
        chosen_ref[rows, :] = jnp.where(place == slot, 1.0, 0.0).astype(BF16)
    packed_ref[0] = dot_nn(wide_ref[...], chosen_ref[...]).astype(BF16)


def pack_turn(slot, grads, owners, capacity):
    users, features, positions = grads.shape
    return pl.pallas_call(
        pack_kernel,
        grid=(owners,),
        out_shape=jax.ShapeDtypeStruct((owners, features, capacity), BF16),
        in_specs=[
            pl.BlockSpec(slot.shape, lambda i: (0, 0)),
            pl.BlockSpec(grads.shape, lambda i: (0, 0, 0)),
        ],
        out_specs=pl.BlockSpec((1, features, capacity), lambda i: (i, 0, 0)),
        scratch_shapes=[
            pltpu.VMEM((features, users * positions), BF16),
            pltpu.VMEM((users * positions, capacity), BF16),
        ],
        compiler_params=pltpu.CompilerParams(vmem_limit_bytes=VMEM_BYTES),
        cost_estimate=pl.CostEstimate(flops=3 * 10**9, bytes_accessed=10**6, transcendentals=0),
        name="pack_turn",
    )(slot, grads)


def scatter_kernel(stack, low_ref, high_ref, recv_ref, *refs):
    *before_ref, out_ref, spread_ref = refs
    users, features, capacity = recv_ref.shape
    step = pl.program_id(0)
    for user in range(users):
        high = high_ref[pl.ds(user, 1), :]
        for part in range(stack):
            wanted = (step * stack + part + 1).astype(F32)
            chosen = jnp.where(high == wanted, 1.0, 0.0).astype(BF16)
            spread_ref[pl.ds(part * features, features), pl.ds(user * capacity, capacity)] = (
                recv_ref[user] * chosen
            )
    sums = dot_nn(spread_ref[...], low_ref[...])
    for part in range(stack):
        columns = pl.ds(part * LOW, LOW)
        term = sums[part * features : (part + 1) * features]
        out_ref[:, columns] = term + before_ref[0][:, columns] if before_ref else term


def scatter_slots(low, high, received, own, before=None):
    users, features, capacity = received.shape
    stack = min(STACK, own // LOW)
    block = pl.BlockSpec((features, stack * LOW), lambda i: (0, i))
    extra = [] if before is None else [before]
    return pl.pallas_call(
        functools.partial(scatter_kernel, stack),
        grid=(own // (LOW * stack),),
        out_shape=jax.ShapeDtypeStruct((features, own), F32),
        in_specs=[
            pl.BlockSpec((users * capacity, LOW), lambda i: (0, 0)),
            pl.BlockSpec(high.shape, lambda i: (0, 0)),
            pl.BlockSpec(received.shape, lambda i: (0, 0, 0)),
        ]
        + [block] * len(extra),
        out_specs=block,
        scratch_shapes=[pltpu.VMEM((stack * features, users * capacity), BF16)],
        input_output_aliases={3: 0} if extra else {},
        compiler_params=pltpu.CompilerParams(vmem_limit_bytes=VMEM_BYTES),
        cost_estimate=pl.CostEstimate(flops=4 * 10**9, bytes_accessed=10**7, transcendentals=0),
        name="scatter_slots",
    )(low.reshape(users * capacity, LOW), high, received, *extra)


def swap(value, axis, distance):
    size = lax.axis_size(axis)
    return lax.ppermute(value, axis, [(i, i ^ distance) for i in range(size)])


def exchange(value, axis):
    return lax.all_to_all(value, axis, split_axis=0, concat_axis=0, tiled=True)


def on_device(item_ids, user_len, emb_table, cotangent, w_uvqk, w_out, gain_in, gain_mid):
    dp_size = lax.axis_size("dp")
    table_size = lax.axis_size("table")
    users = user_len.shape[0]
    features, vocab = emb_table.shape
    rows = item_ids.shape[0]
    positions = rows // users
    width = features * table_size
    own = vocab // dp_size
    capacity = -(-(rows // dp_size * 5 // 4) // LANES) * LANES
    assert users == table_size and users <= LANES and positions <= 256 and own // LOW <= 255
    assert dp_size & (dp_size - 1) == 0
    me = lax.axis_index("table").astype(jnp.int32).reshape(1)
    home = lax.axis_index("dp").astype(jnp.int32).reshape(1)

    cot_send = jnp.transpose(cotangent.reshape(features, users, positions), (1, 0, 2))
    cot_cols = exchange(cot_send, "table")
    ids = item_ids.reshape(users, positions)
    order = jnp.arange(positions, dtype=jnp.int32)
    valid_ids = jnp.where(order[None, :] < user_len[:, None], ids, vocab)
    emb_send = gather_columns(item_ids, ids, emb_table)
    emb_cols = exchange(emb_send, "table")
    all_ids = jnp.stack([valid_ids] + [swap(valid_ids, "dp", k) for k in range(1, dp_size)])
    all_ids, _ = lax.optimization_barrier((all_ids, emb_send))
    low, high, slot, most = plan_turn(home, jnp.zeros((1,), jnp.int32), all_ids, own, capacity)
    emb_cols, low, high, slot = lax.optimization_barrier((emb_cols, low, high, slot))
    out_cols, grad_cols = run_layer(
        me,
        user_len,
        emb_cols.reshape(width, positions),
        cot_cols.reshape(width, positions),
        w_uvqk,
        w_out,
        gain_in,
        gain_mid,
    )
    per_peer = (table_size, features, positions)
    grad_home = exchange(grad_cols.reshape(per_peer), "table")
    packed = pack_turn(slot, grad_home, dp_size, capacity)
    out_cols, packed = lax.optimization_barrier((out_cols, packed))
    lists = exchange(packed, "dp")
    out_home = exchange(out_cols.reshape(per_peer), "table")
    table_grad = scatter_slots(low, high, lists, own)
    layer_out = jnp.transpose(out_home, (1, 0, 2)).reshape(features, rows)

    turns = (most[0] + capacity - 1) // capacity

    def another(state):
        turn, sums = state
        more_low, more_high, more_slot, _ = plan_turn(home, turn.reshape(1), all_ids, own, capacity)
        arrived = exchange(pack_turn(more_slot, grad_home, dp_size, capacity), "dp")
        return turn + 1, scatter_slots(more_low, more_high, arrived, own, sums)

    _, table_grad = lax.while_loop(
        lambda state: state[0] < turns, another, (jnp.int32(1), table_grad)
    )
    return (layer_out, table_grad)


def solution(mesh):
    return jax.shard_map(
        on_device,
        mesh=mesh,
        in_specs=(P("dp"), P("dp"), P("table", None), P("table", "dp"), P(), P(), P(), P()),
        out_specs=(P("table", "dp"), P("table", "dp")),
        check_vma=False,
    )
```

```python
import functools

import jax
import jax.numpy as jnp
from jax import lax
from jax.experimental import pallas as pl
from jax.experimental.pallas import tpu as pltpu
from jax.sharding import PartitionSpec as P

HEADS = 8
NORM_EPS = 1e-05
LANES = 128
VMEM_BYTES = 48 * 1024 * 1024

F32 = jnp.float32
BF16 = jnp.bfloat16


def dot_nn(left, right):
    return jnp.dot(left, right, preferred_element_type=F32)


def dot_nt(left, right):
    return lax.dot_general(left, right, (((1,), (1,)), ((), ())), preferred_element_type=F32)


def dot_tn(left, right):
    return lax.dot_general(left, right, (((0,), (0,)), ((), ())), preferred_element_type=F32)


BLOCK = 256
UNROLL = 32


def gather_kernel(row_ref, ids_ref, table_ref, out_ref, rows_ref, picked_ref):
    users, _, positions = out_ref.shape
    features, wide = table_ref.shape
    pack = LANES // features
    span = BLOCK * pack
    step = pl.program_id(0)
    for part in range(wide // span):
        stack = jnp.concatenate(
            [
                table_ref[:, part * span + s * BLOCK : part * span + (s + 1) * BLOCK]
                for s in range(pack)
            ],
            axis=0,
        )
        at = pl.multiple_of((step * (wide // span) + part) * BLOCK, BLOCK)
        rows_ref[pl.ds(at, BLOCK), :] = stack.astype(F32).T

    @pl.when(step == pl.num_programs(0) - 1)
    def _():
        row = lax.broadcasted_iota(jnp.int32, (LANES, LANES), 0)
        column = lax.broadcasted_iota(jnp.int32, (LANES, LANES), 1)
        same = jnp.where(row == column, 1.0, 0.0).astype(BF16)
        for user in range(users):

            def some(part, carry):
                for slot in range(UNROLL):
                    position = part * UNROLL + slot
                    row = row_ref[user * positions + position]
                    picked_ref[pl.ds(position, 1), :] = rows_ref[pl.ds(row, 1), :]
                return carry

            lax.fori_loop(0, positions // UNROLL, some, 0)
            turned = dot_nt(same, picked_ref[...].astype(BF16))
            items = ids_ref[pl.ds(user * positions, positions)].reshape(1, positions)
            group = (items >> (BLOCK.bit_length() - 1)) & (pack - 1)
            total = jnp.zeros((features, positions), F32)
            for s in range(pack):
                total += jnp.where(group == s, turned[s * features : (s + 1) * features], 0.0)
            out_ref[user] = total.astype(BF16)


def gather_columns(item_ids, table, users):
    positions = item_ids.shape[0] // users
    features, vocab = table.shape
    pack = LANES // features
    wide = 8 * BLOCK * pack
    shape = (users, features, positions)
    row = ((item_ids >> ((BLOCK * pack).bit_length() - 1)) * BLOCK) | (item_ids & (BLOCK - 1))
    return pl.pallas_call(
        gather_kernel,
        grid=(vocab // wide,),
        out_shape=jax.ShapeDtypeStruct(shape, table.dtype),
        in_specs=[
            pl.BlockSpec(memory_space=pltpu.SMEM),
            pl.BlockSpec(item_ids.shape, lambda i: (0,)),
            pl.BlockSpec((features, wide), lambda i: (0, i)),
        ],
        out_specs=pl.BlockSpec(shape, lambda i: (0, 0, 0)),
        scratch_shapes=[
            pltpu.VMEM((vocab // pack, LANES), F32),
            pltpu.VMEM((positions, LANES), F32),
        ],
        compiler_params=pltpu.CompilerParams(vmem_limit_bytes=61 * 1024 * 1024),
        cost_estimate=pl.CostEstimate(flops=8 * 10**9, bytes_accessed=5 * 10**6, transcendentals=0),
        name="gather_columns",
    )(row, item_ids, table)


def norm_forward(values):
    centred = values - jnp.mean(values, axis=0, keepdims=True)
    inverse = lax.rsqrt(jnp.mean(centred * centred, axis=0, keepdims=True) + NORM_EPS)
    return centred * inverse, inverse


def norm_backward(grad, normal, inverse):
    shift = jnp.mean(grad, axis=0, keepdims=True)
    slope = jnp.mean(grad * normal, axis=0, keepdims=True)
    return (grad - shift - normal * slope) * inverse


def silu_pair(z):
    gate = 0.5 + 0.5 * jnp.tanh(0.5 * z)
    value = z * gate
    return value, gate + value * (1.0 - gate)


def layer_kernel(
    me_ref,
    len_ref,
    emb_ref,
    cot_ref,
    w_in_ref,
    w_in_t_ref,
    w_out_ref,
    w_out_t_ref,
    gain_in_row_ref,
    gain_mid_row_ref,
    out_ref,
    grad_ref,
    proj_ref,
    slope_ref,
    weight_ref,
    score_slope_ref,
    att_ref,
    dproj_ref,
    gain_in_ref,
    gain_mid_ref,
):
    width, positions = emb_ref.shape
    head_dim = width // HEADS
    half = positions // 2
    length = len_ref[me_ref[0]]
    share = 1.0 / length.astype(F32)
    for row_ref, column_ref in ((gain_in_row_ref, gain_in_ref), (gain_mid_row_ref, gain_mid_ref)):
        row = row_ref[...].reshape(1, width)
        column_ref[...] = jnp.broadcast_to(row, (positions, width)).T

    embedded = emb_ref[...].astype(F32)
    normal_in, inverse_in = norm_forward(embedded)
    normed = (normal_in * gain_in_ref[...]).astype(BF16)
    for part in range(4):
        rows = pl.ds(part * width, width)
        value, slope = silu_pair(dot_nn(w_in_t_ref[rows, :], normed))
        proj_ref[rows, :] = value.astype(BF16)
        slope_ref[rows, :] = slope

    def mask(key_start, query_start, shape):
        key = lax.broadcasted_iota(jnp.int32, shape, 0) + key_start
        query = lax.broadcasted_iota(jnp.int32, shape, 1) + query_start
        return (key <= query) & (key < length)

    low = mask(0, 0, (half, positions))
    high = mask(half, half, (half, half))
    scale = head_dim ** (-0.5)
    for head in range(HEADS):
        at = head * head_dim
        values = proj_ref[pl.ds(width + at, head_dim), :]
        queries = proj_ref[pl.ds(2 * width + at, head_dim), :]
        keys = proj_ref[pl.ds(3 * width + at, head_dim), :]
        for start, allowed in ((0, low), (half, high)):
            scores = dot_tn(keys[:, start : start + half], queries[:, start:]) * scale
            value, slope = silu_pair(scores)
            weight_ref[head, pl.ds(start, half), pl.ds(start, positions - start)] = jnp.where(
                allowed, value * share, 0.0
            ).astype(BF16)
            score_slope_ref[head, pl.ds(start, half), pl.ds(start, positions - start)] = jnp.where(
                allowed, slope * (share * scale), 0.0
            )
        weight_ref[head, pl.ds(half, half), pl.ds(0, half)] = jnp.zeros((half, half), BF16)
        att_ref[pl.ds(at, head_dim), :] = dot_nn(values, weight_ref[head])

    normal_mid, inverse_mid = norm_forward(att_ref[...])
    gate_rows = proj_ref[pl.ds(0, width), :].astype(F32)
    scaled = normal_mid * gain_mid_ref[...]
    mixed = (scaled * gate_rows).astype(BF16)
    out_ref[...] = (embedded + dot_nn(w_out_t_ref[...], mixed)).astype(BF16)

    valid = lax.broadcasted_iota(jnp.int32, (width, positions), 1) < length
    cotangent = jnp.where(valid, cot_ref[...].astype(F32), 0.0)
    d_mixed = dot_nn(w_out_ref[...], cotangent.astype(BF16))
    dproj_ref[pl.ds(0, width), :] = (d_mixed * scaled * slope_ref[pl.ds(0, width), :]).astype(BF16)
    d_att = norm_backward(d_mixed * gate_rows * gain_mid_ref[...], normal_mid, inverse_mid)
    att_ref[...] = d_att
    for head in range(HEADS):
        at = head * head_dim
        v_rows = pl.ds(width + at, head_dim)
        q_rows = pl.ds(2 * width + at, head_dim)
        k_rows = pl.ds(3 * width + at, head_dim)
        values, queries, keys = proj_ref[v_rows, :], proj_ref[q_rows, :], proj_ref[k_rows, :]
        d_head = att_ref[pl.ds(at, head_dim), :].astype(BF16)
        low_scores = (
            dot_tn(values[:, :half], d_head) * score_slope_ref[head, pl.ds(0, half), :]
        ).astype(BF16)
        high_scores = (
            dot_tn(values[:, half:], d_head[:, half:])
            * score_slope_ref[head, pl.ds(half, half), pl.ds(half, half)]
        ).astype(BF16)
        d_scores = jnp.concatenate(
            [
                low_scores,
                jnp.concatenate([jnp.zeros((half, half), BF16), high_scores], axis=1),
            ],
            axis=0,
        )
        d_values = dot_nt(d_head, weight_ref[head])
        d_queries = dot_nn(keys, d_scores)
        d_keys = dot_nt(queries, d_scores)
        dproj_ref[v_rows, :] = (d_values * slope_ref[v_rows, :]).astype(BF16)
        dproj_ref[q_rows, :] = (d_queries * slope_ref[q_rows, :]).astype(BF16)
        dproj_ref[k_rows, :] = (d_keys * slope_ref[k_rows, :]).astype(BF16)
    d_normed = dot_nn(w_in_ref[...], dproj_ref[...])
    d_embedded = norm_backward(d_normed * gain_in_ref[...], normal_in, inverse_in)
    grad_ref[...] = (cotangent + d_embedded).astype(BF16)


def run_layer(me, lengths, embedded, cotangent, w_in, w_out, gain_in, gain_mid):
    width, positions = embedded.shape
    smem, vmem = pl.BlockSpec(memory_space=pltpu.SMEM), pl.BlockSpec(memory_space=pltpu.VMEM)
    shape = jax.ShapeDtypeStruct((width, positions), BF16)
    return pl.pallas_call(
        layer_kernel,
        out_shape=[shape, shape],
        in_specs=[smem] * 2 + [vmem] * 8,
        out_specs=[vmem] * 2,
        scratch_shapes=[
            pltpu.VMEM((4 * width, positions), BF16),
            pltpu.VMEM((4 * width, positions), F32),
            pltpu.VMEM((HEADS, positions, positions), BF16),
            pltpu.VMEM((HEADS, positions, positions), F32),
            pltpu.VMEM((width, positions), F32),
            pltpu.VMEM((4 * width, positions), BF16),
            pltpu.VMEM((width, positions), F32),
            pltpu.VMEM((width, positions), F32),
        ],
        compiler_params=pltpu.CompilerParams(vmem_limit_bytes=VMEM_BYTES),
        cost_estimate=pl.CostEstimate(flops=10**10, bytes_accessed=10**7, transcendentals=10**6),
        name="layer",
    )(
        me,
        lengths,
        embedded,
        cotangent,
        w_in,
        w_in.T,
        w_out,
        w_out.T,
        gain_in,
        gain_mid,
    )


LOW = 256
STACK = 8


def ranks(member):
    users, positions = member.shape
    ones = jnp.where(member, 1.0, 0.0)
    row = lax.broadcasted_iota(jnp.int32, (positions, positions), 0)
    column = lax.broadcasted_iota(jnp.int32, (positions, positions), 1)
    before = jnp.where(row < column, 1.0, 0.0).astype(BF16)
    totals = jnp.sum(ones, axis=1, keepdims=True)
    user = lax.broadcasted_iota(jnp.int32, (users, 1), 0)
    earlier = jnp.zeros((users, 1), F32)
    for other in range(users - 1):
        earlier += jnp.where(user > other, totals[other : other + 1], 0.0)
    rank = dot_nn(ones.astype(BF16), before) + earlier
    return rank.astype(jnp.int32), jnp.sum(totals)


def plan_kernel(own, home_ref, turn_ref, ids_ref, low_ref, high_ref, slot_ref, most_ref, *scratch):
    chosen_ref, digit_ref, wide_ref = scratch
    groups, users, positions = ids_ref.shape
    capacity = low_ref.shape[1]
    home = home_ref[0]
    first = turn_ref[0] * capacity
    digit = lax.broadcasted_iota(jnp.int32, (LOW, positions), 0)
    place = lax.broadcasted_iota(jnp.int32, (capacity, positions), 0)

    def one_group(group, most):
        items = ids_ref[group]
        for owner in range(groups):
            count = jnp.sum(jnp.where(items // own == owner, 1.0, 0.0))
            most = jnp.maximum(most, count)
        local = items - home * own
        mine = (local >= 0) & (local < own)
        rank, _ = ranks(mine)
        slot = jnp.where(mine, rank - first, -1)
        low = local & (LOW - 1)
        high = jnp.where(mine, (local >> (LOW.bit_length() - 1)) + 1, 0).astype(F32)
        for user in range(users):
            columns = pl.ds(user * positions, positions)
            chosen_ref[:, columns] = jnp.where(place == slot[user : user + 1], 1.0, 0.0).astype(BF16)
            digit_ref[:, columns] = jnp.where(digit == low[user : user + 1], 1.0, 0.0).astype(BF16)
            wide_ref[:, columns] = jnp.broadcast_to(high[user : user + 1], (16, positions)).astype(BF16)
        low_ref[group] = dot_nt(chosen_ref[...], digit_ref[...]).astype(BF16)
        high_ref[pl.ds(group, 1), :] = dot_nt(wide_ref[...], chosen_ref[...])[:1]
        return most

    most_ref[0] = lax.fori_loop(0, groups, one_group, jnp.float32(0)).astype(jnp.int32)

    items = ids_ref[0]
    slot = jnp.full(items.shape, -1, jnp.int32)
    for owner in range(groups):
        belongs = items // own == owner
        rank = ranks(belongs)[0] - first
        fits = belongs & (rank >= 0) & (rank < capacity)
        slot = jnp.where(fits, rank + owner * capacity, slot)
    padded = jnp.concatenate(
        [slot.astype(F32), jnp.zeros((LANES - users, positions), F32)], axis=0
    )
    slot_ref[...] = padded.T.astype(jnp.int32)


def plan_turn(home, turn, all_ids, own, capacity):
    groups, users, positions = all_ids.shape
    smem, vmem = pl.BlockSpec(memory_space=pltpu.SMEM), pl.BlockSpec(memory_space=pltpu.VMEM)
    return pl.pallas_call(
        functools.partial(plan_kernel, own),
        out_shape=[
            jax.ShapeDtypeStruct((groups, capacity, LOW), BF16),
            jax.ShapeDtypeStruct((groups, capacity), F32),
            jax.ShapeDtypeStruct((positions, LANES), jnp.int32),
            jax.ShapeDtypeStruct((1,), jnp.int32),
        ],
        in_specs=[smem, smem, vmem],
        out_specs=[vmem, vmem, vmem, smem],
        scratch_shapes=[
            pltpu.VMEM((capacity, users * positions), BF16),
            pltpu.VMEM((LOW, users * positions), BF16),
            pltpu.VMEM((16, users * positions), BF16),
        ],
        compiler_params=pltpu.CompilerParams(vmem_limit_bytes=VMEM_BYTES),
        cost_estimate=pl.CostEstimate(flops=4 * 10**9, bytes_accessed=5 * 10**6, transcendentals=0),
        name="plan_turn",
    )(home, turn, all_ids)


def pack_kernel(home_ref, slot_ref, grad_ref, *refs):
    *packed_refs, wide_ref, chosen_ref = refs
    users, _, positions = grad_ref.shape
    capacity = packed_refs[0].shape[1]
    step = pl.program_id(0)
    owner = home_ref[0] ^ step
    place = lax.broadcasted_iota(jnp.int32, (positions, capacity), 1) + owner * capacity
    for user in range(users):
        rows = pl.ds(user * positions, positions)
        wide_ref[:, rows] = grad_ref[user]
        slot = slot_ref[:, user : user + 1]
        chosen_ref[rows, :] = jnp.where(place == slot, 1.0, 0.0).astype(BF16)
    packed = dot_nn(wide_ref[...], chosen_ref[...]).astype(BF16)
    for place, packed_ref in enumerate(packed_refs):

        @pl.when(step == place)
        def _():
            packed_ref[...] = packed


def pack_turn(home, slot, grads, owners, capacity):
    users, features, positions = grads.shape
    return pl.pallas_call(
        pack_kernel,
        grid=(owners,),
        out_shape=[jax.ShapeDtypeStruct((features, capacity), BF16)] * owners,
        in_specs=[
            pl.BlockSpec(memory_space=pltpu.SMEM),
            pl.BlockSpec(slot.shape, lambda i: (0, 0)),
            pl.BlockSpec(grads.shape, lambda i: (0, 0, 0)),
        ],
        out_specs=[pl.BlockSpec((features, capacity), lambda i: (0, 0))] * owners,
        scratch_shapes=[
            pltpu.VMEM((features, users * positions), BF16),
            pltpu.VMEM((users * positions, capacity), BF16),
        ],
        compiler_params=pltpu.CompilerParams(vmem_limit_bytes=VMEM_BYTES),
        cost_estimate=pl.CostEstimate(flops=3 * 10**9, bytes_accessed=10**6, transcendentals=0),
        name="pack_turn",
    )(home, slot, grads)


def scatter_kernel(groups, stack, low_ref, high_ref, *refs):
    list_refs, (*before_ref, out_ref, spread_ref) = refs[:groups], refs[groups:]
    features, capacity = list_refs[0].shape
    step = pl.program_id(0)
    for group, list_ref in enumerate(list_refs):
        high = high_ref[pl.ds(group, 1), :]
        for part in range(stack):
            wanted = (step * stack + part + 1).astype(F32)
            chosen = jnp.where(high == wanted, 1.0, 0.0).astype(BF16)
            spread_ref[pl.ds(part * features, features), pl.ds(group * capacity, capacity)] = (
                list_ref[...] * chosen
            )
    sums = dot_nn(spread_ref[...], low_ref[...])
    for part in range(stack):
        columns = pl.ds(part * LOW, LOW)
        term = sums[part * features : (part + 1) * features]
        out_ref[:, columns] = term + before_ref[0][:, columns] if before_ref else term


def scatter_slots(low, high, lists, own, before=None):
    groups = len(lists)
    features, capacity = lists[0].shape
    stack = min(STACK, own // LOW)
    block = pl.BlockSpec((features, stack * LOW), lambda i: (0, i))
    extra = [] if before is None else [before]
    return pl.pallas_call(
        functools.partial(scatter_kernel, groups, stack),
        grid=(own // (LOW * stack),),
        out_shape=jax.ShapeDtypeStruct((features, own), F32),
        in_specs=[
            pl.BlockSpec((groups * capacity, LOW), lambda i: (0, 0)),
            pl.BlockSpec(high.shape, lambda i: (0, 0)),
        ]
        + [pl.BlockSpec((features, capacity), lambda i: (0, 0))] * groups
        + [block] * len(extra),
        out_specs=block,
        scratch_shapes=[pltpu.VMEM((stack * features, groups * capacity), BF16)],
        input_output_aliases={2 + groups: 0} if extra else {},
        compiler_params=pltpu.CompilerParams(vmem_limit_bytes=VMEM_BYTES),
        cost_estimate=pl.CostEstimate(flops=4 * 10**9, bytes_accessed=10**7, transcendentals=0),
        name="scatter_slots",
    )(low.reshape(groups * capacity, LOW), high, *lists, *extra)


def swap(value, axis, distance):
    size = lax.axis_size(axis)
    return lax.ppermute(value, axis, [(i, i ^ distance) for i in range(size)])


def swap_lists(lists, axis):
    received = {k: swap(lists[k], axis, k) for k in reversed(range(1, len(lists)))}
    return [lists[0]] + [received[k] for k in range(1, len(lists))]


def exchange(value, axis):
    return lax.all_to_all(value, axis, split_axis=0, concat_axis=0, tiled=True)


def on_device(item_ids, user_len, emb_table, cotangent, w_uvqk, w_out, gain_in, gain_mid):
    dp_size = lax.axis_size("dp")
    table_size = lax.axis_size("table")
    users = user_len.shape[0]
    features, vocab = emb_table.shape
    rows = item_ids.shape[0]
    positions = rows // users
    width = features * table_size
    own = vocab // dp_size
    capacity = -(-(rows // dp_size * 5 // 4) // LANES) * LANES
    assert users == table_size and users <= LANES and positions <= 256 and own // LOW <= 255
    assert dp_size & (dp_size - 1) == 0
    me = lax.axis_index("table").astype(jnp.int32).reshape(1)
    home = lax.axis_index("dp").astype(jnp.int32).reshape(1)

    cot_send = jnp.transpose(cotangent.reshape(features, users, positions), (1, 0, 2))
    cot_cols = exchange(cot_send, "table")
    ids = item_ids.reshape(users, positions)
    order = jnp.arange(positions, dtype=jnp.int32)
    valid_ids = jnp.where(order[None, :] < user_len[:, None], ids, vocab)
    emb_send = gather_columns(item_ids, emb_table, users)
    emb_send, cot_cols = lax.optimization_barrier((emb_send, cot_cols))
    emb_cols = exchange(emb_send, "table")
    all_ids = jnp.stack([valid_ids] + [swap(valid_ids, "dp", k) for k in range(1, dp_size)])
    out_cols, grad_cols = run_layer(
        me,
        user_len,
        emb_cols.reshape(width, positions),
        cot_cols.reshape(width, positions),
        w_uvqk,
        w_out,
        gain_in,
        gain_mid,
    )
    per_peer = (table_size, features, positions)
    all_ids, grad_cols = lax.optimization_barrier((all_ids, grad_cols))
    low, high, slot, most = plan_turn(home, jnp.zeros((1,), jnp.int32), all_ids, own, capacity)
    grad_home = exchange(grad_cols.reshape(per_peer), "table")
    out_cols, grad_home = lax.optimization_barrier((out_cols, grad_home))
    out_home = exchange(out_cols.reshape(per_peer), "table")
    lists = swap_lists(pack_turn(home, slot, grad_home, dp_size, capacity), "dp")
    table_grad = scatter_slots(low, high, lists, own)
    layer_out = jnp.transpose(out_home, (1, 0, 2)).reshape(features, rows)

    turns = (most[0] + capacity - 1) // capacity

    def another(state):
        turn, sums = state
        more_low, more_high, more_slot, _ = plan_turn(home, turn.reshape(1), all_ids, own, capacity)
        arrived = swap_lists(pack_turn(home, more_slot, grad_home, dp_size, capacity), "dp")
        return turn + 1, scatter_slots(more_low, more_high, arrived, own, sums)

    _, table_grad = lax.while_loop(
        lambda state: state[0] < turns, another, (jnp.int32(1), table_grad)
    )
    return (layer_out, table_grad)


def solution(mesh):
    return jax.shard_map(
        on_device,
        mesh=mesh,
        in_specs=(P("dp"), P("dp"), P("table", None), P("table", "dp"), P(), P(), P(), P()),
        out_specs=(P("table", "dp"), P("table", "dp")),
        check_vma=False,
    )
```

```python
import functools

import jax
import jax.numpy as jnp
from jax import lax
from jax.experimental import pallas as pl
from jax.experimental.pallas import tpu as pltpu
from jax.sharding import PartitionSpec as P

HEADS = 8
NORM_EPS = 1e-05
LANES = 128
VMEM_BYTES = 48 * 1024 * 1024

F32 = jnp.float32
BF16 = jnp.bfloat16


def dot_nn(left, right):
    return jnp.dot(left, right, preferred_element_type=F32)


def dot_nt(left, right):
    return lax.dot_general(left, right, (((1,), (1,)), ((), ())), preferred_element_type=F32)


def dot_tn(left, right):
    return lax.dot_general(left, right, (((0,), (0,)), ((), ())), preferred_element_type=F32)


BLOCK = 256
UNROLL = 64
CHUNKS = 8


def gather_kernel(
    len_ref,
    ids_ref,
    table_ref,
    out_ref,
    valid_ref,
    chunk_ref,
    rows_ref,
    picked_ref,
    turned_ref,
    row_vector_ref,
    row_ref,
    chunk_sems,
    row_sem,
    out_sems,
):
    users, features, positions = out_ref.shape
    vocab = table_ref.shape[1]
    pack = LANES // features
    span = BLOCK * pack
    wide = vocab // CHUNKS
    block_bits = BLOCK.bit_length() - 1

    def chunk_copy(chunk):
        columns = pl.ds(chunk * wide, wide)
        return pltpu.make_async_copy(
            table_ref.at[:, columns], chunk_ref.at[:, columns], chunk_sems.at[chunk]
        )

    for chunk in range(CHUNKS):
        chunk_copy(chunk).start()
    items = ids_ref[...]
    row_vector_ref[...] = ((items >> (span.bit_length() - 1)) << block_bits) | (items & (BLOCK - 1))
    row_copy = pltpu.make_async_copy(row_vector_ref, row_ref, row_sem)
    row_copy.start()
    order = lax.broadcasted_iota(jnp.int32, (1, positions), 1)
    for user in range(users):
        own_items = ids_ref[pl.ds(user * positions, positions)].reshape(1, positions)
        valid_ref[pl.ds(user, 1), :] = jnp.where(order < len_ref[user], own_items, vocab)

    for chunk in range(CHUNKS):
        chunk_copy(chunk).wait()
        for part in range(chunk * wide // span, (chunk + 1) * wide // span):
            stack = jnp.concatenate(
                [
                    chunk_ref[:, part * span + s * BLOCK : part * span + (s + 1) * BLOCK]
                    for s in range(pack)
                ],
                axis=0,
            )
            rows_ref[pl.ds(part * BLOCK, BLOCK), :] = stack.T.astype(F32)
    row_copy.wait()

    def some(part, carry):
        start = pl.multiple_of(part * UNROLL, UNROLL)
        for slot in range(UNROLL):
            row = row_ref[start + slot]
            picked_ref[pl.ds(start + slot, 1), :] = rows_ref[pl.ds(row, 1), :]
        return carry

    lax.fori_loop(0, users * positions // UNROLL, some, 0)
    row = lax.broadcasted_iota(jnp.int32, (LANES, LANES), 0)
    column = lax.broadcasted_iota(jnp.int32, (LANES, LANES), 1)
    same = jnp.where(row == column, 1.0, 0.0).astype(BF16)
    for user in range(users):
        places = pl.ds(user * positions, positions)
        turned = dot_nt(same, picked_ref[places, :].astype(BF16))
        own_items = ids_ref[places].reshape(1, positions)
        group = (own_items >> block_bits) & (pack - 1)
        total = turned[:features]
        for s in range(1, pack):
            total = jnp.where(group == s, turned[s * features : (s + 1) * features], total)
        turned_ref[user] = total.astype(BF16)
        pltpu.make_async_copy(turned_ref.at[user], out_ref.at[user], out_sems.at[user]).start()
    for user in range(users):
        pltpu.make_async_copy(turned_ref.at[user], out_ref.at[user], out_sems.at[user]).wait()


def gather_columns(item_ids, lengths, table):
    users = lengths.shape[0]
    rows = item_ids.shape[0]
    positions = rows // users
    features, vocab = table.shape
    pack = LANES // features
    shape = (users, features, positions)
    hbm = pl.BlockSpec(memory_space=pltpu.HBM)
    vmem = pl.BlockSpec(memory_space=pltpu.VMEM)
    return pl.pallas_call(
        gather_kernel,
        out_shape=[
            jax.ShapeDtypeStruct(shape, table.dtype),
            jax.ShapeDtypeStruct((users, positions), jnp.int32),
        ],
        in_specs=[pl.BlockSpec(memory_space=pltpu.SMEM), vmem, hbm],
        out_specs=[hbm, vmem],
        scratch_shapes=[
            pltpu.VMEM((features, vocab), table.dtype),
            pltpu.VMEM((vocab // pack, LANES), F32),
            pltpu.VMEM((rows, LANES), F32),
            pltpu.VMEM(shape, table.dtype),
            pltpu.VMEM((rows,), jnp.int32),
            pltpu.SMEM((rows,), jnp.int32),
            pltpu.SemaphoreType.DMA((CHUNKS,)),
            pltpu.SemaphoreType.DMA,
            pltpu.SemaphoreType.DMA((users,)),
        ],
        compiler_params=pltpu.CompilerParams(vmem_limit_bytes=VMEM_BYTES),
        cost_estimate=pl.CostEstimate(flops=8 * 10**9, bytes_accessed=5 * 10**6, transcendentals=0),
        name="gather_columns",
    )(lengths, item_ids, table)


def norm_forward(values):
    centred = values - jnp.mean(values, axis=0, keepdims=True)
    inverse = lax.rsqrt(jnp.mean(centred * centred, axis=0, keepdims=True) + NORM_EPS)
    return centred * inverse, inverse


def norm_backward(grad, normal, inverse):
    shift = jnp.mean(grad, axis=0, keepdims=True)
    slope = jnp.mean(grad * normal, axis=0, keepdims=True)
    return (grad - shift - normal * slope) * inverse


def silu_pair(z):
    gate = 0.5 + 0.5 * jnp.tanh(0.5 * z)
    value = z * gate
    return value, gate + value * (1.0 - gate)


def layer_kernel(
    me_ref,
    len_ref,
    emb_ref,
    cot_hbm_ref,
    w_in_hbm_ref,
    w_in_t_hbm_ref,
    w_out_hbm_ref,
    gain_in_row_ref,
    gain_mid_row_ref,
    out_hbm_ref,
    grad_hbm_ref,
    cot_ref,
    w_in_ref,
    w_in_t_ref,
    w_out_ref,
    out_ref,
    grad_ref,
    proj_ref,
    slope_ref,
    weight_ref,
    score_slope_ref,
    att_ref,
    dproj_ref,
    gain_in_ref,
    gain_mid_ref,
    part_sems,
    sems,
):
    width, positions = emb_ref.shape
    head_dim = width // HEADS
    half = positions // 2

    def part_copy(part):
        rows = pl.ds(part * width, width)
        return pltpu.make_async_copy(
            w_in_t_hbm_ref.at[rows, :], w_in_t_ref.at[rows, :], part_sems.at[part]
        )

    for part in range(4):
        part_copy(part).start()
    w_out_copy = pltpu.make_async_copy(w_out_hbm_ref, w_out_ref, sems.at[0])
    cot_copy = pltpu.make_async_copy(cot_hbm_ref, cot_ref, sems.at[1])
    w_in_copy = pltpu.make_async_copy(w_in_hbm_ref, w_in_ref, sems.at[2])
    out_copy = pltpu.make_async_copy(out_ref, out_hbm_ref, sems.at[3])
    grad_copy = pltpu.make_async_copy(grad_ref, grad_hbm_ref, sems.at[4])
    w_out_copy.start()
    cot_copy.start()
    w_in_copy.start()
    length = len_ref[me_ref[0]]
    share = 1.0 / length.astype(F32)
    for row_ref, column_ref in ((gain_in_row_ref, gain_in_ref), (gain_mid_row_ref, gain_mid_ref)):
        row = row_ref[...].reshape(1, width)
        column_ref[...] = jnp.broadcast_to(row, (positions, width)).T

    embedded = emb_ref[...].astype(F32)
    normal_in, inverse_in = norm_forward(embedded)
    normed = (normal_in * gain_in_ref[...]).astype(BF16)
    for part in range(4):
        rows = pl.ds(part * width, width)
        part_copy(part).wait()
        value, slope = silu_pair(dot_nn(w_in_t_ref[rows, :], normed))
        proj_ref[rows, :] = value.astype(BF16)
        slope_ref[rows, :] = slope

    def mask(key_start, query_start, shape):
        key = lax.broadcasted_iota(jnp.int32, shape, 0) + key_start
        query = lax.broadcasted_iota(jnp.int32, shape, 1) + query_start
        return (key <= query) & (key < length)

    low = mask(0, 0, (half, positions))
    high = mask(half, half, (half, half))
    scale = head_dim ** (-0.5)
    for head in range(HEADS):
        at = head * head_dim
        values = proj_ref[pl.ds(width + at, head_dim), :]
        queries = proj_ref[pl.ds(2 * width + at, head_dim), :]
        keys = proj_ref[pl.ds(3 * width + at, head_dim), :]
        for start, allowed in ((0, low), (half, high)):
            scores = dot_tn(keys[:, start : start + half], queries[:, start:]) * scale
            value, slope = silu_pair(scores)
            weight_ref[head, pl.ds(start, half), pl.ds(start, positions - start)] = jnp.where(
                allowed, value * share, 0.0
            ).astype(BF16)
            score_slope_ref[head, pl.ds(start, half), pl.ds(start, positions - start)] = jnp.where(
                allowed, slope * (share * scale), 0.0
            )
        weight_ref[head, pl.ds(half, half), pl.ds(0, half)] = jnp.zeros((half, half), BF16)
        att_ref[pl.ds(at, head_dim), :] = dot_nn(values, weight_ref[head])

    normal_mid, inverse_mid = norm_forward(att_ref[...])
    gate_rows = proj_ref[pl.ds(0, width), :].astype(F32)
    scaled = normal_mid * gain_mid_ref[...]
    mixed = (scaled * gate_rows).astype(BF16)
    w_out_copy.wait()
    out_ref[...] = (embedded + dot_tn(w_out_ref[...], mixed)).astype(BF16)
    out_copy.start()
    cot_copy.wait()

    valid = lax.broadcasted_iota(jnp.int32, (width, positions), 1) < length
    cotangent = jnp.where(valid, cot_ref[...].astype(F32), 0.0)
    d_mixed = dot_nn(w_out_ref[...], cotangent.astype(BF16))
    dproj_ref[pl.ds(0, width), :] = (d_mixed * scaled * slope_ref[pl.ds(0, width), :]).astype(BF16)
    d_att = norm_backward(d_mixed * gate_rows * gain_mid_ref[...], normal_mid, inverse_mid)
    att_ref[...] = d_att
    for head in range(HEADS):
        at = head * head_dim
        v_rows = pl.ds(width + at, head_dim)
        q_rows = pl.ds(2 * width + at, head_dim)
        k_rows = pl.ds(3 * width + at, head_dim)
        values, queries, keys = proj_ref[v_rows, :], proj_ref[q_rows, :], proj_ref[k_rows, :]
        d_head = att_ref[pl.ds(at, head_dim), :].astype(BF16)
        low_scores = (
            dot_tn(values[:, :half], d_head) * score_slope_ref[head, pl.ds(0, half), :]
        ).astype(BF16)
        high_scores = (
            dot_tn(values[:, half:], d_head[:, half:])
            * score_slope_ref[head, pl.ds(half, half), pl.ds(half, half)]
        ).astype(BF16)
        d_scores = jnp.concatenate(
            [
                low_scores,
                jnp.concatenate([jnp.zeros((half, half), BF16), high_scores], axis=1),
            ],
            axis=0,
        )
        d_values = dot_nt(d_head, weight_ref[head])
        d_queries = dot_nn(keys, d_scores)
        d_keys = dot_nt(queries, d_scores)
        dproj_ref[v_rows, :] = (d_values * slope_ref[v_rows, :]).astype(BF16)
        dproj_ref[q_rows, :] = (d_queries * slope_ref[q_rows, :]).astype(BF16)
        dproj_ref[k_rows, :] = (d_keys * slope_ref[k_rows, :]).astype(BF16)
    w_in_copy.wait()
    d_normed = dot_nn(w_in_ref[...], dproj_ref[...])
    d_embedded = norm_backward(d_normed * gain_in_ref[...], normal_in, inverse_in)
    grad_ref[...] = (cotangent + d_embedded).astype(BF16)
    grad_copy.start()
    out_copy.wait()
    grad_copy.wait()


def run_layer(me, lengths, embedded, cotangent, w_in, w_out, gain_in, gain_mid):
    width, positions = embedded.shape
    smem, vmem = pl.BlockSpec(memory_space=pltpu.SMEM), pl.BlockSpec(memory_space=pltpu.VMEM)
    hbm = pl.BlockSpec(memory_space=pltpu.HBM)
    shape = jax.ShapeDtypeStruct((width, positions), BF16)
    return pl.pallas_call(
        layer_kernel,
        out_shape=[shape, shape],
        in_specs=[smem, smem, vmem, hbm, hbm, hbm, hbm, vmem, vmem],
        out_specs=[hbm, hbm],
        scratch_shapes=[
            pltpu.VMEM((width, positions), BF16),
            pltpu.VMEM((width, 4 * width), BF16),
            pltpu.VMEM((4 * width, width), BF16),
            pltpu.VMEM((width, width), BF16),
            pltpu.VMEM((width, positions), BF16),
            pltpu.VMEM((width, positions), BF16),
            pltpu.VMEM((4 * width, positions), BF16),
            pltpu.VMEM((4 * width, positions), F32),
            pltpu.VMEM((HEADS, positions, positions), BF16),
            pltpu.VMEM((HEADS, positions, positions), F32),
            pltpu.VMEM((width, positions), F32),
            pltpu.VMEM((4 * width, positions), BF16),
            pltpu.VMEM((width, positions), F32),
            pltpu.VMEM((width, positions), F32),
            pltpu.SemaphoreType.DMA((4,)),
            pltpu.SemaphoreType.DMA((5,)),
        ],
        compiler_params=pltpu.CompilerParams(vmem_limit_bytes=VMEM_BYTES),
        cost_estimate=pl.CostEstimate(flops=10**10, bytes_accessed=10**7, transcendentals=10**6),
        name="layer",
    )(
        me,
        lengths,
        embedded,
        cotangent,
        w_in,
        w_in.T,
        w_out,
        gain_in,
        gain_mid,
    )


LOW = 256
STACK = 8


def ranks(member):
    users, positions = member.shape
    ones = jnp.where(member, 1.0, 0.0)
    row = lax.broadcasted_iota(jnp.int32, (positions, positions), 0)
    column = lax.broadcasted_iota(jnp.int32, (positions, positions), 1)
    before = jnp.where(row < column, 1.0, 0.0).astype(BF16)
    totals = jnp.sum(ones, axis=1, keepdims=True)
    user = lax.broadcasted_iota(jnp.int32, (users, 1), 0)
    earlier = jnp.zeros((users, 1), F32)
    for other in range(users - 1):
        earlier += jnp.where(user > other, totals[other : other + 1], 0.0)
    rank = dot_nn(ones.astype(BF16), before) + earlier
    return rank.astype(jnp.int32), jnp.sum(totals)


def plan_kernel(own, home_ref, turn_ref, ids_ref, low_ref, high_ref, slot_ref, most_ref, *scratch):
    chosen_ref, digit_ref, wide_ref = scratch
    groups, users, positions = ids_ref.shape
    capacity = low_ref.shape[1]
    home = home_ref[0]
    first = turn_ref[0] * capacity
    digit = lax.broadcasted_iota(jnp.int32, (LOW, positions), 0)
    place = lax.broadcasted_iota(jnp.int32, (capacity, positions), 0)

    def one_group(group, most):
        items = ids_ref[group]
        for owner in range(groups):
            count = jnp.sum(jnp.where(items // own == owner, 1.0, 0.0))
            most = jnp.maximum(most, count)
        local = items - home * own
        mine = (local >= 0) & (local < own)
        rank, _ = ranks(mine)
        slot = jnp.where(mine, rank - first, -1)
        low = local & (LOW - 1)
        high = jnp.where(mine, (local >> (LOW.bit_length() - 1)) + 1, 0).astype(F32)
        for user in range(users):
            columns = pl.ds(user * positions, positions)
            chosen_ref[:, columns] = jnp.where(place == slot[user : user + 1], 1.0, 0.0).astype(BF16)
            digit_ref[:, columns] = jnp.where(digit == low[user : user + 1], 1.0, 0.0).astype(BF16)
            wide_ref[:, columns] = jnp.broadcast_to(high[user : user + 1], (16, positions)).astype(BF16)
        low_ref[group] = dot_nt(chosen_ref[...], digit_ref[...]).astype(BF16)
        high_ref[pl.ds(group, 1), :] = dot_nt(wide_ref[...], chosen_ref[...])[:1]
        return most

    most_ref[0] = lax.fori_loop(0, groups, one_group, jnp.float32(0)).astype(jnp.int32)

    items = ids_ref[0]
    slot = jnp.full(items.shape, -1, jnp.int32)
    for owner in range(groups):
        belongs = items // own == owner
        rank = ranks(belongs)[0] - first
        fits = belongs & (rank >= 0) & (rank < capacity)
        slot = jnp.where(fits, rank + owner * capacity, slot)
    padded = jnp.concatenate(
        [slot.astype(F32), jnp.zeros((LANES - users, positions), F32)], axis=0
    )
    slot_ref[...] = padded.T.astype(jnp.int32)


def plan_turn(home, turn, all_ids, own, capacity):
    groups, users, positions = all_ids.shape
    smem, vmem = pl.BlockSpec(memory_space=pltpu.SMEM), pl.BlockSpec(memory_space=pltpu.VMEM)
    return pl.pallas_call(
        functools.partial(plan_kernel, own),
        out_shape=[
            jax.ShapeDtypeStruct((groups, capacity, LOW), BF16),
            jax.ShapeDtypeStruct((groups, capacity), F32),
            jax.ShapeDtypeStruct((positions, LANES), jnp.int32),
            jax.ShapeDtypeStruct((1,), jnp.int32),
        ],
        in_specs=[smem, smem, vmem],
        out_specs=[vmem, vmem, vmem, smem],
        scratch_shapes=[
            pltpu.VMEM((capacity, users * positions), BF16),
            pltpu.VMEM((LOW, users * positions), BF16),
            pltpu.VMEM((16, users * positions), BF16),
        ],
        compiler_params=pltpu.CompilerParams(vmem_limit_bytes=VMEM_BYTES),
        cost_estimate=pl.CostEstimate(flops=4 * 10**9, bytes_accessed=5 * 10**6, transcendentals=0),
        name="plan_turn",
    )(home, turn, all_ids)


def pack_kernel(home_ref, slot_ref, grad_ref, *refs):
    *packed_refs, wide_ref, chosen_ref = refs
    users, _, positions = grad_ref.shape
    capacity = packed_refs[0].shape[1]
    step = pl.program_id(0)
    owner = home_ref[0] ^ step
    lane = lax.broadcasted_iota(jnp.int32, (positions, LANES), 1)
    for user in range(users):
        rows = pl.ds(user * positions, positions)
        wide_ref[:, rows] = grad_ref[user]
        slot = jnp.broadcast_to(slot_ref[:, user : user + 1], (positions, LANES)) - owner * capacity
        ones = jnp.where((slot & (LANES - 1)) == lane, 1.0, 0.0).astype(BF16)
        tile = jnp.clip(slot >> (LANES.bit_length() - 1), -1, capacity // LANES).astype(F32).astype(BF16)
        for part in range(capacity // LANES):
            chosen_ref[rows, pl.ds(part * LANES, LANES)] = jnp.where(
                tile == BF16(part), ones, jnp.zeros_like(ones)
            )
    packed = dot_nn(wide_ref[...], chosen_ref[...]).astype(BF16)
    for place, packed_ref in enumerate(packed_refs):

        @pl.when(step == place)
        def _():
            packed_ref[...] = packed


def pack_turn(home, slot, grads, owners, capacity):
    users, features, positions = grads.shape
    return pl.pallas_call(
        pack_kernel,
        grid=(owners,),
        out_shape=[jax.ShapeDtypeStruct((features, capacity), BF16)] * owners,
        in_specs=[
            pl.BlockSpec(memory_space=pltpu.SMEM),
            pl.BlockSpec(slot.shape, lambda i: (0, 0)),
            pl.BlockSpec(grads.shape, lambda i: (0, 0, 0)),
        ],
        out_specs=[pl.BlockSpec((features, capacity), lambda i: (0, 0))] * owners,
        scratch_shapes=[
            pltpu.VMEM((features, users * positions), BF16),
            pltpu.VMEM((users * positions, capacity), BF16),
        ],
        compiler_params=pltpu.CompilerParams(vmem_limit_bytes=VMEM_BYTES),
        cost_estimate=pl.CostEstimate(flops=3 * 10**9, bytes_accessed=10**6, transcendentals=0),
        name="pack_turn",
    )(home, slot, grads)


def scatter_kernel(groups, stack, low_ref, high_ref, *refs):
    list_refs, (*before_ref, out_ref, spread_ref) = refs[:groups], refs[groups:]
    features, capacity = list_refs[0].shape
    step = pl.program_id(0)
    for group, list_ref in enumerate(list_refs):
        high = high_ref[pl.ds(group, 1), :]
        for part in range(stack):
            wanted = (step * stack + part + 1).astype(F32)
            chosen = jnp.where(high == wanted, 1.0, 0.0).astype(BF16)
            spread_ref[pl.ds(part * features, features), pl.ds(group * capacity, capacity)] = (
                list_ref[...] * chosen
            )
    sums = dot_nn(spread_ref[...], low_ref[...])
    for part in range(stack):
        columns = pl.ds(part * LOW, LOW)
        term = sums[part * features : (part + 1) * features]
        out_ref[:, columns] = term + before_ref[0][:, columns] if before_ref else term


def scatter_slots(low, high, lists, own, before=None):
    groups = len(lists)
    features, capacity = lists[0].shape
    stack = min(STACK, own // LOW)
    block = pl.BlockSpec((features, stack * LOW), lambda i: (0, i))
    extra = [] if before is None else [before]
    return pl.pallas_call(
        functools.partial(scatter_kernel, groups, stack),
        grid=(own // (LOW * stack),),
        out_shape=jax.ShapeDtypeStruct((features, own), F32),
        in_specs=[
            pl.BlockSpec((groups * capacity, LOW), lambda i: (0, 0)),
            pl.BlockSpec(high.shape, lambda i: (0, 0)),
        ]
        + [pl.BlockSpec((features, capacity), lambda i: (0, 0))] * groups
        + [block] * len(extra),
        out_specs=block,
        scratch_shapes=[pltpu.VMEM((stack * features, groups * capacity), BF16)],
        input_output_aliases={2 + groups: 0} if extra else {},
        compiler_params=pltpu.CompilerParams(vmem_limit_bytes=VMEM_BYTES),
        cost_estimate=pl.CostEstimate(flops=4 * 10**9, bytes_accessed=10**7, transcendentals=0),
        name="scatter_slots",
    )(low.reshape(groups * capacity, LOW), high, *lists, *extra)


def swap(value, axis, distance):
    size = lax.axis_size(axis)
    return lax.ppermute(value, axis, [(i, i ^ distance) for i in range(size)])


def swap_lists(lists, axis):
    received = {k: swap(lists[k], axis, k) for k in reversed(range(1, len(lists)))}
    return [lists[0]] + [received[k] for k in range(1, len(lists))]


def exchange(value, axis):
    return lax.all_to_all(value, axis, split_axis=0, concat_axis=0, tiled=True)


def on_device(item_ids, user_len, emb_table, cotangent, w_uvqk, w_out, gain_in, gain_mid):
    dp_size = lax.axis_size("dp")
    table_size = lax.axis_size("table")
    users = user_len.shape[0]
    features, vocab = emb_table.shape
    rows = item_ids.shape[0]
    positions = rows // users
    width = features * table_size
    own = vocab // dp_size
    capacity = -(-(rows // dp_size * 5 // 4) // LANES) * LANES
    assert users == table_size and users <= LANES and positions <= 256 and own // LOW <= 255
    assert dp_size & (dp_size - 1) == 0
    me = lax.axis_index("table").astype(jnp.int32).reshape(1)
    home = lax.axis_index("dp").astype(jnp.int32).reshape(1)

    cot_send = jnp.transpose(cotangent.reshape(features, users, positions), (1, 0, 2))
    cot_cols = exchange(cot_send, "table")
    emb_send, valid_ids = gather_columns(item_ids, user_len, emb_table)
    emb_send, valid_ids, cot_cols = lax.optimization_barrier((emb_send, valid_ids, cot_cols))
    emb_cols = exchange(emb_send, "table")
    all_ids = jnp.stack([valid_ids] + [swap(valid_ids, "dp", k) for k in range(1, dp_size)])
    out_cols, grad_cols = run_layer(
        me,
        user_len,
        emb_cols.reshape(width, positions),
        cot_cols.reshape(width, positions),
        w_uvqk,
        w_out,
        gain_in,
        gain_mid,
    )
    per_peer = (table_size, features, positions)
    all_ids, grad_cols = lax.optimization_barrier((all_ids, grad_cols))
    low, high, slot, most = plan_turn(home, jnp.zeros((1,), jnp.int32), all_ids, own, capacity)
    grad_home = exchange(grad_cols.reshape(per_peer), "table")
    out_cols, grad_home = lax.optimization_barrier((out_cols, grad_home))
    out_home = exchange(out_cols.reshape(per_peer), "table")
    lists = swap_lists(pack_turn(home, slot, grad_home, dp_size, capacity), "dp")
    table_grad = scatter_slots(low, high, lists, own)
    layer_out = jnp.transpose(out_home, (1, 0, 2)).reshape(features, rows)

    turns = (most[0] + capacity - 1) // capacity

    def another(state):
        turn, sums = state
        more_low, more_high, more_slot, _ = plan_turn(home, turn.reshape(1), all_ids, own, capacity)
        arrived = swap_lists(pack_turn(home, more_slot, grad_home, dp_size, capacity), "dp")
        return turn + 1, scatter_slots(more_low, more_high, arrived, own, sums)

    _, table_grad = lax.while_loop(
        lambda state: state[0] < turns, another, (jnp.int32(1), table_grad)
    )
    return (layer_out, table_grad)


def solution(mesh):
    return jax.shard_map(
        on_device,
        mesh=mesh,
        in_specs=(P("dp"), P("dp"), P("table", None), P("table", "dp"), P(), P(), P(), P()),
        out_specs=(P("table", "dp"), P("table", "dp")),
        check_vma=False,
    )
```

```python
import functools

import jax
import jax.numpy as jnp
from jax import lax
from jax.experimental import pallas as pl
from jax.experimental.pallas import tpu as pltpu
from jax.sharding import PartitionSpec as P

HEADS = 8
NORM_EPS = 1e-05
LANES = 128
VMEM_BYTES = 48 * 1024 * 1024
WHOLE_VMEM_BYTES = 61 * 1024 * 1024

F32 = jnp.float32
BF16 = jnp.bfloat16


def dot_nn(left, right):
    return jnp.dot(left, right, preferred_element_type=F32)


def dot_nt(left, right):
    return lax.dot_general(left, right, (((1,), (1,)), ((), ())), preferred_element_type=F32)


def dot_tn(left, right):
    return lax.dot_general(left, right, (((0,), (0,)), ((), ())), preferred_element_type=F32)


BLOCK = 256
UNROLL = 64
CHUNKS = 8


def gather_kernel(
    len_ref,
    ids_ref,
    cot_ref,
    table_ref,
    out_ref,
    valid_ref,
    chunk_ref,
    rows_ref,
    picked_ref,
    turned_ref,
    row_vector_ref,
    row_ref,
    chunk_sems,
    row_sem,
    out_sems,
    cot_sems,
):
    users, _, positions = out_ref.shape
    features, vocab = table_ref.shape
    pack = LANES // features
    span = BLOCK * pack
    wide = vocab // CHUNKS
    block_bits = BLOCK.bit_length() - 1

    def chunk_copy(chunk):
        columns = pl.ds(chunk * wide, wide)
        return pltpu.make_async_copy(
            table_ref.at[:, columns], chunk_ref.at[:, columns], chunk_sems.at[chunk]
        )

    def cot_copy(user):
        return pltpu.make_async_copy(
            cot_ref.at[:, pl.ds(user * positions, positions)],
            out_ref.at[user, pl.ds(features, features), :],
            cot_sems.at[user],
        )

    def out_copy(user):
        return pltpu.make_async_copy(
            turned_ref.at[user], out_ref.at[user, pl.ds(0, features), :], out_sems.at[user]
        )

    for chunk in range(CHUNKS):
        chunk_copy(chunk).start()
    for user in range(users):
        cot_copy(user).start()
    items = ids_ref[...]
    row_vector_ref[...] = ((items >> (span.bit_length() - 1)) << block_bits) | (items & (BLOCK - 1))
    row_copy = pltpu.make_async_copy(row_vector_ref, row_ref, row_sem)
    row_copy.start()
    order = lax.broadcasted_iota(jnp.int32, (1, positions), 1)
    for user in range(users):
        own_items = ids_ref[pl.ds(user * positions, positions)].reshape(1, positions)
        valid_ref[pl.ds(user, 1), :] = jnp.where(order < len_ref[user], own_items, vocab)

    for chunk in range(CHUNKS):
        chunk_copy(chunk).wait()
        for part in range(chunk * wide // span, (chunk + 1) * wide // span):
            stack = jnp.concatenate(
                [
                    chunk_ref[:, part * span + s * BLOCK : part * span + (s + 1) * BLOCK]
                    for s in range(pack)
                ],
                axis=0,
            )
            rows_ref[pl.ds(part * BLOCK, BLOCK), :] = stack.T.astype(F32)
    row_copy.wait()

    def some(part, carry):
        start = pl.multiple_of(part * UNROLL, UNROLL)
        for slot in range(UNROLL):
            row = row_ref[start + slot]
            picked_ref[pl.ds(start + slot, 1), :] = rows_ref[pl.ds(row, 1), :]
        return carry

    lax.fori_loop(0, users * positions // UNROLL, some, 0)
    row = lax.broadcasted_iota(jnp.int32, (LANES, LANES), 0)
    column = lax.broadcasted_iota(jnp.int32, (LANES, LANES), 1)
    same = jnp.where(row == column, 1.0, 0.0).astype(BF16)
    for user in range(users):
        places = pl.ds(user * positions, positions)
        turned = dot_nt(same, picked_ref[places, :].astype(BF16))
        own_items = ids_ref[places].reshape(1, positions)
        group = (own_items >> block_bits) & (pack - 1)
        total = turned[:features]
        for s in range(1, pack):
            total = jnp.where(group == s, turned[s * features : (s + 1) * features], total)
        turned_ref[user] = total.astype(BF16)
        out_copy(user).start()
    for user in range(users):
        cot_copy(user).wait()
        out_copy(user).wait()


def gather_columns(item_ids, lengths, cotangent, table):
    users = lengths.shape[0]
    rows = item_ids.shape[0]
    positions = rows // users
    features, vocab = table.shape
    pack = LANES // features
    shape = (users, features, positions)
    hbm = pl.BlockSpec(memory_space=pltpu.HBM)
    vmem = pl.BlockSpec(memory_space=pltpu.VMEM)
    return pl.pallas_call(
        gather_kernel,
        out_shape=[
            jax.ShapeDtypeStruct((users, 2 * features, positions), table.dtype),
            jax.ShapeDtypeStruct((users, positions), jnp.int32),
        ],
        in_specs=[pl.BlockSpec(memory_space=pltpu.SMEM), vmem, hbm, hbm],
        out_specs=[hbm, vmem],
        scratch_shapes=[
            pltpu.VMEM((features, vocab), table.dtype),
            pltpu.VMEM((vocab // pack, LANES), F32),
            pltpu.VMEM((rows, LANES), F32),
            pltpu.VMEM(shape, table.dtype),
            pltpu.VMEM((rows,), jnp.int32),
            pltpu.SMEM((rows,), jnp.int32),
            pltpu.SemaphoreType.DMA((CHUNKS,)),
            pltpu.SemaphoreType.DMA,
            pltpu.SemaphoreType.DMA((users,)),
            pltpu.SemaphoreType.DMA((users,)),
        ],
        compiler_params=pltpu.CompilerParams(vmem_limit_bytes=WHOLE_VMEM_BYTES),
        cost_estimate=pl.CostEstimate(flops=8 * 10**9, bytes_accessed=5 * 10**6, transcendentals=0),
        name="gather_columns",
    )(lengths, item_ids, cotangent, table)


def norm_forward(values):
    centred = values - jnp.mean(values, axis=0, keepdims=True)
    inverse = lax.rsqrt(jnp.mean(centred * centred, axis=0, keepdims=True) + NORM_EPS)
    return centred * inverse, inverse


def norm_backward(grad, normal, inverse):
    shift = jnp.mean(grad, axis=0, keepdims=True)
    slope = jnp.mean(grad * normal, axis=0, keepdims=True)
    return (grad - shift - normal * slope) * inverse


def silu_pair(z):
    gate = 0.5 + 0.5 * jnp.tanh(0.5 * z)
    value = z * gate
    return value, gate + value * (1.0 - gate)


def layer_kernel(
    me_ref,
    len_ref,
    recv_hbm_ref,
    w_in_hbm_ref,
    w_in_t_hbm_ref,
    w_out_hbm_ref,
    gain_in_row_ref,
    gain_mid_row_ref,
    out_hbm_ref,
    grad_hbm_ref,
    emb_ref,
    cot_ref,
    w_in_ref,
    w_in_t_ref,
    w_out_ref,
    out_ref,
    grad_ref,
    proj_ref,
    slope_ref,
    weight_ref,
    score_slope_ref,
    att_ref,
    dproj_ref,
    gain_in_ref,
    gain_mid_ref,
    recv_sems,
    part_sems,
    sems,
):
    peers, both, positions = recv_hbm_ref.shape
    features = both // 2
    width = peers * features
    head_dim = width // HEADS
    half = positions // 2

    def recv_copy(kind, peer):
        target_ref = (emb_ref, cot_ref)[kind]
        return pltpu.make_async_copy(
            recv_hbm_ref.at[peer, pl.ds(kind * features, features), :],
            target_ref.at[pl.ds(peer * features, features), :],
            recv_sems.at[kind, peer],
        )

    def part_copy(part):
        rows = pl.ds(part * width, width)
        return pltpu.make_async_copy(
            w_in_t_hbm_ref.at[rows, :], w_in_t_ref.at[rows, :], part_sems.at[part]
        )

    for peer in range(peers):
        recv_copy(0, peer).start()
    for part in (2, 3, 1, 0):
        part_copy(part).start()
    for peer in range(peers):
        recv_copy(1, peer).start()
    w_out_copy = pltpu.make_async_copy(w_out_hbm_ref, w_out_ref, sems.at[0])
    w_in_copy = pltpu.make_async_copy(w_in_hbm_ref, w_in_ref, sems.at[1])
    out_copy = pltpu.make_async_copy(out_ref, out_hbm_ref, sems.at[2])
    grad_copy = pltpu.make_async_copy(grad_ref, grad_hbm_ref, sems.at[3])
    w_out_copy.start()
    w_in_copy.start()
    length = len_ref[me_ref[0]]
    share = 1.0 / length.astype(F32)
    for row_ref, column_ref in ((gain_in_row_ref, gain_in_ref), (gain_mid_row_ref, gain_mid_ref)):
        row = row_ref[...].reshape(1, width)
        column_ref[...] = jnp.broadcast_to(row, (positions, width)).T

    for peer in range(peers):
        recv_copy(0, peer).wait()
    embedded = emb_ref[...].astype(F32)
    normal_in, inverse_in = norm_forward(embedded)
    normed = (normal_in * gain_in_ref[...]).astype(BF16)

    def project(part):
        part_copy(part).wait()
        return dot_nn(w_in_t_ref[pl.ds(part * width, width), :], normed)

    def store_projected(part, z):
        rows = pl.ds(part * width, width)
        value, slope = silu_pair(z)
        proj_ref[rows, :] = value.astype(BF16)
        slope_ref[rows, :] = slope

    waiting = None
    for part in (2, 3, 1, 0):
        z = project(part)
        if waiting is not None:
            store_projected(*waiting)
        waiting = (part, z)
    store_projected(*waiting)

    def mask(key_start, query_start, shape):
        key = lax.broadcasted_iota(jnp.int32, shape, 0) + key_start
        query = lax.broadcasted_iota(jnp.int32, shape, 1) + query_start
        return (key <= query) & (key < length)

    blocks = ((0, mask(0, 0, (half, positions))), (half, mask(half, half, (half, half))))
    scale = head_dim ** (-0.5)

    def head_rows(kind, head):
        return pl.ds(kind * width + head * head_dim, head_dim)

    def score(head):
        queries, keys = proj_ref[head_rows(2, head), :], proj_ref[head_rows(3, head), :]
        return [dot_tn(keys[:, start : start + half], queries[:, start:]) for start, _ in blocks]

    def store_weights(head, scores):
        for (start, allowed), block in zip(blocks, scores):
            value, slope = silu_pair(block * scale)
            places = (pl.ds(start, half), pl.ds(start, positions - start))
            weight_ref[head, *places] = jnp.where(allowed, value * share, 0.0).astype(BF16)
            score_slope_ref[head, *places] = jnp.where(allowed, slope * (share * scale), 0.0)
        weight_ref[head, pl.ds(half, half), pl.ds(0, half)] = jnp.zeros((half, half), BF16)

    def attend(head):
        att_ref[pl.ds(head * head_dim, head_dim), :] = dot_nn(
            proj_ref[head_rows(1, head), :], weight_ref[head]
        )

    scores = score(0)
    for head in range(HEADS):
        following = score(head + 1) if head + 1 < HEADS else None
        store_weights(head, scores)
        if head:
            attend(head - 1)
        scores = following
    attend(HEADS - 1)

    normal_mid, inverse_mid = norm_forward(att_ref[...])
    gate_rows = proj_ref[pl.ds(0, width), :].astype(F32)
    scaled = normal_mid * gain_mid_ref[...]
    mixed = (scaled * gate_rows).astype(BF16)
    for peer in range(peers):
        recv_copy(1, peer).wait()
    valid = lax.broadcasted_iota(jnp.int32, (width, positions), 1) < length
    cotangent = jnp.where(valid, cot_ref[...].astype(F32), 0.0)
    w_out_copy.wait()
    d_mixed = dot_nn(w_out_ref[...], cotangent.astype(BF16))
    out_ref[...] = (embedded + dot_tn(w_out_ref[...], mixed)).astype(BF16)
    out_copy.start()

    dproj_ref[pl.ds(0, width), :] = (d_mixed * scaled * slope_ref[pl.ds(0, width), :]).astype(BF16)
    d_att = norm_backward(d_mixed * gate_rows * gain_mid_ref[...], normal_mid, inverse_mid)
    att_ref[...] = d_att

    def d_weights(head):
        values = proj_ref[head_rows(1, head), :]
        d_head = att_ref[pl.ds(head * head_dim, head_dim), :].astype(BF16)
        return [dot_tn(values[:, start : start + half], d_head[:, start:]) for start, _ in blocks]

    def d_scores(head, products):
        low, high = (
            (block * score_slope_ref[head, pl.ds(start, half), pl.ds(start, positions - start)]).astype(
                BF16
            )
            for (start, _), block in zip(blocks, products)
        )
        empty = jnp.zeros((half, half), BF16)
        return jnp.concatenate([low, jnp.concatenate([empty, high], axis=1)], axis=0)

    def d_project(head, d_score):
        d_head = att_ref[pl.ds(head * head_dim, head_dim), :].astype(BF16)
        queries, keys = proj_ref[head_rows(2, head), :], proj_ref[head_rows(3, head), :]
        products = (
            dot_nt(d_head, weight_ref[head]),
            dot_nn(keys, d_score),
            dot_nt(queries, d_score),
        )
        for kind, product in zip((1, 2, 3), products):
            rows = head_rows(kind, head)
            dproj_ref[rows, :] = (product * slope_ref[rows, :]).astype(BF16)

    products, before = d_weights(0), None
    for head in range(HEADS):
        following = d_weights(head + 1) if head + 1 < HEADS else None
        d_score = d_scores(head, products)
        if head:
            d_project(head - 1, before)
        products, before = following, d_score
    d_project(HEADS - 1, before)

    w_in_copy.wait()
    d_normed = dot_nn(w_in_ref[...], dproj_ref[...])
    d_embedded = norm_backward(d_normed * gain_in_ref[...], normal_in, inverse_in)
    grad_ref[...] = (cotangent + d_embedded).astype(BF16)
    grad_copy.start()
    out_copy.wait()
    grad_copy.wait()


def run_layer(me, lengths, received, w_in, w_out, gain_in, gain_mid):
    peers, _, positions = received.shape
    width = w_out.shape[0]
    smem, vmem = pl.BlockSpec(memory_space=pltpu.SMEM), pl.BlockSpec(memory_space=pltpu.VMEM)
    hbm = pl.BlockSpec(memory_space=pltpu.HBM)
    shape = jax.ShapeDtypeStruct((width, positions), BF16)
    return pl.pallas_call(
        layer_kernel,
        out_shape=[shape, shape],
        in_specs=[smem, smem, hbm, hbm, hbm, hbm, vmem, vmem],
        out_specs=[hbm, hbm],
        scratch_shapes=[
            pltpu.VMEM((width, positions), BF16),
            pltpu.VMEM((width, positions), BF16),
            pltpu.VMEM((width, 4 * width), BF16),
            pltpu.VMEM((4 * width, width), BF16),
            pltpu.VMEM((width, width), BF16),
            pltpu.VMEM((width, positions), BF16),
            pltpu.VMEM((width, positions), BF16),
            pltpu.VMEM((4 * width, positions), BF16),
            pltpu.VMEM((4 * width, positions), F32),
            pltpu.VMEM((HEADS, positions, positions), BF16),
            pltpu.VMEM((HEADS, positions, positions), F32),
            pltpu.VMEM((width, positions), F32),
            pltpu.VMEM((4 * width, positions), BF16),
            pltpu.VMEM((width, positions), F32),
            pltpu.VMEM((width, positions), F32),
            pltpu.SemaphoreType.DMA((2, peers)),
            pltpu.SemaphoreType.DMA((4,)),
            pltpu.SemaphoreType.DMA((4,)),
        ],
        compiler_params=pltpu.CompilerParams(vmem_limit_bytes=WHOLE_VMEM_BYTES),
        cost_estimate=pl.CostEstimate(flops=10**10, bytes_accessed=10**7, transcendentals=10**6),
        name="layer",
    )(me, lengths, received, w_in, w_in.T, w_out, gain_in, gain_mid)


LOW = 256
STACK = 8


def ranks(member):
    users, positions = member.shape
    ones = jnp.where(member, 1.0, 0.0)
    row = lax.broadcasted_iota(jnp.int32, (positions, positions), 0)
    column = lax.broadcasted_iota(jnp.int32, (positions, positions), 1)
    before = jnp.where(row < column, 1.0, 0.0).astype(BF16)
    totals = jnp.sum(ones, axis=1, keepdims=True)
    user = lax.broadcasted_iota(jnp.int32, (users, 1), 0)
    earlier = jnp.zeros((users, 1), F32)
    for other in range(users - 1):
        earlier += jnp.where(user > other, totals[other : other + 1], 0.0)
    rank = dot_nn(ones.astype(BF16), before) + earlier
    return rank.astype(jnp.int32), jnp.sum(totals)


def plan_kernel(own, home_ref, turn_ref, ids_ref, low_ref, high_ref, slot_ref, most_ref, *scratch):
    chosen_ref, digit_ref, wide_ref = scratch
    groups, users, positions = ids_ref.shape
    capacity = low_ref.shape[1]
    home = home_ref[0]
    first = turn_ref[0] * capacity
    digit = lax.broadcasted_iota(jnp.int32, (LOW, positions), 0)
    place = lax.broadcasted_iota(jnp.int32, (capacity, positions), 0)

    def one_group(group, most):
        items = ids_ref[group]
        for owner in range(groups):
            count = jnp.sum(jnp.where(items // own == owner, 1.0, 0.0))
            most = jnp.maximum(most, count)
        local = items - home * own
        mine = (local >= 0) & (local < own)
        rank, _ = ranks(mine)
        slot = jnp.where(mine, rank - first, -1)
        low = local & (LOW - 1)
        high = jnp.where(mine, (local >> (LOW.bit_length() - 1)) + 1, 0).astype(F32)
        for user in range(users):
            columns = pl.ds(user * positions, positions)
            chosen_ref[:, columns] = jnp.where(place == slot[user : user + 1], 1.0, 0.0).astype(BF16)
            digit_ref[:, columns] = jnp.where(digit == low[user : user + 1], 1.0, 0.0).astype(BF16)
            wide_ref[:, columns] = jnp.broadcast_to(high[user : user + 1], (16, positions)).astype(BF16)
        low_ref[group] = dot_nt(chosen_ref[...], digit_ref[...]).astype(BF16)
        high_ref[pl.ds(group, 1), :] = dot_nt(wide_ref[...], chosen_ref[...])[:1]
        return most

    most_ref[0] = lax.fori_loop(0, groups, one_group, jnp.float32(0)).astype(jnp.int32)

    items = ids_ref[0]
    slot = jnp.full(items.shape, -1, jnp.int32)
    for owner in range(groups):
        belongs = items // own == owner
        rank = ranks(belongs)[0] - first
        fits = belongs & (rank >= 0) & (rank < capacity)
        slot = jnp.where(fits, rank + owner * capacity, slot)
    slot_ref[...] = slot


def plan_turn(home, turn, all_ids, own, capacity):
    groups, users, positions = all_ids.shape
    smem, vmem = pl.BlockSpec(memory_space=pltpu.SMEM), pl.BlockSpec(memory_space=pltpu.VMEM)
    return pl.pallas_call(
        functools.partial(plan_kernel, own),
        out_shape=[
            jax.ShapeDtypeStruct((groups, capacity, LOW), BF16),
            jax.ShapeDtypeStruct((groups, capacity), F32),
            jax.ShapeDtypeStruct((users, positions), jnp.int32),
            jax.ShapeDtypeStruct((1,), jnp.int32),
        ],
        in_specs=[smem, smem, vmem],
        out_specs=[vmem, vmem, vmem, smem],
        scratch_shapes=[
            pltpu.VMEM((capacity, users * positions), BF16),
            pltpu.VMEM((LOW, users * positions), BF16),
            pltpu.VMEM((16, users * positions), BF16),
        ],
        compiler_params=pltpu.CompilerParams(vmem_limit_bytes=VMEM_BYTES),
        cost_estimate=pl.CostEstimate(flops=4 * 10**9, bytes_accessed=5 * 10**6, transcendentals=0),
        name="plan_turn",
    )(home, turn, all_ids)


def pack_kernel(home_ref, slot_ref, grad_ref, *refs):
    *packed_refs, wide_ref, chosen_ref = refs
    users, _, positions = grad_ref.shape
    capacity = packed_refs[0].shape[1]
    step = pl.program_id(0)
    owner = home_ref[0] ^ step
    parts = capacity // LANES
    digit = lax.broadcasted_iota(jnp.int32, (LANES, positions), 0)
    for user in range(users):
        columns = pl.ds(user * positions, positions)
        wide_ref[:, columns] = grad_ref[user]
        slot = slot_ref[pl.ds(user, 1), :]
        ones = jnp.where(digit == (slot & (LANES - 1)), 1.0, 0.0).astype(BF16)
        high = slot >> (LANES.bit_length() - 1)
        for part in range(parts):
            chosen = jnp.where(high == owner * parts + part, 1.0, 0.0).astype(BF16)
            chosen_ref[pl.ds(part * LANES, LANES), columns] = ones * chosen
    packed = dot_nt(wide_ref[...], chosen_ref[...]).astype(BF16)
    for place, packed_ref in enumerate(packed_refs):

        @pl.when(step == place)
        def _():
            packed_ref[...] = packed


def pack_turn(home, slot, grads, owners, capacity):
    users, features, positions = grads.shape
    return pl.pallas_call(
        pack_kernel,
        grid=(owners,),
        out_shape=[jax.ShapeDtypeStruct((features, capacity), BF16)] * owners,
        in_specs=[
            pl.BlockSpec(memory_space=pltpu.SMEM),
            pl.BlockSpec(slot.shape, lambda i: (0, 0)),
            pl.BlockSpec(grads.shape, lambda i: (0, 0, 0)),
        ],
        out_specs=[pl.BlockSpec((features, capacity), lambda i: (0, 0))] * owners,
        scratch_shapes=[
            pltpu.VMEM((features, users * positions), BF16),
            pltpu.VMEM((capacity, users * positions), BF16),
        ],
        compiler_params=pltpu.CompilerParams(vmem_limit_bytes=VMEM_BYTES),
        cost_estimate=pl.CostEstimate(flops=3 * 10**9, bytes_accessed=10**6, transcendentals=0),
        name="pack_turn",
    )(home, slot, grads)


def scatter_kernel(groups, stack, low_ref, high_ref, *refs):
    list_refs, (*before_ref, out_ref, spread_ref) = refs[:groups], refs[groups:]
    features, capacity = list_refs[0].shape
    step = pl.program_id(0)
    for group, list_ref in enumerate(list_refs):
        high = high_ref[pl.ds(group, 1), :]
        for part in range(stack):
            wanted = (step * stack + part + 1).astype(F32)
            chosen = jnp.where(high == wanted, 1.0, 0.0).astype(BF16)
            spread_ref[pl.ds(part * features, features), pl.ds(group * capacity, capacity)] = (
                list_ref[...] * chosen
            )
    sums = dot_nn(spread_ref[...], low_ref[...])
    for part in range(stack):
        columns = pl.ds(part * LOW, LOW)
        term = sums[part * features : (part + 1) * features]
        out_ref[:, columns] = term + before_ref[0][:, columns] if before_ref else term


def scatter_slots(low, high, lists, own, before=None):
    groups = len(lists)
    features, capacity = lists[0].shape
    stack = min(STACK, own // LOW)
    block = pl.BlockSpec((features, stack * LOW), lambda i: (0, i))
    extra = [] if before is None else [before]
    return pl.pallas_call(
        functools.partial(scatter_kernel, groups, stack),
        grid=(own // (LOW * stack),),
        out_shape=jax.ShapeDtypeStruct((features, own), F32),
        in_specs=[
            pl.BlockSpec((groups * capacity, LOW), lambda i: (0, 0)),
            pl.BlockSpec(high.shape, lambda i: (0, 0)),
        ]
        + [pl.BlockSpec((features, capacity), lambda i: (0, 0))] * groups
        + [block] * len(extra),
        out_specs=block,
        scratch_shapes=[pltpu.VMEM((stack * features, groups * capacity), BF16)],
        input_output_aliases={2 + groups: 0} if extra else {},
        compiler_params=pltpu.CompilerParams(vmem_limit_bytes=VMEM_BYTES),
        cost_estimate=pl.CostEstimate(flops=4 * 10**9, bytes_accessed=10**7, transcendentals=0),
        name="scatter_slots",
    )(low.reshape(groups * capacity, LOW), high, *lists, *extra)


def swap(value, axis, distance):
    size = lax.axis_size(axis)
    return lax.ppermute(value, axis, [(i, i ^ distance) for i in range(size)])


def swap_lists(lists, axis):
    received = {k: swap(lists[k], axis, k) for k in reversed(range(1, len(lists)))}
    return [lists[0]] + [received[k] for k in range(1, len(lists))]


def exchange(value, axis):
    return lax.all_to_all(value, axis, split_axis=0, concat_axis=0, tiled=True)


def on_device(item_ids, user_len, emb_table, cotangent, w_uvqk, w_out, gain_in, gain_mid):
    dp_size = lax.axis_size("dp")
    table_size = lax.axis_size("table")
    users = user_len.shape[0]
    features, vocab = emb_table.shape
    rows = item_ids.shape[0]
    positions = rows // users
    own = vocab // dp_size
    capacity = -(-(rows // dp_size * 5 // 4) // LANES) * LANES
    assert users == table_size and users <= LANES and positions <= 256 and own // LOW <= 255
    assert dp_size & (dp_size - 1) == 0
    me = lax.axis_index("table").astype(jnp.int32).reshape(1)
    home = lax.axis_index("dp").astype(jnp.int32).reshape(1)

    send, valid_ids = gather_columns(item_ids, user_len, cotangent, emb_table)
    received = exchange(send, "table")
    all_ids = jnp.stack([valid_ids] + [swap(valid_ids, "dp", k) for k in range(1, dp_size)])
    plan = plan_turn(home, jnp.zeros((1,), jnp.int32), all_ids, own, capacity)
    received, (low, high, slot, most) = lax.optimization_barrier((received, plan))
    out_cols, grad_cols = run_layer(me, user_len, received, w_uvqk, w_out, gain_in, gain_mid)
    per_peer = (table_size, features, positions)
    grad_home = exchange(grad_cols.reshape(per_peer), "table")
    out_cols, grad_home = lax.optimization_barrier((out_cols, grad_home))
    out_home = exchange(out_cols.reshape(per_peer), "table")
    lists = swap_lists(pack_turn(home, slot, grad_home, dp_size, capacity), "dp")
    table_grad = scatter_slots(low, high, lists, own)
    layer_out = jnp.transpose(out_home, (1, 0, 2)).reshape(features, rows)

    turns = (most[0] + capacity - 1) // capacity

    def another(state):
        turn, sums = state
        more_low, more_high, more_slot, _ = plan_turn(home, turn.reshape(1), all_ids, own, capacity)
        arrived = swap_lists(pack_turn(home, more_slot, grad_home, dp_size, capacity), "dp")
        return turn + 1, scatter_slots(more_low, more_high, arrived, own, sums)

    _, table_grad = lax.while_loop(
        lambda state: state[0] < turns, another, (jnp.int32(1), table_grad)
    )
    return (layer_out, table_grad)


def solution(mesh):
    return jax.shard_map(
        on_device,
        mesh=mesh,
        in_specs=(P("dp"), P("dp"), P("table", None), P("table", "dp"), P(), P(), P(), P()),
        out_specs=(P("table", "dp"), P("table", "dp")),
        check_vma=False,
    )
```

```python
import functools

import jax
import jax.numpy as jnp
from jax import lax
from jax.experimental import pallas as pl
from jax.experimental.pallas import tpu as pltpu
from jax.sharding import PartitionSpec as P

HEADS = 8
NORM_EPS = 1e-05
LANES = 128
VMEM_BYTES = 48 * 1024 * 1024
WHOLE_VMEM_BYTES = 61 * 1024 * 1024
LAYER_VMEM_BYTES = 32 * 1024 * 1024

F32 = jnp.float32
BF16 = jnp.bfloat16


def dot_nn(left, right):
    return jnp.dot(left, right, preferred_element_type=F32)


def dot_nt(left, right):
    return lax.dot_general(left, right, (((1,), (1,)), ((), ())), preferred_element_type=F32)


def dot_tn(left, right):
    return lax.dot_general(left, right, (((0,), (0,)), ((), ())), preferred_element_type=F32)


BLOCK = 256
UNROLL = 64
CHUNK_ROWS = 16


def gather_kernel(
    len_ref,
    ids_ref,
    cot_hbm_ref,
    table_hbm_ref,
    out_ref,
    valid_ref,
    table_ref,
    cot_ref,
    rows_ref,
    picked_ref,
    turned_ref,
    row_vector_ref,
    row_ref,
    chunk_sems,
    row_sem,
    out_sems,
    cot_sem,
):
    users, _, positions = out_ref.shape
    features, vocab = table_hbm_ref.shape
    pack = LANES // features
    span = BLOCK * pack
    block_bits = BLOCK.bit_length() - 1

    def chunk_copy(chunk):
        rows = pl.ds(chunk * CHUNK_ROWS, CHUNK_ROWS)
        return pltpu.make_async_copy(
            table_hbm_ref.at[rows, :], table_ref.at[rows, :], chunk_sems.at[chunk]
        )

    def out_copy(user):
        return pltpu.make_async_copy(turned_ref.at[user], out_ref.at[user], out_sems.at[user])

    for chunk in range(features // CHUNK_ROWS):
        chunk_copy(chunk).start()
    cot_copy = pltpu.make_async_copy(cot_hbm_ref, cot_ref, cot_sem)
    cot_copy.start()
    items = ids_ref[...]
    row_vector_ref[...] = ((items >> (span.bit_length() - 1)) << block_bits) | (items & (BLOCK - 1))
    row_copy = pltpu.make_async_copy(row_vector_ref, row_ref, row_sem)
    row_copy.start()
    order = lax.broadcasted_iota(jnp.int32, (1, positions), 1)
    for user in range(users):
        own_items = ids_ref[pl.ds(user * positions, positions)].reshape(1, positions)
        valid_ref[pl.ds(user, 1), :] = jnp.where(order < len_ref[user], own_items, vocab)

    cot_copy.wait()
    for user in range(users):
        turned_ref[user, pl.ds(features, features), :] = cot_ref[:, pl.ds(user * positions, positions)]

    for chunk in range(features // CHUNK_ROWS):
        chunk_copy(chunk).wait()
    for part in range(vocab // span):
        stack = jnp.concatenate(
            [
                table_ref[:, part * span + s * BLOCK : part * span + (s + 1) * BLOCK]
                for s in range(pack)
            ],
            axis=0,
        )
        rows_ref[pl.ds(part * BLOCK, BLOCK), :] = stack.T.astype(F32)
    row_copy.wait()

    def some(part, carry):
        start = pl.multiple_of(part * UNROLL, UNROLL)
        for slot in range(UNROLL):
            row = row_ref[start + slot]
            picked_ref[pl.ds(start + slot, 1), :] = rows_ref[pl.ds(row, 1), :]
        return carry

    lax.fori_loop(0, users * positions // UNROLL, some, 0)
    row = lax.broadcasted_iota(jnp.int32, (LANES, LANES), 0)
    column = lax.broadcasted_iota(jnp.int32, (LANES, LANES), 1)
    same = jnp.where(row == column, 1.0, 0.0).astype(BF16)
    for user in range(users):
        places = pl.ds(user * positions, positions)
        turned = dot_nt(same, picked_ref[places, :].astype(BF16))
        own_items = ids_ref[places].reshape(1, positions)
        group = (own_items >> block_bits) & (pack - 1)
        total = turned[:features]
        for s in range(1, pack):
            total = jnp.where(group == s, turned[s * features : (s + 1) * features], total)
        turned_ref[user, pl.ds(0, features), :] = total.astype(BF16)
        out_copy(user).start()
    for user in range(users):
        out_copy(user).wait()


def gather_columns(item_ids, lengths, cotangent, table):
    users = lengths.shape[0]
    rows = item_ids.shape[0]
    positions = rows // users
    features, vocab = table.shape
    pack = LANES // features
    shape = (users, 2 * features, positions)
    hbm = pl.BlockSpec(memory_space=pltpu.HBM)
    vmem = pl.BlockSpec(memory_space=pltpu.VMEM)
    return pl.pallas_call(
        gather_kernel,
        out_shape=[
            jax.ShapeDtypeStruct(shape, table.dtype),
            jax.ShapeDtypeStruct((users, positions), jnp.int32),
        ],
        in_specs=[pl.BlockSpec(memory_space=pltpu.SMEM), vmem, hbm, hbm],
        out_specs=[hbm, vmem],
        scratch_shapes=[
            pltpu.VMEM((features, vocab), table.dtype),
            pltpu.VMEM((features, rows), table.dtype),
            pltpu.VMEM((vocab // pack, LANES), F32),
            pltpu.VMEM((rows, LANES), F32),
            pltpu.VMEM(shape, table.dtype),
            pltpu.VMEM((rows,), jnp.int32),
            pltpu.SMEM((rows,), jnp.int32),
            pltpu.SemaphoreType.DMA((features // CHUNK_ROWS,)),
            pltpu.SemaphoreType.DMA,
            pltpu.SemaphoreType.DMA((users,)),
            pltpu.SemaphoreType.DMA,
        ],
        compiler_params=pltpu.CompilerParams(vmem_limit_bytes=WHOLE_VMEM_BYTES),
        cost_estimate=pl.CostEstimate(flops=8 * 10**9, bytes_accessed=5 * 10**6, transcendentals=0),
        name="gather_columns",
    )(lengths, item_ids, cotangent, table)


def norm_forward(values):
    centred = values - jnp.mean(values, axis=0, keepdims=True)
    inverse = lax.rsqrt(jnp.mean(centred * centred, axis=0, keepdims=True) + NORM_EPS)
    return centred * inverse, inverse


def norm_backward(grad, normal, inverse):
    shift = jnp.mean(grad, axis=0, keepdims=True)
    slope = jnp.mean(grad * normal, axis=0, keepdims=True)
    return (grad - shift - normal * slope) * inverse


def silu_pair(half):
    turn = jnp.tanh(half)
    twice = 1.0 + turn
    value = half * twice
    return value, twice + value * (1.0 - turn)


def layer_kernel(
    me_ref,
    len_ref,
    recv_ref,
    w_in_ref,
    w_in_t_ref,
    w_out_ref,
    gain_in_row_ref,
    gain_mid_row_ref,
    out_hbm_ref,
    grad_hbm_ref,
    out_ref,
    grad_ref,
    proj_ref,
    slope_ref,
    weight_ref,
    score_slope_ref,
    att_ref,
    dproj_ref,
    gain_in_ref,
    gain_mid_ref,
    share_ref,
    sems,
):
    peers, both, positions = recv_ref.shape
    features = both // 2
    width = peers * features
    head_dim = width // HEADS
    half = positions // 2

    out_copy = pltpu.make_async_copy(out_ref, out_hbm_ref, sems.at[0])
    grad_copy = pltpu.make_async_copy(grad_ref, grad_hbm_ref, sems.at[1])
    length = len_ref[me_ref[0]]
    share = 1.0 / length.astype(F32)
    for row_ref, column_ref in ((gain_in_row_ref, gain_in_ref), (gain_mid_row_ref, gain_mid_ref)):
        row = row_ref[...].reshape(1, width)
        column_ref[...] = jnp.broadcast_to(row, (positions, width)).T

    key = lax.broadcasted_iota(jnp.int32, (positions, positions), 0)
    query = lax.broadcasted_iota(jnp.int32, (positions, positions), 1)
    share_ref[...] = jnp.where((key <= query) & (key < length), share, 0.0)

    def joined(kind):
        rows = pl.ds(kind * features, features)
        return jnp.concatenate([recv_ref[peer, rows, :] for peer in range(peers)], axis=0)

    embedded = joined(0).astype(F32)
    normal_in, inverse_in = norm_forward(embedded)
    normed = (normal_in * gain_in_ref[...]).astype(BF16)

    def project(part):
        return dot_nn(w_in_t_ref[pl.ds(part * width, width), :], normed)

    def store_projected(part, z):
        rows = pl.ds(part * width, width)
        value, slope = silu_pair(0.5 * z)
        proj_ref[rows, :] = value.astype(BF16)
        slope_ref[rows, :] = slope

    waiting = None
    for part in (2, 3, 1, 0):
        z = project(part)
        if waiting is not None:
            store_projected(*waiting)
        waiting = (part, z)
    store_projected(*waiting)

    starts = (0, half)
    scale = head_dim ** (-0.5)

    def head_rows(kind, head):
        return pl.ds(kind * width + head * head_dim, head_dim)

    def score(head):
        queries, keys = proj_ref[head_rows(2, head), :], proj_ref[head_rows(3, head), :]
        return [dot_tn(keys[:, start : start + half], queries[:, start:]) for start in starts]

    def store_weights(head, scores):
        for start, block in zip(starts, scores):
            value, slope = silu_pair(block * (0.5 * scale))
            places = (pl.ds(start, half), pl.ds(start, positions - start))
            weight_ref[head, *places] = (value * share_ref[*places]).astype(BF16)
            score_slope_ref[head, *places] = slope * share_ref[*places]
        weight_ref[head, pl.ds(half, half), pl.ds(0, half)] = jnp.zeros((half, half), BF16)

    def attend(head):
        att_ref[pl.ds(head * head_dim, head_dim), :] = dot_nn(
            proj_ref[head_rows(1, head), :], weight_ref[head]
        )

    scores = score(0)
    for head in range(HEADS):
        following = score(head + 1) if head + 1 < HEADS else None
        store_weights(head, scores)
        if head:
            attend(head - 1)
        scores = following
    attend(HEADS - 1)

    normal_mid, inverse_mid = norm_forward(att_ref[...])
    gate_rows = proj_ref[pl.ds(0, width), :].astype(F32)
    scaled = normal_mid * gain_mid_ref[...]
    mixed = (scaled * gate_rows).astype(BF16)
    valid = lax.broadcasted_iota(jnp.int32, (width, positions), 1) < length
    cotangent = jnp.where(valid, joined(1).astype(F32), 0.0)
    d_mixed = dot_nn(w_out_ref[...], cotangent.astype(BF16))
    out_ref[...] = (embedded + dot_tn(w_out_ref[...], mixed)).astype(BF16)
    out_copy.start()

    dproj_ref[pl.ds(0, width), :] = (d_mixed * scaled * slope_ref[pl.ds(0, width), :]).astype(BF16)
    d_att = norm_backward(d_mixed * gate_rows * gain_mid_ref[...], normal_mid, inverse_mid)
    att_ref[...] = d_att

    def d_weights(head):
        values = proj_ref[head_rows(1, head), :]
        d_head = att_ref[pl.ds(head * head_dim, head_dim), :].astype(BF16)
        return [dot_tn(values[:, start : start + half], d_head[:, start:]) for start in starts]

    def d_scores(head, products):
        low, high = (
            (block * score_slope_ref[head, pl.ds(start, half), pl.ds(start, positions - start)]).astype(
                BF16
            )
            for start, block in zip(starts, products)
        )
        empty = jnp.zeros((half, half), BF16)
        return jnp.concatenate([low, jnp.concatenate([empty, high], axis=1)], axis=0)

    def d_project(head, d_score):
        d_head = att_ref[pl.ds(head * head_dim, head_dim), :].astype(BF16)
        queries, keys = proj_ref[head_rows(2, head), :], proj_ref[head_rows(3, head), :]
        products = (
            dot_nt(d_head, weight_ref[head]),
            dot_nn(keys, d_score) * (0.5 * scale),
            dot_nt(queries, d_score) * (0.5 * scale),
        )
        for kind, product in zip((1, 2, 3), products):
            rows = head_rows(kind, head)
            dproj_ref[rows, :] = (product * slope_ref[rows, :]).astype(BF16)

    products, before = d_weights(0), None
    for head in range(HEADS):
        following = d_weights(head + 1) if head + 1 < HEADS else None
        d_score = d_scores(head, products)
        if head:
            d_project(head - 1, before)
        products, before = following, d_score
    d_project(HEADS - 1, before)

    d_normed = dot_nn(w_in_ref[...], dproj_ref[...])
    d_embedded = norm_backward(d_normed * (0.5 * gain_in_ref[...]), normal_in, inverse_in)
    grad_ref[...] = (cotangent + d_embedded).astype(BF16)
    grad_copy.start()
    out_copy.wait()
    grad_copy.wait()


def run_layer(me, lengths, received, w_in, w_out, gain_in, gain_mid):
    peers, _, positions = received.shape
    width = w_out.shape[0]
    smem, vmem = pl.BlockSpec(memory_space=pltpu.SMEM), pl.BlockSpec(memory_space=pltpu.VMEM)
    hbm = pl.BlockSpec(memory_space=pltpu.HBM)
    shape = jax.ShapeDtypeStruct((width, positions), BF16)
    return pl.pallas_call(
        layer_kernel,
        out_shape=[shape, shape],
        in_specs=[smem, smem] + [vmem] * 6,
        out_specs=[hbm, hbm],
        scratch_shapes=[
            pltpu.VMEM((width, positions), BF16),
            pltpu.VMEM((width, positions), BF16),
            pltpu.VMEM((4 * width, positions), BF16),
            pltpu.VMEM((4 * width, positions), F32),
            pltpu.VMEM((HEADS, positions, positions), BF16),
            pltpu.VMEM((HEADS, positions, positions), F32),
            pltpu.VMEM((width, positions), F32),
            pltpu.VMEM((4 * width, positions), BF16),
            pltpu.VMEM((width, positions), F32),
            pltpu.VMEM((width, positions), F32),
            pltpu.VMEM((positions, positions), F32),
            pltpu.SemaphoreType.DMA((2,)),
        ],
        compiler_params=pltpu.CompilerParams(vmem_limit_bytes=LAYER_VMEM_BYTES),
        cost_estimate=pl.CostEstimate(flops=10**10, bytes_accessed=10**7, transcendentals=10**6),
        name="layer",
    )(me, lengths, received, w_in, w_in.T, w_out, gain_in, gain_mid)


LOW = 256
STACK = 16


def ranks(member):
    users, positions = member.shape
    ones = jnp.where(member, 1.0, 0.0)
    row = lax.broadcasted_iota(jnp.int32, (positions, positions), 0)
    column = lax.broadcasted_iota(jnp.int32, (positions, positions), 1)
    before = jnp.where(row < column, 1.0, 0.0).astype(BF16)
    totals = jnp.sum(ones, axis=1, keepdims=True)
    user = lax.broadcasted_iota(jnp.int32, (users, 1), 0)
    earlier = jnp.zeros((users, 1), F32)
    for other in range(users - 1):
        earlier += jnp.where(user > other, totals[other : other + 1], 0.0)
    rank = dot_nn(ones.astype(BF16), before) + earlier
    return rank.astype(jnp.int32), jnp.sum(totals)


EARLY = 2


def plan_kernel(own, home_ref, turn_ref, ids_ref, *refs):
    early_refs, late_refs, refs = refs[:2], refs[2:4], refs[4:]
    slot_ref, most_ref, chosen_ref, digit_ref, wide_ref = refs
    groups, users, positions = ids_ref.shape
    capacity = chosen_ref.shape[0]
    home = home_ref[0]
    first = turn_ref[0] * capacity
    digit = lax.broadcasted_iota(jnp.int32, (LOW, positions), 0)
    place = lax.broadcasted_iota(jnp.int32, (capacity, positions), 0)

    def one_group(low_ref, high_ref, before, group, most):
        items = ids_ref[before + group]
        for owner in range(groups):
            count = jnp.sum(jnp.where(items // own == owner, 1.0, 0.0))
            most = jnp.maximum(most, count)
        local = items - home * own
        mine = (local >= 0) & (local < own)
        rank, _ = ranks(mine)
        slot = jnp.where(mine, rank - first, -1)
        low = local & (LOW - 1)
        high = jnp.where(mine, (local >> (LOW.bit_length() - 1)) + 1, 0).astype(F32)
        for user in range(users):
            columns = pl.ds(user * positions, positions)
            chosen_ref[:, columns] = jnp.where(place == slot[user : user + 1], 1.0, 0.0).astype(BF16)
            digit_ref[:, columns] = jnp.where(digit == low[user : user + 1], 1.0, 0.0).astype(BF16)
            wide_ref[:, columns] = jnp.broadcast_to(high[user : user + 1], (16, positions)).astype(BF16)
        low_ref[group] = dot_nt(chosen_ref[...], digit_ref[...]).astype(BF16)
        high_ref[pl.ds(group, 1), :] = dot_nt(wide_ref[...], chosen_ref[...])[:1]
        return most

    most = jnp.float32(0)
    for before, part_refs in ((0, early_refs), (EARLY, late_refs)):
        step = functools.partial(one_group, *part_refs, before)
        most = lax.fori_loop(0, part_refs[0].shape[0], step, most)
    most_ref[0] = most.astype(jnp.int32)

    items = ids_ref[0]
    slot = jnp.full(items.shape, -1, jnp.int32)
    for owner in range(groups):
        belongs = items // own == owner
        rank = ranks(belongs)[0] - first
        fits = belongs & (rank >= 0) & (rank < capacity)
        slot = jnp.where(fits, rank + owner * capacity, slot)
    slot_ref[...] = slot


def plan_turn(home, turn, all_ids, own, capacity):
    groups, users, positions = all_ids.shape
    smem, vmem = pl.BlockSpec(memory_space=pltpu.SMEM), pl.BlockSpec(memory_space=pltpu.VMEM)
    return pl.pallas_call(
        functools.partial(plan_kernel, own),
        out_shape=[
            jax.ShapeDtypeStruct((EARLY, capacity, LOW), BF16),
            jax.ShapeDtypeStruct((EARLY, capacity), F32),
            jax.ShapeDtypeStruct((groups - EARLY, capacity, LOW), BF16),
            jax.ShapeDtypeStruct((groups - EARLY, capacity), F32),
            jax.ShapeDtypeStruct((users, positions), jnp.int32),
            jax.ShapeDtypeStruct((1,), jnp.int32),
        ],
        in_specs=[smem, smem, vmem],
        out_specs=[vmem] * 5 + [smem],
        scratch_shapes=[
            pltpu.VMEM((capacity, users * positions), BF16),
            pltpu.VMEM((LOW, users * positions), BF16),
            pltpu.VMEM((16, users * positions), BF16),
        ],
        compiler_params=pltpu.CompilerParams(vmem_limit_bytes=VMEM_BYTES),
        cost_estimate=pl.CostEstimate(flops=4 * 10**9, bytes_accessed=5 * 10**6, transcendentals=0),
        name="plan_turn",
    )(home, turn, all_ids)


def pack_kernel(distances, home_ref, slot_ref, grad_ref, *refs):
    *packed_refs, wide_ref, chosen_ref = refs
    users, _, positions = grad_ref.shape
    capacity = packed_refs[0].shape[1]
    padded = jnp.concatenate(
        [slot_ref[...].astype(F32), jnp.zeros((LANES - users, positions), F32)], axis=0
    )
    slots = padded.T.astype(jnp.int32)
    place = lax.broadcasted_iota(jnp.int32, (positions, capacity), 1)
    for user in range(users):
        wide_ref[:, pl.ds(user * positions, positions)] = grad_ref[user]
    for distance, packed_ref in zip(distances, packed_refs):
        first = (home_ref[0] ^ distance) * capacity
        for user in range(users):
            chosen_ref[pl.ds(user * positions, positions), :] = jnp.where(
                place == slots[:, user : user + 1] - first, 1.0, 0.0
            ).astype(BF16)
        packed_ref[...] = dot_nn(wide_ref[...], chosen_ref[...]).astype(BF16)


def pack_lists(distances, home, slot, grads, capacity):
    users, features, positions = grads.shape
    smem, vmem = pl.BlockSpec(memory_space=pltpu.SMEM), pl.BlockSpec(memory_space=pltpu.VMEM)
    return pl.pallas_call(
        functools.partial(pack_kernel, distances),
        out_shape=[jax.ShapeDtypeStruct((features, capacity), BF16)] * len(distances),
        in_specs=[smem, vmem, vmem],
        out_specs=[vmem] * len(distances),
        scratch_shapes=[
            pltpu.VMEM((features, users * positions), BF16),
            pltpu.VMEM((users * positions, capacity), BF16),
        ],
        compiler_params=pltpu.CompilerParams(vmem_limit_bytes=LAYER_VMEM_BYTES),
        cost_estimate=pl.CostEstimate(
            flops=len(distances) * 8 * 10**8, bytes_accessed=10**6, transcendentals=0
        ),
        name="pack_lists",
    )(home, slot, grads)


def scatter_kernel(groups, stack, low_ref, high_ref, *refs):
    list_refs, (*before_ref, out_ref, spread_ref) = refs[:groups], refs[groups:]
    features, capacity = list_refs[0].shape
    step = pl.program_id(0)
    for group, list_ref in enumerate(list_refs):
        high = high_ref[pl.ds(group, 1), :]
        for part in range(stack):
            wanted = (step * stack + part + 1).astype(F32)
            chosen = jnp.where(high == wanted, 1.0, 0.0).astype(BF16)
            spread_ref[pl.ds(part * features, features), pl.ds(group * capacity, capacity)] = (
                list_ref[...] * chosen
            )
    sums = dot_nn(spread_ref[...], low_ref[...])
    for part in range(stack):
        columns = pl.ds(part * LOW, LOW)
        term = sums[part * features : (part + 1) * features]
        out_ref[:, columns] = term + before_ref[0][:, columns] if before_ref else term


def scatter_slots(low, high, lists, own, before=None):
    groups = len(lists)
    features, capacity = lists[0].shape
    low = low.reshape(groups * capacity, LOW)
    stack = min(STACK, own // LOW)
    block = pl.BlockSpec((features, stack * LOW), lambda i: (0, i))
    extra = [] if before is None else [before]
    return pl.pallas_call(
        functools.partial(scatter_kernel, groups, stack),
        grid=(own // (LOW * stack),),
        out_shape=jax.ShapeDtypeStruct((features, own), F32),
        in_specs=[
            pl.BlockSpec((groups * capacity, LOW), lambda i: (0, 0)),
            pl.BlockSpec(high.shape, lambda i: (0, 0)),
        ]
        + [pl.BlockSpec((features, capacity), lambda i: (0, 0))] * groups
        + [block] * len(extra),
        out_specs=block,
        scratch_shapes=[pltpu.VMEM((stack * features, groups * capacity), BF16)],
        input_output_aliases={2 + groups: 0} if extra else {},
        compiler_params=pltpu.CompilerParams(vmem_limit_bytes=VMEM_BYTES),
        cost_estimate=pl.CostEstimate(flops=4 * 10**9, bytes_accessed=10**7, transcendentals=0),
        name="scatter_slots",
    )(low, high, *lists, *extra)


def swap(value, axis, distance):
    size = lax.axis_size(axis)
    return lax.ppermute(value, axis, [(i, i ^ distance) for i in range(size)])


def deliver(home, plan, grads, own, capacity, before=None):
    early_low, early_high, late_low, late_high, slot, _ = plan
    farthest = early_low.shape[0] + late_low.shape[0] - 1
    near = tuple(range(farthest))
    (far_list,) = pack_lists((farthest,), home, slot, grads, capacity)
    far_list = swap(far_list, "dp", farthest)
    own_list, *near_lists = pack_lists(near, home, slot, grads, capacity)
    near_lists = [swap(near_list, "dp", k) for k, near_list in zip(near[1:], near_lists)]
    sums = scatter_slots(early_low, early_high, [own_list, far_list], own, before)
    return scatter_slots(late_low, late_high, near_lists, own, sums)


def exchange(value, axis):
    return lax.all_to_all(value, axis, split_axis=0, concat_axis=0, tiled=True)


def on_device(item_ids, user_len, emb_table, cotangent, w_uvqk, w_out, gain_in, gain_mid):
    dp_size = lax.axis_size("dp")
    table_size = lax.axis_size("table")
    users = user_len.shape[0]
    features, vocab = emb_table.shape
    rows = item_ids.shape[0]
    positions = rows // users
    own = vocab // dp_size
    capacity = -(-(rows // dp_size * 5 // 4) // LANES) * LANES
    assert users == table_size and users <= LANES and positions <= 256 and own // LOW <= 255
    assert dp_size & (dp_size - 1) == 0 and dp_size > EARLY
    me = lax.axis_index("table").astype(jnp.int32).reshape(1)
    home = lax.axis_index("dp").astype(jnp.int32).reshape(1)

    send, valid_ids = gather_columns(item_ids, user_len, cotangent, emb_table)
    received = exchange(send, "table")
    distances = [dp_size - 1] + list(range(1, dp_size - 1))
    all_ids = jnp.stack([valid_ids] + [swap(valid_ids, "dp", k) for k in distances])
    plan = plan_turn(home, jnp.zeros((1,), jnp.int32), all_ids, own, capacity)
    received, plan = lax.optimization_barrier((received, plan))
    out_cols, grad_cols = run_layer(me, user_len, received, w_uvqk, w_out, gain_in, gain_mid)
    per_peer = (table_size, features, positions)
    grad_home = exchange(grad_cols.reshape(per_peer), "table")
    out_cols, grad_home = lax.optimization_barrier((out_cols, grad_home))
    out_home = exchange(out_cols.reshape(per_peer), "table")
    table_grad = deliver(home, plan, grad_home, own, capacity)
    layer_out = jnp.transpose(out_home, (1, 0, 2)).reshape(features, rows)

    turns = (plan[-1][0] + capacity - 1) // capacity

    def another(state):
        turn, sums = state
        more = plan_turn(home, turn.reshape(1), all_ids, own, capacity)
        return turn + 1, deliver(home, more, grad_home, own, capacity, sums)

    _, table_grad = lax.while_loop(
        lambda state: state[0] < turns, another, (jnp.int32(1), table_grad)
    )
    return (layer_out, table_grad)


def solution(mesh):
    return jax.shard_map(
        on_device,
        mesh=mesh,
        in_specs=(P("dp"), P("dp"), P("table", None), P("table", "dp"), P(), P(), P(), P()),
        out_specs=(P("table", "dp"), P("table", "dp")),
        check_vma=False,
    )
```

```python
import functools

import jax
import jax.numpy as jnp
from jax import lax
from jax.experimental import pallas as pl
from jax.experimental.pallas import tpu as pltpu
from jax.sharding import PartitionSpec as P

HEADS = 8
NORM_EPS = 1e-05
LANES = 128
VMEM_BYTES = 48 * 1024 * 1024
WHOLE_VMEM_BYTES = 61 * 1024 * 1024
LAYER_VMEM_BYTES = 60 * 1024 * 1024
LIST_VMEM_BYTES = 32 * 1024 * 1024

F32 = jnp.float32
BF16 = jnp.bfloat16


def dot_nn(left, right):
    return jnp.dot(left, right, preferred_element_type=F32)


def dot_nt(left, right):
    return lax.dot_general(left, right, (((1,), (1,)), ((), ())), preferred_element_type=F32)


def dot_tn(left, right):
    return lax.dot_general(left, right, (((0,), (0,)), ((), ())), preferred_element_type=F32)


BLOCK = 256
UNROLL = 64
CHUNK_ROWS = 16


def gather_kernel(
    len_ref,
    ids_ref,
    cot_hbm_ref,
    table_hbm_ref,
    out_ref,
    valid_ref,
    table_ref,
    cot_ref,
    rows_ref,
    picked_ref,
    turned_ref,
    row_vector_ref,
    row_ref,
    chunk_sems,
    row_sem,
    out_sems,
    cot_sem,
):
    users, _, positions = out_ref.shape
    features, vocab = table_hbm_ref.shape
    pack = LANES // features
    span = BLOCK * pack
    block_bits = BLOCK.bit_length() - 1

    def chunk_copy(chunk):
        rows = pl.ds(chunk * CHUNK_ROWS, CHUNK_ROWS)
        return pltpu.make_async_copy(
            table_hbm_ref.at[rows, :], table_ref.at[rows, :], chunk_sems.at[chunk]
        )

    def out_copy(user):
        return pltpu.make_async_copy(turned_ref.at[user], out_ref.at[user], out_sems.at[user])

    for chunk in range(features // CHUNK_ROWS):
        chunk_copy(chunk).start()
    cot_copy = pltpu.make_async_copy(cot_hbm_ref, cot_ref, cot_sem)
    cot_copy.start()
    items = ids_ref[...]
    row_vector_ref[...] = ((items >> (span.bit_length() - 1)) << block_bits) | (items & (BLOCK - 1))
    row_copy = pltpu.make_async_copy(row_vector_ref, row_ref, row_sem)
    row_copy.start()
    order = lax.broadcasted_iota(jnp.int32, (1, positions), 1)
    for user in range(users):
        own_items = ids_ref[pl.ds(user * positions, positions)].reshape(1, positions)
        valid_ref[pl.ds(user, 1), :] = jnp.where(order < len_ref[user], own_items, vocab)

    cot_copy.wait()
    for user in range(users):
        turned_ref[user, pl.ds(features, features), :] = cot_ref[:, pl.ds(user * positions, positions)]

    for chunk in range(features // CHUNK_ROWS):
        chunk_copy(chunk).wait()
    for part in range(vocab // span):
        stack = jnp.concatenate(
            [
                table_ref[:, part * span + s * BLOCK : part * span + (s + 1) * BLOCK]
                for s in range(pack)
            ],
            axis=0,
        )
        rows_ref[pl.ds(part * BLOCK, BLOCK), :] = stack.T.astype(F32)
    row_copy.wait()

    def some(part, carry):
        start = pl.multiple_of(part * UNROLL, UNROLL)
        for slot in range(UNROLL):
            row = row_ref[start + slot]
            picked_ref[pl.ds(start + slot, 1), :] = rows_ref[pl.ds(row, 1), :]
        return carry

    lax.fori_loop(0, users * positions // UNROLL, some, 0)
    row = lax.broadcasted_iota(jnp.int32, (LANES, LANES), 0)
    column = lax.broadcasted_iota(jnp.int32, (LANES, LANES), 1)
    same = jnp.where(row == column, 1.0, 0.0).astype(BF16)
    for user in range(users):
        places = pl.ds(user * positions, positions)
        turned = dot_nt(same, picked_ref[places, :].astype(BF16))
        own_items = ids_ref[places].reshape(1, positions)
        group = (own_items >> block_bits) & (pack - 1)
        total = turned[:features]
        for s in range(1, pack):
            total = jnp.where(group == s, turned[s * features : (s + 1) * features], total)
        turned_ref[user, pl.ds(0, features), :] = total.astype(BF16)
        out_copy(user).start()
    for user in range(users):
        out_copy(user).wait()


def gather_columns(item_ids, lengths, cotangent, table):
    users = lengths.shape[0]
    rows = item_ids.shape[0]
    positions = rows // users
    features, vocab = table.shape
    pack = LANES // features
    shape = (users, 2 * features, positions)
    hbm = pl.BlockSpec(memory_space=pltpu.HBM)
    vmem = pl.BlockSpec(memory_space=pltpu.VMEM)
    return pl.pallas_call(
        gather_kernel,
        out_shape=[
            jax.ShapeDtypeStruct(shape, table.dtype),
            jax.ShapeDtypeStruct((users, positions), jnp.int32),
        ],
        in_specs=[pl.BlockSpec(memory_space=pltpu.SMEM), vmem, hbm, hbm],
        out_specs=[hbm, vmem],
        scratch_shapes=[
            pltpu.VMEM((features, vocab), table.dtype),
            pltpu.VMEM((features, rows), table.dtype),
            pltpu.VMEM((vocab // pack, LANES), F32),
            pltpu.VMEM((rows, LANES), F32),
            pltpu.VMEM(shape, table.dtype),
            pltpu.VMEM((rows,), jnp.int32),
            pltpu.SMEM((rows,), jnp.int32),
            pltpu.SemaphoreType.DMA((features // CHUNK_ROWS,)),
            pltpu.SemaphoreType.DMA,
            pltpu.SemaphoreType.DMA((users,)),
            pltpu.SemaphoreType.DMA,
        ],
        compiler_params=pltpu.CompilerParams(vmem_limit_bytes=WHOLE_VMEM_BYTES),
        cost_estimate=pl.CostEstimate(flops=8 * 10**9, bytes_accessed=5 * 10**6, transcendentals=0),
        name="gather_columns",
    )(lengths, item_ids, cotangent, table)


def norm_forward(values):
    centred = values - jnp.mean(values, axis=0, keepdims=True)
    inverse = lax.rsqrt(jnp.mean(centred * centred, axis=0, keepdims=True) + NORM_EPS)
    return centred * inverse, inverse


def norm_backward(grad, normal, inverse):
    shift = jnp.mean(grad, axis=0, keepdims=True)
    slope = jnp.mean(grad * normal, axis=0, keepdims=True)
    return (grad - shift - normal * slope) * inverse


def silu_pair(half):
    turn = jnp.tanh(half)
    twice = 1.0 + turn
    value = half * twice
    return value, twice + value * (1.0 - turn)


def layer_kernel(
    me_ref,
    len_ref,
    recv_ref,
    w_in_hbm_ref,
    w_t_hbm_ref,
    w_out_hbm_ref,
    gain_in_row_ref,
    gain_mid_row_ref,
    out_hbm_ref,
    grad_hbm_ref,
    w_in_ref,
    w_t_ref,
    w_out_ref,
    out_ref,
    grad_ref,
    proj_ref,
    slope_ref,
    weight_ref,
    score_slope_ref,
    att_ref,
    dproj_ref,
    gain_in_ref,
    gain_mid_ref,
    share_ref,
    part_sems,
    sems,
):
    peers, both, positions = recv_ref.shape
    features = both // 2
    width = peers * features
    head_dim = width // HEADS
    half = positions // 2

    def part_copy(part):
        rows = pl.ds(part * width, width)
        return pltpu.make_async_copy(w_t_hbm_ref.at[rows, :], w_t_ref.at[rows, :], part_sems.at[part])

    for part in (2, 3, 1, 0, 4):
        part_copy(part).start()
    w_out_copy = pltpu.make_async_copy(w_out_hbm_ref, w_out_ref, sems.at[2])
    w_in_copy = pltpu.make_async_copy(w_in_hbm_ref, w_in_ref, sems.at[3])
    w_out_copy.start()
    w_in_copy.start()
    out_copy = pltpu.make_async_copy(out_ref, out_hbm_ref, sems.at[0])
    grad_copy = pltpu.make_async_copy(grad_ref, grad_hbm_ref, sems.at[1])
    length = len_ref[me_ref[0]]
    share = 1.0 / length.astype(F32)
    for row_ref, column_ref in ((gain_in_row_ref, gain_in_ref), (gain_mid_row_ref, gain_mid_ref)):
        row = row_ref[...].reshape(1, width)
        column_ref[...] = jnp.broadcast_to(row, (positions, width)).T

    key = lax.broadcasted_iota(jnp.int32, (positions, positions), 0)
    query = lax.broadcasted_iota(jnp.int32, (positions, positions), 1)
    share_ref[...] = jnp.where((key <= query) & (key < length), share, 0.0)

    def joined(kind):
        rows = pl.ds(kind * features, features)
        return jnp.concatenate([recv_ref[peer, rows, :] for peer in range(peers)], axis=0)

    embedded = joined(0).astype(F32)
    normal_in, inverse_in = norm_forward(embedded)
    normed = (normal_in * gain_in_ref[...]).astype(BF16)

    def project(part):
        part_copy(part).wait()
        return dot_nn(w_t_ref[pl.ds(part * width, width), :], normed)

    def store_projected(part, z):
        rows = pl.ds(part * width, width)
        value, slope = silu_pair(0.5 * z)
        proj_ref[rows, :] = value.astype(BF16)
        slope_ref[rows, :] = slope

    waiting = None
    for part in (2, 3, 1, 0):
        z = project(part)
        if waiting is not None:
            store_projected(*waiting)
        waiting = (part, z)
    store_projected(*waiting)

    starts = (0, half)
    scale = head_dim ** (-0.5)

    def head_rows(kind, head):
        return pl.ds(kind * width + head * head_dim, head_dim)

    def score(head):
        queries, keys = proj_ref[head_rows(2, head), :], proj_ref[head_rows(3, head), :]
        return [dot_tn(keys[:, start : start + half], queries[:, start:]) for start in starts]

    def store_weights(head, scores):
        for start, block in zip(starts, scores):
            value, slope = silu_pair(block * (0.5 * scale))
            places = (pl.ds(start, half), pl.ds(start, positions - start))
            weight_ref[head, *places] = (value * share_ref[*places]).astype(BF16)
            score_slope_ref[head, *places] = slope * share_ref[*places]
        weight_ref[head, pl.ds(half, half), pl.ds(0, half)] = jnp.zeros((half, half), BF16)

    def attend(head):
        att_ref[pl.ds(head * head_dim, head_dim), :] = dot_nn(
            proj_ref[head_rows(1, head), :], weight_ref[head]
        )

    scores = score(0)
    for head in range(HEADS):
        following = score(head + 1) if head + 1 < HEADS else None
        store_weights(head, scores)
        if head:
            attend(head - 1)
        scores = following
    attend(HEADS - 1)

    normal_mid, inverse_mid = norm_forward(att_ref[...])
    gate_rows = proj_ref[pl.ds(0, width), :].astype(F32)
    scaled = normal_mid * gain_mid_ref[...]
    mixed = (scaled * gate_rows).astype(BF16)
    valid = lax.broadcasted_iota(jnp.int32, (width, positions), 1) < length
    cotangent = jnp.where(valid, joined(1).astype(F32), 0.0)
    w_out_copy.wait()
    d_mixed = dot_nn(w_out_ref[...], cotangent.astype(BF16))
    part_copy(4).wait()
    update = dot_nn(w_t_ref[pl.ds(4 * width, width), :], mixed)
    out_ref[...] = (embedded + update).astype(BF16)
    out_copy.start()

    dproj_ref[pl.ds(0, width), :] = (d_mixed * scaled * slope_ref[pl.ds(0, width), :]).astype(BF16)
    d_att = norm_backward(d_mixed * gate_rows * gain_mid_ref[...], normal_mid, inverse_mid)
    att_ref[...] = d_att

    def d_weights(head):
        values = proj_ref[head_rows(1, head), :]
        d_head = att_ref[pl.ds(head * head_dim, head_dim), :].astype(BF16)
        return [dot_tn(values[:, start : start + half], d_head[:, start:]) for start in starts]

    def d_scores(head, products):
        low, high = (
            (block * score_slope_ref[head, pl.ds(start, half), pl.ds(start, positions - start)]).astype(
                BF16
            )
            for start, block in zip(starts, products)
        )
        empty = jnp.zeros((half, half), BF16)
        return jnp.concatenate([low, jnp.concatenate([empty, high], axis=1)], axis=0)

    def d_project(head, d_score):
        d_head = att_ref[pl.ds(head * head_dim, head_dim), :].astype(BF16)
        queries, keys = proj_ref[head_rows(2, head), :], proj_ref[head_rows(3, head), :]
        products = (
            dot_nt(d_head, weight_ref[head]),
            dot_nn(keys, d_score) * (0.5 * scale),
            dot_nt(queries, d_score) * (0.5 * scale),
        )
        for kind, product in zip((1, 2, 3), products):
            rows = head_rows(kind, head)
            dproj_ref[rows, :] = (product * slope_ref[rows, :]).astype(BF16)

    products, before = d_weights(0), None
    for head in range(HEADS):
        following = d_weights(head + 1) if head + 1 < HEADS else None
        d_score = d_scores(head, products)
        if head:
            d_project(head - 1, before)
        products, before = following, d_score
    d_project(HEADS - 1, before)

    w_in_copy.wait()
    d_normed = dot_nn(w_in_ref[...], dproj_ref[...])
    d_embedded = norm_backward(d_normed * (0.5 * gain_in_ref[...]), normal_in, inverse_in)
    grad_ref[...] = (cotangent + d_embedded).astype(BF16)
    grad_copy.start()
    out_copy.wait()
    grad_copy.wait()


def run_layer(me, lengths, received, w_in, w_out, gain_in, gain_mid):
    peers, _, positions = received.shape
    width = w_out.shape[0]
    smem, vmem = pl.BlockSpec(memory_space=pltpu.SMEM), pl.BlockSpec(memory_space=pltpu.VMEM)
    hbm = pl.BlockSpec(memory_space=pltpu.HBM)
    shape = jax.ShapeDtypeStruct((width, positions), BF16)
    return pl.pallas_call(
        layer_kernel,
        out_shape=[shape, shape],
        in_specs=[smem, smem, vmem, hbm, hbm, hbm, vmem, vmem],
        out_specs=[hbm, hbm],
        scratch_shapes=[
            pltpu.VMEM((width, 4 * width), BF16),
            pltpu.VMEM((5 * width, width), BF16),
            pltpu.VMEM((width, width), BF16),
            pltpu.VMEM((width, positions), BF16),
            pltpu.VMEM((width, positions), BF16),
            pltpu.VMEM((4 * width, positions), BF16),
            pltpu.VMEM((4 * width, positions), F32),
            pltpu.VMEM((HEADS, positions, positions), BF16),
            pltpu.VMEM((HEADS, positions, positions), F32),
            pltpu.VMEM((width, positions), F32),
            pltpu.VMEM((4 * width, positions), BF16),
            pltpu.VMEM((width, positions), F32),
            pltpu.VMEM((width, positions), F32),
            pltpu.VMEM((positions, positions), F32),
            pltpu.SemaphoreType.DMA((5,)),
            pltpu.SemaphoreType.DMA((4,)),
        ],
        compiler_params=pltpu.CompilerParams(vmem_limit_bytes=LAYER_VMEM_BYTES),
        cost_estimate=pl.CostEstimate(flops=10**10, bytes_accessed=10**7, transcendentals=10**6),
        name="layer",
    )(
        me,
        lengths,
        received,
        w_in,
        jnp.concatenate([w_in.T, w_out.T], axis=0),
        w_out,
        gain_in,
        gain_mid,
    )


LOW = 256
STACK = 16


def ranks(member, users):
    rows, positions = member.shape
    ones = jnp.where(member, 1.0, 0.0).astype(BF16)

    def iota(shape, dimension):
        return lax.broadcasted_iota(jnp.int32, shape, dimension)

    square = (positions, positions)
    before = jnp.where(iota(square, 0) < iota(square, 1), 1.0, 0.0).astype(BF16)
    row, other = iota((rows, rows), 0), iota((rows, rows), 1)
    shift = users.bit_length() - 1
    above = (other < row) & ((other >> shift) == (row >> shift))
    earlier = dot_nn(jnp.where(above, 1.0, 0.0).astype(BF16), ones)
    return (dot_nn(ones, before) + jnp.sum(earlier, axis=1, keepdims=True)).astype(jnp.int32)


def plan_kernel(own, home_ref, turn_ref, ids_ref, low_ref, high_ref, slot_ref, most_ref, *scratch):
    chosen_ref, digit_ref, wide_ref, rank_ref = scratch
    groups, users, positions = ids_ref.shape
    capacity = low_ref.shape[1]
    home = home_ref[0]
    first = turn_ref[0] * capacity
    own_bits, low_bits = own.bit_length() - 1, LOW.bit_length() - 1

    all_items = ids_ref[...].reshape(groups * users, positions)
    sent = jnp.concatenate([ids_ref[0] >> own_bits == owner for owner in range(groups)], axis=0)
    arriving = all_items >> own_bits == home
    rank_ref[...] = ranks(jnp.concatenate([arriving, sent], axis=0), users) - first
    slot = jnp.full((users, positions), -1, jnp.int32)
    for owner in range(groups):
        rank = rank_ref[pl.ds((groups + owner) * users, users), :]
        fits = (ids_ref[0] >> own_bits == owner) & (rank >= 0) & (rank < capacity)
        slot = jnp.where(fits, rank + owner * capacity, slot)
    slot_ref[...] = slot

    digit = lax.broadcasted_iota(jnp.int32, (LOW, positions), 0)
    place = lax.broadcasted_iota(jnp.int32, (capacity, positions), 0)

    def one_group(group, most):
        items = ids_ref[group]
        for owner in range(groups):
            count = jnp.sum(jnp.where(items >> own_bits == owner, 1.0, 0.0))
            most = jnp.maximum(most, count)
        mine = items >> own_bits == home
        local = items & (own - 1)
        rank = rank_ref[pl.ds(pl.multiple_of(group * users, users), users), :]
        slot = jnp.where(mine, rank, -1)
        low = local & (LOW - 1)
        high = jnp.where(mine, (local >> low_bits) + 1, 0).astype(F32)
        for user in range(users):
            columns = pl.ds(user * positions, positions)
            chosen_ref[:, columns] = jnp.where(place == slot[user : user + 1], 1.0, 0.0).astype(BF16)
            digit_ref[:, columns] = jnp.where(digit == low[user : user + 1], 1.0, 0.0).astype(BF16)
            wide_ref[:, columns] = jnp.broadcast_to(high[user : user + 1], (16, positions)).astype(BF16)
        low_ref[group] = dot_nt(chosen_ref[...], digit_ref[...]).astype(BF16)
        high_ref[pl.ds(group, 1), :] = dot_nt(wide_ref[...], chosen_ref[...])[:1]
        return most

    most_ref[0] = lax.fori_loop(0, groups, one_group, jnp.float32(0)).astype(jnp.int32)


def plan_turn(home, turn, all_ids, own, capacity):
    groups, users, positions = all_ids.shape
    smem, vmem = pl.BlockSpec(memory_space=pltpu.SMEM), pl.BlockSpec(memory_space=pltpu.VMEM)
    return pl.pallas_call(
        functools.partial(plan_kernel, own),
        out_shape=[
            jax.ShapeDtypeStruct((groups, capacity, LOW), BF16),
            jax.ShapeDtypeStruct((groups, capacity), F32),
            jax.ShapeDtypeStruct((users, positions), jnp.int32),
            jax.ShapeDtypeStruct((1,), jnp.int32),
        ],
        in_specs=[smem, smem, vmem],
        out_specs=[vmem] * 3 + [smem],
        scratch_shapes=[
            pltpu.VMEM((capacity, users * positions), BF16),
            pltpu.VMEM((LOW, users * positions), BF16),
            pltpu.VMEM((16, users * positions), BF16),
            pltpu.VMEM((2 * groups * users, positions), jnp.int32),
        ],
        compiler_params=pltpu.CompilerParams(vmem_limit_bytes=VMEM_BYTES),
        cost_estimate=pl.CostEstimate(flops=4 * 10**9, bytes_accessed=5 * 10**6, transcendentals=0),
        name="plan_turn",
    )(home, turn, all_ids)


def pack_kernel(distances, home_ref, slot_ref, grad_ref, *refs):
    *packed_refs, wide_ref, chosen_ref = refs
    users, _, positions = grad_ref.shape
    capacity = packed_refs[0].shape[1]
    padded = jnp.concatenate(
        [slot_ref[...].astype(F32), jnp.zeros((LANES - users, positions), F32)], axis=0
    )
    slots = padded.T.astype(jnp.int32)
    place = lax.broadcasted_iota(jnp.int32, (positions, capacity), 1)
    for user in range(users):
        wide_ref[:, pl.ds(user * positions, positions)] = grad_ref[user]
    for distance, packed_ref in zip(distances, packed_refs):
        first = (home_ref[0] ^ distance) * capacity
        for user in range(users):
            chosen_ref[pl.ds(user * positions, positions), :] = jnp.where(
                place == slots[:, user : user + 1] - first, 1.0, 0.0
            ).astype(BF16)
        packed_ref[...] = dot_nn(wide_ref[...], chosen_ref[...]).astype(BF16)


def pack_lists(distances, home, slot, grads, capacity):
    users, features, positions = grads.shape
    smem, vmem = pl.BlockSpec(memory_space=pltpu.SMEM), pl.BlockSpec(memory_space=pltpu.VMEM)
    return pl.pallas_call(
        functools.partial(pack_kernel, distances),
        out_shape=[jax.ShapeDtypeStruct((features, capacity), BF16)] * len(distances),
        in_specs=[smem, vmem, vmem],
        out_specs=[vmem] * len(distances),
        scratch_shapes=[
            pltpu.VMEM((features, users * positions), BF16),
            pltpu.VMEM((users * positions, capacity), BF16),
        ],
        compiler_params=pltpu.CompilerParams(vmem_limit_bytes=LIST_VMEM_BYTES),
        cost_estimate=pl.CostEstimate(
            flops=len(distances) * 8 * 10**8, bytes_accessed=10**6, transcendentals=0
        ),
        name="pack_lists",
    )(home, slot, grads)


def scatter_kernel(groups, stack, low_ref, high_ref, *refs):
    list_refs, (*before_ref, out_ref, spread_ref) = refs[:groups], refs[groups:]
    features, capacity = list_refs[0].shape
    step = pl.program_id(0)
    for group, list_ref in enumerate(list_refs):
        high = high_ref[pl.ds(group, 1), :]
        for part in range(stack):
            wanted = (step * stack + part + 1).astype(F32)
            chosen = jnp.where(high == wanted, 1.0, 0.0).astype(BF16)
            spread_ref[pl.ds(part * features, features), pl.ds(group * capacity, capacity)] = (
                list_ref[...] * chosen
            )
    sums = dot_nn(spread_ref[...], low_ref[...])
    for part in range(stack):
        columns = pl.ds(part * LOW, LOW)
        term = sums[part * features : (part + 1) * features]
        out_ref[:, columns] = term + before_ref[0][:, columns] if before_ref else term


def scatter_slots(low, high, lists, own, before=None):
    groups = len(lists)
    features, capacity = lists[0].shape
    low = low.reshape(groups * capacity, LOW)
    stack = min(STACK, own // LOW)
    block = pl.BlockSpec((features, stack * LOW), lambda i: (0, i))
    extra = [] if before is None else [before]
    return pl.pallas_call(
        functools.partial(scatter_kernel, groups, stack),
        grid=(own // (LOW * stack),),
        out_shape=jax.ShapeDtypeStruct((features, own), F32),
        in_specs=[
            pl.BlockSpec((groups * capacity, LOW), lambda i: (0, 0)),
            pl.BlockSpec(high.shape, lambda i: (0, 0)),
        ]
        + [pl.BlockSpec((features, capacity), lambda i: (0, 0))] * groups
        + [block] * len(extra),
        out_specs=block,
        scratch_shapes=[pltpu.VMEM((stack * features, groups * capacity), BF16)],
        input_output_aliases={2 + groups: 0} if extra else {},
        compiler_params=pltpu.CompilerParams(vmem_limit_bytes=VMEM_BYTES),
        cost_estimate=pl.CostEstimate(flops=3 * 10**9, bytes_accessed=10**6, transcendentals=0),
        name="scatter_slots",
    )(low, high, *lists, *extra)


def swap(value, axis, distance):
    size = lax.axis_size(axis)
    return lax.ppermute(value, axis, [(i, i ^ distance) for i in range(size)])


def deliver(home, plan, grads, own, capacity, before=None):
    low, high, slot, _ = plan
    farthest = low.shape[0] - 1
    near = tuple(range(farthest))
    (far_list,) = pack_lists((farthest,), home, slot, grads, capacity)
    far_list = swap(far_list, "dp", farthest)
    own_list, *near_lists = pack_lists(near, home, slot, grads, capacity)
    near_lists = [swap(near_list, "dp", k) for k, near_list in zip(near[1:], near_lists)]
    return scatter_slots(low, high, [own_list, *near_lists, far_list], own, before)


def exchange(value, axis):
    return lax.all_to_all(value, axis, split_axis=0, concat_axis=0, tiled=True)


def on_device(item_ids, user_len, emb_table, cotangent, w_uvqk, w_out, gain_in, gain_mid):
    dp_size = lax.axis_size("dp")
    table_size = lax.axis_size("table")
    users = user_len.shape[0]
    features, vocab = emb_table.shape
    rows = item_ids.shape[0]
    positions = rows // users
    own = vocab // dp_size
    capacity = -(-(rows // dp_size * 5 // 4) // LANES) * LANES
    assert users == table_size and users <= LANES and positions <= 256 and own // LOW <= 255
    assert dp_size & (dp_size - 1) == 0 and users & (users - 1) == 0 and own & (own - 1) == 0
    me = lax.axis_index("table").astype(jnp.int32).reshape(1)
    home = lax.axis_index("dp").astype(jnp.int32).reshape(1)

    send, valid_ids = gather_columns(item_ids, user_len, cotangent, emb_table)
    received = exchange(send, "table")
    all_ids = jnp.stack([valid_ids] + [swap(valid_ids, "dp", k) for k in range(1, dp_size)])
    out_cols, grad_cols = run_layer(me, user_len, received, w_uvqk, w_out, gain_in, gain_mid)
    per_peer = (table_size, features, positions)
    all_ids, grad_cols = lax.optimization_barrier((all_ids, grad_cols))
    plan = plan_turn(home, jnp.zeros((1,), jnp.int32), all_ids, own, capacity)
    grad_home = exchange(grad_cols.reshape(per_peer), "table")
    out_cols, grad_home = lax.optimization_barrier((out_cols, grad_home))
    out_home = exchange(out_cols.reshape(per_peer), "table")
    table_grad = deliver(home, plan, grad_home, own, capacity)
    layer_out = jnp.transpose(out_home, (1, 0, 2)).reshape(features, rows)

    turns = (plan[-1][0] + capacity - 1) // capacity

    def another(state):
        turn, sums = state
        more = plan_turn(home, turn.reshape(1), all_ids, own, capacity)
        return turn + 1, deliver(home, more, grad_home, own, capacity, sums)

    _, table_grad = lax.while_loop(
        lambda state: state[0] < turns, another, (jnp.int32(1), table_grad)
    )
    return (layer_out, table_grad)


def solution(mesh):
    return jax.shard_map(
        on_device,
        mesh=mesh,
        in_specs=(P("dp"), P("dp"), P("table", None), P("table", "dp"), P(), P(), P(), P()),
        out_specs=(P("table", "dp"), P("table", "dp")),
        check_vma=False,
    )
```

```python
import functools

import jax
import jax.numpy as jnp
from jax import lax
from jax.experimental import pallas as pl
from jax.experimental.pallas import tpu as pltpu
from jax.sharding import PartitionSpec as P

HEADS = 8
NORM_EPS = 1e-05
LANES = 128
WHOLE_VMEM_BYTES = 61 * 1024 * 1024
LAYER_VMEM_BYTES = 20 * 1024 * 1024
PLAN_VMEM_BYTES = 16 * 1024 * 1024
LIST_VMEM_BYTES = 24 * 1024 * 1024

F32 = jnp.float32
BF16 = jnp.bfloat16


def dot_nn(left, right):
    return jnp.dot(left, right, preferred_element_type=F32)


def dot_nt(left, right):
    return lax.dot_general(left, right, (((1,), (1,)), ((), ())), preferred_element_type=F32)


def dot_tn(left, right):
    return lax.dot_general(left, right, (((0,), (0,)), ((), ())), preferred_element_type=F32)


BLOCK = 256
UNROLL = 64
CHUNK_ROWS = 16


def gather_kernel(
    len_ref,
    ids_ref,
    cot_hbm_ref,
    table_hbm_ref,
    out_ref,
    valid_ref,
    table_ref,
    cot_ref,
    rows_ref,
    picked_ref,
    turned_ref,
    row_vector_ref,
    row_ref,
    chunk_sems,
    row_sem,
    out_sems,
    cot_sem,
):
    users, _, positions = out_ref.shape
    features, vocab = table_hbm_ref.shape
    pack = LANES // features
    span = BLOCK * pack
    block_bits = BLOCK.bit_length() - 1

    def chunk_copy(chunk):
        rows = pl.ds(chunk * CHUNK_ROWS, CHUNK_ROWS)
        return pltpu.make_async_copy(
            table_hbm_ref.at[rows, :], table_ref.at[rows, :], chunk_sems.at[chunk]
        )

    def out_copy(user):
        return pltpu.make_async_copy(turned_ref.at[user], out_ref.at[user], out_sems.at[user])

    for chunk in range(features // CHUNK_ROWS):
        chunk_copy(chunk).start()
    cot_copy = pltpu.make_async_copy(cot_hbm_ref, cot_ref, cot_sem)
    cot_copy.start()
    items = ids_ref[...]
    row_vector_ref[...] = ((items >> (span.bit_length() - 1)) << block_bits) | (items & (BLOCK - 1))
    row_copy = pltpu.make_async_copy(row_vector_ref, row_ref, row_sem)
    row_copy.start()
    order = lax.broadcasted_iota(jnp.int32, (1, positions), 1)
    for user in range(users):
        own_items = ids_ref[pl.ds(user * positions, positions)].reshape(1, positions)
        valid_ref[pl.ds(user, 1), :] = jnp.where(order < len_ref[user], own_items, vocab)

    cot_copy.wait()
    for user in range(users):
        turned_ref[user, pl.ds(features, features), :] = cot_ref[:, pl.ds(user * positions, positions)]

    for chunk in range(features // CHUNK_ROWS):
        chunk_copy(chunk).wait()
    for part in range(vocab // span):
        stack = jnp.concatenate(
            [
                table_ref[:, part * span + s * BLOCK : part * span + (s + 1) * BLOCK]
                for s in range(pack)
            ],
            axis=0,
        )
        rows_ref[pl.ds(part * BLOCK, BLOCK), :] = stack.T.astype(F32)
    row_copy.wait()

    def some(part, carry):
        start = pl.multiple_of(part * UNROLL, UNROLL)
        for slot in range(UNROLL):
            row = row_ref[start + slot]
            picked_ref[pl.ds(start + slot, 1), :] = rows_ref[pl.ds(row, 1), :]
        return carry

    lax.fori_loop(0, users * positions // UNROLL, some, 0)
    row = lax.broadcasted_iota(jnp.int32, (LANES, LANES), 0)
    column = lax.broadcasted_iota(jnp.int32, (LANES, LANES), 1)
    same = jnp.where(row == column, 1.0, 0.0).astype(BF16)
    for user in range(users):
        places = pl.ds(user * positions, positions)
        turned = dot_nt(same, picked_ref[places, :].astype(BF16))
        own_items = ids_ref[places].reshape(1, positions)
        group = (own_items >> block_bits) & (pack - 1)
        total = turned[:features]
        for s in range(1, pack):
            total = jnp.where(group == s, turned[s * features : (s + 1) * features], total)
        turned_ref[user, pl.ds(0, features), :] = total.astype(BF16)
        out_copy(user).start()
    for user in range(users):
        out_copy(user).wait()


def gather_columns(item_ids, lengths, cotangent, table):
    users = lengths.shape[0]
    rows = item_ids.shape[0]
    positions = rows // users
    features, vocab = table.shape
    pack = LANES // features
    shape = (users, 2 * features, positions)
    hbm = pl.BlockSpec(memory_space=pltpu.HBM)
    vmem = pl.BlockSpec(memory_space=pltpu.VMEM)
    return pl.pallas_call(
        gather_kernel,
        out_shape=[
            jax.ShapeDtypeStruct(shape, table.dtype),
            jax.ShapeDtypeStruct((users, positions), jnp.int32),
        ],
        in_specs=[pl.BlockSpec(memory_space=pltpu.SMEM), vmem, hbm, hbm],
        out_specs=[hbm, vmem],
        scratch_shapes=[
            pltpu.VMEM((features, vocab), table.dtype),
            pltpu.VMEM((features, rows), table.dtype),
            pltpu.VMEM((vocab // pack, LANES), F32),
            pltpu.VMEM((rows, LANES), F32),
            pltpu.VMEM(shape, table.dtype),
            pltpu.VMEM((rows,), jnp.int32),
            pltpu.SMEM((rows,), jnp.int32),
            pltpu.SemaphoreType.DMA((features // CHUNK_ROWS,)),
            pltpu.SemaphoreType.DMA,
            pltpu.SemaphoreType.DMA((users,)),
            pltpu.SemaphoreType.DMA,
        ],
        compiler_params=pltpu.CompilerParams(vmem_limit_bytes=WHOLE_VMEM_BYTES),
        cost_estimate=pl.CostEstimate(flops=8 * 10**9, bytes_accessed=5 * 10**6, transcendentals=0),
        name="gather_columns",
    )(lengths, item_ids, cotangent, table)


def norm_forward(values):
    centred = values - jnp.mean(values, axis=0, keepdims=True)
    inverse = lax.rsqrt(jnp.mean(centred * centred, axis=0, keepdims=True) + NORM_EPS)
    return centred * inverse, inverse


def norm_backward(grad, normal, inverse):
    shift = jnp.mean(grad, axis=0, keepdims=True)
    slope = jnp.mean(grad * normal, axis=0, keepdims=True)
    return (grad - shift - normal * slope) * inverse


def silu_pair(half):
    turn = jnp.tanh(half)
    twice = 1.0 + turn
    value = half * twice
    return value, twice + value * (1.0 - turn)


def layer_kernel(
    me_ref,
    len_ref,
    recv_ref,
    w_in_ref,
    w_in_t_ref,
    w_out_ref,
    w_out_t_ref,
    gain_in_row_ref,
    gain_mid_row_ref,
    out_hbm_ref,
    grad_hbm_ref,
    out_ref,
    grad_ref,
    proj_ref,
    slope_ref,
    weight_ref,
    score_slope_ref,
    att_ref,
    dproj_ref,
    gain_in_ref,
    gain_mid_ref,
    share_ref,
    sems,
):
    peers, both, positions = recv_ref.shape
    features = both // 2
    width = peers * features
    head_dim = width // HEADS
    half = positions // 2

    out_copy = pltpu.make_async_copy(out_ref, out_hbm_ref, sems.at[0])
    grad_copy = pltpu.make_async_copy(grad_ref, grad_hbm_ref, sems.at[1])
    length = len_ref[me_ref[0]]
    share = 1.0 / length.astype(F32)
    for row_ref, column_ref in ((gain_in_row_ref, gain_in_ref), (gain_mid_row_ref, gain_mid_ref)):
        row = row_ref[...].reshape(1, width)
        column_ref[...] = jnp.broadcast_to(row, (positions, width)).T

    key = lax.broadcasted_iota(jnp.int32, (positions, positions), 0)
    query = lax.broadcasted_iota(jnp.int32, (positions, positions), 1)
    share_ref[...] = jnp.where((key <= query) & (key < length), share, 0.0)

    def joined(kind):
        rows = pl.ds(kind * features, features)
        return jnp.concatenate([recv_ref[peer, rows, :] for peer in range(peers)], axis=0)

    embedded = joined(0).astype(F32)
    normal_in, inverse_in = norm_forward(embedded)
    normed = (normal_in * gain_in_ref[...]).astype(BF16)

    def project(part):
        return dot_nn(w_in_t_ref[pl.ds(part * width, width), :], normed)

    def store_projected(part, z):
        rows = pl.ds(part * width, width)
        value, slope = silu_pair(0.5 * z)
        proj_ref[rows, :] = value.astype(BF16)
        slope_ref[rows, :] = slope

    waiting = None
    for part in (2, 3, 1, 0):
        z = project(part)
        if waiting is not None:
            store_projected(*waiting)
        waiting = (part, z)
    store_projected(*waiting)

    starts = (0, half)
    scale = head_dim ** (-0.5)

    def head_rows(kind, head):
        return pl.ds(kind * width + head * head_dim, head_dim)

    def score(head):
        queries, keys = proj_ref[head_rows(2, head), :], proj_ref[head_rows(3, head), :]
        return [dot_tn(keys[:, start : start + half], queries[:, start:]) for start in starts]

    def store_weights(head, scores):
        for start, block in zip(starts, scores):
            value, slope = silu_pair(block * (0.5 * scale))
            places = (pl.ds(start, half), pl.ds(start, positions - start))
            weight_ref[head, *places] = (value * share_ref[*places]).astype(BF16)
            score_slope_ref[head, *places] = slope * share_ref[*places]
        weight_ref[head, pl.ds(half, half), pl.ds(0, half)] = jnp.zeros((half, half), BF16)

    def attend(head):
        att_ref[pl.ds(head * head_dim, head_dim), :] = dot_nn(
            proj_ref[head_rows(1, head), :], weight_ref[head]
        )

    scores = score(0)
    for head in range(HEADS):
        following = score(head + 1) if head + 1 < HEADS else None
        store_weights(head, scores)
        if head:
            attend(head - 1)
        scores = following
    attend(HEADS - 1)

    normal_mid, inverse_mid = norm_forward(att_ref[...])
    gate_rows = proj_ref[pl.ds(0, width), :].astype(F32)
    scaled = normal_mid * gain_mid_ref[...]
    mixed = (scaled * gate_rows).astype(BF16)
    valid = lax.broadcasted_iota(jnp.int32, (width, positions), 1) < length
    cotangent = jnp.where(valid, joined(1).astype(F32), 0.0)
    d_mixed = dot_nn(w_out_ref[...], cotangent.astype(BF16))
    out_ref[...] = (embedded + dot_nn(w_out_t_ref[...], mixed)).astype(BF16)
    out_copy.start()

    dproj_ref[pl.ds(0, width), :] = (d_mixed * scaled * slope_ref[pl.ds(0, width), :]).astype(BF16)
    d_att = norm_backward(d_mixed * gate_rows * gain_mid_ref[...], normal_mid, inverse_mid)
    att_ref[...] = d_att

    def d_weights(head):
        values = proj_ref[head_rows(1, head), :]
        d_head = att_ref[pl.ds(head * head_dim, head_dim), :].astype(BF16)
        return [dot_tn(values[:, start : start + half], d_head[:, start:]) for start in starts]

    def d_scores(head, products):
        low, high = (
            (block * score_slope_ref[head, pl.ds(start, half), pl.ds(start, positions - start)]).astype(
                BF16
            )
            for start, block in zip(starts, products)
        )
        empty = jnp.zeros((half, half), BF16)
        return jnp.concatenate([low, jnp.concatenate([empty, high], axis=1)], axis=0)

    def d_project(head, d_score):
        d_head = att_ref[pl.ds(head * head_dim, head_dim), :].astype(BF16)
        queries, keys = proj_ref[head_rows(2, head), :], proj_ref[head_rows(3, head), :]
        products = (
            dot_nt(d_head, weight_ref[head]),
            dot_nn(keys, d_score) * (0.5 * scale),
            dot_nt(queries, d_score) * (0.5 * scale),
        )
        for kind, product in zip((1, 2, 3), products):
            rows = head_rows(kind, head)
            dproj_ref[rows, :] = (product * slope_ref[rows, :]).astype(BF16)

    products, before = d_weights(0), None
    for head in range(HEADS):
        following = d_weights(head + 1) if head + 1 < HEADS else None
        d_score = d_scores(head, products)
        if head:
            d_project(head - 1, before)
        products, before = following, d_score
    d_project(HEADS - 1, before)

    d_normed = dot_nn(w_in_ref[...], dproj_ref[...])
    d_embedded = norm_backward(d_normed * (0.5 * gain_in_ref[...]), normal_in, inverse_in)
    grad_ref[...] = (cotangent + d_embedded).astype(BF16)
    grad_copy.start()
    out_copy.wait()
    grad_copy.wait()


def run_layer(me, lengths, received, w_in, w_out, gain_in, gain_mid):
    peers, _, positions = received.shape
    width = w_out.shape[0]
    smem, vmem = pl.BlockSpec(memory_space=pltpu.SMEM), pl.BlockSpec(memory_space=pltpu.VMEM)
    hbm = pl.BlockSpec(memory_space=pltpu.HBM)
    shape = jax.ShapeDtypeStruct((width, positions), BF16)
    return pl.pallas_call(
        layer_kernel,
        out_shape=[shape, shape],
        in_specs=[smem, smem] + [vmem] * 7,
        out_specs=[hbm, hbm],
        scratch_shapes=[
            pltpu.VMEM((width, positions), BF16),
            pltpu.VMEM((width, positions), BF16),
            pltpu.VMEM((4 * width, positions), BF16),
            pltpu.VMEM((4 * width, positions), F32),
            pltpu.VMEM((HEADS, positions, positions), BF16),
            pltpu.VMEM((HEADS, positions, positions), F32),
            pltpu.VMEM((width, positions), F32),
            pltpu.VMEM((4 * width, positions), BF16),
            pltpu.VMEM((width, positions), F32),
            pltpu.VMEM((width, positions), F32),
            pltpu.VMEM((positions, positions), F32),
            pltpu.SemaphoreType.DMA((2,)),
        ],
        compiler_params=pltpu.CompilerParams(vmem_limit_bytes=LAYER_VMEM_BYTES),
        cost_estimate=pl.CostEstimate(flops=10**10, bytes_accessed=10**7, transcendentals=10**6),
        name="layer",
    )(
        me,
        lengths,
        received,
        w_in,
        w_in.T,
        w_out,
        w_out.T,
        gain_in,
        gain_mid,
    )


LOW = 256
STACK = 16


def ranks(member, users):
    rows, positions = member.shape
    ones = jnp.where(member, 1.0, 0.0).astype(BF16)

    def iota(shape, dimension):
        return lax.broadcasted_iota(jnp.int32, shape, dimension)

    square = (positions, positions)
    before = jnp.where(iota(square, 0) < iota(square, 1), 1.0, 0.0).astype(BF16)
    row, other = iota((rows, rows), 0), iota((rows, rows), 1)
    shift = users.bit_length() - 1
    above = (other < row) & ((other >> shift) == (row >> shift))
    earlier = dot_nn(jnp.where(above, 1.0, 0.0).astype(BF16), ones)
    return (dot_nn(ones, before) + jnp.sum(earlier, axis=1, keepdims=True)).astype(jnp.int32)


def plan_kernel(own, home_ref, turn_ref, ids_ref, low_ref, high_ref, slot_ref, most_ref, *scratch):
    chosen_ref, digit_ref, wide_ref, rank_ref = scratch
    groups, users, positions = ids_ref.shape
    capacity = low_ref.shape[1]
    home = home_ref[0]
    first = turn_ref[0] * capacity
    own_bits, low_bits = own.bit_length() - 1, LOW.bit_length() - 1

    all_items = ids_ref[...].reshape(groups * users, positions)
    sent = jnp.concatenate([ids_ref[0] >> own_bits == owner for owner in range(groups)], axis=0)
    arriving = all_items >> own_bits == home
    rank_ref[...] = ranks(jnp.concatenate([arriving, sent], axis=0), users) - first
    slot = jnp.full((users, positions), -1, jnp.int32)
    for owner in range(groups):
        rank = rank_ref[pl.ds((groups + owner) * users, users), :]
        fits = (ids_ref[0] >> own_bits == owner) & (rank >= 0) & (rank < capacity)
        slot = jnp.where(fits, rank + owner * capacity, slot)
    slot_ref[...] = slot

    digit = lax.broadcasted_iota(jnp.int32, (LOW, positions), 0)
    place = lax.broadcasted_iota(jnp.int32, (capacity, positions), 0)

    def one_group(group, most):
        items = ids_ref[group]
        for owner in range(groups):
            count = jnp.sum(jnp.where(items >> own_bits == owner, 1.0, 0.0))
            most = jnp.maximum(most, count)
        mine = items >> own_bits == home
        local = items & (own - 1)
        rank = rank_ref[pl.ds(pl.multiple_of(group * users, users), users), :]
        slot = jnp.where(mine, rank, -1)
        low = local & (LOW - 1)
        high = jnp.where(mine, (local >> low_bits) + 1, 0).astype(F32)
        for user in range(users):
            columns = pl.ds(user * positions, positions)
            chosen_ref[:, columns] = jnp.where(place == slot[user : user + 1], 1.0, 0.0).astype(BF16)
            digit_ref[:, columns] = jnp.where(digit == low[user : user + 1], 1.0, 0.0).astype(BF16)
            wide_ref[:, columns] = jnp.broadcast_to(high[user : user + 1], (16, positions)).astype(BF16)
        low_ref[group] = dot_nt(chosen_ref[...], digit_ref[...]).astype(BF16)
        high_ref[pl.ds(group, 1), :] = dot_nt(wide_ref[...], chosen_ref[...])[:1]
        return most

    most_ref[0] = lax.fori_loop(0, groups, one_group, jnp.float32(0)).astype(jnp.int32)


def plan_turn(home, turn, all_ids, own, capacity):
    groups, users, positions = all_ids.shape
    smem, vmem = pl.BlockSpec(memory_space=pltpu.SMEM), pl.BlockSpec(memory_space=pltpu.VMEM)
    return pl.pallas_call(
        functools.partial(plan_kernel, own),
        out_shape=[
            jax.ShapeDtypeStruct((groups, capacity, LOW), BF16),
            jax.ShapeDtypeStruct((groups, capacity), F32),
            jax.ShapeDtypeStruct((users, positions), jnp.int32),
            jax.ShapeDtypeStruct((1,), jnp.int32),
        ],
        in_specs=[smem, smem, vmem],
        out_specs=[vmem] * 3 + [smem],
        scratch_shapes=[
            pltpu.VMEM((capacity, users * positions), BF16),
            pltpu.VMEM((LOW, users * positions), BF16),
            pltpu.VMEM((16, users * positions), BF16),
            pltpu.VMEM((2 * groups * users, positions), jnp.int32),
        ],
        compiler_params=pltpu.CompilerParams(vmem_limit_bytes=PLAN_VMEM_BYTES),
        cost_estimate=pl.CostEstimate(flops=4 * 10**9, bytes_accessed=5 * 10**6, transcendentals=0),
        name="plan_turn",
    )(home, turn, all_ids)


def pack_kernel(distances, home_ref, slot_ref, grad_ref, *refs):
    *packed_refs, wide_ref, chosen_ref = refs
    users, _, positions = grad_ref.shape
    capacity = packed_refs[0].shape[1]
    padded = jnp.concatenate(
        [slot_ref[...].astype(F32), jnp.zeros((LANES - users, positions), F32)], axis=0
    )
    slots = padded.T.astype(jnp.int32)
    place = lax.broadcasted_iota(jnp.int32, (positions, capacity), 1)
    for user in range(users):
        wide_ref[:, pl.ds(user * positions, positions)] = grad_ref[user]
    for distance, packed_ref in zip(distances, packed_refs):
        first = (home_ref[0] ^ distance) * capacity
        for user in range(users):
            chosen_ref[pl.ds(user * positions, positions), :] = jnp.where(
                place == slots[:, user : user + 1] - first, 1.0, 0.0
            ).astype(BF16)
        packed_ref[...] = dot_nn(wide_ref[...], chosen_ref[...]).astype(BF16)


def pack_lists(distances, home, slot, grads, capacity):
    users, features, positions = grads.shape
    smem, vmem = pl.BlockSpec(memory_space=pltpu.SMEM), pl.BlockSpec(memory_space=pltpu.VMEM)
    return pl.pallas_call(
        functools.partial(pack_kernel, distances),
        out_shape=[jax.ShapeDtypeStruct((features, capacity), BF16)] * len(distances),
        in_specs=[smem, vmem, vmem],
        out_specs=[vmem] * len(distances),
        scratch_shapes=[
            pltpu.VMEM((features, users * positions), BF16),
            pltpu.VMEM((users * positions, capacity), BF16),
        ],
        compiler_params=pltpu.CompilerParams(vmem_limit_bytes=LIST_VMEM_BYTES),
        cost_estimate=pl.CostEstimate(
            flops=len(distances) * 8 * 10**8, bytes_accessed=10**6, transcendentals=0
        ),
        name="pack_lists",
    )(home, slot, grads)


def scatter_kernel(groups, stack, low_ref, high_ref, *refs):
    list_refs, (*before_ref, out_ref, spread_ref) = refs[:groups], refs[groups:]
    features, capacity = list_refs[0].shape
    step = pl.program_id(0)
    for group, list_ref in enumerate(list_refs):
        high = high_ref[pl.ds(group, 1), :]
        for part in range(stack):
            wanted = (step * stack + part + 1).astype(F32)
            chosen = jnp.where(high == wanted, 1.0, 0.0).astype(BF16)
            spread_ref[pl.ds(part * features, features), pl.ds(group * capacity, capacity)] = (
                list_ref[...] * chosen
            )
    sums = dot_nn(spread_ref[...], low_ref[...])
    for part in range(stack):
        columns = pl.ds(part * LOW, LOW)
        term = sums[part * features : (part + 1) * features]
        out_ref[:, columns] = term + before_ref[0][:, columns] if before_ref else term


def scatter_slots(low, high, lists, own, before=None):
    groups = len(lists)
    features, capacity = lists[0].shape
    low = low.reshape(groups * capacity, LOW)
    stack = min(STACK, own // LOW)
    block = pl.BlockSpec((features, stack * LOW), lambda i: (0, i))
    extra = [] if before is None else [before]
    return pl.pallas_call(
        functools.partial(scatter_kernel, groups, stack),
        grid=(own // (LOW * stack),),
        out_shape=jax.ShapeDtypeStruct((features, own), F32),
        in_specs=[
            pl.BlockSpec((groups * capacity, LOW), lambda i: (0, 0)),
            pl.BlockSpec(high.shape, lambda i: (0, 0)),
        ]
        + [pl.BlockSpec((features, capacity), lambda i: (0, 0))] * groups
        + [block] * len(extra),
        out_specs=block,
        scratch_shapes=[pltpu.VMEM((stack * features, groups * capacity), BF16)],
        input_output_aliases={2 + groups: 0} if extra else {},
        compiler_params=pltpu.CompilerParams(vmem_limit_bytes=LIST_VMEM_BYTES),
        cost_estimate=pl.CostEstimate(flops=3 * 10**9, bytes_accessed=10**6, transcendentals=0),
        name="scatter_slots",
    )(low, high, *lists, *extra)


def swap(value, axis, distance):
    size = lax.axis_size(axis)
    return lax.ppermute(value, axis, [(i, i ^ distance) for i in range(size)])


def deliver(home, plan, grads, own, capacity, before=None):
    low, high, slot, _ = plan
    farthest = low.shape[0] - 1
    near = tuple(range(farthest))
    (far_list,) = pack_lists((farthest,), home, slot, grads, capacity)
    far_list, slot = lax.optimization_barrier((far_list, slot))
    far_list = swap(far_list, "dp", farthest)
    own_list, *near_lists = pack_lists(near, home, slot, grads, capacity)
    near_lists = [swap(near_list, "dp", k) for k, near_list in zip(near[1:], near_lists)]
    return scatter_slots(low, high, [own_list, *near_lists, far_list], own, before)


def exchange(value, axis):
    return lax.all_to_all(value, axis, split_axis=0, concat_axis=0, tiled=True)


def on_device(item_ids, user_len, emb_table, cotangent, w_uvqk, w_out, gain_in, gain_mid):
    dp_size = lax.axis_size("dp")
    table_size = lax.axis_size("table")
    users = user_len.shape[0]
    features, vocab = emb_table.shape
    rows = item_ids.shape[0]
    positions = rows // users
    own = vocab // dp_size
    capacity = -(-(rows // dp_size * 5 // 4) // LANES) * LANES
    assert users == table_size and users <= LANES and positions <= 256 and own // LOW <= 255
    assert dp_size & (dp_size - 1) == 0 and users & (users - 1) == 0 and own & (own - 1) == 0
    me = lax.axis_index("table").astype(jnp.int32).reshape(1)
    home = lax.axis_index("dp").astype(jnp.int32).reshape(1)

    send, valid_ids = gather_columns(item_ids, user_len, cotangent, emb_table)
    received = exchange(send, "table")
    all_ids = jnp.stack([valid_ids] + [swap(valid_ids, "dp", k) for k in range(1, dp_size)])
    out_cols, grad_cols = run_layer(me, user_len, received, w_uvqk, w_out, gain_in, gain_mid)
    per_peer = (table_size, features, positions)
    all_ids, grad_cols = lax.optimization_barrier((all_ids, grad_cols))
    plan = plan_turn(home, jnp.zeros((1,), jnp.int32), all_ids, own, capacity)
    grad_home = exchange(grad_cols.reshape(per_peer), "table")
    out_cols, grad_home = lax.optimization_barrier((out_cols, grad_home))
    out_home = exchange(out_cols.reshape(per_peer), "table")
    table_grad = deliver(home, plan, grad_home, own, capacity)
    layer_out = jnp.transpose(out_home, (1, 0, 2)).reshape(features, rows)

    turns = (plan[-1][0] + capacity - 1) // capacity

    def another(state):
        turn, sums = state
        more = plan_turn(home, turn.reshape(1), all_ids, own, capacity)
        return turn + 1, deliver(home, more, grad_home, own, capacity, sums)

    _, table_grad = lax.while_loop(
        lambda state: state[0] < turns, another, (jnp.int32(1), table_grad)
    )
    return (layer_out, table_grad)


def solution(mesh):
    return jax.shard_map(
        on_device,
        mesh=mesh,
        in_specs=(P("dp"), P("dp"), P("table", None), P("table", "dp"), P(), P(), P(), P()),
        out_specs=(P("table", "dp"), P("table", "dp")),
        check_vma=False,
    )
```

```python
import functools

import jax
import jax.numpy as jnp
from jax import lax
from jax.experimental import pallas as pl
from jax.experimental.pallas import tpu as pltpu
from jax.sharding import PartitionSpec as P

HEADS = 8
NORM_EPS = 1e-05
LANES = 128
WHOLE_VMEM_BYTES = 61 * 1024 * 1024
LAYER_VMEM_BYTES = 20 * 1024 * 1024
PLAN_VMEM_BYTES = 16 * 1024 * 1024
LIST_VMEM_BYTES = 24 * 1024 * 1024

F32 = jnp.float32
BF16 = jnp.bfloat16


def dot_nn(left, right):
    return jnp.dot(left, right, preferred_element_type=F32)


def dot_nt(left, right):
    return lax.dot_general(left, right, (((1,), (1,)), ((), ())), preferred_element_type=F32)


def dot_tn(left, right):
    return lax.dot_general(left, right, (((0,), (0,)), ((), ())), preferred_element_type=F32)


BLOCK = 256
UNROLL = 64
CHUNK_ROWS = 16


def gather_kernel(
    len_ref,
    ids_ref,
    cot_hbm_ref,
    table_hbm_ref,
    out_ref,
    valid_ref,
    table_ref,
    cot_ref,
    rows_ref,
    picked_ref,
    turned_ref,
    row_vector_ref,
    row_ref,
    chunk_sems,
    row_sem,
    out_sems,
    cot_sem,
):
    users, _, positions = out_ref.shape
    features, vocab = table_hbm_ref.shape
    pack = LANES // features
    span = BLOCK * pack
    block_bits = BLOCK.bit_length() - 1

    def chunk_copy(chunk):
        rows = pl.ds(chunk * CHUNK_ROWS, CHUNK_ROWS)
        return pltpu.make_async_copy(
            table_hbm_ref.at[rows, :], table_ref.at[rows, :], chunk_sems.at[chunk]
        )

    def out_copy(user):
        return pltpu.make_async_copy(turned_ref.at[user], out_ref.at[user], out_sems.at[user])

    for chunk in range(features // CHUNK_ROWS):
        chunk_copy(chunk).start()
    cot_copy = pltpu.make_async_copy(cot_hbm_ref, cot_ref, cot_sem)
    cot_copy.start()
    items = ids_ref[...]
    row_vector_ref[...] = ((items >> (span.bit_length() - 1)) << block_bits) | (items & (BLOCK - 1))
    row_copy = pltpu.make_async_copy(row_vector_ref, row_ref, row_sem)
    row_copy.start()
    order = lax.broadcasted_iota(jnp.int32, (1, positions), 1)
    for user in range(users):
        own_items = ids_ref[pl.ds(user * positions, positions)].reshape(1, positions)
        valid_ref[pl.ds(user, 1), :] = jnp.where(order < len_ref[user], own_items, vocab)

    cot_copy.wait()
    for user in range(users):
        turned_ref[user, pl.ds(features, features), :] = cot_ref[:, pl.ds(user * positions, positions)]

    for chunk in range(features // CHUNK_ROWS):
        chunk_copy(chunk).wait()
    for part in range(vocab // span):
        stack = jnp.concatenate(
            [
                table_ref[:, part * span + s * BLOCK : part * span + (s + 1) * BLOCK]
                for s in range(pack)
            ],
            axis=0,
        )
        rows_ref[pl.ds(part * BLOCK, BLOCK), :] = stack.T.astype(F32)
    row_copy.wait()

    def some(part, carry):
        start = pl.multiple_of(part * UNROLL, UNROLL)
        for slot in range(UNROLL):
            row = row_ref[start + slot]
            picked_ref[pl.ds(start + slot, 1), :] = rows_ref[pl.ds(row, 1), :]
        return carry

    lax.fori_loop(0, users * positions // UNROLL, some, 0)
    row = lax.broadcasted_iota(jnp.int32, (LANES, LANES), 0)
    column = lax.broadcasted_iota(jnp.int32, (LANES, LANES), 1)
    same = jnp.where(row == column, 1.0, 0.0).astype(BF16)
    for user in range(users):
        places = pl.ds(user * positions, positions)
        turned = dot_nt(same, picked_ref[places, :].astype(BF16))
        own_items = ids_ref[places].reshape(1, positions)
        group = (own_items >> block_bits) & (pack - 1)
        total = turned[:features]
        for s in range(1, pack):
            total = jnp.where(group == s, turned[s * features : (s + 1) * features], total)
        turned_ref[user, pl.ds(0, features), :] = total.astype(BF16)
        out_copy(user).start()
    for user in range(users):
        out_copy(user).wait()


def gather_columns(item_ids, lengths, cotangent, table):
    users = lengths.shape[0]
    rows = item_ids.shape[0]
    positions = rows // users
    features, vocab = table.shape
    pack = LANES // features
    shape = (users, 2 * features, positions)
    hbm = pl.BlockSpec(memory_space=pltpu.HBM)
    vmem = pl.BlockSpec(memory_space=pltpu.VMEM)
    return pl.pallas_call(
        gather_kernel,
        out_shape=[
            jax.ShapeDtypeStruct(shape, table.dtype),
            jax.ShapeDtypeStruct((users, positions), jnp.int32),
        ],
        in_specs=[pl.BlockSpec(memory_space=pltpu.SMEM), vmem, hbm, hbm],
        out_specs=[hbm, vmem],
        scratch_shapes=[
            pltpu.VMEM((features, vocab), table.dtype),
            pltpu.VMEM((features, rows), table.dtype),
            pltpu.VMEM((vocab // pack, LANES), F32),
            pltpu.VMEM((rows, LANES), F32),
            pltpu.VMEM(shape, table.dtype),
            pltpu.VMEM((rows,), jnp.int32),
            pltpu.SMEM((rows,), jnp.int32),
            pltpu.SemaphoreType.DMA((features // CHUNK_ROWS,)),
            pltpu.SemaphoreType.DMA,
            pltpu.SemaphoreType.DMA((users,)),
            pltpu.SemaphoreType.DMA,
        ],
        compiler_params=pltpu.CompilerParams(vmem_limit_bytes=WHOLE_VMEM_BYTES),
        cost_estimate=pl.CostEstimate(flops=8 * 10**9, bytes_accessed=5 * 10**6, transcendentals=0),
        name="gather_columns",
    )(lengths, item_ids, cotangent, table)


def norm_forward(values):
    centred = values - jnp.mean(values, axis=0, keepdims=True)
    inverse = lax.rsqrt(jnp.mean(centred * centred, axis=0, keepdims=True) + NORM_EPS)
    return centred * inverse, inverse


def norm_backward(grad, normal, inverse):
    shift = jnp.mean(grad, axis=0, keepdims=True)
    slope = jnp.mean(grad * normal, axis=0, keepdims=True)
    return (grad - shift - normal * slope) * inverse


def silu_pair(half):
    turn = jnp.tanh(half)
    twice = 1.0 + turn
    value = half * twice
    return value, twice + value * (1.0 - turn)


def layer_kernel(
    me_ref,
    len_ref,
    recv_ref,
    w_in_ref,
    w_in_t_ref,
    w_out_ref,
    w_out_t_ref,
    gain_in_row_ref,
    gain_mid_row_ref,
    out_hbm_ref,
    grad_hbm_ref,
    out_ref,
    grad_ref,
    proj_ref,
    slope_ref,
    weight_ref,
    score_slope_ref,
    att_ref,
    dproj_ref,
    gain_in_ref,
    gain_mid_ref,
    share_ref,
    sems,
):
    peers, both, positions = recv_ref.shape
    features = both // 2
    width = peers * features
    head_dim = width // HEADS
    half = positions // 2

    out_copy = pltpu.make_async_copy(out_ref, out_hbm_ref, sems.at[0])
    grad_copy = pltpu.make_async_copy(grad_ref, grad_hbm_ref, sems.at[1])
    length = len_ref[me_ref[0]]
    share = 1.0 / length.astype(F32)
    for row_ref, column_ref in ((gain_in_row_ref, gain_in_ref), (gain_mid_row_ref, gain_mid_ref)):
        row = row_ref[...].reshape(1, width)
        column_ref[...] = jnp.broadcast_to(row, (positions, width)).T

    key = lax.broadcasted_iota(jnp.int32, (positions, positions), 0)
    query = lax.broadcasted_iota(jnp.int32, (positions, positions), 1)
    share_ref[...] = jnp.where((key <= query) & (key < length), share, 0.0)

    def joined(kind):
        rows = pl.ds(kind * features, features)
        return jnp.concatenate([recv_ref[peer, rows, :] for peer in range(peers)], axis=0)

    embedded = joined(0).astype(F32)
    normal_in, inverse_in = norm_forward(embedded)
    normed = (normal_in * gain_in_ref[...]).astype(BF16)

    def project(part):
        return dot_nn(w_in_t_ref[pl.ds(part * width, width), :], normed)

    def store_projected(part, z):
        rows = pl.ds(part * width, width)
        value, slope = silu_pair(0.5 * z)
        proj_ref[rows, :] = value.astype(BF16)
        slope_ref[rows, :] = slope

    waiting = None
    for part in (2, 3, 1, 0):
        z = project(part)
        if waiting is not None:
            store_projected(*waiting)
        waiting = (part, z)
    store_projected(*waiting)

    starts = (0, half)
    scale = head_dim ** (-0.5)

    def head_rows(kind, head):
        return pl.ds(kind * width + head * head_dim, head_dim)

    def score(head):
        queries, keys = proj_ref[head_rows(2, head), :], proj_ref[head_rows(3, head), :]
        return [dot_tn(keys[:, start : start + half], queries[:, start:]) for start in starts]

    def store_weights(head, scores):
        for start, block in zip(starts, scores):
            value, slope = silu_pair(block * (0.5 * scale))
            places = (pl.ds(start, half), pl.ds(start, positions - start))
            weight_ref[head, *places] = (value * share_ref[*places]).astype(BF16)
            score_slope_ref[head, *places] = slope * share_ref[*places]
        weight_ref[head, pl.ds(half, half), pl.ds(0, half)] = jnp.zeros((half, half), BF16)

    def attend(head):
        att_ref[pl.ds(head * head_dim, head_dim), :] = dot_nn(
            proj_ref[head_rows(1, head), :], weight_ref[head]
        )

    scores = score(0)
    for head in range(HEADS):
        following = score(head + 1) if head + 1 < HEADS else None
        store_weights(head, scores)
        if head:
            attend(head - 1)
        scores = following
    attend(HEADS - 1)

    normal_mid, inverse_mid = norm_forward(att_ref[...])
    gate_rows = proj_ref[pl.ds(0, width), :].astype(F32)
    scaled = normal_mid * gain_mid_ref[...]
    mixed = (scaled * gate_rows).astype(BF16)
    valid = lax.broadcasted_iota(jnp.int32, (width, positions), 1) < length
    cotangent = jnp.where(valid, joined(1).astype(F32), 0.0)
    d_mixed = dot_nn(w_out_ref[...], cotangent.astype(BF16))
    out_ref[...] = (embedded + dot_nn(w_out_t_ref[...], mixed)).astype(BF16)
    out_copy.start()

    dproj_ref[pl.ds(0, width), :] = (d_mixed * scaled * slope_ref[pl.ds(0, width), :]).astype(BF16)
    d_att = norm_backward(d_mixed * gate_rows * gain_mid_ref[...], normal_mid, inverse_mid)
    att_ref[...] = d_att

    def d_weights(head):
        values = proj_ref[head_rows(1, head), :]
        d_head = att_ref[pl.ds(head * head_dim, head_dim), :].astype(BF16)
        return [dot_tn(values[:, start : start + half], d_head[:, start:]) for start in starts]

    def d_scores(head, products):
        low, high = (
            (block * score_slope_ref[head, pl.ds(start, half), pl.ds(start, positions - start)]).astype(
                BF16
            )
            for start, block in zip(starts, products)
        )
        empty = jnp.zeros((half, half), BF16)
        return jnp.concatenate([low, jnp.concatenate([empty, high], axis=1)], axis=0)

    def d_project(head, d_score):
        d_head = att_ref[pl.ds(head * head_dim, head_dim), :].astype(BF16)
        queries, keys = proj_ref[head_rows(2, head), :], proj_ref[head_rows(3, head), :]
        products = (
            dot_nt(d_head, weight_ref[head]),
            dot_nn(keys, d_score) * (0.5 * scale),
            dot_nt(queries, d_score) * (0.5 * scale),
        )
        for kind, product in zip((1, 2, 3), products):
            rows = head_rows(kind, head)
            dproj_ref[rows, :] = (product * slope_ref[rows, :]).astype(BF16)

    products, before = d_weights(0), None
    for head in range(HEADS):
        following = d_weights(head + 1) if head + 1 < HEADS else None
        d_score = d_scores(head, products)
        if head:
            d_project(head - 1, before)
        products, before = following, d_score
    d_project(HEADS - 1, before)

    d_normed = dot_nn(w_in_ref[...], dproj_ref[...])
    d_embedded = norm_backward(d_normed * (0.5 * gain_in_ref[...]), normal_in, inverse_in)
    grad_ref[...] = (cotangent + d_embedded).astype(BF16)
    grad_copy.start()
    out_copy.wait()
    grad_copy.wait()


def turn_kernel(w_in_ref, w_out_ref, w_in_t_ref, w_out_t_ref):
    width = w_out_ref.shape[0]
    for part in range(w_in_ref.shape[1] // width):
        places = pl.ds(part * width, width)
        w_in_t_ref[places, :] = w_in_ref[:, places].T
    w_out_t_ref[...] = w_out_ref[...].T


def turn_weights(w_in, w_out):
    vmem = pl.BlockSpec(memory_space=pltpu.VMEM)
    return pl.pallas_call(
        turn_kernel,
        out_shape=[jax.ShapeDtypeStruct(w.shape[::-1], w.dtype) for w in (w_in, w_out)],
        in_specs=[vmem] * 2,
        out_specs=[vmem] * 2,
        compiler_params=pltpu.CompilerParams(vmem_limit_bytes=LAYER_VMEM_BYTES),
        cost_estimate=pl.CostEstimate(flops=10**9, bytes_accessed=5 * 10**6, transcendentals=0),
        name="turn_weights",
    )(w_in, w_out)


def run_layer(me, lengths, received, w_in, w_in_t, w_out, w_out_t, gain_in, gain_mid):
    peers, _, positions = received.shape
    width = w_out.shape[0]
    smem, vmem = pl.BlockSpec(memory_space=pltpu.SMEM), pl.BlockSpec(memory_space=pltpu.VMEM)
    hbm = pl.BlockSpec(memory_space=pltpu.HBM)
    shape = jax.ShapeDtypeStruct((width, positions), BF16)
    return pl.pallas_call(
        layer_kernel,
        out_shape=[shape, shape],
        in_specs=[smem, smem] + [vmem] * 7,
        out_specs=[hbm, hbm],
        scratch_shapes=[
            pltpu.VMEM((width, positions), BF16),
            pltpu.VMEM((width, positions), BF16),
            pltpu.VMEM((4 * width, positions), BF16),
            pltpu.VMEM((4 * width, positions), F32),
            pltpu.VMEM((HEADS, positions, positions), BF16),
            pltpu.VMEM((HEADS, positions, positions), F32),
            pltpu.VMEM((width, positions), F32),
            pltpu.VMEM((4 * width, positions), BF16),
            pltpu.VMEM((width, positions), F32),
            pltpu.VMEM((width, positions), F32),
            pltpu.VMEM((positions, positions), F32),
            pltpu.SemaphoreType.DMA((2,)),
        ],
        compiler_params=pltpu.CompilerParams(vmem_limit_bytes=LAYER_VMEM_BYTES),
        cost_estimate=pl.CostEstimate(flops=10**10, bytes_accessed=10**7, transcendentals=10**6),
        name="layer",
    )(
        me,
        lengths,
        received,
        w_in,
        w_in_t,
        w_out,
        w_out_t,
        gain_in,
        gain_mid,
    )


LOW = 256
STACK = 16


def ranks(member, users):
    rows, positions = member.shape
    ones = jnp.where(member, 1.0, 0.0).astype(BF16)

    def iota(shape, dimension):
        return lax.broadcasted_iota(jnp.int32, shape, dimension)

    square = (positions, positions)
    before = jnp.where(iota(square, 0) < iota(square, 1), 1.0, 0.0).astype(BF16)
    row, other = iota((rows, rows), 0), iota((rows, rows), 1)
    shift = users.bit_length() - 1
    above = (other < row) & ((other >> shift) == (row >> shift))
    earlier = dot_nn(jnp.where(above, 1.0, 0.0).astype(BF16), ones)
    return (dot_nn(ones, before) + jnp.sum(earlier, axis=1, keepdims=True)).astype(jnp.int32)


def plan_kernel(own, home_ref, turn_ref, ids_ref, low_ref, high_ref, slot_ref, most_ref, *scratch):
    chosen_ref, digit_ref, wide_ref, rank_ref = scratch
    groups, users, positions = ids_ref.shape
    capacity = low_ref.shape[1]
    home = home_ref[0]
    first = turn_ref[0] * capacity
    own_bits, low_bits = own.bit_length() - 1, LOW.bit_length() - 1

    all_items = ids_ref[...].reshape(groups * users, positions)
    sent = jnp.concatenate([ids_ref[0] >> own_bits == owner for owner in range(groups)], axis=0)
    arriving = all_items >> own_bits == home
    rank_ref[...] = ranks(jnp.concatenate([arriving, sent], axis=0), users) - first
    slot = jnp.full((users, positions), -1, jnp.int32)
    for owner in range(groups):
        rank = rank_ref[pl.ds((groups + owner) * users, users), :]
        fits = (ids_ref[0] >> own_bits == owner) & (rank >= 0) & (rank < capacity)
        slot = jnp.where(fits, rank + owner * capacity, slot)
    slot_ref[...] = slot

    digit = lax.broadcasted_iota(jnp.int32, (LOW, positions), 0)
    place = lax.broadcasted_iota(jnp.int32, (capacity, positions), 0)

    def one_group(group, most):
        items = ids_ref[group]
        for owner in range(groups):
            count = jnp.sum(jnp.where(items >> own_bits == owner, 1.0, 0.0))
            most = jnp.maximum(most, count)
        mine = items >> own_bits == home
        local = items & (own - 1)
        rank = rank_ref[pl.ds(pl.multiple_of(group * users, users), users), :]
        slot = jnp.where(mine, rank, -1)
        low = local & (LOW - 1)
        high = jnp.where(mine, (local >> low_bits) + 1, 0).astype(F32)
        for user in range(users):
            columns = pl.ds(user * positions, positions)
            chosen_ref[:, columns] = jnp.where(place == slot[user : user + 1], 1.0, 0.0).astype(BF16)
            digit_ref[:, columns] = jnp.where(digit == low[user : user + 1], 1.0, 0.0).astype(BF16)
            wide_ref[:, columns] = jnp.broadcast_to(high[user : user + 1], (16, positions)).astype(BF16)
        low_ref[group] = dot_nt(chosen_ref[...], digit_ref[...]).astype(BF16)
        high_ref[pl.ds(group, 1), :] = dot_nt(wide_ref[...], chosen_ref[...])[:1]
        return most

    most_ref[0] = lax.fori_loop(0, groups, one_group, jnp.float32(0)).astype(jnp.int32)


def plan_turn(home, turn, all_ids, own, capacity):
    groups, users, positions = all_ids.shape
    smem, vmem = pl.BlockSpec(memory_space=pltpu.SMEM), pl.BlockSpec(memory_space=pltpu.VMEM)
    return pl.pallas_call(
        functools.partial(plan_kernel, own),
        out_shape=[
            jax.ShapeDtypeStruct((groups, capacity, LOW), BF16),
            jax.ShapeDtypeStruct((groups, capacity), F32),
            jax.ShapeDtypeStruct((users, positions), jnp.int32),
            jax.ShapeDtypeStruct((1,), jnp.int32),
        ],
        in_specs=[smem, smem, vmem],
        out_specs=[vmem] * 3 + [smem],
        scratch_shapes=[
            pltpu.VMEM((capacity, users * positions), BF16),
            pltpu.VMEM((LOW, users * positions), BF16),
            pltpu.VMEM((16, users * positions), BF16),
            pltpu.VMEM((2 * groups * users, positions), jnp.int32),
        ],
        compiler_params=pltpu.CompilerParams(vmem_limit_bytes=PLAN_VMEM_BYTES),
        cost_estimate=pl.CostEstimate(flops=4 * 10**9, bytes_accessed=5 * 10**6, transcendentals=0),
        name="plan_turn",
    )(home, turn, all_ids)


def pack_kernel(distances, home_ref, slot_ref, grad_ref, *refs):
    *packed_refs, wide_ref, chosen_ref = refs
    users, _, positions = grad_ref.shape
    capacity = packed_refs[0].shape[1]
    padded = jnp.concatenate(
        [slot_ref[...].astype(F32), jnp.zeros((LANES - users, positions), F32)], axis=0
    )
    slots = padded.T.astype(jnp.int32)
    place = lax.broadcasted_iota(jnp.int32, (positions, capacity), 1)
    for user in range(users):
        wide_ref[:, pl.ds(user * positions, positions)] = grad_ref[user]
    for distance, packed_ref in zip(distances, packed_refs):
        first = (home_ref[0] ^ distance) * capacity
        for user in range(users):
            chosen_ref[pl.ds(user * positions, positions), :] = jnp.where(
                place == slots[:, user : user + 1] - first, 1.0, 0.0
            ).astype(BF16)
        packed_ref[...] = dot_nn(wide_ref[...], chosen_ref[...]).astype(BF16)


def pack_lists(distances, home, slot, grads, capacity):
    users, features, positions = grads.shape
    smem, vmem = pl.BlockSpec(memory_space=pltpu.SMEM), pl.BlockSpec(memory_space=pltpu.VMEM)
    return pl.pallas_call(
        functools.partial(pack_kernel, distances),
        out_shape=[jax.ShapeDtypeStruct((features, capacity), BF16)] * len(distances),
        in_specs=[smem, vmem, vmem],
        out_specs=[vmem] * len(distances),
        scratch_shapes=[
            pltpu.VMEM((features, users * positions), BF16),
            pltpu.VMEM((users * positions, capacity), BF16),
        ],
        compiler_params=pltpu.CompilerParams(vmem_limit_bytes=LIST_VMEM_BYTES),
        cost_estimate=pl.CostEstimate(
            flops=len(distances) * 8 * 10**8, bytes_accessed=10**6, transcendentals=0
        ),
        name="pack_lists",
    )(home, slot, grads)


def scatter_kernel(groups, stack, low_ref, high_ref, *refs):
    list_refs, (*before_ref, out_ref, spread_ref) = refs[:groups], refs[groups:]
    features, capacity = list_refs[0].shape
    step = pl.program_id(0)
    for group, list_ref in enumerate(list_refs):
        high = high_ref[pl.ds(group, 1), :]
        for part in range(stack):
            wanted = (step * stack + part + 1).astype(F32)
            chosen = jnp.where(high == wanted, 1.0, 0.0).astype(BF16)
            spread_ref[pl.ds(part * features, features), pl.ds(group * capacity, capacity)] = (
                list_ref[...] * chosen
            )
    sums = dot_nn(spread_ref[...], low_ref[...])
    for part in range(stack):
        columns = pl.ds(part * LOW, LOW)
        term = sums[part * features : (part + 1) * features]
        out_ref[:, columns] = term + before_ref[0][:, columns] if before_ref else term


def scatter_slots(low, high, lists, own, before=None):
    groups = len(lists)
    features, capacity = lists[0].shape
    low = low.reshape(groups * capacity, LOW)
    stack = min(STACK, own // LOW)
    block = pl.BlockSpec((features, stack * LOW), lambda i: (0, i))
    extra = [] if before is None else [before]
    return pl.pallas_call(
        functools.partial(scatter_kernel, groups, stack),
        grid=(own // (LOW * stack),),
        out_shape=jax.ShapeDtypeStruct((features, own), F32),
        in_specs=[
            pl.BlockSpec((groups * capacity, LOW), lambda i: (0, 0)),
            pl.BlockSpec(high.shape, lambda i: (0, 0)),
        ]
        + [pl.BlockSpec((features, capacity), lambda i: (0, 0))] * groups
        + [block] * len(extra),
        out_specs=block,
        scratch_shapes=[pltpu.VMEM((stack * features, groups * capacity), BF16)],
        input_output_aliases={2 + groups: 0} if extra else {},
        compiler_params=pltpu.CompilerParams(vmem_limit_bytes=LIST_VMEM_BYTES),
        cost_estimate=pl.CostEstimate(flops=3 * 10**9, bytes_accessed=10**6, transcendentals=0),
        name="scatter_slots",
    )(low, high, *lists, *extra)


def swap(value, axis, distance):
    size = lax.axis_size(axis)
    return lax.ppermute(value, axis, [(i, i ^ distance) for i in range(size)])


def send_lists(home, slot, grads, owners, capacity):
    lists = [None] * owners
    for distances in ((owners - 1,), tuple(range(1, owners - 1)), (0,)):
        made = pack_lists(distances, home, slot, grads, capacity)
        slot, made = lax.optimization_barrier((slot, made))
        for distance, one_list in zip(distances, made):
            lists[distance] = swap(one_list, "dp", distance) if distance else one_list
    return lists


def exchange(value, axis):
    return lax.all_to_all(value, axis, split_axis=0, concat_axis=0, tiled=True)


def on_device(item_ids, user_len, emb_table, cotangent, w_uvqk, w_out, gain_in, gain_mid):
    dp_size = lax.axis_size("dp")
    table_size = lax.axis_size("table")
    users = user_len.shape[0]
    features, vocab = emb_table.shape
    rows = item_ids.shape[0]
    positions = rows // users
    own = vocab // dp_size
    capacity = -(-(rows // dp_size * 5 // 4) // LANES) * LANES
    assert users == table_size and users <= LANES and positions <= 256 and own // LOW <= 255
    assert dp_size & (dp_size - 1) == 0 and users & (users - 1) == 0 and own & (own - 1) == 0
    me = lax.axis_index("table").astype(jnp.int32).reshape(1)
    home = lax.axis_index("dp").astype(jnp.int32).reshape(1)

    send, valid_ids = gather_columns(item_ids, user_len, cotangent, emb_table)
    received = exchange(send, "table")
    all_ids = jnp.stack([valid_ids] + [swap(valid_ids, "dp", k) for k in range(1, dp_size)])
    valid_ids, w_in, w_out = lax.optimization_barrier((valid_ids, w_uvqk, w_out))
    w_in_t, w_out_t = turn_weights(w_in, w_out)
    out_cols, grad_cols = run_layer(
        me, user_len, received, w_in, w_in_t, w_out, w_out_t, gain_in, gain_mid
    )
    per_peer = (table_size, features, positions)
    all_ids, grad_cols = lax.optimization_barrier((all_ids, grad_cols))
    plan = plan_turn(home, jnp.zeros((1,), jnp.int32), all_ids, own, capacity)
    grad_home = exchange(grad_cols.reshape(per_peer), "table")
    out_cols, grad_home = lax.optimization_barrier((out_cols, grad_home))
    out_home = exchange(out_cols.reshape(per_peer), "table")
    low, high, slot, most = plan
    lists = send_lists(home, slot, grad_home, dp_size, capacity)
    layer_out = jnp.transpose(out_home, (1, 0, 2)).reshape(features, rows)
    layer_out, lists = lax.optimization_barrier((layer_out, lists))
    table_grad = scatter_slots(low, high, lists, own)

    turns = (most[0] + capacity - 1) // capacity

    def another(state):
        turn, sums = state
        more_low, more_high, more_slot, _ = plan_turn(home, turn.reshape(1), all_ids, own, capacity)
        more_lists = send_lists(home, more_slot, grad_home, dp_size, capacity)
        return turn + 1, scatter_slots(more_low, more_high, more_lists, own, sums)

    _, table_grad = lax.while_loop(
        lambda state: state[0] < turns, another, (jnp.int32(1), table_grad)
    )
    return (layer_out, table_grad)


def solution(mesh):
    return jax.shard_map(
        on_device,
        mesh=mesh,
        in_specs=(P("dp"), P("dp"), P("table", None), P("table", "dp"), P(), P(), P(), P()),
        out_specs=(P("table", "dp"), P("table", "dp")),
        check_vma=False,
    )
```

```python
import functools

import jax
import jax.numpy as jnp
from jax import lax
from jax.experimental import pallas as pl
from jax.experimental.pallas import tpu as pltpu
from jax.sharding import PartitionSpec as P

HEADS = 8
NORM_EPS = 1e-05
LANES = 128
WHOLE_VMEM_BYTES = 61 * 1024 * 1024
LAYER_VMEM_BYTES = 20 * 1024 * 1024
PLAN_VMEM_BYTES = 16 * 1024 * 1024
LIST_VMEM_BYTES = 24 * 1024 * 1024

F32 = jnp.float32
BF16 = jnp.bfloat16


def dot_nn(left, right):
    return jnp.dot(left, right, preferred_element_type=F32)


def dot_nt(left, right):
    return lax.dot_general(left, right, (((1,), (1,)), ((), ())), preferred_element_type=F32)


def dot_tn(left, right):
    return lax.dot_general(left, right, (((0,), (0,)), ((), ())), preferred_element_type=F32)


BLOCK = 256
UNROLL = 64
CHUNKS = 4


def gather_kernel(
    len_ref,
    ids_ref,
    cot_hbm_ref,
    table_hbm_ref,
    out_ref,
    valid_ref,
    table_ref,
    cot_ref,
    rows_ref,
    picked_ref,
    turned_ref,
    row_vector_ref,
    row_ref,
    chunk_sems,
    row_sem,
    out_sems,
    cot_sem,
):
    users, _, positions = out_ref.shape
    features, vocab = table_hbm_ref.shape
    pack = LANES // features
    span = BLOCK * pack
    block_bits = BLOCK.bit_length() - 1

    def chunk_copy(chunk):
        columns = pl.ds(chunk * (vocab // CHUNKS), vocab // CHUNKS)
        return pltpu.make_async_copy(
            table_hbm_ref.at[:, columns], table_ref.at[:, columns], chunk_sems.at[chunk]
        )

    def out_copy(user):
        return pltpu.make_async_copy(turned_ref.at[user], out_ref.at[user], out_sems.at[user])

    for chunk in range(CHUNKS):
        chunk_copy(chunk).start()
    cot_copy = pltpu.make_async_copy(cot_hbm_ref, cot_ref, cot_sem)
    cot_copy.start()
    items = ids_ref[...]
    row_vector_ref[...] = ((items >> (span.bit_length() - 1)) << block_bits) | (items & (BLOCK - 1))
    row_copy = pltpu.make_async_copy(row_vector_ref, row_ref, row_sem)
    row_copy.start()
    order = lax.broadcasted_iota(jnp.int32, (1, positions), 1)
    for user in range(users):
        own_items = ids_ref[pl.ds(user * positions, positions)].reshape(1, positions)
        valid_ref[pl.ds(user, 1), :] = jnp.where(order < len_ref[user], own_items, vocab)

    cot_copy.wait()
    for user in range(users):
        turned_ref[user, pl.ds(features, features), :] = cot_ref[:, pl.ds(user * positions, positions)]

    parts = vocab // span
    for part in range(parts):
        if part % (parts // CHUNKS) == 0:
            chunk_copy(part // (parts // CHUNKS)).wait()
        stack = jnp.concatenate(
            [
                table_ref[:, part * span + s * BLOCK : part * span + (s + 1) * BLOCK]
                for s in range(pack)
            ],
            axis=0,
        )
        rows_ref[pl.ds(part * BLOCK, BLOCK), :] = stack.T.astype(F32)
    row_copy.wait()

    def some(part, carry):
        start = pl.multiple_of(part * UNROLL, UNROLL)
        for slot in range(UNROLL):
            row = row_ref[start + slot]
            picked_ref[pl.ds(start + slot, 1), :] = rows_ref[pl.ds(row, 1), :]
        return carry

    lax.fori_loop(0, users * positions // UNROLL, some, 0)
    row = lax.broadcasted_iota(jnp.int32, (LANES, LANES), 0)
    column = lax.broadcasted_iota(jnp.int32, (LANES, LANES), 1)
    same = jnp.where(row == column, 1.0, 0.0).astype(BF16)
    for user in range(users):
        places = pl.ds(user * positions, positions)
        turned = dot_nt(same, picked_ref[places, :].astype(BF16))
        own_items = ids_ref[places].reshape(1, positions)
        group = (own_items >> block_bits) & (pack - 1)
        total = turned[:features]
        for s in range(1, pack):
            total = jnp.where(group == s, turned[s * features : (s + 1) * features], total)
        turned_ref[user, pl.ds(0, features), :] = total.astype(BF16)
        out_copy(user).start()
    for user in range(users):
        out_copy(user).wait()


def gather_columns(item_ids, lengths, cotangent, table):
    users = lengths.shape[0]
    rows = item_ids.shape[0]
    positions = rows // users
    features, vocab = table.shape
    pack = LANES // features
    shape = (users, 2 * features, positions)
    hbm = pl.BlockSpec(memory_space=pltpu.HBM)
    vmem = pl.BlockSpec(memory_space=pltpu.VMEM)
    return pl.pallas_call(
        gather_kernel,
        out_shape=[
            jax.ShapeDtypeStruct(shape, table.dtype),
            jax.ShapeDtypeStruct((users, positions), jnp.int32),
        ],
        in_specs=[pl.BlockSpec(memory_space=pltpu.SMEM), vmem, hbm, hbm],
        out_specs=[hbm, vmem],
        scratch_shapes=[
            pltpu.VMEM((features, vocab), table.dtype),
            pltpu.VMEM((features, rows), table.dtype),
            pltpu.VMEM((vocab // pack, LANES), F32),
            pltpu.VMEM((rows, LANES), F32),
            pltpu.VMEM(shape, table.dtype),
            pltpu.VMEM((rows,), jnp.int32),
            pltpu.SMEM((rows,), jnp.int32),
            pltpu.SemaphoreType.DMA((CHUNKS,)),
            pltpu.SemaphoreType.DMA,
            pltpu.SemaphoreType.DMA((users,)),
            pltpu.SemaphoreType.DMA,
        ],
        compiler_params=pltpu.CompilerParams(vmem_limit_bytes=WHOLE_VMEM_BYTES),
        cost_estimate=pl.CostEstimate(flops=8 * 10**9, bytes_accessed=5 * 10**6, transcendentals=0),
        name="gather_columns",
    )(lengths, item_ids, cotangent, table)


def norm_forward(values):
    centred = values - jnp.mean(values, axis=0, keepdims=True)
    inverse = lax.rsqrt(jnp.mean(centred * centred, axis=0, keepdims=True) + NORM_EPS)
    return centred * inverse, inverse


def norm_backward(grad, normal, inverse):
    shift = jnp.mean(grad, axis=0, keepdims=True)
    slope = jnp.mean(grad * normal, axis=0, keepdims=True)
    return (grad - shift - normal * slope) * inverse


def silu_pair(half):
    turn = jnp.tanh(half)
    twice = 1.0 + turn
    value = half * twice
    return value, twice + value * (1.0 - turn)


def layer_kernel(
    me_ref,
    len_ref,
    recv_ref,
    w_in_ref,
    w_out_ref,
    gain_in_row_ref,
    gain_mid_row_ref,
    out_hbm_ref,
    grad_hbm_ref,
    out_ref,
    grad_ref,
    proj_ref,
    slope_ref,
    weight_ref,
    score_slope_ref,
    att_ref,
    dproj_ref,
    gain_in_ref,
    gain_mid_ref,
    share_ref,
    sems,
):
    peers, both, positions = recv_ref.shape
    features = both // 2
    width = peers * features
    head_dim = width // HEADS
    half = positions // 2

    out_copy = pltpu.make_async_copy(out_ref, out_hbm_ref, sems.at[0])
    grad_copy = pltpu.make_async_copy(grad_ref, grad_hbm_ref, sems.at[1])
    length = len_ref[me_ref[0]]
    share = 1.0 / length.astype(F32)
    for row_ref, column_ref in ((gain_in_row_ref, gain_in_ref), (gain_mid_row_ref, gain_mid_ref)):
        row = row_ref[...].reshape(1, width)
        tile = jnp.broadcast_to(row, (LANES, width)).T
        column_ref[...] = jnp.concatenate([tile] * (positions // LANES), axis=1)

    key = lax.broadcasted_iota(jnp.int32, (positions, positions), 0)
    query = lax.broadcasted_iota(jnp.int32, (positions, positions), 1)
    share_ref[...] = jnp.where((key <= query) & (key < length), share, 0.0)

    def joined(kind):
        rows = pl.ds(kind * features, features)
        return jnp.concatenate([recv_ref[peer, rows, :] for peer in range(peers)], axis=0)

    embedded = joined(0).astype(F32)
    normal_in, inverse_in = norm_forward(embedded)
    normed = (normal_in * gain_in_ref[...]).astype(BF16)

    def project(part):
        return dot_nn(w_in_ref[:, pl.ds(part * width, width)].T, normed)

    def store_projected(part, z):
        rows = pl.ds(part * width, width)
        value, slope = silu_pair(0.5 * z)
        proj_ref[rows, :] = value.astype(BF16)
        slope_ref[rows, :] = slope

    waiting = None
    for part in (2, 3, 1, 0):
        z = project(part)
        if waiting is not None:
            store_projected(*waiting)
        waiting = (part, z)
    store_projected(*waiting)

    starts = (0, half)
    scale = head_dim ** (-0.5)

    def head_rows(kind, head):
        return pl.ds(kind * width + head * head_dim, head_dim)

    def score(head):
        queries, keys = proj_ref[head_rows(2, head), :], proj_ref[head_rows(3, head), :]
        return [dot_tn(keys[:, start : start + half], queries[:, start:]) for start in starts]

    def store_weights(head, scores):
        for start, block in zip(starts, scores):
            value, slope = silu_pair(block * (0.5 * scale))
            places = (pl.ds(start, half), pl.ds(start, positions - start))
            weight_ref[head, *places] = (value * share_ref[*places]).astype(BF16)
            score_slope_ref[head, *places] = slope * share_ref[*places]
        weight_ref[head, pl.ds(half, half), pl.ds(0, half)] = jnp.zeros((half, half), BF16)

    def attend(head):
        att_ref[pl.ds(head * head_dim, head_dim), :] = dot_nn(
            proj_ref[head_rows(1, head), :], weight_ref[head]
        )

    scores = score(0)
    for head in range(HEADS):
        following = score(head + 1) if head + 1 < HEADS else None
        store_weights(head, scores)
        if head:
            attend(head - 1)
        scores = following
    attend(HEADS - 1)

    normal_mid, inverse_mid = norm_forward(att_ref[...])
    gate_rows = proj_ref[pl.ds(0, width), :].astype(F32)
    scaled = normal_mid * gain_mid_ref[...]
    mixed = (scaled * gate_rows).astype(BF16)
    valid = lax.broadcasted_iota(jnp.int32, (width, positions), 1) < length
    cotangent = jnp.where(valid, joined(1).astype(F32), 0.0)
    d_mixed = dot_nn(w_out_ref[...], cotangent.astype(BF16))
    out_ref[...] = (embedded + dot_nn(w_out_ref[...].T, mixed)).astype(BF16)
    out_copy.start()

    dproj_ref[pl.ds(0, width), :] = (d_mixed * scaled * slope_ref[pl.ds(0, width), :]).astype(BF16)
    d_att = norm_backward(d_mixed * gate_rows * gain_mid_ref[...], normal_mid, inverse_mid)
    att_ref[...] = d_att

    def d_weights(head):
        values = proj_ref[head_rows(1, head), :]
        d_head = att_ref[pl.ds(head * head_dim, head_dim), :].astype(BF16)
        return [dot_tn(values[:, start : start + half], d_head[:, start:]) for start in starts]

    def d_scores(head, products):
        low, high = (
            (block * score_slope_ref[head, pl.ds(start, half), pl.ds(start, positions - start)]).astype(
                BF16
            )
            for start, block in zip(starts, products)
        )
        empty = jnp.zeros((half, half), BF16)
        return jnp.concatenate([low, jnp.concatenate([empty, high], axis=1)], axis=0)

    def d_project(head, d_score):
        d_head = att_ref[pl.ds(head * head_dim, head_dim), :].astype(BF16)
        queries, keys = proj_ref[head_rows(2, head), :], proj_ref[head_rows(3, head), :]
        products = (
            dot_nt(d_head, weight_ref[head]),
            dot_nn(keys, d_score) * (0.5 * scale),
            dot_nt(queries, d_score) * (0.5 * scale),
        )
        for kind, product in zip((1, 2, 3), products):
            rows = head_rows(kind, head)
            dproj_ref[rows, :] = (product * slope_ref[rows, :]).astype(BF16)

    products, before = d_weights(0), None
    for head in range(HEADS):
        following = d_weights(head + 1) if head + 1 < HEADS else None
        d_score = d_scores(head, products)
        if head:
            d_project(head - 1, before)
        products, before = following, d_score
    d_project(HEADS - 1, before)

    d_normed = dot_nn(w_in_ref[...], dproj_ref[...])
    d_embedded = norm_backward(d_normed * (0.5 * gain_in_ref[...]), normal_in, inverse_in)
    grad_ref[...] = (cotangent + d_embedded).astype(BF16)
    grad_copy.start()
    out_copy.wait()
    grad_copy.wait()


def run_layer(me, lengths, received, w_in, w_out, gain_in, gain_mid):
    peers, _, positions = received.shape
    width = w_out.shape[0]
    smem, vmem = pl.BlockSpec(memory_space=pltpu.SMEM), pl.BlockSpec(memory_space=pltpu.VMEM)
    hbm = pl.BlockSpec(memory_space=pltpu.HBM)
    shape = jax.ShapeDtypeStruct((width, positions), BF16)
    return pl.pallas_call(
        layer_kernel,
        out_shape=[shape, shape],
        in_specs=[smem, smem] + [vmem] * 5,
        out_specs=[hbm, hbm],
        scratch_shapes=[
            pltpu.VMEM((width, positions), BF16),
            pltpu.VMEM((width, positions), BF16),
            pltpu.VMEM((4 * width, positions), BF16),
            pltpu.VMEM((4 * width, positions), F32),
            pltpu.VMEM((HEADS, positions, positions), BF16),
            pltpu.VMEM((HEADS, positions, positions), F32),
            pltpu.VMEM((width, positions), F32),
            pltpu.VMEM((4 * width, positions), BF16),
            pltpu.VMEM((width, positions), F32),
            pltpu.VMEM((width, positions), F32),
            pltpu.VMEM((positions, positions), F32),
            pltpu.SemaphoreType.DMA((2,)),
        ],
        compiler_params=pltpu.CompilerParams(vmem_limit_bytes=LAYER_VMEM_BYTES),
        cost_estimate=pl.CostEstimate(flops=10**10, bytes_accessed=10**7, transcendentals=10**6),
        name="layer",
    )(
        me,
        lengths,
        received,
        w_in,
        w_out,
        gain_in,
        gain_mid,
    )


LOW = 256
STACK = 16


def ranks(member, users):
    rows, positions = member.shape
    ones = jnp.where(member, 1.0, 0.0).astype(BF16)

    def iota(shape, dimension):
        return lax.broadcasted_iota(jnp.int32, shape, dimension)

    square = (positions, positions)
    before = jnp.where(iota(square, 0) < iota(square, 1), 1.0, 0.0).astype(BF16)
    row, other = iota((rows, rows), 0), iota((rows, rows), 1)
    shift = users.bit_length() - 1
    above = (other < row) & ((other >> shift) == (row >> shift))
    earlier = dot_nn(jnp.where(above, 1.0, 0.0).astype(BF16), ones)
    return (dot_nn(ones, before) + jnp.sum(earlier, axis=1, keepdims=True)).astype(jnp.int32)


def plan_kernel(own, home_ref, turn_ref, ids_ref, low_ref, high_ref, slot_ref, most_ref, *scratch):
    chosen_ref, digit_ref, wide_ref, rank_ref = scratch
    groups, users, positions = ids_ref.shape
    capacity = low_ref.shape[1]
    home = home_ref[0]
    first = turn_ref[0] * capacity
    own_bits, low_bits = own.bit_length() - 1, LOW.bit_length() - 1

    all_items = ids_ref[...].reshape(groups * users, positions)
    sent = jnp.concatenate([ids_ref[0] >> own_bits == owner for owner in range(groups)], axis=0)
    arriving = all_items >> own_bits == home
    rank_ref[...] = ranks(jnp.concatenate([arriving, sent], axis=0), users) - first
    slot = jnp.full((users, positions), -1, jnp.int32)
    for owner in range(groups):
        rank = rank_ref[pl.ds((groups + owner) * users, users), :]
        fits = (ids_ref[0] >> own_bits == owner) & (rank >= 0) & (rank < capacity)
        slot = jnp.where(fits, rank + owner * capacity, slot)
    slot_ref[...] = slot

    digit = lax.broadcasted_iota(jnp.int32, (LOW, positions), 0)
    place = lax.broadcasted_iota(jnp.int32, (capacity, positions), 0)

    def one_group(group, most):
        items = ids_ref[group]
        for owner in range(groups):
            count = jnp.sum(jnp.where(items >> own_bits == owner, 1.0, 0.0))
            most = jnp.maximum(most, count)
        mine = items >> own_bits == home
        local = items & (own - 1)
        rank = rank_ref[pl.ds(pl.multiple_of(group * users, users), users), :]
        slot = jnp.where(mine, rank, -1)
        low = local & (LOW - 1)
        high = jnp.where(mine, (local >> low_bits) + 1, 0).astype(F32)
        for user in range(users):
            columns = pl.ds(user * positions, positions)
            chosen_ref[:, columns] = jnp.where(place == slot[user : user + 1], 1.0, 0.0).astype(BF16)
            digit_ref[:, columns] = jnp.where(digit == low[user : user + 1], 1.0, 0.0).astype(BF16)
            wide_ref[:, columns] = jnp.broadcast_to(high[user : user + 1], (16, positions)).astype(BF16)
        low_ref[group] = dot_nt(chosen_ref[...], digit_ref[...]).astype(BF16)
        high_ref[pl.ds(group, 1), :] = dot_nt(wide_ref[...], chosen_ref[...])[:1]
        return most

    most_ref[0] = lax.fori_loop(0, groups, one_group, jnp.float32(0)).astype(jnp.int32)


def plan_turn(home, turn, all_ids, own, capacity):
    groups, users, positions = all_ids.shape
    smem, vmem = pl.BlockSpec(memory_space=pltpu.SMEM), pl.BlockSpec(memory_space=pltpu.VMEM)
    return pl.pallas_call(
        functools.partial(plan_kernel, own),
        out_shape=[
            jax.ShapeDtypeStruct((groups, capacity, LOW), BF16),
            jax.ShapeDtypeStruct((groups, capacity), F32),
            jax.ShapeDtypeStruct((users, positions), jnp.int32),
            jax.ShapeDtypeStruct((1,), jnp.int32),
        ],
        in_specs=[smem, smem, vmem],
        out_specs=[vmem] * 3 + [smem],
        scratch_shapes=[
            pltpu.VMEM((capacity, users * positions), BF16),
            pltpu.VMEM((LOW, users * positions), BF16),
            pltpu.VMEM((16, users * positions), BF16),
            pltpu.VMEM((2 * groups * users, positions), jnp.int32),
        ],
        compiler_params=pltpu.CompilerParams(vmem_limit_bytes=PLAN_VMEM_BYTES),
        cost_estimate=pl.CostEstimate(flops=4 * 10**9, bytes_accessed=5 * 10**6, transcendentals=0),
        name="plan_turn",
    )(home, turn, all_ids)


def pack_kernel(distances, home_ref, slot_ref, grad_ref, *refs):
    *packed_refs, wide_ref, chosen_ref = refs
    users, _, positions = grad_ref.shape
    capacity = packed_refs[0].shape[1]
    padded = jnp.concatenate(
        [slot_ref[...].astype(F32), jnp.zeros((LANES - users, positions), F32)], axis=0
    )
    slots = padded.T.astype(jnp.int32)
    place = lax.broadcasted_iota(jnp.int32, (positions, capacity), 1)
    for user in range(users):
        wide_ref[:, pl.ds(user * positions, positions)] = grad_ref[user]
    for distance, packed_ref in zip(distances, packed_refs):
        first = (home_ref[0] ^ distance) * capacity
        for user in range(users):
            chosen_ref[pl.ds(user * positions, positions), :] = jnp.where(
                place == slots[:, user : user + 1] - first, 1.0, 0.0
            ).astype(BF16)
        packed_ref[...] = dot_nn(wide_ref[...], chosen_ref[...]).astype(BF16)


def pack_lists(distances, home, slot, grads, capacity):
    users, features, positions = grads.shape
    smem, vmem = pl.BlockSpec(memory_space=pltpu.SMEM), pl.BlockSpec(memory_space=pltpu.VMEM)
    return pl.pallas_call(
        functools.partial(pack_kernel, distances),
        out_shape=[jax.ShapeDtypeStruct((features, capacity), BF16)] * len(distances),
        in_specs=[smem, vmem, vmem],
        out_specs=[vmem] * len(distances),
        scratch_shapes=[
            pltpu.VMEM((features, users * positions), BF16),
            pltpu.VMEM((users * positions, capacity), BF16),
        ],
        compiler_params=pltpu.CompilerParams(vmem_limit_bytes=LIST_VMEM_BYTES),
        cost_estimate=pl.CostEstimate(
            flops=len(distances) * 8 * 10**8, bytes_accessed=10**6, transcendentals=0
        ),
        name="pack_lists",
    )(home, slot, grads)


def scatter_kernel(groups, stack, low_ref, high_ref, *refs):
    list_refs, (*before_ref, out_ref, spread_ref) = refs[:groups], refs[groups:]
    features, capacity = list_refs[0].shape
    step = pl.program_id(0)
    for group, list_ref in enumerate(list_refs):
        high = high_ref[pl.ds(group, 1), :]
        for part in range(stack):
            wanted = (step * stack + part + 1).astype(F32)
            chosen = jnp.where(high == wanted, 1.0, 0.0).astype(BF16)
            spread_ref[pl.ds(part * features, features), pl.ds(group * capacity, capacity)] = (
                list_ref[...] * chosen
            )
    sums = dot_nn(spread_ref[...], low_ref[...])
    for part in range(stack):
        columns = pl.ds(part * LOW, LOW)
        term = sums[part * features : (part + 1) * features]
        out_ref[:, columns] = term + before_ref[0][:, columns] if before_ref else term


def scatter_slots(low, high, lists, own, before=None):
    groups = len(lists)
    features, capacity = lists[0].shape
    low = low.reshape(groups * capacity, LOW)
    stack = min(STACK, own // LOW)
    block = pl.BlockSpec((features, stack * LOW), lambda i: (0, i))
    extra = [] if before is None else [before]
    return pl.pallas_call(
        functools.partial(scatter_kernel, groups, stack),
        grid=(own // (LOW * stack),),
        out_shape=jax.ShapeDtypeStruct((features, own), F32),
        in_specs=[
            pl.BlockSpec((groups * capacity, LOW), lambda i: (0, 0)),
            pl.BlockSpec(high.shape, lambda i: (0, 0)),
        ]
        + [pl.BlockSpec((features, capacity), lambda i: (0, 0))] * groups
        + [block] * len(extra),
        out_specs=block,
        scratch_shapes=[pltpu.VMEM((stack * features, groups * capacity), BF16)],
        input_output_aliases={2 + groups: 0} if extra else {},
        compiler_params=pltpu.CompilerParams(vmem_limit_bytes=LIST_VMEM_BYTES),
        cost_estimate=pl.CostEstimate(flops=3 * 10**9, bytes_accessed=10**6, transcendentals=0),
        name="scatter_slots",
    )(low, high, *lists, *extra)


def swap(value, axis, distance):
    size = lax.axis_size(axis)
    return lax.ppermute(value, axis, [(i, i ^ distance) for i in range(size)])


def send_lists(home, slot, grads, owners, capacity):
    lists = [None] * owners
    for distances in ((owners - 1,), tuple(range(1, owners - 1)), (0,)):
        made = pack_lists(distances, home, slot, grads, capacity)
        slot, made = lax.optimization_barrier((slot, made))
        for distance, one_list in zip(distances, made):
            lists[distance] = swap(one_list, "dp", distance) if distance else one_list
    return lists


def exchange(value, axis):
    return lax.all_to_all(value, axis, split_axis=0, concat_axis=0, tiled=True)


def on_device(item_ids, user_len, emb_table, cotangent, w_uvqk, w_out, gain_in, gain_mid):
    dp_size = lax.axis_size("dp")
    table_size = lax.axis_size("table")
    users = user_len.shape[0]
    features, vocab = emb_table.shape
    rows = item_ids.shape[0]
    positions = rows // users
    own = vocab // dp_size
    capacity = -(-(rows // dp_size * 5 // 4) // LANES) * LANES
    assert users == table_size and users <= LANES and positions <= 256 and own // LOW <= 255
    assert dp_size & (dp_size - 1) == 0 and users & (users - 1) == 0 and own & (own - 1) == 0
    me = lax.axis_index("table").astype(jnp.int32).reshape(1)
    home = lax.axis_index("dp").astype(jnp.int32).reshape(1)

    send, valid_ids = gather_columns(item_ids, user_len, cotangent, emb_table)
    received = exchange(send, "table")
    all_ids = jnp.stack([valid_ids] + [swap(valid_ids, "dp", k) for k in range(1, dp_size)])
    out_cols, grad_cols = run_layer(me, user_len, received, w_uvqk, w_out, gain_in, gain_mid)
    per_peer = (table_size, features, positions)
    all_ids, grad_cols = lax.optimization_barrier((all_ids, grad_cols))
    plan = plan_turn(home, jnp.zeros((1,), jnp.int32), all_ids, own, capacity)
    grad_home = exchange(grad_cols.reshape(per_peer), "table")
    out_cols, grad_home, plan = lax.optimization_barrier((out_cols, grad_home, plan))
    out_home = exchange(out_cols.reshape(per_peer), "table")
    low, high, slot, most = plan
    lists = send_lists(home, slot, grad_home, dp_size, capacity)
    layer_out = jnp.transpose(out_home, (1, 0, 2)).reshape(features, rows)
    layer_out, lists = lax.optimization_barrier((layer_out, lists))
    table_grad = scatter_slots(low, high, lists, own)

    turns = (most[0] + capacity - 1) // capacity

    def another(state):
        turn, sums = state
        more_low, more_high, more_slot, _ = plan_turn(home, turn.reshape(1), all_ids, own, capacity)
        more_lists = send_lists(home, more_slot, grad_home, dp_size, capacity)
        return turn + 1, scatter_slots(more_low, more_high, more_lists, own, sums)

    _, table_grad = lax.while_loop(
        lambda state: state[0] < turns, another, (jnp.int32(1), table_grad)
    )
    return (layer_out, table_grad)


def solution(mesh):
    return jax.shard_map(
        on_device,
        mesh=mesh,
        in_specs=(P("dp"), P("dp"), P("table", None), P("table", "dp"), P(), P(), P(), P()),
        out_specs=(P("table", "dp"), P("table", "dp")),
        check_vma=False,
    )
```

```python
import functools

import jax
import jax.numpy as jnp
from jax import lax
from jax.experimental import pallas as pl
from jax.experimental.pallas import tpu as pltpu
from jax.sharding import PartitionSpec as P

HEADS = 8
NORM_EPS = 1e-05
LANES = 128
WHOLE_VMEM_BYTES = 61 * 1024 * 1024
LAYER_VMEM_BYTES = 20 * 1024 * 1024
PLAN_VMEM_BYTES = 16 * 1024 * 1024
LIST_VMEM_BYTES = 24 * 1024 * 1024

F32 = jnp.float32
BF16 = jnp.bfloat16


def dot_nn(left, right):
    return jnp.dot(left, right, preferred_element_type=F32)


def dot_nt(left, right):
    return lax.dot_general(left, right, (((1,), (1,)), ((), ())), preferred_element_type=F32)


def dot_tn(left, right):
    return lax.dot_general(left, right, (((0,), (0,)), ((), ())), preferred_element_type=F32)


BLOCK = 256
UNROLL = 64
AT_ONCE = 16
CHUNKS = 4


def gather_kernel(
    len_ref,
    ids_ref,
    cot_hbm_ref,
    table_hbm_ref,
    out_ref,
    valid_ref,
    table_ref,
    cot_ref,
    rows_ref,
    picked_ref,
    turned_ref,
    row_vector_ref,
    row_ref,
    chunk_sems,
    row_sem,
    out_sems,
    cot_sems,
    cot_sem,
):
    users, _, positions = out_ref.shape
    features, vocab = table_hbm_ref.shape
    pack = LANES // features
    span = BLOCK * pack
    block_bits = BLOCK.bit_length() - 1

    def chunk_copy(chunk):
        columns = pl.ds(chunk * (vocab // CHUNKS), vocab // CHUNKS)
        return pltpu.make_async_copy(
            table_hbm_ref.at[:, columns], table_ref.at[:, columns], chunk_sems.at[chunk]
        )

    def cot_out_copy(user):
        return pltpu.make_async_copy(
            cot_ref.at[:, pl.ds(user * positions, positions)],
            out_ref.at[user, pl.ds(features, features), :],
            cot_sems.at[user],
        )

    def out_copy(user):
        return pltpu.make_async_copy(
            turned_ref.at[user], out_ref.at[user, pl.ds(0, features), :], out_sems.at[user]
        )

    for chunk in range(CHUNKS):
        chunk_copy(chunk).start()
    cot_copy = pltpu.make_async_copy(cot_hbm_ref, cot_ref, cot_sem)
    cot_copy.start()
    items = ids_ref[...]
    row_vector_ref[...] = ((items >> (span.bit_length() - 1)) << block_bits) | (items & (BLOCK - 1))
    row_copy = pltpu.make_async_copy(row_vector_ref, row_ref, row_sem)
    row_copy.start()
    order = lax.broadcasted_iota(jnp.int32, (1, positions), 1)
    for user in range(users):
        own_items = ids_ref[pl.ds(user * positions, positions)].reshape(1, positions)
        valid_ref[pl.ds(user, 1), :] = jnp.where(order < len_ref[user], own_items, vocab)

    parts = vocab // span
    for part in range(parts):
        if part % (parts // CHUNKS) == 0:
            chunk_copy(part // (parts // CHUNKS)).wait()
        stack = jnp.concatenate(
            [
                table_ref[:, part * span + s * BLOCK : part * span + (s + 1) * BLOCK]
                for s in range(pack)
            ],
            axis=0,
        )
        rows_ref[pl.ds(part * BLOCK, BLOCK), :] = stack.T.astype(F32)
    cot_copy.wait()
    for user in range(users):
        cot_out_copy(user).start()
    row_copy.wait()

    def some(part, carry):
        start = pl.multiple_of(part * UNROLL, UNROLL)
        for first in range(0, UNROLL, AT_ONCE):
            slots = range(first, first + AT_ONCE)
            rows = [rows_ref[pl.ds(row_ref[start + slot], 1), :] for slot in slots]
            for slot, row in zip(slots, rows):
                picked_ref[pl.ds(start + slot, 1), :] = row
        return carry

    lax.fori_loop(0, users * positions // UNROLL, some, 0)
    row = lax.broadcasted_iota(jnp.int32, (LANES, LANES), 0)
    column = lax.broadcasted_iota(jnp.int32, (LANES, LANES), 1)
    same = jnp.where(row == column, 1.0, 0.0).astype(BF16)
    for user in range(users):
        places = pl.ds(user * positions, positions)
        turned = dot_nt(same, picked_ref[places, :].astype(BF16))
        own_items = ids_ref[places].reshape(1, positions)
        group = (own_items >> block_bits) & (pack - 1)
        total = turned[:features]
        for s in range(1, pack):
            total = jnp.where(group == s, turned[s * features : (s + 1) * features], total)
        turned_ref[user] = total.astype(BF16)
        out_copy(user).start()
    for user in range(users):
        cot_out_copy(user).wait()
        out_copy(user).wait()


def gather_columns(item_ids, lengths, cotangent, table):
    users = lengths.shape[0]
    rows = item_ids.shape[0]
    positions = rows // users
    features, vocab = table.shape
    pack = LANES // features
    shape = (users, 2 * features, positions)
    hbm = pl.BlockSpec(memory_space=pltpu.HBM)
    vmem = pl.BlockSpec(memory_space=pltpu.VMEM)
    return pl.pallas_call(
        gather_kernel,
        out_shape=[
            jax.ShapeDtypeStruct(shape, table.dtype),
            jax.ShapeDtypeStruct((users, positions), jnp.int32),
        ],
        in_specs=[pl.BlockSpec(memory_space=pltpu.SMEM), vmem, hbm, hbm],
        out_specs=[hbm, vmem],
        scratch_shapes=[
            pltpu.VMEM((features, vocab), table.dtype),
            pltpu.VMEM((features, rows), table.dtype),
            pltpu.VMEM((vocab // pack, LANES), F32),
            pltpu.VMEM((rows, LANES), F32),
            pltpu.VMEM((users, features, positions), table.dtype),
            pltpu.VMEM((rows,), jnp.int32),
            pltpu.SMEM((rows,), jnp.int32),
            pltpu.SemaphoreType.DMA((CHUNKS,)),
            pltpu.SemaphoreType.DMA,
            pltpu.SemaphoreType.DMA((users,)),
            pltpu.SemaphoreType.DMA((users,)),
            pltpu.SemaphoreType.DMA,
        ],
        compiler_params=pltpu.CompilerParams(vmem_limit_bytes=WHOLE_VMEM_BYTES),
        cost_estimate=pl.CostEstimate(flops=8 * 10**9, bytes_accessed=5 * 10**6, transcendentals=0),
        name="gather_columns",
    )(lengths, item_ids, cotangent, table)


def norm_forward(values):
    centred = values - jnp.mean(values, axis=0, keepdims=True)
    inverse = lax.rsqrt(jnp.mean(centred * centred, axis=0, keepdims=True) + NORM_EPS)
    return centred * inverse, inverse


def norm_backward(grad, normal, inverse):
    shift = jnp.mean(grad, axis=0, keepdims=True)
    slope = jnp.mean(grad * normal, axis=0, keepdims=True)
    return (grad - shift - normal * slope) * inverse


def silu_pair(half):
    turn = jnp.tanh(half)
    twice = 1.0 + turn
    value = half * twice
    return value, twice + value * (1.0 - turn)


def layer_kernel(
    me_ref,
    len_ref,
    recv_ref,
    w_in_ref,
    w_out_ref,
    gain_in_row_ref,
    gain_mid_row_ref,
    out_hbm_ref,
    grad_hbm_ref,
    out_ref,
    grad_ref,
    proj_ref,
    slope_ref,
    weight_ref,
    score_slope_ref,
    att_ref,
    dproj_ref,
    gain_in_ref,
    gain_mid_ref,
    share_ref,
    sems,
):
    peers, both, positions = recv_ref.shape
    features = both // 2
    width = peers * features
    head_dim = width // HEADS
    half = positions // 2

    out_copy = pltpu.make_async_copy(out_ref, out_hbm_ref, sems.at[0])
    grad_copy = pltpu.make_async_copy(grad_ref, grad_hbm_ref, sems.at[1])
    length = len_ref[me_ref[0]]
    share = 1.0 / length.astype(F32)
    for row_ref, column_ref in ((gain_in_row_ref, gain_in_ref), (gain_mid_row_ref, gain_mid_ref)):
        row = row_ref[...].reshape(1, width)
        tile = jnp.broadcast_to(row, (LANES, width)).T
        column_ref[...] = jnp.concatenate([tile] * (positions // LANES), axis=1)

    key = lax.broadcasted_iota(jnp.int32, (positions, positions), 0)
    query = lax.broadcasted_iota(jnp.int32, (positions, positions), 1)
    share_ref[...] = jnp.where((key <= query) & (key < length), share, 0.0)

    def joined(kind):
        rows = pl.ds(kind * features, features)
        return jnp.concatenate([recv_ref[peer, rows, :] for peer in range(peers)], axis=0)

    embedded = joined(0).astype(F32)
    normal_in, inverse_in = norm_forward(embedded)
    normed = (normal_in * gain_in_ref[...]).astype(BF16)

    def project(part):
        return dot_nn(w_in_ref[:, pl.ds(part * width, width)].T, normed)

    def store_projected(part, z):
        rows = pl.ds(part * width, width)
        value, slope = silu_pair(0.5 * z)
        proj_ref[rows, :] = value.astype(BF16)
        slope_ref[rows, :] = slope

    waiting = None
    for part in (2, 3, 1, 0):
        z = project(part)
        if waiting is not None:
            store_projected(*waiting)
        waiting = (part, z)
    store_projected(*waiting)

    starts = (0, half)
    scale = head_dim ** (-0.5)

    def head_rows(kind, head):
        return pl.ds(kind * width + head * head_dim, head_dim)

    def score(head):
        queries, keys = proj_ref[head_rows(2, head), :], proj_ref[head_rows(3, head), :]
        return [dot_tn(keys[:, start : start + half], queries[:, start:]) for start in starts]

    def store_weights(head, scores):
        for start, block in zip(starts, scores):
            value, slope = silu_pair(block * (0.5 * scale))
            places = (pl.ds(start, half), pl.ds(start, positions - start))
            weight_ref[head, *places] = (value * share_ref[*places]).astype(BF16)
            score_slope_ref[head, *places] = slope * share_ref[*places]
        weight_ref[head, pl.ds(half, half), pl.ds(0, half)] = jnp.zeros((half, half), BF16)

    def attend(head):
        att_ref[pl.ds(head * head_dim, head_dim), :] = dot_nn(
            proj_ref[head_rows(1, head), :], weight_ref[head]
        )

    scores = score(0)
    for head in range(HEADS):
        following = score(head + 1) if head + 1 < HEADS else None
        store_weights(head, scores)
        if head:
            attend(head - 1)
        scores = following
    attend(HEADS - 1)

    normal_mid, inverse_mid = norm_forward(att_ref[...])
    gate_rows = proj_ref[pl.ds(0, width), :].astype(F32)
    scaled = normal_mid * gain_mid_ref[...]
    mixed = (scaled * gate_rows).astype(BF16)
    valid = lax.broadcasted_iota(jnp.int32, (width, positions), 1) < length
    cotangent = jnp.where(valid, joined(1).astype(F32), 0.0)
    d_mixed = dot_nn(w_out_ref[...], cotangent.astype(BF16))
    out_ref[...] = (embedded + dot_nn(w_out_ref[...].T, mixed)).astype(BF16)
    out_copy.start()

    dproj_ref[pl.ds(0, width), :] = (d_mixed * scaled * slope_ref[pl.ds(0, width), :]).astype(BF16)
    d_att = norm_backward(d_mixed * gate_rows * gain_mid_ref[...], normal_mid, inverse_mid)
    att_ref[...] = d_att

    def d_weights(head):
        values = proj_ref[head_rows(1, head), :]
        d_head = att_ref[pl.ds(head * head_dim, head_dim), :].astype(BF16)
        return [dot_tn(values[:, start : start + half], d_head[:, start:]) for start in starts]

    def d_scores(head, products):
        low, high = (
            (block * score_slope_ref[head, pl.ds(start, half), pl.ds(start, positions - start)]).astype(
                BF16
            )
            for start, block in zip(starts, products)
        )
        empty = jnp.zeros((half, half), BF16)
        return jnp.concatenate([low, jnp.concatenate([empty, high], axis=1)], axis=0)

    def d_project(head, d_score):
        d_head = att_ref[pl.ds(head * head_dim, head_dim), :].astype(BF16)
        queries, keys = proj_ref[head_rows(2, head), :], proj_ref[head_rows(3, head), :]
        products = (
            dot_nt(d_head, weight_ref[head]),
            dot_nn(keys, d_score) * (0.5 * scale),
            dot_nt(queries, d_score) * (0.5 * scale),
        )
        for kind, product in zip((1, 2, 3), products):
            rows = head_rows(kind, head)
            dproj_ref[rows, :] = (product * slope_ref[rows, :]).astype(BF16)

    products, before = d_weights(0), None
    for head in range(HEADS):
        following = d_weights(head + 1) if head + 1 < HEADS else None
        d_score = d_scores(head, products)
        if head:
            d_project(head - 1, before)
        products, before = following, d_score
    d_project(HEADS - 1, before)

    d_normed = dot_nn(w_in_ref[...], dproj_ref[...])
    d_embedded = norm_backward(d_normed * (0.5 * gain_in_ref[...]), normal_in, inverse_in)
    grad_ref[...] = (cotangent + d_embedded).astype(BF16)
    grad_copy.start()
    out_copy.wait()
    grad_copy.wait()


def run_layer(me, lengths, received, w_in, w_out, gain_in, gain_mid):
    peers, _, positions = received.shape
    width = w_out.shape[0]
    smem, vmem = pl.BlockSpec(memory_space=pltpu.SMEM), pl.BlockSpec(memory_space=pltpu.VMEM)
    hbm = pl.BlockSpec(memory_space=pltpu.HBM)
    shape = jax.ShapeDtypeStruct((width, positions), BF16)
    return pl.pallas_call(
        layer_kernel,
        out_shape=[shape, shape],
        in_specs=[smem, smem] + [vmem] * 5,
        out_specs=[hbm, hbm],
        scratch_shapes=[
            pltpu.VMEM((width, positions), BF16),
            pltpu.VMEM((width, positions), BF16),
            pltpu.VMEM((4 * width, positions), BF16),
            pltpu.VMEM((4 * width, positions), F32),
            pltpu.VMEM((HEADS, positions, positions), BF16),
            pltpu.VMEM((HEADS, positions, positions), F32),
            pltpu.VMEM((width, positions), F32),
            pltpu.VMEM((4 * width, positions), BF16),
            pltpu.VMEM((width, positions), F32),
            pltpu.VMEM((width, positions), F32),
            pltpu.VMEM((positions, positions), F32),
            pltpu.SemaphoreType.DMA((2,)),
        ],
        compiler_params=pltpu.CompilerParams(vmem_limit_bytes=LAYER_VMEM_BYTES),
        cost_estimate=pl.CostEstimate(flops=10**10, bytes_accessed=10**7, transcendentals=10**6),
        name="layer",
    )(
        me,
        lengths,
        received,
        w_in,
        w_out,
        gain_in,
        gain_mid,
    )


LOW = 256
STACK = 16


def ranks(member, users):
    rows, positions = member.shape
    ones = jnp.where(member, 1.0, 0.0).astype(BF16)

    def iota(shape, dimension):
        return lax.broadcasted_iota(jnp.int32, shape, dimension)

    square = (positions, positions)
    before = jnp.where(iota(square, 0) < iota(square, 1), 1.0, 0.0).astype(BF16)
    row, other = iota((rows, rows), 0), iota((rows, rows), 1)
    shift = users.bit_length() - 1
    above = (other < row) & ((other >> shift) == (row >> shift))
    earlier = dot_nn(jnp.where(above, 1.0, 0.0).astype(BF16), ones)
    return (dot_nn(ones, before) + jnp.sum(earlier, axis=1, keepdims=True)).astype(jnp.int32)


def plan_kernel(own, home_ref, turn_ref, ids_ref, low_ref, high_ref, slot_ref, most_ref, *scratch):
    chosen_ref, digit_ref, wide_ref, rank_ref = scratch
    groups, users, positions = ids_ref.shape
    capacity = low_ref.shape[1]
    home = home_ref[0]
    first = turn_ref[0] * capacity
    own_bits, low_bits = own.bit_length() - 1, LOW.bit_length() - 1

    all_items = ids_ref[...].reshape(groups * users, positions)
    sent = jnp.concatenate([ids_ref[0] >> own_bits == owner for owner in range(groups)], axis=0)
    arriving = all_items >> own_bits == home
    rank_ref[...] = ranks(jnp.concatenate([arriving, sent], axis=0), users) - first
    slot = jnp.full((users, positions), -1, jnp.int32)
    for owner in range(groups):
        rank = rank_ref[pl.ds((groups + owner) * users, users), :]
        fits = (ids_ref[0] >> own_bits == owner) & (rank >= 0) & (rank < capacity)
        slot = jnp.where(fits, rank + owner * capacity, slot)
    slot_ref[...] = slot

    digit = lax.broadcasted_iota(jnp.int32, (LOW, positions), 0)
    place = lax.broadcasted_iota(jnp.int32, (capacity, positions), 0)

    def one_group(group, most):
        items = ids_ref[group]
        for owner in range(groups):
            count = jnp.sum(jnp.where(items >> own_bits == owner, 1.0, 0.0))
            most = jnp.maximum(most, count)
        mine = items >> own_bits == home
        local = items & (own - 1)
        rank = rank_ref[pl.ds(pl.multiple_of(group * users, users), users), :]
        slot = jnp.where(mine, rank, -1)
        low = local & (LOW - 1)
        high = jnp.where(mine, (local >> low_bits) + 1, 0).astype(F32)
        for user in range(users):
            columns = pl.ds(user * positions, positions)
            chosen_ref[:, columns] = jnp.where(place == slot[user : user + 1], 1.0, 0.0).astype(BF16)
            digit_ref[:, columns] = jnp.where(digit == low[user : user + 1], 1.0, 0.0).astype(BF16)
            wide_ref[:, columns] = jnp.broadcast_to(high[user : user + 1], (16, positions)).astype(BF16)
        low_ref[group] = dot_nt(chosen_ref[...], digit_ref[...]).astype(BF16)
        high_ref[pl.ds(group, 1), :] = dot_nt(wide_ref[...], chosen_ref[...])[:1]
        return most

    most_ref[0] = lax.fori_loop(0, groups, one_group, jnp.float32(0)).astype(jnp.int32)


def plan_turn(home, turn, all_ids, own, capacity):
    groups, users, positions = all_ids.shape
    smem, vmem = pl.BlockSpec(memory_space=pltpu.SMEM), pl.BlockSpec(memory_space=pltpu.VMEM)
    return pl.pallas_call(
        functools.partial(plan_kernel, own),
        out_shape=[
            jax.ShapeDtypeStruct((groups, capacity, LOW), BF16),
            jax.ShapeDtypeStruct((groups, capacity), F32),
            jax.ShapeDtypeStruct((users, positions), jnp.int32),
            jax.ShapeDtypeStruct((1,), jnp.int32),
        ],
        in_specs=[smem, smem, vmem],
        out_specs=[vmem] * 3 + [smem],
        scratch_shapes=[
            pltpu.VMEM((capacity, users * positions), BF16),
            pltpu.VMEM((LOW, users * positions), BF16),
            pltpu.VMEM((16, users * positions), BF16),
            pltpu.VMEM((2 * groups * users, positions), jnp.int32),
        ],
        compiler_params=pltpu.CompilerParams(vmem_limit_bytes=PLAN_VMEM_BYTES),
        cost_estimate=pl.CostEstimate(flops=4 * 10**9, bytes_accessed=5 * 10**6, transcendentals=0),
        name="plan_turn",
    )(home, turn, all_ids)


def pack_kernel(distances, home_ref, slot_ref, grad_ref, *refs):
    *packed_refs, wide_ref, chosen_ref = refs
    users, _, positions = grad_ref.shape
    capacity = packed_refs[0].shape[1]
    padded = jnp.concatenate(
        [slot_ref[...].astype(F32), jnp.zeros((LANES - users, positions), F32)], axis=0
    )
    slots = padded.T.astype(jnp.int32)
    place = lax.broadcasted_iota(jnp.int32, (positions, capacity), 1)
    for user in range(users):
        wide_ref[:, pl.ds(user * positions, positions)] = grad_ref[user]
    for distance, packed_ref in zip(distances, packed_refs):
        first = (home_ref[0] ^ distance) * capacity
        for user in range(users):
            chosen_ref[pl.ds(user * positions, positions), :] = jnp.where(
                place == slots[:, user : user + 1] - first, 1.0, 0.0
            ).astype(BF16)
        packed_ref[...] = dot_nn(wide_ref[...], chosen_ref[...]).astype(BF16)


def pack_lists(distances, home, slot, grads, capacity):
    users, features, positions = grads.shape
    smem, vmem = pl.BlockSpec(memory_space=pltpu.SMEM), pl.BlockSpec(memory_space=pltpu.VMEM)
    return pl.pallas_call(
        functools.partial(pack_kernel, distances),
        out_shape=[jax.ShapeDtypeStruct((features, capacity), BF16)] * len(distances),
        in_specs=[smem, vmem, vmem],
        out_specs=[vmem] * len(distances),
        scratch_shapes=[
            pltpu.VMEM((features, users * positions), BF16),
            pltpu.VMEM((users * positions, capacity), BF16),
        ],
        compiler_params=pltpu.CompilerParams(vmem_limit_bytes=LIST_VMEM_BYTES),
        cost_estimate=pl.CostEstimate(
            flops=len(distances) * 10**8, bytes_accessed=10**5, transcendentals=0
        ),
        name="pack_lists",
    )(home, slot, grads)


def scatter_kernel(groups, stack, low_ref, high_ref, *refs):
    list_refs, (*before_ref, out_ref, spread_ref) = refs[:groups], refs[groups:]
    features, capacity = list_refs[0].shape
    step = pl.program_id(0)
    for group, list_ref in enumerate(list_refs):
        high = high_ref[pl.ds(group, 1), :]
        for part in range(stack):
            wanted = (step * stack + part + 1).astype(F32)
            chosen = jnp.where(high == wanted, 1.0, 0.0).astype(BF16)
            spread_ref[pl.ds(part * features, features), pl.ds(group * capacity, capacity)] = (
                list_ref[...] * chosen
            )
    sums = dot_nn(spread_ref[...], low_ref[...])
    for part in range(stack):
        columns = pl.ds(part * LOW, LOW)
        term = sums[part * features : (part + 1) * features]
        out_ref[:, columns] = term + before_ref[0][:, columns] if before_ref else term


def scatter_slots(low, high, lists, own, before=None):
    groups = len(lists)
    features, capacity = lists[0].shape
    low = low.reshape(groups * capacity, LOW)
    stack = min(STACK, own // LOW)
    block = pl.BlockSpec((features, stack * LOW), lambda i: (0, i))
    extra = [] if before is None else [before]
    return pl.pallas_call(
        functools.partial(scatter_kernel, groups, stack),
        grid=(own // (LOW * stack),),
        out_shape=jax.ShapeDtypeStruct((features, own), F32),
        in_specs=[
            pl.BlockSpec((groups * capacity, LOW), lambda i: (0, 0)),
            pl.BlockSpec(high.shape, lambda i: (0, 0)),
        ]
        + [pl.BlockSpec((features, capacity), lambda i: (0, 0))] * groups
        + [block] * len(extra),
        out_specs=block,
        scratch_shapes=[pltpu.VMEM((stack * features, groups * capacity), BF16)],
        input_output_aliases={2 + groups: 0} if extra else {},
        compiler_params=pltpu.CompilerParams(vmem_limit_bytes=LIST_VMEM_BYTES),
        cost_estimate=pl.CostEstimate(flops=5 * 10**8, bytes_accessed=10**5, transcendentals=0),
        name="scatter_slots",
    )(low, high, *lists, *extra)


def swap(value, axis, distance):
    size = lax.axis_size(axis)
    return lax.ppermute(value, axis, [(i, i ^ distance) for i in range(size)])


def send_lists(home, slot, grads, owners, capacity):
    lists = [None] * owners
    for distances in (tuple(reversed(range(1, owners))), (0,)):
        made = pack_lists(distances, home, slot, grads, capacity)
        slot, made = lax.optimization_barrier((slot, made))
        for distance, one_list in zip(distances, made):
            lists[distance] = swap(one_list, "dp", distance) if distance else one_list
    return lists


def exchange(value, axis):
    return lax.all_to_all(value, axis, split_axis=0, concat_axis=0, tiled=True)


def on_device(item_ids, user_len, emb_table, cotangent, w_uvqk, w_out, gain_in, gain_mid):
    dp_size = lax.axis_size("dp")
    table_size = lax.axis_size("table")
    users = user_len.shape[0]
    features, vocab = emb_table.shape
    rows = item_ids.shape[0]
    positions = rows // users
    own = vocab // dp_size
    capacity = -(-(rows // dp_size * 5 // 4) // LANES) * LANES
    assert users == table_size and users <= LANES and positions <= 256 and own // LOW <= 255
    assert dp_size & (dp_size - 1) == 0 and users & (users - 1) == 0 and own & (own - 1) == 0
    me = lax.axis_index("table").astype(jnp.int32).reshape(1)
    home = lax.axis_index("dp").astype(jnp.int32).reshape(1)

    send, valid_ids = gather_columns(item_ids, user_len, cotangent, emb_table)
    received = exchange(send, "table")
    all_ids = jnp.stack([valid_ids] + [swap(valid_ids, "dp", k) for k in range(1, dp_size)])
    out_cols, grad_cols = run_layer(me, user_len, received, w_uvqk, w_out, gain_in, gain_mid)
    per_peer = (table_size, features, positions)
    all_ids, grad_cols = lax.optimization_barrier((all_ids, grad_cols))
    plan = plan_turn(home, jnp.zeros((1,), jnp.int32), all_ids, own, capacity)
    grad_home = exchange(grad_cols.reshape(per_peer), "table")
    out_cols, plan = lax.optimization_barrier((out_cols, plan))
    out_home = exchange(out_cols.reshape(per_peer), "table")
    low, high, slot, most = plan
    lists = send_lists(home, slot, grad_home, dp_size, capacity)
    layer_out = jnp.transpose(out_home, (1, 0, 2)).reshape(features, rows)
    layer_out, lists = lax.optimization_barrier((layer_out, lists))
    table_grad = scatter_slots(low, high, lists, own)

    turns = (most[0] + capacity - 1) // capacity

    def another(state):
        turn, sums = state
        more_low, more_high, more_slot, _ = plan_turn(home, turn.reshape(1), all_ids, own, capacity)
        more_lists = send_lists(home, more_slot, grad_home, dp_size, capacity)
        return turn + 1, scatter_slots(more_low, more_high, more_lists, own, sums)

    _, table_grad = lax.while_loop(
        lambda state: state[0] < turns, another, (jnp.int32(1), table_grad)
    )
    return (layer_out, table_grad)


def solution(mesh):
    return jax.shard_map(
        on_device,
        mesh=mesh,
        in_specs=(P("dp"), P("dp"), P("table", None), P("table", "dp"), P(), P(), P(), P()),
        out_specs=(P("table", "dp"), P("table", "dp")),
        check_vma=False,
    )
```

```python
import functools

import jax
import jax.numpy as jnp
from jax import lax
from jax.experimental import pallas as pl
from jax.experimental.pallas import tpu as pltpu
from jax.sharding import PartitionSpec as P

HEADS = 8
NORM_EPS = 1e-05
LANES = 128
WHOLE_VMEM_BYTES = 61 * 1024 * 1024
LAYER_VMEM_BYTES = 20 * 1024 * 1024
PLAN_VMEM_BYTES = 16 * 1024 * 1024
LIST_VMEM_BYTES = 24 * 1024 * 1024

F32 = jnp.float32
BF16 = jnp.bfloat16


def dot_nn(left, right):
    return jnp.dot(left, right, preferred_element_type=F32)


def dot_nt(left, right):
    return lax.dot_general(left, right, (((1,), (1,)), ((), ())), preferred_element_type=F32)


def dot_tn(left, right):
    return lax.dot_general(left, right, (((0,), (0,)), ((), ())), preferred_element_type=F32)


BLOCK = 256
UNROLL = 128
AT_ONCE = 32
CHUNKS = 4


def gather_kernel(
    len_ref,
    ids_ref,
    cot_hbm_ref,
    table_hbm_ref,
    out_ref,
    valid_ref,
    table_ref,
    cot_ref,
    rows_ref,
    picked_ref,
    turned_ref,
    row_vector_ref,
    row_ref,
    chunk_sems,
    row_sem,
    out_sems,
    cot_sems,
    cot_sem,
):
    users, _, positions = out_ref.shape
    features, vocab = table_hbm_ref.shape
    pack = LANES // features
    span = BLOCK * pack
    block_bits = BLOCK.bit_length() - 1

    def chunk_copy(chunk):
        columns = pl.ds(chunk * (vocab // CHUNKS), vocab // CHUNKS)
        return pltpu.make_async_copy(
            table_hbm_ref.at[:, columns], table_ref.at[:, columns], chunk_sems.at[chunk]
        )

    def cot_out_copy(user):
        return pltpu.make_async_copy(
            cot_ref.at[:, pl.ds(user * positions, positions)],
            out_ref.at[user, pl.ds(features, features), :],
            cot_sems.at[user],
        )

    def out_copy(user):
        return pltpu.make_async_copy(
            turned_ref.at[user], out_ref.at[user, pl.ds(0, features), :], out_sems.at[user]
        )

    for chunk in range(CHUNKS):
        chunk_copy(chunk).start()
    cot_copy = pltpu.make_async_copy(cot_hbm_ref, cot_ref, cot_sem)
    cot_copy.start()
    items = ids_ref[...]
    row_vector_ref[...] = ((items >> (span.bit_length() - 1)) << block_bits) | (items & (BLOCK - 1))
    row_copy = pltpu.make_async_copy(row_vector_ref, row_ref, row_sem)
    row_copy.start()
    order = lax.broadcasted_iota(jnp.int32, (1, positions), 1)
    for user in range(users):
        own_items = ids_ref[pl.ds(user * positions, positions)].reshape(1, positions)
        valid_ref[pl.ds(user, 1), :] = jnp.where(order < len_ref[user], own_items, vocab)

    parts = vocab // span
    for part in range(parts):
        if part % (parts // CHUNKS) == 0:
            chunk_copy(part // (parts // CHUNKS)).wait()
        stack = jnp.concatenate(
            [
                table_ref[:, part * span + s * BLOCK : part * span + (s + 1) * BLOCK]
                for s in range(pack)
            ],
            axis=0,
        )
        rows_ref[pl.ds(part * BLOCK, BLOCK), :] = stack.T.astype(F32)
    cot_copy.wait()
    for user in range(users):
        cot_out_copy(user).start()
    row_copy.wait()

    def some(part, carry):
        start = pl.multiple_of(part * UNROLL, UNROLL)
        for first in range(0, UNROLL, AT_ONCE):
            slots = range(first, first + AT_ONCE)
            rows = [rows_ref[pl.ds(row_ref[start + slot], 1), :] for slot in slots]
            for slot, row in zip(slots, rows):
                picked_ref[pl.ds(start + slot, 1), :] = row
        return carry

    lax.fori_loop(0, users * positions // UNROLL, some, 0)
    row = lax.broadcasted_iota(jnp.int32, (LANES, LANES), 0)
    column = lax.broadcasted_iota(jnp.int32, (LANES, LANES), 1)
    same = jnp.where(row == column, 1.0, 0.0).astype(BF16)
    for user in range(users):
        places = pl.ds(user * positions, positions)
        turned = dot_nt(same, picked_ref[places, :].astype(BF16))
        own_items = ids_ref[places].reshape(1, positions)
        group = (own_items >> block_bits) & (pack - 1)
        total = turned[:features]
        for s in range(1, pack):
            total = jnp.where(group == s, turned[s * features : (s + 1) * features], total)
        turned_ref[user] = total.astype(BF16)
        out_copy(user).start()
    for user in range(users):
        cot_out_copy(user).wait()
        out_copy(user).wait()


def gather_columns(item_ids, lengths, cotangent, table):
    users = lengths.shape[0]
    rows = item_ids.shape[0]
    positions = rows // users
    features, vocab = table.shape
    pack = LANES // features
    shape = (users, 2 * features, positions)
    hbm = pl.BlockSpec(memory_space=pltpu.HBM)
    vmem = pl.BlockSpec(memory_space=pltpu.VMEM)
    return pl.pallas_call(
        gather_kernel,
        out_shape=[
            jax.ShapeDtypeStruct(shape, table.dtype),
            jax.ShapeDtypeStruct((users, positions), jnp.int32),
        ],
        in_specs=[pl.BlockSpec(memory_space=pltpu.SMEM), vmem, hbm, hbm],
        out_specs=[hbm, vmem],
        scratch_shapes=[
            pltpu.VMEM((features, vocab), table.dtype),
            pltpu.VMEM((features, rows), table.dtype),
            pltpu.VMEM((vocab // pack, LANES), F32),
            pltpu.VMEM((rows, LANES), F32),
            pltpu.VMEM((users, features, positions), table.dtype),
            pltpu.VMEM((rows,), jnp.int32),
            pltpu.SMEM((rows,), jnp.int32),
            pltpu.SemaphoreType.DMA((CHUNKS,)),
            pltpu.SemaphoreType.DMA,
            pltpu.SemaphoreType.DMA((users,)),
            pltpu.SemaphoreType.DMA((users,)),
            pltpu.SemaphoreType.DMA,
        ],
        compiler_params=pltpu.CompilerParams(vmem_limit_bytes=WHOLE_VMEM_BYTES),
        cost_estimate=pl.CostEstimate(flops=8 * 10**9, bytes_accessed=5 * 10**6, transcendentals=0),
        name="gather_columns",
    )(lengths, item_ids, cotangent, table)


def norm_forward(values):
    centred = values - jnp.mean(values, axis=0, keepdims=True)
    inverse = lax.rsqrt(jnp.mean(centred * centred, axis=0, keepdims=True) + NORM_EPS)
    return centred * inverse, inverse


def norm_backward(grad, normal, inverse):
    shift = jnp.mean(grad, axis=0, keepdims=True)
    slope = jnp.mean(grad * normal, axis=0, keepdims=True)
    return (grad - shift - normal * slope) * inverse


def silu_pair(half):
    turn = jnp.tanh(half)
    twice = 1.0 + turn
    value = half * twice
    return value, twice + value * (1.0 - turn)


def layer_kernel(
    me_ref,
    len_ref,
    recv_ref,
    w_in_ref,
    w_out_ref,
    gain_in_row_ref,
    gain_mid_row_ref,
    out_hbm_ref,
    grad_hbm_ref,
    out_ref,
    grad_ref,
    proj_ref,
    slope_ref,
    weight_ref,
    score_slope_ref,
    att_ref,
    dproj_ref,
    gain_in_ref,
    gain_mid_ref,
    share_ref,
    sems,
):
    peers, both, positions = recv_ref.shape
    features = both // 2
    width = peers * features
    head_dim = width // HEADS
    half = positions // 2

    out_copy = pltpu.make_async_copy(out_ref, out_hbm_ref, sems.at[0])
    grad_copy = pltpu.make_async_copy(grad_ref, grad_hbm_ref, sems.at[1])
    length = len_ref[me_ref[0]]
    share = 1.0 / length.astype(F32)
    for row_ref, column_ref in ((gain_in_row_ref, gain_in_ref), (gain_mid_row_ref, gain_mid_ref)):
        row = row_ref[...].reshape(1, width)
        tile = jnp.broadcast_to(row, (LANES, width)).T
        column_ref[...] = jnp.concatenate([tile] * (positions // LANES), axis=1)

    key = lax.broadcasted_iota(jnp.int32, (positions, positions), 0)
    query = lax.broadcasted_iota(jnp.int32, (positions, positions), 1)
    share_ref[...] = jnp.where((key <= query) & (key < length), share, 0.0)

    def joined(kind):
        rows = pl.ds(kind * features, features)
        return jnp.concatenate([recv_ref[peer, rows, :] for peer in range(peers)], axis=0)

    embedded = joined(0).astype(F32)
    normal_in, inverse_in = norm_forward(embedded)
    normed = (normal_in * gain_in_ref[...]).astype(BF16)

    def project(part):
        return dot_nn(w_in_ref[:, pl.ds(part * width, width)].T, normed)

    def store_projected(part, z):
        rows = pl.ds(part * width, width)
        value, slope = silu_pair(0.5 * z)
        proj_ref[rows, :] = value.astype(BF16)
        slope_ref[rows, :] = slope

    waiting = None
    for part in (2, 3, 1, 0):
        z = project(part)
        if waiting is not None:
            store_projected(*waiting)
        waiting = (part, z)
    store_projected(*waiting)

    starts = (0, half)
    scale = head_dim ** (-0.5)

    def head_rows(kind, head):
        return pl.ds(kind * width + head * head_dim, head_dim)

    def score(head):
        queries, keys = proj_ref[head_rows(2, head), :], proj_ref[head_rows(3, head), :]
        return [dot_tn(keys[:, start : start + half], queries[:, start:]) for start in starts]

    def store_weights(head, scores):
        for start, block in zip(starts, scores):
            value, slope = silu_pair(block * (0.5 * scale))
            places = (pl.ds(start, half), pl.ds(start, positions - start))
            weight_ref[head, *places] = (value * share_ref[*places]).astype(BF16)
            score_slope_ref[head, *places] = slope * share_ref[*places]
        weight_ref[head, pl.ds(half, half), pl.ds(0, half)] = jnp.zeros((half, half), BF16)

    def attend(head):
        att_ref[pl.ds(head * head_dim, head_dim), :] = dot_nn(
            proj_ref[head_rows(1, head), :], weight_ref[head]
        )

    scores = score(0)
    for head in range(HEADS):
        following = score(head + 1) if head + 1 < HEADS else None
        store_weights(head, scores)
        if head:
            attend(head - 1)
        scores = following
    attend(HEADS - 1)

    normal_mid, inverse_mid = norm_forward(att_ref[...])
    gate_rows = proj_ref[pl.ds(0, width), :].astype(F32)
    scaled = normal_mid * gain_mid_ref[...]
    mixed = (scaled * gate_rows).astype(BF16)
    valid = lax.broadcasted_iota(jnp.int32, (width, positions), 1) < length
    cotangent = jnp.where(valid, joined(1).astype(F32), 0.0)
    d_mixed = dot_nn(w_out_ref[...], cotangent.astype(BF16))
    out_ref[...] = (embedded + dot_nn(w_out_ref[...].T, mixed)).astype(BF16)
    out_copy.start()

    dproj_ref[pl.ds(0, width), :] = (d_mixed * scaled * slope_ref[pl.ds(0, width), :]).astype(BF16)
    d_att = norm_backward(d_mixed * gate_rows * gain_mid_ref[...], normal_mid, inverse_mid)
    att_ref[...] = d_att

    def d_weights(head):
        values = proj_ref[head_rows(1, head), :]
        d_head = att_ref[pl.ds(head * head_dim, head_dim), :].astype(BF16)
        return [dot_tn(values[:, start : start + half], d_head[:, start:]) for start in starts]

    def d_scores(head, products):
        low, high = (
            (block * score_slope_ref[head, pl.ds(start, half), pl.ds(start, positions - start)]).astype(
                BF16
            )
            for start, block in zip(starts, products)
        )
        empty = jnp.zeros((half, half), BF16)
        return jnp.concatenate([low, jnp.concatenate([empty, high], axis=1)], axis=0)

    def d_project(head, d_score):
        d_head = att_ref[pl.ds(head * head_dim, head_dim), :].astype(BF16)
        queries, keys = proj_ref[head_rows(2, head), :], proj_ref[head_rows(3, head), :]
        products = (
            dot_nt(d_head, weight_ref[head]),
            dot_nn(keys, d_score) * (0.5 * scale),
            dot_nt(queries, d_score) * (0.5 * scale),
        )
        for kind, product in zip((1, 2, 3), products):
            rows = head_rows(kind, head)
            dproj_ref[rows, :] = (product * slope_ref[rows, :]).astype(BF16)

    products, before = d_weights(0), None
    for head in range(HEADS):
        following = d_weights(head + 1) if head + 1 < HEADS else None
        d_score = d_scores(head, products)
        if head:
            d_project(head - 1, before)
        products, before = following, d_score
    d_project(HEADS - 1, before)

    d_normed = dot_nn(w_in_ref[...], dproj_ref[...])
    d_embedded = norm_backward(d_normed * (0.5 * gain_in_ref[...]), normal_in, inverse_in)
    grad_ref[...] = (cotangent + d_embedded).astype(BF16)
    grad_copy.start()
    out_copy.wait()
    grad_copy.wait()


def run_layer(me, lengths, received, w_in, w_out, gain_in, gain_mid):
    peers, _, positions = received.shape
    width = w_out.shape[0]
    smem, vmem = pl.BlockSpec(memory_space=pltpu.SMEM), pl.BlockSpec(memory_space=pltpu.VMEM)
    hbm = pl.BlockSpec(memory_space=pltpu.HBM)
    shape = jax.ShapeDtypeStruct((width, positions), BF16)
    return pl.pallas_call(
        layer_kernel,
        out_shape=[shape, shape],
        in_specs=[smem, smem] + [vmem] * 5,
        out_specs=[hbm, hbm],
        scratch_shapes=[
            pltpu.VMEM((width, positions), BF16),
            pltpu.VMEM((width, positions), BF16),
            pltpu.VMEM((4 * width, positions), BF16),
            pltpu.VMEM((4 * width, positions), F32),
            pltpu.VMEM((HEADS, positions, positions), BF16),
            pltpu.VMEM((HEADS, positions, positions), F32),
            pltpu.VMEM((width, positions), F32),
            pltpu.VMEM((4 * width, positions), BF16),
            pltpu.VMEM((width, positions), F32),
            pltpu.VMEM((width, positions), F32),
            pltpu.VMEM((positions, positions), F32),
            pltpu.SemaphoreType.DMA((2,)),
        ],
        compiler_params=pltpu.CompilerParams(vmem_limit_bytes=LAYER_VMEM_BYTES),
        cost_estimate=pl.CostEstimate(flops=10**10, bytes_accessed=10**7, transcendentals=10**6),
        name="layer",
    )(
        me,
        lengths,
        received,
        w_in,
        w_out,
        gain_in,
        gain_mid,
    )


LOW = 512
STACK = 8


def ranks(member, users):
    rows, positions = member.shape
    ones = jnp.where(member, 1.0, 0.0).astype(BF16)

    def iota(shape, dimension):
        return lax.broadcasted_iota(jnp.int32, shape, dimension)

    square = (positions, positions)
    before = jnp.where(iota(square, 0) < iota(square, 1), 1.0, 0.0).astype(BF16)
    row, other = iota((rows, rows), 0), iota((rows, rows), 1)
    shift = users.bit_length() - 1
    above = (other < row) & ((other >> shift) == (row >> shift))
    earlier = dot_nn(jnp.where(above, 1.0, 0.0).astype(BF16), ones)
    return (dot_nn(ones, before) + jnp.sum(earlier, axis=1, keepdims=True)).astype(jnp.int32)


def plan_kernel(own, home_ref, turn_ref, ids_ref, low_ref, high_ref, slot_ref, most_ref, *scratch):
    chosen_ref, digit_ref, wide_ref, rank_ref = scratch
    groups, users, positions = ids_ref.shape
    capacity = low_ref.shape[1]
    home = home_ref[0]
    first = turn_ref[0] * capacity
    own_bits, low_bits = own.bit_length() - 1, LOW.bit_length() - 1

    all_items = ids_ref[...].reshape(groups * users, positions)
    sent = jnp.concatenate([ids_ref[0] >> own_bits == owner for owner in range(groups)], axis=0)
    arriving = all_items >> own_bits == home
    rank_ref[...] = ranks(jnp.concatenate([arriving, sent], axis=0), users) - first
    slot = jnp.full((users, positions), -1, jnp.int32)
    for owner in range(groups):
        rank = rank_ref[pl.ds((groups + owner) * users, users), :]
        fits = (ids_ref[0] >> own_bits == owner) & (rank >= 0) & (rank < capacity)
        slot = jnp.where(fits, rank + owner * capacity, slot)
    slot_ref[...] = slot

    digit = lax.broadcasted_iota(jnp.int32, (LOW, positions), 0)
    place = lax.broadcasted_iota(jnp.int32, (capacity, positions), 0)

    def one_group(group, most):
        items = ids_ref[group]
        for owner in range(groups):
            count = jnp.sum(jnp.where(items >> own_bits == owner, 1.0, 0.0))
            most = jnp.maximum(most, count)
        mine = items >> own_bits == home
        local = items & (own - 1)
        rank = rank_ref[pl.ds(pl.multiple_of(group * users, users), users), :]
        slot = jnp.where(mine, rank, -1)
        low = local & (LOW - 1)
        high = jnp.where(mine, (local >> low_bits) + 1, 0).astype(F32)
        for user in range(users):
            columns = pl.ds(user * positions, positions)
            chosen_ref[:, columns] = jnp.where(place == slot[user : user + 1], 1.0, 0.0).astype(BF16)
            digit_ref[:, columns] = jnp.where(digit == low[user : user + 1], 1.0, 0.0).astype(BF16)
            wide_ref[:, columns] = jnp.broadcast_to(high[user : user + 1], (16, positions)).astype(BF16)
        low_ref[group] = dot_nt(chosen_ref[...], digit_ref[...]).astype(BF16)
        high_ref[pl.ds(group, 1), :] = dot_nt(wide_ref[...], chosen_ref[...])[:1]
        return most

    most_ref[0] = lax.fori_loop(0, groups, one_group, jnp.float32(0)).astype(jnp.int32)


def plan_turn(home, turn, all_ids, own, capacity):
    groups, users, positions = all_ids.shape
    smem, vmem = pl.BlockSpec(memory_space=pltpu.SMEM), pl.BlockSpec(memory_space=pltpu.VMEM)
    return pl.pallas_call(
        functools.partial(plan_kernel, own),
        out_shape=[
            jax.ShapeDtypeStruct((groups, capacity, LOW), BF16),
            jax.ShapeDtypeStruct((groups, capacity), F32),
            jax.ShapeDtypeStruct((users, positions), jnp.int32),
            jax.ShapeDtypeStruct((1,), jnp.int32),
        ],
        in_specs=[smem, smem, vmem],
        out_specs=[vmem] * 3 + [smem],
        scratch_shapes=[
            pltpu.VMEM((capacity, users * positions), BF16),
            pltpu.VMEM((LOW, users * positions), BF16),
            pltpu.VMEM((16, users * positions), BF16),
            pltpu.VMEM((2 * groups * users, positions), jnp.int32),
        ],
        compiler_params=pltpu.CompilerParams(vmem_limit_bytes=PLAN_VMEM_BYTES),
        cost_estimate=pl.CostEstimate(flops=4 * 10**9, bytes_accessed=5 * 10**6, transcendentals=0),
        name="plan_turn",
    )(home, turn, all_ids)


def pack_kernel(distances, home_ref, slot_ref, grad_ref, *refs):
    *packed_refs, wide_ref, chosen_ref = refs
    users, _, positions = grad_ref.shape
    capacity = packed_refs[0].shape[1]
    padded = jnp.concatenate(
        [slot_ref[...].astype(F32), jnp.zeros((LANES - users, positions), F32)], axis=0
    )
    slots = padded.T.astype(jnp.int32)
    place = lax.broadcasted_iota(jnp.int32, (positions, capacity), 1)
    for user in range(users):
        wide_ref[:, pl.ds(user * positions, positions)] = grad_ref[user]
    for distance, packed_ref in zip(distances, packed_refs):
        first = (home_ref[0] ^ distance) * capacity
        for user in range(users):
            chosen_ref[pl.ds(user * positions, positions), :] = jnp.where(
                place == slots[:, user : user + 1] - first, 1.0, 0.0
            ).astype(BF16)
        packed_ref[...] = dot_nn(wide_ref[...], chosen_ref[...]).astype(BF16)


def pack_lists(distances, home, slot, grads, capacity):
    users, features, positions = grads.shape
    smem, vmem = pl.BlockSpec(memory_space=pltpu.SMEM), pl.BlockSpec(memory_space=pltpu.VMEM)
    return pl.pallas_call(
        functools.partial(pack_kernel, distances),
        out_shape=[jax.ShapeDtypeStruct((features, capacity), BF16)] * len(distances),
        in_specs=[smem, vmem, vmem],
        out_specs=[vmem] * len(distances),
        scratch_shapes=[
            pltpu.VMEM((features, users * positions), BF16),
            pltpu.VMEM((users * positions, capacity), BF16),
        ],
        compiler_params=pltpu.CompilerParams(vmem_limit_bytes=LIST_VMEM_BYTES),
        cost_estimate=pl.CostEstimate(
            flops=len(distances) * 8 * 10**8, bytes_accessed=10**6, transcendentals=0
        ),
        name="pack_lists",
    )(home, slot, grads)


def scatter_kernel(groups, stack, low_ref, high_ref, *refs):
    list_refs, (*before_ref, out_ref, spread_ref) = refs[:groups], refs[groups:]
    features, capacity = list_refs[0].shape
    step = pl.program_id(0)
    for group, list_ref in enumerate(list_refs):
        high = high_ref[pl.ds(group, 1), :]
        for part in range(stack):
            wanted = (step * stack + part + 1).astype(F32)
            chosen = jnp.where(high == wanted, 1.0, 0.0).astype(BF16)
            spread_ref[pl.ds(part * features, features), pl.ds(group * capacity, capacity)] = (
                list_ref[...] * chosen
            )
    sums = dot_nn(spread_ref[...], low_ref[...])
    for part in range(stack):
        columns = pl.ds(part * LOW, LOW)
        term = sums[part * features : (part + 1) * features]
        out_ref[:, columns] = term + before_ref[0][:, columns] if before_ref else term


def scatter_slots(low, high, lists, own, before=None):
    groups = len(lists)
    features, capacity = lists[0].shape
    low = low.reshape(groups * capacity, LOW)
    stack = min(STACK, own // LOW)
    block = pl.BlockSpec((features, stack * LOW), lambda i: (0, i))
    extra = [] if before is None else [before]
    return pl.pallas_call(
        functools.partial(scatter_kernel, groups, stack),
        grid=(own // (LOW * stack),),
        out_shape=jax.ShapeDtypeStruct((features, own), F32),
        in_specs=[
            pl.BlockSpec((groups * capacity, LOW), lambda i: (0, 0)),
            pl.BlockSpec(high.shape, lambda i: (0, 0)),
        ]
        + [pl.BlockSpec((features, capacity), lambda i: (0, 0))] * groups
        + [block] * len(extra),
        out_specs=block,
        scratch_shapes=[pltpu.VMEM((stack * features, groups * capacity), BF16)],
        input_output_aliases={2 + groups: 0} if extra else {},
        compiler_params=pltpu.CompilerParams(vmem_limit_bytes=LIST_VMEM_BYTES),
        cost_estimate=pl.CostEstimate(flops=3 * 10**9, bytes_accessed=10**6, transcendentals=0),
        name="scatter_slots",
    )(low, high, *lists, *extra)


def swap(value, axis, distance):
    size = lax.axis_size(axis)
    return lax.ppermute(value, axis, [(i, i ^ distance) for i in range(size)])


def send_lists(home, slot, grads, owners, capacity):
    lists = [None] * owners
    for distances in (tuple(reversed(range(1, owners))), (0,)):
        made = pack_lists(distances, home, slot, grads, capacity)
        slot, made = lax.optimization_barrier((slot, made))
        for distance, one_list in zip(distances, made):
            lists[distance] = swap(one_list, "dp", distance) if distance else one_list
    return lists


def exchange(value, axis):
    return lax.all_to_all(value, axis, split_axis=0, concat_axis=0, tiled=True)


def on_device(item_ids, user_len, emb_table, cotangent, w_uvqk, w_out, gain_in, gain_mid):
    dp_size = lax.axis_size("dp")
    table_size = lax.axis_size("table")
    users = user_len.shape[0]
    features, vocab = emb_table.shape
    rows = item_ids.shape[0]
    positions = rows // users
    own = vocab // dp_size
    capacity = -(-(rows // dp_size * 5 // 4) // LANES) * LANES
    assert users == table_size and users <= LANES and positions <= 256 and own // LOW <= 255
    assert dp_size & (dp_size - 1) == 0 and users & (users - 1) == 0 and own & (own - 1) == 0
    me = lax.axis_index("table").astype(jnp.int32).reshape(1)
    home = lax.axis_index("dp").astype(jnp.int32).reshape(1)

    send, valid_ids = gather_columns(item_ids, user_len, cotangent, emb_table)
    received = exchange(send, "table")
    all_ids = jnp.stack([valid_ids] + [swap(valid_ids, "dp", k) for k in range(1, dp_size)])
    out_cols, grad_cols = run_layer(me, user_len, received, w_uvqk, w_out, gain_in, gain_mid)
    per_peer = (table_size, features, positions)
    all_ids, grad_cols = lax.optimization_barrier((all_ids, grad_cols))
    plan = plan_turn(home, jnp.zeros((1,), jnp.int32), all_ids, own, capacity)
    grad_home = exchange(grad_cols.reshape(per_peer), "table")
    out_cols, grad_home, plan = lax.optimization_barrier((out_cols, grad_home, plan))
    out_home = exchange(out_cols.reshape(per_peer), "table")
    low, high, slot, most = plan
    lists = send_lists(home, slot, grad_home, dp_size, capacity)
    own_list, out_home = lax.optimization_barrier((lists[0], out_home))
    lists = [own_list] + lists[1:]
    layer_out = jnp.transpose(out_home, (1, 0, 2)).reshape(features, rows)
    layer_out, lists = lax.optimization_barrier((layer_out, lists))
    table_grad = scatter_slots(low, high, lists, own)

    turns = (most[0] + capacity - 1) // capacity

    def another(state):
        turn, sums = state
        more_low, more_high, more_slot, _ = plan_turn(home, turn.reshape(1), all_ids, own, capacity)
        more_lists = send_lists(home, more_slot, grad_home, dp_size, capacity)
        return turn + 1, scatter_slots(more_low, more_high, more_lists, own, sums)

    _, table_grad = lax.while_loop(
        lambda state: state[0] < turns, another, (jnp.int32(1), table_grad)
    )
    return (layer_out, table_grad)


def solution(mesh):
    return jax.shard_map(
        on_device,
        mesh=mesh,
        in_specs=(P("dp"), P("dp"), P("table", None), P("table", "dp"), P(), P(), P(), P()),
        out_specs=(P("table", "dp"), P("table", "dp")),
        check_vma=False,
    )
```

```python
import functools

import jax
import jax.numpy as jnp
from jax import lax
from jax.experimental import pallas as pl
from jax.experimental.pallas import tpu as pltpu
from jax.sharding import PartitionSpec as P

HEADS = 8
NORM_EPS = 1e-05
LANES = 128
WHOLE_VMEM_BYTES = 61 * 1024 * 1024
LAYER_VMEM_BYTES = 20 * 1024 * 1024
PLAN_VMEM_BYTES = 16 * 1024 * 1024
LIST_VMEM_BYTES = 24 * 1024 * 1024

F32 = jnp.float32
BF16 = jnp.bfloat16


def dot_nn(left, right):
    return jnp.dot(left, right, preferred_element_type=F32)


def dot_nt(left, right):
    return lax.dot_general(left, right, (((1,), (1,)), ((), ())), preferred_element_type=F32)


def dot_tn(left, right):
    return lax.dot_general(left, right, (((0,), (0,)), ((), ())), preferred_element_type=F32)


BLOCK = 256
UNROLL = 128
AT_ONCE = 32
CHUNKS = 4


def gather_kernel(
    len_ref,
    ids_ref,
    cot_hbm_ref,
    table_hbm_ref,
    out_ref,
    valid_ref,
    table_ref,
    cot_ref,
    rows_ref,
    picked_ref,
    turned_ref,
    row_vector_ref,
    row_ref,
    chunk_sems,
    row_sem,
    out_sems,
    cot_sems,
    cot_sem,
):
    users, _, positions = out_ref.shape
    features, vocab = table_hbm_ref.shape
    pack = LANES // features
    span = BLOCK * pack
    block_bits = BLOCK.bit_length() - 1

    def chunk_copy(chunk):
        columns = pl.ds(chunk * (vocab // CHUNKS), vocab // CHUNKS)
        return pltpu.make_async_copy(
            table_hbm_ref.at[:, columns], table_ref.at[:, columns], chunk_sems.at[chunk]
        )

    def cot_out_copy(user):
        return pltpu.make_async_copy(
            cot_ref.at[:, pl.ds(user * positions, positions)],
            out_ref.at[user, pl.ds(features, features), :],
            cot_sems.at[user],
        )

    def out_copy(user):
        return pltpu.make_async_copy(
            turned_ref.at[user], out_ref.at[user, pl.ds(0, features), :], out_sems.at[user]
        )

    for chunk in range(CHUNKS):
        chunk_copy(chunk).start()
    cot_copy = pltpu.make_async_copy(cot_hbm_ref, cot_ref, cot_sem)
    cot_copy.start()
    items = ids_ref[...]
    row_vector_ref[...] = ((items >> (span.bit_length() - 1)) << block_bits) | (items & (BLOCK - 1))
    row_copy = pltpu.make_async_copy(row_vector_ref, row_ref, row_sem)
    row_copy.start()
    order = lax.broadcasted_iota(jnp.int32, (1, positions), 1)
    for user in range(users):
        own_items = ids_ref[pl.ds(user * positions, positions)].reshape(1, positions)
        valid_ref[pl.ds(user, 1), :] = jnp.where(order < len_ref[user], own_items, vocab)

    parts = vocab // span
    for part in range(parts):
        if part % (parts // CHUNKS) == 0:
            chunk_copy(part // (parts // CHUNKS)).wait()
        stack = jnp.concatenate(
            [
                table_ref[:, part * span + s * BLOCK : part * span + (s + 1) * BLOCK]
                for s in range(pack)
            ],
            axis=0,
        )
        rows_ref[pl.ds(part * BLOCK, BLOCK), :] = stack.T.astype(F32)
    cot_copy.wait()
    for user in range(users):
        cot_out_copy(user).start()
    row_copy.wait()

    def some(part, carry):
        start = pl.multiple_of(part * UNROLL, UNROLL)
        for first in range(0, UNROLL, AT_ONCE):
            slots = range(first, first + AT_ONCE)
            rows = [rows_ref[pl.ds(row_ref[start + slot], 1), :] for slot in slots]
            for slot, row in zip(slots, rows):
                picked_ref[pl.ds(start + slot, 1), :] = row
        return carry

    lax.fori_loop(0, users * positions // UNROLL, some, 0)
    row = lax.broadcasted_iota(jnp.int32, (LANES, LANES), 0)
    column = lax.broadcasted_iota(jnp.int32, (LANES, LANES), 1)
    same = jnp.where(row == column, 1.0, 0.0).astype(BF16)
    for user in range(users):
        places = pl.ds(user * positions, positions)
        turned = dot_nt(same, picked_ref[places, :].astype(BF16))
        own_items = ids_ref[places].reshape(1, positions)
        group = (own_items >> block_bits) & (pack - 1)
        total = turned[:features]
        for s in range(1, pack):
            total = jnp.where(group == s, turned[s * features : (s + 1) * features], total)
        turned_ref[user] = total.astype(BF16)
        out_copy(user).start()
    for user in range(users):
        cot_out_copy(user).wait()
        out_copy(user).wait()


def gather_columns(item_ids, lengths, cotangent, table):
    users = lengths.shape[0]
    rows = item_ids.shape[0]
    positions = rows // users
    features, vocab = table.shape
    pack = LANES // features
    shape = (users, 2 * features, positions)
    hbm = pl.BlockSpec(memory_space=pltpu.HBM)
    vmem = pl.BlockSpec(memory_space=pltpu.VMEM)
    return pl.pallas_call(
        gather_kernel,
        out_shape=[
            jax.ShapeDtypeStruct(shape, table.dtype),
            jax.ShapeDtypeStruct((users, positions), jnp.int32),
        ],
        in_specs=[pl.BlockSpec(memory_space=pltpu.SMEM), vmem, hbm, hbm],
        out_specs=[hbm, vmem],
        scratch_shapes=[
            pltpu.VMEM((features, vocab), table.dtype),
            pltpu.VMEM((features, rows), table.dtype),
            pltpu.VMEM((vocab // pack, LANES), F32),
            pltpu.VMEM((rows, LANES), F32),
            pltpu.VMEM((users, features, positions), table.dtype),
            pltpu.VMEM((rows,), jnp.int32),
            pltpu.SMEM((rows,), jnp.int32),
            pltpu.SemaphoreType.DMA((CHUNKS,)),
            pltpu.SemaphoreType.DMA,
            pltpu.SemaphoreType.DMA((users,)),
            pltpu.SemaphoreType.DMA((users,)),
            pltpu.SemaphoreType.DMA,
        ],
        compiler_params=pltpu.CompilerParams(vmem_limit_bytes=WHOLE_VMEM_BYTES),
        cost_estimate=pl.CostEstimate(flops=8 * 10**9, bytes_accessed=5 * 10**6, transcendentals=0),
        name="gather_columns",
    )(lengths, item_ids, cotangent, table)


def norm_forward(values):
    centred = values - jnp.mean(values, axis=0, keepdims=True)
    inverse = lax.rsqrt(jnp.mean(centred * centred, axis=0, keepdims=True) + NORM_EPS)
    return centred * inverse, inverse


def norm_backward(grad, normal, inverse):
    shift = jnp.mean(grad, axis=0, keepdims=True)
    slope = jnp.mean(grad * normal, axis=0, keepdims=True)
    return (grad - shift - normal * slope) * inverse


def silu_pair(half):
    turn = jnp.tanh(half)
    twice = 1.0 + turn
    value = half * twice
    return value, twice + value * (1.0 - turn)


def layer_kernel(
    me_ref,
    len_ref,
    recv_ref,
    w_in_ref,
    w_out_ref,
    gain_in_row_ref,
    gain_mid_row_ref,
    out_hbm_ref,
    grad_hbm_ref,
    out_ref,
    grad_ref,
    proj_ref,
    slope_ref,
    weight_ref,
    score_slope_ref,
    att_ref,
    dproj_ref,
    gain_in_ref,
    gain_mid_ref,
    share_ref,
    sems,
):
    peers, both, positions = recv_ref.shape
    features = both // 2
    width = peers * features
    head_dim = width // HEADS
    half = positions // 2

    out_copy = pltpu.make_async_copy(out_ref, out_hbm_ref, sems.at[0])
    grad_copy = pltpu.make_async_copy(grad_ref, grad_hbm_ref, sems.at[1])
    length = len_ref[me_ref[0]]
    share = 1.0 / length.astype(F32)
    for row_ref, column_ref in ((gain_in_row_ref, gain_in_ref), (gain_mid_row_ref, gain_mid_ref)):
        row = row_ref[...].reshape(1, width)
        tile = jnp.broadcast_to(row, (LANES, width)).T
        column_ref[...] = jnp.concatenate([tile] * (positions // LANES), axis=1)

    key = lax.broadcasted_iota(jnp.int32, (positions, positions), 0)
    query = lax.broadcasted_iota(jnp.int32, (positions, positions), 1)
    share_ref[...] = jnp.where((key <= query) & (key < length), share, 0.0)

    def joined(kind):
        rows = pl.ds(kind * features, features)
        return jnp.concatenate([recv_ref[peer, rows, :] for peer in range(peers)], axis=0)

    embedded = joined(0).astype(F32)
    normal_in, inverse_in = norm_forward(embedded)
    normed = (normal_in * gain_in_ref[...]).astype(BF16)

    def project(part):
        return dot_nn(w_in_ref[:, pl.ds(part * width, width)].T, normed)

    def store_projected(part, z):
        rows = pl.ds(part * width, width)
        value, slope = silu_pair(0.5 * z)
        proj_ref[rows, :] = value.astype(BF16)
        slope_ref[rows, :] = slope

    waiting = None
    for part in (2, 3, 1, 0):
        z = project(part)
        if waiting is not None:
            store_projected(*waiting)
        waiting = (part, z)
    store_projected(*waiting)

    starts = (0, half)
    scale = head_dim ** (-0.5)

    def head_rows(kind, head):
        return pl.ds(kind * width + head * head_dim, head_dim)

    def score(head):
        queries, keys = proj_ref[head_rows(2, head), :], proj_ref[head_rows(3, head), :]
        return [dot_tn(keys[:, start : start + half], queries[:, start:]) for start in starts]

    def store_weights(head, scores):
        for start, block in zip(starts, scores):
            value, slope = silu_pair(block * (0.5 * scale))
            places = (pl.ds(start, half), pl.ds(start, positions - start))
            weight_ref[head, *places] = (value * share_ref[*places]).astype(BF16)
            score_slope_ref[head, *places] = slope * share_ref[*places]
        weight_ref[head, pl.ds(half, half), pl.ds(0, half)] = jnp.zeros((half, half), BF16)

    def attend(head):
        att_ref[pl.ds(head * head_dim, head_dim), :] = dot_nn(
            proj_ref[head_rows(1, head), :], weight_ref[head]
        )

    scores = score(0)
    for head in range(HEADS):
        following = score(head + 1) if head + 1 < HEADS else None
        store_weights(head, scores)
        if head:
            attend(head - 1)
        scores = following
    attend(HEADS - 1)

    normal_mid, inverse_mid = norm_forward(att_ref[...])
    gate_rows = proj_ref[pl.ds(0, width), :].astype(F32)
    scaled = normal_mid * gain_mid_ref[...]
    mixed = (scaled * gate_rows).astype(BF16)
    valid = lax.broadcasted_iota(jnp.int32, (width, positions), 1) < length
    cotangent = jnp.where(valid, joined(1).astype(F32), 0.0)
    d_mixed = dot_nn(w_out_ref[...], cotangent.astype(BF16))
    out_ref[...] = (embedded + dot_nn(w_out_ref[...].T, mixed)).astype(BF16)
    out_copy.start()

    dproj_ref[pl.ds(0, width), :] = (d_mixed * scaled * slope_ref[pl.ds(0, width), :]).astype(BF16)
    d_att = norm_backward(d_mixed * gate_rows * gain_mid_ref[...], normal_mid, inverse_mid)
    att_ref[...] = d_att

    def d_weights(head):
        values = proj_ref[head_rows(1, head), :]
        d_head = att_ref[pl.ds(head * head_dim, head_dim), :].astype(BF16)
        return [dot_tn(values[:, start : start + half], d_head[:, start:]) for start in starts]

    def d_scores(head, products):
        low, high = (
            (block * score_slope_ref[head, pl.ds(start, half), pl.ds(start, positions - start)]).astype(
                BF16
            )
            for start, block in zip(starts, products)
        )
        empty = jnp.zeros((half, half), BF16)
        return jnp.concatenate([low, jnp.concatenate([empty, high], axis=1)], axis=0)

    def d_project(head, d_score):
        d_head = att_ref[pl.ds(head * head_dim, head_dim), :].astype(BF16)
        queries, keys = proj_ref[head_rows(2, head), :], proj_ref[head_rows(3, head), :]
        products = (
            dot_nt(d_head, weight_ref[head]),
            dot_nn(keys, d_score) * (0.5 * scale),
            dot_nt(queries, d_score) * (0.5 * scale),
        )
        for kind, product in zip((1, 2, 3), products):
            rows = head_rows(kind, head)
            dproj_ref[rows, :] = (product * slope_ref[rows, :]).astype(BF16)

    products, before = d_weights(0), None
    for head in range(HEADS):
        following = d_weights(head + 1) if head + 1 < HEADS else None
        d_score = d_scores(head, products)
        if head:
            d_project(head - 1, before)
        products, before = following, d_score
    d_project(HEADS - 1, before)

    d_normed = dot_nn(w_in_ref[...], dproj_ref[...])
    d_embedded = norm_backward(d_normed * (0.5 * gain_in_ref[...]), normal_in, inverse_in)
    grad_ref[...] = (cotangent + d_embedded).astype(BF16)
    grad_copy.start()
    out_copy.wait()
    grad_copy.wait()


def run_layer(me, lengths, received, w_in, w_out, gain_in, gain_mid):
    peers, _, positions = received.shape
    width = w_out.shape[0]
    smem, vmem = pl.BlockSpec(memory_space=pltpu.SMEM), pl.BlockSpec(memory_space=pltpu.VMEM)
    hbm = pl.BlockSpec(memory_space=pltpu.HBM)
    shape = jax.ShapeDtypeStruct((width, positions), BF16)
    return pl.pallas_call(
        layer_kernel,
        out_shape=[shape, shape],
        in_specs=[smem, smem] + [vmem] * 5,
        out_specs=[hbm, hbm],
        scratch_shapes=[
            pltpu.VMEM((width, positions), BF16),
            pltpu.VMEM((width, positions), BF16),
            pltpu.VMEM((4 * width, positions), BF16),
            pltpu.VMEM((4 * width, positions), F32),
            pltpu.VMEM((HEADS, positions, positions), BF16),
            pltpu.VMEM((HEADS, positions, positions), F32),
            pltpu.VMEM((width, positions), F32),
            pltpu.VMEM((4 * width, positions), BF16),
            pltpu.VMEM((width, positions), F32),
            pltpu.VMEM((width, positions), F32),
            pltpu.VMEM((positions, positions), F32),
            pltpu.SemaphoreType.DMA((2,)),
        ],
        compiler_params=pltpu.CompilerParams(vmem_limit_bytes=LAYER_VMEM_BYTES),
        cost_estimate=pl.CostEstimate(flops=10**10, bytes_accessed=10**7, transcendentals=10**6),
        name="layer",
    )(
        me,
        lengths,
        received,
        w_in,
        w_out,
        gain_in,
        gain_mid,
    )


LOW = 256
STACK = 8


def ranks(member, users):
    rows, positions = member.shape
    ones = jnp.where(member, 1.0, 0.0).astype(BF16)

    def iota(shape, dimension):
        return lax.broadcasted_iota(jnp.int32, shape, dimension)

    square = (positions, positions)
    before = jnp.where(iota(square, 0) < iota(square, 1), 1.0, 0.0).astype(BF16)
    row, other = iota((rows, rows), 0), iota((rows, rows), 1)
    shift = users.bit_length() - 1
    above = (other < row) & ((other >> shift) == (row >> shift))
    earlier = dot_nn(jnp.where(above, 1.0, 0.0).astype(BF16), ones)
    return (dot_nn(ones, before) + jnp.sum(earlier, axis=1, keepdims=True)).astype(jnp.int32)


def plan_kernel(own, home_ref, turn_ref, ids_ref, low_ref, high_ref, slot_ref, most_ref, *scratch):
    chosen_ref, digit_ref, wide_ref, rank_ref = scratch
    groups, users, positions = ids_ref.shape
    capacity = low_ref.shape[1]
    home = home_ref[0]
    first = turn_ref[0] * capacity
    own_bits, low_bits = own.bit_length() - 1, LOW.bit_length() - 1

    all_items = ids_ref[...].reshape(groups * users, positions)
    sent = jnp.concatenate([ids_ref[0] >> own_bits == owner for owner in range(groups)], axis=0)
    arriving = all_items >> own_bits == home
    rank_ref[...] = ranks(jnp.concatenate([arriving, sent], axis=0), users) - first
    slot = jnp.full((users, positions), -1, jnp.int32)
    for owner in range(groups):
        rank = rank_ref[pl.ds((groups + owner) * users, users), :]
        fits = (ids_ref[0] >> own_bits == owner) & (rank >= 0) & (rank < capacity)
        slot = jnp.where(fits, rank + owner * capacity, slot)
    slot_ref[...] = slot

    digit = lax.broadcasted_iota(jnp.int32, (LOW, positions), 0)
    place = lax.broadcasted_iota(jnp.int32, (capacity, positions), 0)

    def one_group(group, most):
        items = ids_ref[group]
        for owner in range(groups):
            count = jnp.sum(jnp.where(items >> own_bits == owner, 1.0, 0.0))
            most = jnp.maximum(most, count)
        mine = items >> own_bits == home
        local = items & (own - 1)
        rank = rank_ref[pl.ds(pl.multiple_of(group * users, users), users), :]
        slot = jnp.where(mine, rank, -1)
        low = local & (LOW - 1)
        high = jnp.where(mine, (local >> low_bits) + 1, 0).astype(F32)
        for user in range(users):
            columns = pl.ds(user * positions, positions)
            chosen_ref[:, columns] = jnp.where(place == slot[user : user + 1], 1.0, 0.0).astype(BF16)
            digit_ref[:, columns] = jnp.where(digit == low[user : user + 1], 1.0, 0.0).astype(BF16)
            wide_ref[:, columns] = jnp.broadcast_to(high[user : user + 1], (16, positions)).astype(BF16)
        low_ref[group] = dot_nt(chosen_ref[...], digit_ref[...]).astype(BF16)
        high_ref[pl.ds(group, 1), :] = dot_nt(wide_ref[...], chosen_ref[...])[:1]
        return most

    most_ref[0] = lax.fori_loop(0, groups, one_group, jnp.float32(0)).astype(jnp.int32)


def plan_turn(home, turn, all_ids, own, capacity):
    groups, users, positions = all_ids.shape
    smem, vmem = pl.BlockSpec(memory_space=pltpu.SMEM), pl.BlockSpec(memory_space=pltpu.VMEM)
    return pl.pallas_call(
        functools.partial(plan_kernel, own),
        out_shape=[
            jax.ShapeDtypeStruct((groups, capacity, LOW), BF16),
            jax.ShapeDtypeStruct((groups, capacity), F32),
            jax.ShapeDtypeStruct((users, positions), jnp.int32),
            jax.ShapeDtypeStruct((1,), jnp.int32),
        ],
        in_specs=[smem, smem, vmem],
        out_specs=[vmem] * 3 + [smem],
        scratch_shapes=[
            pltpu.VMEM((capacity, users * positions), BF16),
            pltpu.VMEM((LOW, users * positions), BF16),
            pltpu.VMEM((16, users * positions), BF16),
            pltpu.VMEM((2 * groups * users, positions), jnp.int32),
        ],
        compiler_params=pltpu.CompilerParams(vmem_limit_bytes=PLAN_VMEM_BYTES),
        cost_estimate=pl.CostEstimate(flops=4 * 10**9, bytes_accessed=5 * 10**6, transcendentals=0),
        name="plan_turn",
    )(home, turn, all_ids)


def pack_kernel(distances, home_ref, slot_ref, grad_ref, *refs):
    *packed_refs, wide_ref, chosen_ref = refs
    users, _, positions = grad_ref.shape
    capacity = packed_refs[0].shape[1]
    padded = jnp.concatenate(
        [slot_ref[...].astype(F32), jnp.zeros((LANES - users, positions), F32)], axis=0
    )
    slots = padded.T.astype(jnp.int32)
    place = lax.broadcasted_iota(jnp.int32, (positions, capacity), 1)
    for user in range(users):
        wide_ref[:, pl.ds(user * positions, positions)] = grad_ref[user]
    for distance, packed_ref in zip(distances, packed_refs):
        first = (home_ref[0] ^ distance) * capacity
        for user in range(users):
            chosen_ref[pl.ds(user * positions, positions), :] = jnp.where(
                place == slots[:, user : user + 1] - first, 1.0, 0.0
            ).astype(BF16)
        packed_ref[...] = dot_nn(wide_ref[...], chosen_ref[...]).astype(BF16)


def pack_lists(distances, home, slot, grads, capacity):
    users, features, positions = grads.shape
    smem, vmem = pl.BlockSpec(memory_space=pltpu.SMEM), pl.BlockSpec(memory_space=pltpu.VMEM)
    return pl.pallas_call(
        functools.partial(pack_kernel, distances),
        out_shape=[jax.ShapeDtypeStruct((features, capacity), BF16)] * len(distances),
        in_specs=[smem, vmem, vmem],
        out_specs=[vmem] * len(distances),
        scratch_shapes=[
            pltpu.VMEM((features, users * positions), BF16),
            pltpu.VMEM((users * positions, capacity), BF16),
        ],
        compiler_params=pltpu.CompilerParams(vmem_limit_bytes=LIST_VMEM_BYTES),
        cost_estimate=pl.CostEstimate(
            flops=len(distances) * 8 * 10**8, bytes_accessed=10**6, transcendentals=0
        ),
        name="pack_lists",
    )(home, slot, grads)


def scatter_kernel(groups, stack, low_ref, high_ref, *refs):
    list_refs, (before_ref, out_ref, spread_ref) = refs[:groups], refs[groups:]
    features, capacity = list_refs[0].shape
    step = pl.program_id(0)
    for group, list_ref in enumerate(list_refs):
        high = high_ref[pl.ds(group, 1), :]
        for part in range(stack):
            wanted = (step * stack + part + 1).astype(F32)
            chosen = jnp.where(high == wanted, 1.0, 0.0).astype(BF16)
            spread_ref[pl.ds(part * features, features), pl.ds(group * capacity, capacity)] = (
                list_ref[...] * chosen
            )
    sums = dot_nn(spread_ref[...], low_ref[...])
    for part in range(stack):
        columns = pl.ds(part * LOW, LOW)
        term = sums[part * features : (part + 1) * features]
        out_ref[:, columns] = before_ref[:, columns] + term


def scatter_more(low, high, lists, own, before):
    groups = len(lists)
    features, capacity = lists[0].shape
    low = low.reshape(groups * capacity, LOW)
    stack = min(STACK, own // LOW)
    block = pl.BlockSpec((features, stack * LOW), lambda i: (0, i))
    return pl.pallas_call(
        functools.partial(scatter_kernel, groups, stack),
        grid=(own // (LOW * stack),),
        out_shape=jax.ShapeDtypeStruct((features, own), F32),
        in_specs=[
            pl.BlockSpec((groups * capacity, LOW), lambda i: (0, 0)),
            pl.BlockSpec(high.shape, lambda i: (0, 0)),
        ]
        + [pl.BlockSpec((features, capacity), lambda i: (0, 0))] * groups
        + [block],
        out_specs=block,
        scratch_shapes=[pltpu.VMEM((stack * features, groups * capacity), BF16)],
        input_output_aliases={2 + groups: 0},
        compiler_params=pltpu.CompilerParams(vmem_limit_bytes=LIST_VMEM_BYTES),
        cost_estimate=pl.CostEstimate(flops=3 * 10**9, bytes_accessed=10**6, transcendentals=0),
        name="scatter_more",
    )(low, high, *lists, before)


def scatter_first_kernel(groups, stack, low_ref, high_ref, *refs):
    list_refs, (out_hbm_ref, out_ref, spread_ref, sems) = refs[:groups], refs[groups:]
    features, capacity = list_refs[0].shape
    wide = stack * LOW
    steps = out_ref.shape[1] // wide

    def out_copy(step):
        columns = pl.ds(step * wide, wide)
        return pltpu.make_async_copy(
            out_ref.at[:, columns], out_hbm_ref.at[:, columns], sems.at[step]
        )

    for step in range(steps):
        for group, list_ref in enumerate(list_refs):
            high = high_ref[pl.ds(group, 1), :]
            for part in range(stack):
                chosen = jnp.where(high == float(step * stack + part + 1), 1.0, 0.0).astype(BF16)
                spread_ref[
                    step % 2, pl.ds(part * features, features), pl.ds(group * capacity, capacity)
                ] = list_ref[...] * chosen
        sums = dot_nn(spread_ref[step % 2], low_ref[...])
        for part in range(stack):
            columns = pl.ds(step * wide + part * LOW, LOW)
            out_ref[:, columns] = sums[part * features : (part + 1) * features]
        out_copy(step).start()
    for step in range(steps):
        out_copy(step).wait()


def scatter_first(low, high, lists, own):
    groups = len(lists)
    features, capacity = lists[0].shape
    stack = min(STACK, own // LOW)
    vmem, hbm = pl.BlockSpec(memory_space=pltpu.VMEM), pl.BlockSpec(memory_space=pltpu.HBM)
    return pl.pallas_call(
        functools.partial(scatter_first_kernel, groups, stack),
        out_shape=jax.ShapeDtypeStruct((features, own), F32),
        in_specs=[vmem] * (2 + groups),
        out_specs=hbm,
        scratch_shapes=[
            pltpu.VMEM((features, own), F32),
            pltpu.VMEM((2, stack * features, groups * capacity), BF16),
            pltpu.SemaphoreType.DMA((own // (stack * LOW),)),
        ],
        compiler_params=pltpu.CompilerParams(vmem_limit_bytes=LIST_VMEM_BYTES),
        cost_estimate=pl.CostEstimate(flops=3 * 10**9, bytes_accessed=10**6, transcendentals=0),
        name="scatter_first",
    )(low.reshape(groups * capacity, LOW), high, *lists)


def swap(value, axis, distance):
    size = lax.axis_size(axis)
    return lax.ppermute(value, axis, [(i, i ^ distance) for i in range(size)])


def send_lists(home, slot, grads, owners, capacity):
    lists = [None] * owners
    for distances in (tuple(reversed(range(1, owners))), (0,)):
        made = pack_lists(distances, home, slot, grads, capacity)
        slot, made = lax.optimization_barrier((slot, made))
        for distance, one_list in zip(distances, made):
            lists[distance] = swap(one_list, "dp", distance) if distance else one_list
    return lists


def exchange(value, axis):
    return lax.all_to_all(value, axis, split_axis=0, concat_axis=0, tiled=True)


def on_device(item_ids, user_len, emb_table, cotangent, w_uvqk, w_out, gain_in, gain_mid):
    dp_size = lax.axis_size("dp")
    table_size = lax.axis_size("table")
    users = user_len.shape[0]
    features, vocab = emb_table.shape
    rows = item_ids.shape[0]
    positions = rows // users
    own = vocab // dp_size
    capacity = -(-(rows // dp_size * 5 // 4) // LANES) * LANES
    assert users == table_size and users <= LANES and positions <= 256 and own // LOW <= 255
    assert dp_size & (dp_size - 1) == 0 and users & (users - 1) == 0 and own & (own - 1) == 0
    me = lax.axis_index("table").astype(jnp.int32).reshape(1)
    home = lax.axis_index("dp").astype(jnp.int32).reshape(1)

    send, valid_ids = gather_columns(item_ids, user_len, cotangent, emb_table)
    received = exchange(send, "table")
    all_ids = jnp.stack([valid_ids] + [swap(valid_ids, "dp", k) for k in range(1, dp_size)])
    out_cols, grad_cols = run_layer(me, user_len, received, w_uvqk, w_out, gain_in, gain_mid)
    per_peer = (table_size, features, positions)
    all_ids, grad_cols = lax.optimization_barrier((all_ids, grad_cols))
    plan = plan_turn(home, jnp.zeros((1,), jnp.int32), all_ids, own, capacity)
    grad_home = exchange(grad_cols.reshape(per_peer), "table")
    out_cols, grad_home, plan = lax.optimization_barrier((out_cols, grad_home, plan))
    out_home = exchange(out_cols.reshape(per_peer), "table")
    low, high, slot, most = plan
    lists = send_lists(home, slot, grad_home, dp_size, capacity)
    own_list, out_home = lax.optimization_barrier((lists[0], out_home))
    lists = [own_list] + lists[1:]
    layer_out = jnp.transpose(out_home, (1, 0, 2)).reshape(features, rows)
    layer_out, lists = lax.optimization_barrier((layer_out, lists))
    table_grad = scatter_first(low, high, lists, own)

    turns = (most[0] + capacity - 1) // capacity

    def another(state):
        turn, sums = state
        more_low, more_high, more_slot, _ = plan_turn(home, turn.reshape(1), all_ids, own, capacity)
        more_lists = send_lists(home, more_slot, grad_home, dp_size, capacity)
        return turn + 1, scatter_more(more_low, more_high, more_lists, own, sums)

    _, table_grad = lax.while_loop(
        lambda state: state[0] < turns, another, (jnp.int32(1), table_grad)
    )
    return (layer_out, table_grad)


def solution(mesh):
    return jax.shard_map(
        on_device,
        mesh=mesh,
        in_specs=(P("dp"), P("dp"), P("table", None), P("table", "dp"), P(), P(), P(), P()),
        out_specs=(P("table", "dp"), P("table", "dp")),
        check_vma=False,
    )
```

```python
import functools

import jax
import jax.numpy as jnp
from jax import lax
from jax.experimental import pallas as pl
from jax.experimental.pallas import tpu as pltpu
from jax.sharding import PartitionSpec as P

HEADS = 8
NORM_EPS = 1e-05
LANES = 128
WHOLE_VMEM_BYTES = 61 * 1024 * 1024
LAYER_VMEM_BYTES = 20 * 1024 * 1024
PLAN_VMEM_BYTES = 16 * 1024 * 1024
LIST_VMEM_BYTES = 24 * 1024 * 1024

F32 = jnp.float32
BF16 = jnp.bfloat16


def dot_nn(left, right):
    return jnp.dot(left, right, preferred_element_type=F32)


def dot_nt(left, right):
    return lax.dot_general(left, right, (((1,), (1,)), ((), ())), preferred_element_type=F32)


def dot_tn(left, right):
    return lax.dot_general(left, right, (((0,), (0,)), ((), ())), preferred_element_type=F32)


BLOCK = 256
UNROLL = 128
AT_ONCE = 32
CHUNKS = 4


def gather_kernel(
    len_ref,
    ids_ref,
    cot_hbm_ref,
    table_hbm_ref,
    out_ref,
    valid_ref,
    table_ref,
    cot_ref,
    rows_ref,
    picked_ref,
    turned_ref,
    row_vector_ref,
    row_ref,
    chunk_sems,
    row_sem,
    out_sems,
    cot_sems,
    cot_sem,
):
    users, _, positions = out_ref.shape
    features, vocab = table_hbm_ref.shape
    pack = LANES // features
    span = BLOCK * pack
    block_bits = BLOCK.bit_length() - 1

    def chunk_copy(chunk):
        columns = pl.ds(chunk * (vocab // CHUNKS), vocab // CHUNKS)
        return pltpu.make_async_copy(
            table_hbm_ref.at[:, columns], table_ref.at[:, columns], chunk_sems.at[chunk]
        )

    def cot_out_copy(user):
        return pltpu.make_async_copy(
            cot_ref.at[:, pl.ds(user * positions, positions)],
            out_ref.at[user, pl.ds(features, features), :],
            cot_sems.at[user],
        )

    def out_copy(user):
        return pltpu.make_async_copy(
            turned_ref.at[user], out_ref.at[user, pl.ds(0, features), :], out_sems.at[user]
        )

    for chunk in range(CHUNKS):
        chunk_copy(chunk).start()
    cot_copy = pltpu.make_async_copy(cot_hbm_ref, cot_ref, cot_sem)
    cot_copy.start()
    items = ids_ref[...]
    row_vector_ref[...] = ((items >> (span.bit_length() - 1)) << block_bits) | (items & (BLOCK - 1))
    row_copy = pltpu.make_async_copy(row_vector_ref, row_ref, row_sem)
    row_copy.start()
    order = lax.broadcasted_iota(jnp.int32, (1, positions), 1)
    for user in range(users):
        own_items = ids_ref[pl.ds(user * positions, positions)].reshape(1, positions)
        valid_ref[pl.ds(user, 1), :] = jnp.where(order < len_ref[user], own_items, vocab)

    parts = vocab // span
    for part in range(parts):
        if part % (parts // CHUNKS) == 0:
            chunk_copy(part // (parts // CHUNKS)).wait()
        stack = jnp.concatenate(
            [
                table_ref[:, part * span + s * BLOCK : part * span + (s + 1) * BLOCK]
                for s in range(pack)
            ],
            axis=0,
        )
        rows_ref[pl.ds(part * BLOCK, BLOCK), :] = stack.T.astype(F32)
    cot_copy.wait()
    for user in range(users):
        cot_out_copy(user).start()
    row_copy.wait()

    def some(part, carry):
        start = pl.multiple_of(part * UNROLL, UNROLL)
        for first in range(0, UNROLL, AT_ONCE):
            slots = range(first, first + AT_ONCE)
            rows = [rows_ref[pl.ds(row_ref[start + slot], 1), :] for slot in slots]
            for slot, row in zip(slots, rows):
                picked_ref[pl.ds(start + slot, 1), :] = row
        return carry

    lax.fori_loop(0, users * positions // UNROLL, some, 0)
    row = lax.broadcasted_iota(jnp.int32, (LANES, LANES), 0)
    column = lax.broadcasted_iota(jnp.int32, (LANES, LANES), 1)
    same = jnp.where(row == column, 1.0, 0.0).astype(BF16)
    for user in range(users):
        places = pl.ds(user * positions, positions)
        turned = dot_nt(same, picked_ref[places, :].astype(BF16))
        own_items = ids_ref[places].reshape(1, positions)
        group = (own_items >> block_bits) & (pack - 1)
        total = turned[:features]
        for s in range(1, pack):
            total = jnp.where(group == s, turned[s * features : (s + 1) * features], total)
        turned_ref[user] = total.astype(BF16)
        out_copy(user).start()
    for user in range(users):
        cot_out_copy(user).wait()
        out_copy(user).wait()


def gather_columns(item_ids, lengths, cotangent, table):
    users = lengths.shape[0]
    rows = item_ids.shape[0]
    positions = rows // users
    features, vocab = table.shape
    pack = LANES // features
    shape = (users, 2 * features, positions)
    hbm = pl.BlockSpec(memory_space=pltpu.HBM)
    vmem = pl.BlockSpec(memory_space=pltpu.VMEM)
    return pl.pallas_call(
        gather_kernel,
        out_shape=[
            jax.ShapeDtypeStruct(shape, table.dtype),
            jax.ShapeDtypeStruct((users, positions), jnp.int32),
        ],
        in_specs=[pl.BlockSpec(memory_space=pltpu.SMEM), vmem, hbm, hbm],
        out_specs=[hbm, vmem],
        scratch_shapes=[
            pltpu.VMEM((features, vocab), table.dtype),
            pltpu.VMEM((features, rows), table.dtype),
            pltpu.VMEM((vocab // pack, LANES), F32),
            pltpu.VMEM((rows, LANES), F32),
            pltpu.VMEM((users, features, positions), table.dtype),
            pltpu.VMEM((rows,), jnp.int32),
            pltpu.SMEM((rows,), jnp.int32),
            pltpu.SemaphoreType.DMA((CHUNKS,)),
            pltpu.SemaphoreType.DMA,
            pltpu.SemaphoreType.DMA((users,)),
            pltpu.SemaphoreType.DMA((users,)),
            pltpu.SemaphoreType.DMA,
        ],
        compiler_params=pltpu.CompilerParams(vmem_limit_bytes=WHOLE_VMEM_BYTES),
        cost_estimate=pl.CostEstimate(flops=8 * 10**9, bytes_accessed=5 * 10**6, transcendentals=0),
        name="gather_columns",
    )(lengths, item_ids, cotangent, table)


def norm_forward(values):
    centred = values - jnp.mean(values, axis=0, keepdims=True)
    inverse = lax.rsqrt(jnp.mean(centred * centred, axis=0, keepdims=True) + NORM_EPS)
    return centred * inverse, inverse


def norm_backward_means(grad, normal):
    return jnp.mean(grad, axis=0, keepdims=True), jnp.mean(grad * normal, axis=0, keepdims=True)


def norm_backward(grad, normal, inverse):
    shift, slope = norm_backward_means(grad, normal)
    return (grad - shift - normal * slope) * inverse


def silu_pair(half):
    turn = jnp.tanh(half)
    twice = 1.0 + turn
    value = half * twice
    return value, twice + value * (1.0 - turn)


def layer_kernel(
    me_ref,
    len_ref,
    recv_ref,
    w_in_ref,
    w_out_ref,
    gain_in_row_ref,
    gain_mid_row_ref,
    out_hbm_ref,
    grad_hbm_ref,
    out_ref,
    grad_ref,
    proj_ref,
    slope_ref,
    weight_ref,
    score_slope_ref,
    att_ref,
    dproj_ref,
    gain_in_ref,
    gain_mid_ref,
    share_ref,
    sems,
):
    peers, both, positions = recv_ref.shape
    features = both // 2
    width = peers * features
    head_dim = width // HEADS
    half = positions // 2

    out_copy = pltpu.make_async_copy(out_ref, out_hbm_ref, sems.at[0])

    def grad_copy(peer):
        rows = pl.ds(peer * features, features)
        return pltpu.make_async_copy(
            grad_ref.at[rows, :], grad_hbm_ref.at[rows, :], sems.at[1 + peer]
        )

    length = len_ref[me_ref[0]]
    share = 1.0 / length.astype(F32)
    for row_ref, column_ref in ((gain_in_row_ref, gain_in_ref), (gain_mid_row_ref, gain_mid_ref)):
        row = row_ref[...].reshape(1, width)
        tile = jnp.broadcast_to(row, (LANES, width)).T
        column_ref[...] = jnp.concatenate([tile] * (positions // LANES), axis=1)

    key = lax.broadcasted_iota(jnp.int32, (positions, positions), 0)
    query = lax.broadcasted_iota(jnp.int32, (positions, positions), 1)
    share_ref[...] = jnp.where((key <= query) & (key < length), share, 0.0)

    def joined(kind):
        rows = pl.ds(kind * features, features)
        return jnp.concatenate([recv_ref[peer, rows, :] for peer in range(peers)], axis=0)

    embedded = joined(0).astype(F32)
    normal_in, inverse_in = norm_forward(embedded)
    normed = (normal_in * gain_in_ref[...]).astype(BF16)

    def project(part):
        return dot_nn(w_in_ref[:, pl.ds(part * width, width)].T, normed)

    def store_projected(part, z):
        rows = pl.ds(part * width, width)
        value, slope = silu_pair(0.5 * z)
        proj_ref[rows, :] = value.astype(BF16)
        slope_ref[rows, :] = slope

    waiting = None
    for part in (2, 3, 1, 0):
        z = project(part)
        if waiting is not None:
            store_projected(*waiting)
        waiting = (part, z)
    store_projected(*waiting)

    starts = (0, half)
    scale = head_dim ** (-0.5)

    def head_rows(kind, head):
        return pl.ds(kind * width + head * head_dim, head_dim)

    def score(head):
        queries, keys = proj_ref[head_rows(2, head), :], proj_ref[head_rows(3, head), :]
        return [dot_tn(keys[:, start : start + half], queries[:, start:]) for start in starts]

    def store_weights(head, scores):
        for start, block in zip(starts, scores):
            value, slope = silu_pair(block * (0.5 * scale))
            places = (pl.ds(start, half), pl.ds(start, positions - start))
            weight_ref[head, *places] = (value * share_ref[*places]).astype(BF16)
            score_slope_ref[head, *places] = slope * share_ref[*places]
        weight_ref[head, pl.ds(half, half), pl.ds(0, half)] = jnp.zeros((half, half), BF16)

    def attend(head):
        att_ref[pl.ds(head * head_dim, head_dim), :] = dot_nn(
            proj_ref[head_rows(1, head), :], weight_ref[head]
        )

    scores = score(0)
    for head in range(HEADS):
        following = score(head + 1) if head + 1 < HEADS else None
        store_weights(head, scores)
        if head:
            attend(head - 1)
        scores = following
    attend(HEADS - 1)

    normal_mid, inverse_mid = norm_forward(att_ref[...])
    gate_rows = proj_ref[pl.ds(0, width), :].astype(F32)
    scaled = normal_mid * gain_mid_ref[...]
    mixed = (scaled * gate_rows).astype(BF16)
    valid = lax.broadcasted_iota(jnp.int32, (width, positions), 1) < length
    cotangent = jnp.where(valid, joined(1).astype(F32), 0.0)
    d_mixed = dot_nn(w_out_ref[...], cotangent.astype(BF16))
    out_ref[...] = (embedded + dot_nn(w_out_ref[...].T, mixed)).astype(BF16)
    out_copy.start()

    dproj_ref[pl.ds(0, width), :] = (d_mixed * scaled * slope_ref[pl.ds(0, width), :]).astype(BF16)
    d_att = norm_backward(d_mixed * gate_rows * gain_mid_ref[...], normal_mid, inverse_mid)
    att_ref[...] = d_att

    def d_weights(head):
        values = proj_ref[head_rows(1, head), :]
        d_head = att_ref[pl.ds(head * head_dim, head_dim), :].astype(BF16)
        return [dot_tn(values[:, start : start + half], d_head[:, start:]) for start in starts]

    def d_scores(head, products):
        low, high = (
            (block * score_slope_ref[head, pl.ds(start, half), pl.ds(start, positions - start)]).astype(
                BF16
            )
            for start, block in zip(starts, products)
        )
        empty = jnp.zeros((half, half), BF16)
        return jnp.concatenate([low, jnp.concatenate([empty, high], axis=1)], axis=0)

    def d_project(head, d_score):
        d_head = att_ref[pl.ds(head * head_dim, head_dim), :].astype(BF16)
        queries, keys = proj_ref[head_rows(2, head), :], proj_ref[head_rows(3, head), :]
        products = (
            dot_nt(d_head, weight_ref[head]),
            dot_nn(keys, d_score) * (0.5 * scale),
            dot_nt(queries, d_score) * (0.5 * scale),
        )
        for kind, product in zip((1, 2, 3), products):
            rows = head_rows(kind, head)
            dproj_ref[rows, :] = (product * slope_ref[rows, :]).astype(BF16)

    products, before = d_weights(0), None
    for head in range(HEADS):
        following = d_weights(head + 1) if head + 1 < HEADS else None
        d_score = d_scores(head, products)
        if head:
            d_project(head - 1, before)
        products, before = following, d_score
    d_project(HEADS - 1, before)

    d_normed = dot_nn(w_in_ref[...], dproj_ref[...])
    d_normal = d_normed * (0.5 * gain_in_ref[...])
    shift, slope = norm_backward_means(d_normal, normal_in)
    for peer in range(peers):
        rows = slice(peer * features, (peer + 1) * features)
        d_embedded = (d_normal[rows] - shift - normal_in[rows] * slope) * inverse_in
        grad_ref[rows, :] = (cotangent[rows] + d_embedded).astype(BF16)
        grad_copy(peer).start()
    out_copy.wait()
    for peer in range(peers):
        grad_copy(peer).wait()


def run_layer(me, lengths, received, w_in, w_out, gain_in, gain_mid):
    peers, _, positions = received.shape
    width = w_out.shape[0]
    smem, vmem = pl.BlockSpec(memory_space=pltpu.SMEM), pl.BlockSpec(memory_space=pltpu.VMEM)
    hbm = pl.BlockSpec(memory_space=pltpu.HBM)
    shape = jax.ShapeDtypeStruct((width, positions), BF16)
    return pl.pallas_call(
        layer_kernel,
        out_shape=[shape, shape],
        in_specs=[smem, smem] + [vmem] * 5,
        out_specs=[hbm, hbm],
        scratch_shapes=[
            pltpu.VMEM((width, positions), BF16),
            pltpu.VMEM((width, positions), BF16),
            pltpu.VMEM((4 * width, positions), BF16),
            pltpu.VMEM((4 * width, positions), F32),
            pltpu.VMEM((HEADS, positions, positions), BF16),
            pltpu.VMEM((HEADS, positions, positions), F32),
            pltpu.VMEM((width, positions), F32),
            pltpu.VMEM((4 * width, positions), BF16),
            pltpu.VMEM((width, positions), F32),
            pltpu.VMEM((width, positions), F32),
            pltpu.VMEM((positions, positions), F32),
            pltpu.SemaphoreType.DMA((1 + peers,)),
        ],
        compiler_params=pltpu.CompilerParams(vmem_limit_bytes=LAYER_VMEM_BYTES),
        cost_estimate=pl.CostEstimate(flops=10**10, bytes_accessed=10**7, transcendentals=10**6),
        name="layer",
    )(
        me,
        lengths,
        received,
        w_in,
        w_out,
        gain_in,
        gain_mid,
    )


LOW = 256
STACK = 16


def ranks(member, users):
    rows, positions = member.shape
    ones = jnp.where(member, 1.0, 0.0).astype(BF16)

    def iota(shape, dimension):
        return lax.broadcasted_iota(jnp.int32, shape, dimension)

    square = (positions, positions)
    before = jnp.where(iota(square, 0) < iota(square, 1), 1.0, 0.0).astype(BF16)
    row, other = iota((rows, rows), 0), iota((rows, rows), 1)
    shift = users.bit_length() - 1
    above = (other < row) & ((other >> shift) == (row >> shift))
    earlier = dot_nn(jnp.where(above, 1.0, 0.0).astype(BF16), ones)
    return (dot_nn(ones, before) + jnp.sum(earlier, axis=1, keepdims=True)).astype(jnp.int32)


def plan_kernel(own, home_ref, turn_ref, ids_ref, low_ref, high_ref, slot_ref, most_ref, *scratch):
    chosen_ref, digit_ref, wide_ref, rank_ref = scratch
    groups, users, positions = ids_ref.shape
    capacity = low_ref.shape[1]
    home = home_ref[0]
    first = turn_ref[0] * capacity
    own_bits, low_bits = own.bit_length() - 1, LOW.bit_length() - 1

    all_items = ids_ref[...].reshape(groups * users, positions)
    sent = jnp.concatenate([ids_ref[0] >> own_bits == owner for owner in range(groups)], axis=0)
    arriving = all_items >> own_bits == home
    rank_ref[...] = ranks(jnp.concatenate([arriving, sent], axis=0), users) - first
    slot = jnp.full((users, positions), -1, jnp.int32)
    for owner in range(groups):
        rank = rank_ref[pl.ds((groups + owner) * users, users), :]
        fits = (ids_ref[0] >> own_bits == owner) & (rank >= 0) & (rank < capacity)
        slot = jnp.where(fits, rank + owner * capacity, slot)
    slot_ref[...] = slot

    digit = lax.broadcasted_iota(jnp.int32, (LOW, positions), 0)
    place = lax.broadcasted_iota(jnp.int32, (capacity, positions), 0)

    def one_group(group, most):
        items = ids_ref[group]
        for owner in range(groups):
            count = jnp.sum(jnp.where(items >> own_bits == owner, 1.0, 0.0))
            most = jnp.maximum(most, count)
        mine = items >> own_bits == home
        local = items & (own - 1)
        rank = rank_ref[pl.ds(pl.multiple_of(group * users, users), users), :]
        slot = jnp.where(mine, rank, -1)
        low = local & (LOW - 1)
        high = jnp.where(mine, (local >> low_bits) + 1, 0).astype(F32)
        for user in range(users):
            columns = pl.ds(user * positions, positions)
            chosen_ref[:, columns] = jnp.where(place == slot[user : user + 1], 1.0, 0.0).astype(BF16)
            digit_ref[:, columns] = jnp.where(digit == low[user : user + 1], 1.0, 0.0).astype(BF16)
            wide_ref[:, columns] = jnp.broadcast_to(high[user : user + 1], (16, positions)).astype(BF16)
        low_ref[group] = dot_nt(chosen_ref[...], digit_ref[...]).astype(BF16)
        high_ref[pl.ds(group, 1), :] = dot_nt(wide_ref[...], chosen_ref[...])[:1]
        return most

    most_ref[0] = lax.fori_loop(0, groups, one_group, jnp.float32(0)).astype(jnp.int32)


def plan_turn(home, turn, all_ids, own, capacity):
    groups, users, positions = all_ids.shape
    smem, vmem = pl.BlockSpec(memory_space=pltpu.SMEM), pl.BlockSpec(memory_space=pltpu.VMEM)
    return pl.pallas_call(
        functools.partial(plan_kernel, own),
        out_shape=[
            jax.ShapeDtypeStruct((groups, capacity, LOW), BF16),
            jax.ShapeDtypeStruct((groups, capacity), F32),
            jax.ShapeDtypeStruct((users, positions), jnp.int32),
            jax.ShapeDtypeStruct((1,), jnp.int32),
        ],
        in_specs=[smem, smem, vmem],
        out_specs=[vmem] * 3 + [smem],
        scratch_shapes=[
            pltpu.VMEM((capacity, users * positions), BF16),
            pltpu.VMEM((LOW, users * positions), BF16),
            pltpu.VMEM((16, users * positions), BF16),
            pltpu.VMEM((2 * groups * users, positions), jnp.int32),
        ],
        compiler_params=pltpu.CompilerParams(vmem_limit_bytes=PLAN_VMEM_BYTES),
        cost_estimate=pl.CostEstimate(flops=4 * 10**9, bytes_accessed=5 * 10**6, transcendentals=0),
        name="plan_turn",
    )(home, turn, all_ids)


def pack_kernel(distances, home_ref, slot_ref, grad_ref, *refs):
    *packed_refs, wide_ref, chosen_ref = refs
    users, _, positions = grad_ref.shape
    capacity = packed_refs[0].shape[1]
    padded = jnp.concatenate(
        [slot_ref[...].astype(F32), jnp.zeros((LANES - users, positions), F32)], axis=0
    )
    slots = padded.T.astype(jnp.int32)
    place = lax.broadcasted_iota(jnp.int32, (positions, capacity), 1)
    for user in range(users):
        wide_ref[:, pl.ds(user * positions, positions)] = grad_ref[user]
    for distance, packed_ref in zip(distances, packed_refs):
        first = (home_ref[0] ^ distance) * capacity
        for user in range(users):
            chosen_ref[pl.ds(user * positions, positions), :] = jnp.where(
                place == slots[:, user : user + 1] - first, 1.0, 0.0
            ).astype(BF16)
        packed_ref[...] = dot_nn(wide_ref[...], chosen_ref[...]).astype(BF16)


def pack_lists(distances, home, slot, grads, capacity):
    users, features, positions = grads.shape
    smem, vmem = pl.BlockSpec(memory_space=pltpu.SMEM), pl.BlockSpec(memory_space=pltpu.VMEM)
    return pl.pallas_call(
        functools.partial(pack_kernel, distances),
        out_shape=[jax.ShapeDtypeStruct((features, capacity), BF16)] * len(distances),
        in_specs=[smem, vmem, vmem],
        out_specs=[vmem] * len(distances),
        scratch_shapes=[
            pltpu.VMEM((features, users * positions), BF16),
            pltpu.VMEM((users * positions, capacity), BF16),
        ],
        compiler_params=pltpu.CompilerParams(vmem_limit_bytes=LIST_VMEM_BYTES),
        cost_estimate=pl.CostEstimate(
            flops=len(distances) * 8 * 10**8, bytes_accessed=10**6, transcendentals=0
        ),
        name="pack_lists",
    )(home, slot, grads)


def scatter_kernel(groups, stack, low_ref, high_ref, *refs):
    list_refs, (*before_ref, out_ref, spread_ref) = refs[:groups], refs[groups:]
    features, capacity = list_refs[0].shape
    step = pl.program_id(0)
    for group, list_ref in enumerate(list_refs):
        high = high_ref[pl.ds(group, 1), :]
        for part in range(stack):
            wanted = (step * stack + part + 1).astype(F32)
            chosen = jnp.where(high == wanted, 1.0, 0.0).astype(BF16)
            spread_ref[pl.ds(part * features, features), pl.ds(group * capacity, capacity)] = (
                list_ref[...] * chosen
            )
    sums = dot_nn(spread_ref[...], low_ref[...])
    for part in range(stack):
        columns = pl.ds(part * LOW, LOW)
        term = sums[part * features : (part + 1) * features]
        out_ref[:, columns] = term + before_ref[0][:, columns] if before_ref else term


def scatter_slots(low, high, lists, own, before=None):
    groups = len(lists)
    features, capacity = lists[0].shape
    low = low.reshape(groups * capacity, LOW)
    stack = min(STACK, own // LOW)
    block = pl.BlockSpec((features, stack * LOW), lambda i: (0, i))
    extra = [] if before is None else [before]
    return pl.pallas_call(
        functools.partial(scatter_kernel, groups, stack),
        grid=(own // (LOW * stack),),
        out_shape=jax.ShapeDtypeStruct((features, own), F32),
        in_specs=[
            pl.BlockSpec((groups * capacity, LOW), lambda i: (0, 0)),
            pl.BlockSpec(high.shape, lambda i: (0, 0)),
        ]
        + [pl.BlockSpec((features, capacity), lambda i: (0, 0))] * groups
        + [block] * len(extra),
        out_specs=block,
        scratch_shapes=[pltpu.VMEM((stack * features, groups * capacity), BF16)],
        input_output_aliases={2 + groups: 0} if extra else {},
        compiler_params=pltpu.CompilerParams(vmem_limit_bytes=LIST_VMEM_BYTES),
        cost_estimate=pl.CostEstimate(flops=3 * 10**9, bytes_accessed=10**6, transcendentals=0),
        name="scatter_slots",
    )(low, high, *lists, *extra)


def swap(value, axis, distance):
    size = lax.axis_size(axis)
    return lax.ppermute(value, axis, [(i, i ^ distance) for i in range(size)])


def send_lists(home, slot, grads, owners, capacity):
    lists = [None] * owners
    for distances in ((owners - 1,), tuple(range(1, owners - 1)), (0,)):
        made = pack_lists(distances, home, slot, grads, capacity)
        slot, made = lax.optimization_barrier((slot, made))
        for distance, one_list in zip(distances, made):
            lists[distance] = swap(one_list, "dp", distance) if distance else one_list
    return lists


def exchange(value, axis):
    return lax.all_to_all(value, axis, split_axis=0, concat_axis=0, tiled=True)


def on_device(item_ids, user_len, emb_table, cotangent, w_uvqk, w_out, gain_in, gain_mid):
    dp_size = lax.axis_size("dp")
    table_size = lax.axis_size("table")
    users = user_len.shape[0]
    features, vocab = emb_table.shape
    rows = item_ids.shape[0]
    positions = rows // users
    own = vocab // dp_size
    capacity = -(-(rows // dp_size * 5 // 4) // LANES) * LANES
    assert users == table_size and users <= LANES and positions <= 256 and own // LOW <= 255
    assert dp_size & (dp_size - 1) == 0 and users & (users - 1) == 0 and own & (own - 1) == 0
    me = lax.axis_index("table").astype(jnp.int32).reshape(1)
    home = lax.axis_index("dp").astype(jnp.int32).reshape(1)

    send, valid_ids = gather_columns(item_ids, user_len, cotangent, emb_table)
    received = exchange(send, "table")
    all_ids = jnp.stack([valid_ids] + [swap(valid_ids, "dp", k) for k in range(1, dp_size)])
    out_cols, grad_cols = run_layer(me, user_len, received, w_uvqk, w_out, gain_in, gain_mid)
    per_peer = (table_size, features, positions)
    all_ids, grad_cols = lax.optimization_barrier((all_ids, grad_cols))
    plan = plan_turn(home, jnp.zeros((1,), jnp.int32), all_ids, own, capacity)
    grad_home = exchange(grad_cols.reshape(per_peer), "table")
    out_cols, grad_home, plan = lax.optimization_barrier((out_cols, grad_home, plan))
    out_home = exchange(out_cols.reshape(per_peer), "table")
    low, high, slot, most = plan
    lists = send_lists(home, slot, grad_home, dp_size, capacity)
    own_list, out_home = lax.optimization_barrier((lists[0], out_home))
    lists = [own_list] + lists[1:]
    layer_out = jnp.transpose(out_home, (1, 0, 2)).reshape(features, rows)
    layer_out, lists = lax.optimization_barrier((layer_out, lists))
    table_grad = scatter_slots(low, high, lists, own)

    turns = (most[0] + capacity - 1) // capacity

    def another(state):
        turn, sums = state
        more_low, more_high, more_slot, _ = plan_turn(home, turn.reshape(1), all_ids, own, capacity)
        more_lists = send_lists(home, more_slot, grad_home, dp_size, capacity)
        return turn + 1, scatter_slots(more_low, more_high, more_lists, own, sums)

    _, table_grad = lax.while_loop(
        lambda state: state[0] < turns, another, (jnp.int32(1), table_grad)
    )
    return (layer_out, table_grad)


def solution(mesh):
    return jax.shard_map(
        on_device,
        mesh=mesh,
        in_specs=(P("dp"), P("dp"), P("table", None), P("table", "dp"), P(), P(), P(), P()),
        out_specs=(P("table", "dp"), P("table", "dp")),
        check_vma=False,
    )
```

```python
import functools

import jax
import jax.numpy as jnp
from jax import lax
from jax.experimental import pallas as pl
from jax.experimental.pallas import tpu as pltpu
from jax.sharding import PartitionSpec as P

HEADS = 8
NORM_EPS = 1e-05
LANES = 128
WHOLE_VMEM_BYTES = 61 * 1024 * 1024
LAYER_VMEM_BYTES = 20 * 1024 * 1024
PLAN_VMEM_BYTES = 16 * 1024 * 1024
LIST_VMEM_BYTES = 24 * 1024 * 1024

F32 = jnp.float32
BF16 = jnp.bfloat16


def dot_nn(left, right):
    return jnp.dot(left, right, preferred_element_type=F32)


def dot_nt(left, right):
    return lax.dot_general(left, right, (((1,), (1,)), ((), ())), preferred_element_type=F32)


def dot_tn(left, right):
    return lax.dot_general(left, right, (((0,), (0,)), ((), ())), preferred_element_type=F32)


BLOCK = 256
UNROLL = 128
AT_ONCE = 32
CHUNKS = 8


def gather_kernel(
    len_ref,
    ids_ref,
    cot_hbm_ref,
    table_hbm_ref,
    out_ref,
    valid_ref,
    table_ref,
    cot_ref,
    rows_ref,
    picked_ref,
    turned_ref,
    row_vector_ref,
    row_ref,
    chunk_sems,
    row_sem,
    out_sems,
    cot_sems,
    cot_sem,
):
    users, _, positions = out_ref.shape
    features, vocab = table_hbm_ref.shape
    pack = LANES // features
    span = BLOCK * pack
    block_bits = BLOCK.bit_length() - 1

    def chunk_copy(chunk):
        columns = pl.ds(chunk * (vocab // CHUNKS), vocab // CHUNKS)
        return pltpu.make_async_copy(
            table_hbm_ref.at[:, columns], table_ref.at[:, columns], chunk_sems.at[chunk]
        )

    def cot_out_copy(user):
        return pltpu.make_async_copy(
            cot_ref.at[:, pl.ds(user * positions, positions)],
            out_ref.at[user, pl.ds(features, features), :],
            cot_sems.at[user],
        )

    def out_copy(user):
        return pltpu.make_async_copy(
            turned_ref.at[user], out_ref.at[user, pl.ds(0, features), :], out_sems.at[user]
        )

    for chunk in range(CHUNKS):
        chunk_copy(chunk).start()
    cot_copy = pltpu.make_async_copy(cot_hbm_ref, cot_ref, cot_sem)
    cot_copy.start()
    items = ids_ref[...]
    row_vector_ref[...] = ((items >> (span.bit_length() - 1)) << block_bits) | (items & (BLOCK - 1))
    row_copy = pltpu.make_async_copy(row_vector_ref, row_ref, row_sem)
    row_copy.start()
    order = lax.broadcasted_iota(jnp.int32, (1, positions), 1)
    for user in range(users):
        own_items = ids_ref[pl.ds(user * positions, positions)].reshape(1, positions)
        valid_ref[pl.ds(user, 1), :] = jnp.where(order < len_ref[user], own_items, vocab)

    parts = vocab // span
    for part in range(parts):
        if part % (parts // CHUNKS) == 0:
            chunk_copy(part // (parts // CHUNKS)).wait()
        stack = jnp.concatenate(
            [
                table_ref[:, part * span + s * BLOCK : part * span + (s + 1) * BLOCK]
                for s in range(pack)
            ],
            axis=0,
        )
        rows_ref[pl.ds(part * BLOCK, BLOCK), :] = stack.T.astype(F32)
    cot_copy.wait()
    for user in range(users):
        cot_out_copy(user).start()
    row_copy.wait()

    def some(part, carry):
        start = pl.multiple_of(part * UNROLL, UNROLL)
        for first in range(0, UNROLL, AT_ONCE):
            slots = range(first, first + AT_ONCE)
            rows = [rows_ref[pl.ds(row_ref[start + slot], 1), :] for slot in slots]
            for slot, row in zip(slots, rows):
                picked_ref[pl.ds(start + slot, 1), :] = row
        return carry

    lax.fori_loop(0, users * positions // UNROLL, some, 0)
    row = lax.broadcasted_iota(jnp.int32, (LANES, LANES), 0)
    column = lax.broadcasted_iota(jnp.int32, (LANES, LANES), 1)
    same = jnp.where(row == column, 1.0, 0.0).astype(BF16)
    for user in range(users):
        places = pl.ds(user * positions, positions)
        turned = dot_nt(same, picked_ref[places, :].astype(BF16))
        own_items = ids_ref[places].reshape(1, positions)
        group = (own_items >> block_bits) & (pack - 1)
        total = turned[:features]
        for s in range(1, pack):
            total = jnp.where(group == s, turned[s * features : (s + 1) * features], total)
        turned_ref[user] = total.astype(BF16)
        out_copy(user).start()
    for user in range(users):
        cot_out_copy(user).wait()
        out_copy(user).wait()


def gather_columns(item_ids, lengths, cotangent, table):
    users = lengths.shape[0]
    rows = item_ids.shape[0]
    positions = rows // users
    features, vocab = table.shape
    pack = LANES // features
    shape = (users, 2 * features, positions)
    hbm = pl.BlockSpec(memory_space=pltpu.HBM)
    vmem = pl.BlockSpec(memory_space=pltpu.VMEM)
    return pl.pallas_call(
        gather_kernel,
        out_shape=[
            jax.ShapeDtypeStruct(shape, table.dtype),
            jax.ShapeDtypeStruct((users, positions), jnp.int32),
        ],
        in_specs=[pl.BlockSpec(memory_space=pltpu.SMEM), vmem, hbm, hbm],
        out_specs=[hbm, vmem],
        scratch_shapes=[
            pltpu.VMEM((features, vocab), table.dtype),
            pltpu.VMEM((features, rows), table.dtype),
            pltpu.VMEM((vocab // pack, LANES), F32),
            pltpu.VMEM((rows, LANES), F32),
            pltpu.VMEM((users, features, positions), table.dtype),
            pltpu.VMEM((rows,), jnp.int32),
            pltpu.SMEM((rows,), jnp.int32),
            pltpu.SemaphoreType.DMA((CHUNKS,)),
            pltpu.SemaphoreType.DMA,
            pltpu.SemaphoreType.DMA((users,)),
            pltpu.SemaphoreType.DMA((users,)),
            pltpu.SemaphoreType.DMA,
        ],
        compiler_params=pltpu.CompilerParams(vmem_limit_bytes=WHOLE_VMEM_BYTES),
        cost_estimate=pl.CostEstimate(flops=8 * 10**9, bytes_accessed=5 * 10**6, transcendentals=0),
        name="gather_columns",
    )(lengths, item_ids, cotangent, table)


def norm_forward(values):
    centred = values - jnp.mean(values, axis=0, keepdims=True)
    inverse = lax.rsqrt(jnp.mean(centred * centred, axis=0, keepdims=True) + NORM_EPS)
    return centred * inverse, inverse


def norm_backward_means(grad, normal):
    return jnp.mean(grad, axis=0, keepdims=True), jnp.mean(grad * normal, axis=0, keepdims=True)


def norm_backward(grad, normal, inverse):
    shift, slope = norm_backward_means(grad, normal)
    return (grad - shift - normal * slope) * inverse


def silu_pair(half):
    turn = jnp.tanh(half)
    twice = 1.0 + turn
    value = half * twice
    return value, twice + value * (1.0 - turn)


def layer_kernel(
    me_ref,
    len_ref,
    recv_ref,
    w_in_ref,
    w_out_ref,
    gain_in_row_ref,
    gain_mid_row_ref,
    out_hbm_ref,
    grad_hbm_ref,
    out_ref,
    grad_ref,
    proj_ref,
    slope_ref,
    weight_ref,
    score_slope_ref,
    att_ref,
    dproj_ref,
    gain_in_ref,
    gain_mid_ref,
    share_ref,
    sems,
):
    peers, both, positions = recv_ref.shape
    features = both // 2
    width = peers * features
    head_dim = width // HEADS
    half = positions // 2

    out_copy = pltpu.make_async_copy(out_ref, out_hbm_ref, sems.at[0])

    def grad_copy(peer):
        rows = pl.ds(peer * features, features)
        return pltpu.make_async_copy(
            grad_ref.at[rows, :], grad_hbm_ref.at[rows, :], sems.at[1 + peer]
        )

    length = len_ref[me_ref[0]]
    share = 1.0 / length.astype(F32)
    for row_ref, column_ref in ((gain_in_row_ref, gain_in_ref), (gain_mid_row_ref, gain_mid_ref)):
        row = row_ref[...].reshape(1, width)
        tile = jnp.broadcast_to(row, (LANES, width)).T
        column_ref[...] = jnp.concatenate([tile] * (positions // LANES), axis=1)

    key = lax.broadcasted_iota(jnp.int32, (positions, positions), 0)
    query = lax.broadcasted_iota(jnp.int32, (positions, positions), 1)
    share_ref[...] = jnp.where((key <= query) & (key < length), share, 0.0)

    def joined(kind):
        rows = pl.ds(kind * features, features)
        return jnp.concatenate([recv_ref[peer, rows, :] for peer in range(peers)], axis=0)

    embedded = joined(0).astype(F32)
    normal_in, inverse_in = norm_forward(embedded)
    normed = (normal_in * gain_in_ref[...]).astype(BF16)

    def project(part):
        return dot_nn(w_in_ref[:, pl.ds(part * width, width)].T, normed)

    def store_projected(part, z):
        rows = pl.ds(part * width, width)
        value, slope = silu_pair(0.5 * z)
        proj_ref[rows, :] = value.astype(BF16)
        slope_ref[rows, :] = slope

    waiting = None
    for part in (2, 3, 1, 0):
        z = project(part)
        if waiting is not None:
            store_projected(*waiting)
        waiting = (part, z)
    store_projected(*waiting)

    starts = (0, half)
    scale = head_dim ** (-0.5)

    def head_rows(kind, head):
        return pl.ds(kind * width + head * head_dim, head_dim)

    def score(head):
        queries, keys = proj_ref[head_rows(2, head), :], proj_ref[head_rows(3, head), :]
        return [dot_tn(keys[:, start : start + half], queries[:, start:]) for start in starts]

    def store_weights(head, scores):
        for start, block in zip(starts, scores):
            value, slope = silu_pair(block * (0.5 * scale))
            places = (pl.ds(start, half), pl.ds(start, positions - start))
            weight_ref[head, *places] = (value * share_ref[*places]).astype(BF16)
            score_slope_ref[head, *places] = slope * share_ref[*places]
        weight_ref[head, pl.ds(half, half), pl.ds(0, half)] = jnp.zeros((half, half), BF16)

    def attend(head):
        att_ref[pl.ds(head * head_dim, head_dim), :] = dot_nn(
            proj_ref[head_rows(1, head), :], weight_ref[head]
        )

    scores = score(0)
    for head in range(HEADS):
        following = score(head + 1) if head + 1 < HEADS else None
        store_weights(head, scores)
        if head:
            attend(head - 1)
        scores = following
    attend(HEADS - 1)

    normal_mid, inverse_mid = norm_forward(att_ref[...])
    gate_rows = proj_ref[pl.ds(0, width), :].astype(F32)
    scaled = normal_mid * gain_mid_ref[...]
    mixed = (scaled * gate_rows).astype(BF16)
    valid = lax.broadcasted_iota(jnp.int32, (width, positions), 1) < length
    cotangent = jnp.where(valid, joined(1).astype(F32), 0.0)
    d_mixed = dot_nn(w_out_ref[...], cotangent.astype(BF16))
    out_ref[...] = (embedded + dot_nn(w_out_ref[...].T, mixed)).astype(BF16)
    out_copy.start()

    dproj_ref[pl.ds(0, width), :] = (d_mixed * scaled * slope_ref[pl.ds(0, width), :]).astype(BF16)
    d_att = norm_backward(d_mixed * gate_rows * gain_mid_ref[...], normal_mid, inverse_mid)
    att_ref[...] = d_att

    def d_weights(head):
        values = proj_ref[head_rows(1, head), :]
        d_head = att_ref[pl.ds(head * head_dim, head_dim), :].astype(BF16)
        return [dot_tn(values[:, start : start + half], d_head[:, start:]) for start in starts]

    def d_scores(head, products):
        low, high = (
            (block * score_slope_ref[head, pl.ds(start, half), pl.ds(start, positions - start)]).astype(
                BF16
            )
            for start, block in zip(starts, products)
        )
        empty = jnp.zeros((half, half), BF16)
        return jnp.concatenate([low, jnp.concatenate([empty, high], axis=1)], axis=0)

    def d_project(head, d_score):
        d_head = att_ref[pl.ds(head * head_dim, head_dim), :].astype(BF16)
        queries, keys = proj_ref[head_rows(2, head), :], proj_ref[head_rows(3, head), :]
        products = (
            dot_nt(d_head, weight_ref[head]),
            dot_nn(keys, d_score) * (0.5 * scale),
            dot_nt(queries, d_score) * (0.5 * scale),
        )
        for kind, product in zip((1, 2, 3), products):
            rows = head_rows(kind, head)
            dproj_ref[rows, :] = (product * slope_ref[rows, :]).astype(BF16)

    products, before = d_weights(0), None
    for head in range(HEADS):
        following = d_weights(head + 1) if head + 1 < HEADS else None
        d_score = d_scores(head, products)
        if head:
            d_project(head - 1, before)
        products, before = following, d_score
    d_project(HEADS - 1, before)

    d_normed = dot_nn(w_in_ref[...], dproj_ref[...])
    d_normal = d_normed * (0.5 * gain_in_ref[...])
    shift, slope = norm_backward_means(d_normal, normal_in)
    for peer in range(peers):
        rows = slice(peer * features, (peer + 1) * features)
        d_embedded = (d_normal[rows] - shift - normal_in[rows] * slope) * inverse_in
        grad_ref[rows, :] = (cotangent[rows] + d_embedded).astype(BF16)
        grad_copy(peer).start()
    out_copy.wait()
    for peer in range(peers):
        grad_copy(peer).wait()


def run_layer(me, lengths, received, w_in, w_out, gain_in, gain_mid):
    peers, _, positions = received.shape
    width = w_out.shape[0]
    smem, vmem = pl.BlockSpec(memory_space=pltpu.SMEM), pl.BlockSpec(memory_space=pltpu.VMEM)
    hbm = pl.BlockSpec(memory_space=pltpu.HBM)
    shape = jax.ShapeDtypeStruct((width, positions), BF16)
    return pl.pallas_call(
        layer_kernel,
        out_shape=[shape, shape],
        in_specs=[smem, smem] + [vmem] * 5,
        out_specs=[hbm, hbm],
        scratch_shapes=[
            pltpu.VMEM((width, positions), BF16),
            pltpu.VMEM((width, positions), BF16),
            pltpu.VMEM((4 * width, positions), BF16),
            pltpu.VMEM((4 * width, positions), F32),
            pltpu.VMEM((HEADS, positions, positions), BF16),
            pltpu.VMEM((HEADS, positions, positions), F32),
            pltpu.VMEM((width, positions), F32),
            pltpu.VMEM((4 * width, positions), BF16),
            pltpu.VMEM((width, positions), F32),
            pltpu.VMEM((width, positions), F32),
            pltpu.VMEM((positions, positions), F32),
            pltpu.SemaphoreType.DMA((1 + peers,)),
        ],
        compiler_params=pltpu.CompilerParams(vmem_limit_bytes=LAYER_VMEM_BYTES),
        cost_estimate=pl.CostEstimate(flops=10**10, bytes_accessed=10**7, transcendentals=10**6),
        name="layer",
    )(
        me,
        lengths,
        received,
        w_in,
        w_out,
        gain_in,
        gain_mid,
    )


LOW = 256
STACK = 16


def ranks(member, users):
    rows, positions = member.shape
    ones = jnp.where(member, 1.0, 0.0).astype(BF16)

    def iota(shape, dimension):
        return lax.broadcasted_iota(jnp.int32, shape, dimension)

    square = (positions, positions)
    before = jnp.where(iota(square, 0) < iota(square, 1), 1.0, 0.0).astype(BF16)
    row, other = iota((rows, rows), 0), iota((rows, rows), 1)
    shift = users.bit_length() - 1
    above = (other < row) & ((other >> shift) == (row >> shift))
    earlier = dot_nn(jnp.where(above, 1.0, 0.0).astype(BF16), ones)
    return (dot_nn(ones, before) + jnp.sum(earlier, axis=1, keepdims=True)).astype(jnp.int32)


def plan_kernel(own, home_ref, turn_ref, ids_ref, low_ref, high_ref, slot_ref, most_ref, *scratch):
    chosen_ref, digit_ref, wide_ref, rank_ref = scratch
    groups, users, positions = ids_ref.shape
    capacity = low_ref.shape[1]
    home = home_ref[0]
    first = turn_ref[0] * capacity
    own_bits, low_bits = own.bit_length() - 1, LOW.bit_length() - 1

    all_items = ids_ref[...].reshape(groups * users, positions)
    sent = jnp.concatenate([ids_ref[0] >> own_bits == owner for owner in range(groups)], axis=0)
    arriving = all_items >> own_bits == home
    rank_ref[...] = ranks(jnp.concatenate([arriving, sent], axis=0), users) - first
    slot = jnp.full((users, positions), -1, jnp.int32)
    for owner in range(groups):
        rank = rank_ref[pl.ds((groups + owner) * users, users), :]
        fits = (ids_ref[0] >> own_bits == owner) & (rank >= 0) & (rank < capacity)
        slot = jnp.where(fits, rank + owner * capacity, slot)
    padded = jnp.concatenate(
        [slot.astype(F32), jnp.zeros((LANES - users, positions), F32)], axis=0
    )
    slot_ref[...] = padded.T.astype(jnp.int32)

    digit = lax.broadcasted_iota(jnp.int32, (LOW, positions), 0)
    place = lax.broadcasted_iota(jnp.int32, (capacity, positions), 0)

    def one_group(group, most):
        items = ids_ref[group]
        for owner in range(groups):
            count = jnp.sum(jnp.where(items >> own_bits == owner, 1.0, 0.0))
            most = jnp.maximum(most, count)
        mine = items >> own_bits == home
        local = items & (own - 1)
        rank = rank_ref[pl.ds(pl.multiple_of(group * users, users), users), :]
        slot = jnp.where(mine, rank, -1)
        low = local & (LOW - 1)
        high = jnp.where(mine, (local >> low_bits) + 1, 0).astype(F32)
        for user in range(users):
            columns = pl.ds(user * positions, positions)
            chosen_ref[:, columns] = jnp.where(place == slot[user : user + 1], 1.0, 0.0).astype(BF16)
            digit_ref[:, columns] = jnp.where(digit == low[user : user + 1], 1.0, 0.0).astype(BF16)
            wide_ref[:, columns] = jnp.broadcast_to(high[user : user + 1], (16, positions)).astype(BF16)
        low_ref[group] = dot_nt(chosen_ref[...], digit_ref[...]).astype(BF16)
        high_ref[pl.ds(group, 1), :] = dot_nt(wide_ref[...], chosen_ref[...])[:1]
        return most

    most_ref[0] = lax.fori_loop(0, groups, one_group, jnp.float32(0)).astype(jnp.int32)


def plan_turn(home, turn, all_ids, own, capacity):
    groups, users, positions = all_ids.shape
    smem, vmem = pl.BlockSpec(memory_space=pltpu.SMEM), pl.BlockSpec(memory_space=pltpu.VMEM)
    return pl.pallas_call(
        functools.partial(plan_kernel, own),
        out_shape=[
            jax.ShapeDtypeStruct((groups, capacity, LOW), BF16),
            jax.ShapeDtypeStruct((groups, capacity), F32),
            jax.ShapeDtypeStruct((positions, LANES), jnp.int32),
            jax.ShapeDtypeStruct((1,), jnp.int32),
        ],
        in_specs=[smem, smem, vmem],
        out_specs=[vmem] * 3 + [smem],
        scratch_shapes=[
            pltpu.VMEM((capacity, users * positions), BF16),
            pltpu.VMEM((LOW, users * positions), BF16),
            pltpu.VMEM((16, users * positions), BF16),
            pltpu.VMEM((2 * groups * users, positions), jnp.int32),
        ],
        compiler_params=pltpu.CompilerParams(vmem_limit_bytes=PLAN_VMEM_BYTES),
        cost_estimate=pl.CostEstimate(flops=4 * 10**9, bytes_accessed=5 * 10**6, transcendentals=0),
        name="plan_turn",
    )(home, turn, all_ids)


def pack_kernel(distances, home_ref, slot_ref, grad_ref, *refs):
    *packed_refs, wide_ref, chosen_ref = refs
    users, _, positions = grad_ref.shape
    capacity = packed_refs[0].shape[1]
    place = lax.broadcasted_iota(jnp.int32, (positions, capacity), 1)
    for user in range(users):
        wide_ref[:, pl.ds(user * positions, positions)] = grad_ref[user]
    for distance, packed_ref in zip(distances, packed_refs):
        first = (home_ref[0] ^ distance) * capacity
        for user in range(users):
            chosen_ref[pl.ds(user * positions, positions), :] = jnp.where(
                place == slot_ref[:, user : user + 1] - first, 1.0, 0.0
            ).astype(BF16)
        packed_ref[...] = dot_nn(wide_ref[...], chosen_ref[...]).astype(BF16)


def pack_lists(distances, home, slot, grads, capacity):
    users, features, positions = grads.shape
    smem, vmem = pl.BlockSpec(memory_space=pltpu.SMEM), pl.BlockSpec(memory_space=pltpu.VMEM)
    return pl.pallas_call(
        functools.partial(pack_kernel, distances),
        out_shape=[jax.ShapeDtypeStruct((features, capacity), BF16)] * len(distances),
        in_specs=[smem, vmem, vmem],
        out_specs=[vmem] * len(distances),
        scratch_shapes=[
            pltpu.VMEM((features, users * positions), BF16),
            pltpu.VMEM((users * positions, capacity), BF16),
        ],
        compiler_params=pltpu.CompilerParams(vmem_limit_bytes=LIST_VMEM_BYTES),
        cost_estimate=pl.CostEstimate(
            flops=len(distances) * 8 * 10**8, bytes_accessed=10**6, transcendentals=0
        ),
        name="pack_lists",
    )(home, slot, grads)


def scatter_kernel(groups, stack, low_ref, high_ref, *refs):
    list_refs, (*before_ref, out_ref, spread_ref) = refs[:groups], refs[groups:]
    features, capacity = list_refs[0].shape
    step = pl.program_id(0)
    for group, list_ref in enumerate(list_refs):
        high = high_ref[pl.ds(group, 1), :]
        for part in range(stack):
            wanted = (step * stack + part + 1).astype(F32)
            chosen = jnp.where(high == wanted, 1.0, 0.0).astype(BF16)
            spread_ref[pl.ds(part * features, features), pl.ds(group * capacity, capacity)] = (
                list_ref[...] * chosen
            )
    sums = dot_nn(spread_ref[...], low_ref[...])
    for part in range(stack):
        columns = pl.ds(part * LOW, LOW)
        term = sums[part * features : (part + 1) * features]
        out_ref[:, columns] = term + before_ref[0][:, columns] if before_ref else term


def scatter_slots(low, high, lists, own, before=None):
    groups = len(lists)
    features, capacity = lists[0].shape
    low = low.reshape(groups * capacity, LOW)
    stack = min(STACK, own // LOW)
    block = pl.BlockSpec((features, stack * LOW), lambda i: (0, i))
    extra = [] if before is None else [before]
    return pl.pallas_call(
        functools.partial(scatter_kernel, groups, stack),
        grid=(own // (LOW * stack),),
        out_shape=jax.ShapeDtypeStruct((features, own), F32),
        in_specs=[
            pl.BlockSpec((groups * capacity, LOW), lambda i: (0, 0)),
            pl.BlockSpec(high.shape, lambda i: (0, 0)),
        ]
        + [pl.BlockSpec((features, capacity), lambda i: (0, 0))] * groups
        + [block] * len(extra),
        out_specs=block,
        scratch_shapes=[pltpu.VMEM((stack * features, groups * capacity), BF16)],
        input_output_aliases={2 + groups: 0} if extra else {},
        compiler_params=pltpu.CompilerParams(vmem_limit_bytes=LIST_VMEM_BYTES),
        cost_estimate=pl.CostEstimate(flops=3 * 10**9, bytes_accessed=10**6, transcendentals=0),
        name="scatter_slots",
    )(low, high, *lists, *extra)


def swap(value, axis, distance):
    size = lax.axis_size(axis)
    return lax.ppermute(value, axis, [(i, i ^ distance) for i in range(size)])


def send_lists(home, slot, grads, owners, capacity):
    lists = [None] * owners
    for distances in ((owners - 1,), tuple(range(1, owners - 1)), (0,)):
        made = pack_lists(distances, home, slot, grads, capacity)
        slot, made = lax.optimization_barrier((slot, made))
        for distance, one_list in zip(distances, made):
            lists[distance] = swap(one_list, "dp", distance) if distance else one_list
    return lists


def exchange(value, axis):
    return lax.all_to_all(value, axis, split_axis=0, concat_axis=0, tiled=True)


def on_device(item_ids, user_len, emb_table, cotangent, w_uvqk, w_out, gain_in, gain_mid):
    dp_size = lax.axis_size("dp")
    table_size = lax.axis_size("table")
    users = user_len.shape[0]
    features, vocab = emb_table.shape
    rows = item_ids.shape[0]
    positions = rows // users
    own = vocab // dp_size
    capacity = -(-(rows // dp_size * 5 // 4) // LANES) * LANES
    assert users == table_size and users <= LANES and positions <= 256 and own // LOW <= 255
    assert dp_size & (dp_size - 1) == 0 and users & (users - 1) == 0 and own & (own - 1) == 0
    me = lax.axis_index("table").astype(jnp.int32).reshape(1)
    home = lax.axis_index("dp").astype(jnp.int32).reshape(1)

    send, valid_ids = gather_columns(item_ids, user_len, cotangent, emb_table)
    received = exchange(send, "table")
    all_ids = jnp.stack([valid_ids] + [swap(valid_ids, "dp", k) for k in range(1, dp_size)])
    out_cols, grad_cols = run_layer(me, user_len, received, w_uvqk, w_out, gain_in, gain_mid)
    per_peer = (table_size, features, positions)
    all_ids, grad_cols = lax.optimization_barrier((all_ids, grad_cols))
    plan = plan_turn(home, jnp.zeros((1,), jnp.int32), all_ids, own, capacity)
    grad_home = exchange(grad_cols.reshape(per_peer), "table")
    out_cols, grad_home, plan = lax.optimization_barrier((out_cols, grad_home, plan))
    out_home = exchange(out_cols.reshape(per_peer), "table")
    low, high, slot, most = plan
    lists = send_lists(home, slot, grad_home, dp_size, capacity)
    own_list, out_home = lax.optimization_barrier((lists[0], out_home))
    lists = [own_list] + lists[1:]
    layer_out = jnp.transpose(out_home, (1, 0, 2)).reshape(features, rows)
    layer_out, lists = lax.optimization_barrier((layer_out, lists))
    table_grad = scatter_slots(low, high, lists, own)

    turns = (most[0] + capacity - 1) // capacity

    def another(state):
        turn, sums = state
        more_low, more_high, more_slot, _ = plan_turn(home, turn.reshape(1), all_ids, own, capacity)
        more_lists = send_lists(home, more_slot, grad_home, dp_size, capacity)
        return turn + 1, scatter_slots(more_low, more_high, more_lists, own, sums)

    _, table_grad = lax.while_loop(
        lambda state: state[0] < turns, another, (jnp.int32(1), table_grad)
    )
    return (layer_out, table_grad)


def solution(mesh):
    return jax.shard_map(
        on_device,
        mesh=mesh,
        in_specs=(P("dp"), P("dp"), P("table", None), P("table", "dp"), P(), P(), P(), P()),
        out_specs=(P("table", "dp"), P("table", "dp")),
        check_vma=False,
    )
```

```python
import functools

import jax
import jax.numpy as jnp
from jax import lax
from jax.experimental import pallas as pl
from jax.experimental.pallas import tpu as pltpu
from jax.sharding import PartitionSpec as P

HEADS = 8
NORM_EPS = 1e-05
LANES = 128
WHOLE_VMEM_BYTES = 61 * 1024 * 1024
LAYER_VMEM_BYTES = 20 * 1024 * 1024
PLAN_VMEM_BYTES = 16 * 1024 * 1024
LIST_VMEM_BYTES = 24 * 1024 * 1024

F32 = jnp.float32
BF16 = jnp.bfloat16


def dot_nn(left, right):
    return jnp.dot(left, right, preferred_element_type=F32)


def dot_nt(left, right):
    return lax.dot_general(left, right, (((1,), (1,)), ((), ())), preferred_element_type=F32)


def dot_tn(left, right):
    return lax.dot_general(left, right, (((0,), (0,)), ((), ())), preferred_element_type=F32)


BLOCK = 256
UNROLL = 128
AT_ONCE = 32
CHUNKS = 4


def gather_kernel(
    len_ref,
    ids_ref,
    cot_hbm_ref,
    table_hbm_ref,
    out_ref,
    valid_ref,
    table_ref,
    cot_ref,
    rows_ref,
    picked_ref,
    turned_ref,
    row_vector_ref,
    row_ref,
    chunk_sems,
    row_sem,
    out_sems,
    cot_sems,
    cot_sem,
):
    users, _, positions = out_ref.shape
    features, vocab = table_hbm_ref.shape
    pack = LANES // features
    span = BLOCK * pack
    block_bits = BLOCK.bit_length() - 1

    def chunk_copy(chunk):
        columns = pl.ds(chunk * (vocab // CHUNKS), vocab // CHUNKS)
        return pltpu.make_async_copy(
            table_hbm_ref.at[:, columns], table_ref.at[:, columns], chunk_sems.at[chunk]
        )

    def cot_out_copy(user):
        return pltpu.make_async_copy(
            cot_ref.at[:, pl.ds(user * positions, positions)],
            out_ref.at[user, pl.ds(features, features), :],
            cot_sems.at[user],
        )

    def out_copy(user):
        return pltpu.make_async_copy(
            turned_ref.at[user], out_ref.at[user, pl.ds(0, features), :], out_sems.at[user]
        )

    for chunk in range(CHUNKS):
        chunk_copy(chunk).start()
    cot_copy = pltpu.make_async_copy(cot_hbm_ref, cot_ref, cot_sem)
    cot_copy.start()
    items = ids_ref[...]
    row_vector_ref[...] = ((items >> (span.bit_length() - 1)) << block_bits) | (items & (BLOCK - 1))
    row_copy = pltpu.make_async_copy(row_vector_ref, row_ref, row_sem)
    row_copy.start()
    order = lax.broadcasted_iota(jnp.int32, (1, positions), 1)
    for user in range(users):
        own_items = ids_ref[pl.ds(user * positions, positions)].reshape(1, positions)
        valid_ref[pl.ds(user, 1), :] = jnp.where(order < len_ref[user], own_items, vocab)

    parts = vocab // span
    for part in range(parts):
        if part % (parts // CHUNKS) == 0:
            chunk_copy(part // (parts // CHUNKS)).wait()
        stack = jnp.concatenate(
            [
                table_ref[:, part * span + s * BLOCK : part * span + (s + 1) * BLOCK]
                for s in range(pack)
            ],
            axis=0,
        )
        rows_ref[pl.ds(part * BLOCK, BLOCK), :] = stack.T.astype(F32)
    cot_copy.wait()
    for user in range(users):
        cot_out_copy(user).start()
    row_copy.wait()

    def some(part, carry):
        start = pl.multiple_of(part * UNROLL, UNROLL)
        for first in range(0, UNROLL, AT_ONCE):
            slots = range(first, first + AT_ONCE)
            rows = [rows_ref[pl.ds(row_ref[start + slot], 1), :] for slot in slots]
            for slot, row in zip(slots, rows):
                picked_ref[pl.ds(start + slot, 1), :] = row
        return carry

    lax.fori_loop(0, users * positions // UNROLL, some, 0)
    for user in range(users):
        places = pl.ds(user * positions, positions)
        turned = picked_ref[places, :].T
        own_items = ids_ref[places].reshape(1, positions)
        group = (own_items >> block_bits) & (pack - 1)
        total = turned[:features]
        for s in range(1, pack):
            total = jnp.where(group == s, turned[s * features : (s + 1) * features], total)
        turned_ref[user] = total.astype(BF16)
        out_copy(user).start()
    for user in range(users):
        cot_out_copy(user).wait()
        out_copy(user).wait()


def gather_columns(item_ids, lengths, cotangent, table):
    users = lengths.shape[0]
    rows = item_ids.shape[0]
    positions = rows // users
    features, vocab = table.shape
    pack = LANES // features
    shape = (users, 2 * features, positions)
    hbm = pl.BlockSpec(memory_space=pltpu.HBM)
    vmem = pl.BlockSpec(memory_space=pltpu.VMEM)
    return pl.pallas_call(
        gather_kernel,
        out_shape=[
            jax.ShapeDtypeStruct(shape, table.dtype),
            jax.ShapeDtypeStruct((users, positions), jnp.int32),
        ],
        in_specs=[pl.BlockSpec(memory_space=pltpu.SMEM), vmem, hbm, hbm],
        out_specs=[hbm, vmem],
        scratch_shapes=[
            pltpu.VMEM((features, vocab), table.dtype),
            pltpu.VMEM((features, rows), table.dtype),
            pltpu.VMEM((vocab // pack, LANES), F32),
            pltpu.VMEM((rows, LANES), F32),
            pltpu.VMEM((users, features, positions), table.dtype),
            pltpu.VMEM((rows,), jnp.int32),
            pltpu.SMEM((rows,), jnp.int32),
            pltpu.SemaphoreType.DMA((CHUNKS,)),
            pltpu.SemaphoreType.DMA,
            pltpu.SemaphoreType.DMA((users,)),
            pltpu.SemaphoreType.DMA((users,)),
            pltpu.SemaphoreType.DMA,
        ],
        compiler_params=pltpu.CompilerParams(vmem_limit_bytes=WHOLE_VMEM_BYTES),
        cost_estimate=pl.CostEstimate(flops=8 * 10**9, bytes_accessed=5 * 10**6, transcendentals=0),
        name="gather_columns",
    )(lengths, item_ids, cotangent, table)


def norm_forward(values):
    centred = values - jnp.mean(values, axis=0, keepdims=True)
    inverse = lax.rsqrt(jnp.mean(centred * centred, axis=0, keepdims=True) + NORM_EPS)
    return centred * inverse, inverse


def norm_backward_means(grad, normal):
    return jnp.mean(grad, axis=0, keepdims=True), jnp.mean(grad * normal, axis=0, keepdims=True)


def norm_backward(grad, normal, inverse):
    shift, slope = norm_backward_means(grad, normal)
    return (grad - shift - normal * slope) * inverse


def silu_pair(half):
    turn = jnp.tanh(half)
    twice = 1.0 + turn
    value = half * twice
    return value, twice + value * (1.0 - turn)


def layer_kernel(
    me_ref,
    len_ref,
    recv_ref,
    w_in_ref,
    w_out_ref,
    gain_in_row_ref,
    gain_mid_row_ref,
    out_hbm_ref,
    grad_hbm_ref,
    out_ref,
    grad_ref,
    proj_ref,
    slope_ref,
    weight_ref,
    score_slope_ref,
    att_ref,
    dproj_ref,
    gain_in_ref,
    gain_mid_ref,
    share_ref,
    sems,
):
    peers, both, positions = recv_ref.shape
    features = both // 2
    width = peers * features
    head_dim = width // HEADS
    half = positions // 2

    out_copy = pltpu.make_async_copy(out_ref, out_hbm_ref, sems.at[0])

    def grad_copy(peer):
        rows = pl.ds(peer * features, features)
        return pltpu.make_async_copy(
            grad_ref.at[rows, :], grad_hbm_ref.at[rows, :], sems.at[1 + peer]
        )

    length = len_ref[me_ref[0]]
    share = 1.0 / length.astype(F32)
    for row_ref, column_ref in ((gain_in_row_ref, gain_in_ref), (gain_mid_row_ref, gain_mid_ref)):
        row = row_ref[...].reshape(1, width)
        tile = jnp.broadcast_to(row, (LANES, width)).T
        column_ref[...] = jnp.concatenate([tile] * (positions // LANES), axis=1)

    key = lax.broadcasted_iota(jnp.int32, (positions, positions), 0)
    query = lax.broadcasted_iota(jnp.int32, (positions, positions), 1)
    share_ref[...] = jnp.where((key <= query) & (key < length), share, 0.0)

    def joined(kind):
        rows = pl.ds(kind * features, features)
        return jnp.concatenate([recv_ref[peer, rows, :] for peer in range(peers)], axis=0)

    embedded = joined(0).astype(F32)
    normal_in, inverse_in = norm_forward(embedded)
    normed = (normal_in * gain_in_ref[...]).astype(BF16)

    def project(part):
        return dot_nn(w_in_ref[:, pl.ds(part * width, width)].T, normed)

    def store_projected(part, z):
        rows = pl.ds(part * width, width)
        value, slope = silu_pair(0.5 * z)
        proj_ref[rows, :] = value.astype(BF16)
        slope_ref[rows, :] = slope

    waiting = None
    for part in (2, 3, 1, 0):
        z = project(part)
        if waiting is not None:
            store_projected(*waiting)
        waiting = (part, z)
    store_projected(*waiting)

    starts = (0, half)
    scale = head_dim ** (-0.5)

    def head_rows(kind, head):
        return pl.ds(kind * width + head * head_dim, head_dim)

    def score(head):
        queries, keys = proj_ref[head_rows(2, head), :], proj_ref[head_rows(3, head), :]
        return [dot_tn(keys[:, start : start + half], queries[:, start:]) for start in starts]

    def store_weights(head, scores):
        for start, block in zip(starts, scores):
            value, slope = silu_pair(block * (0.5 * scale))
            places = (pl.ds(start, half), pl.ds(start, positions - start))
            weight_ref[head, *places] = (value * share_ref[*places]).astype(BF16)
            score_slope_ref[head, *places] = slope * share_ref[*places]
        weight_ref[head, pl.ds(half, half), pl.ds(0, half)] = jnp.zeros((half, half), BF16)

    def attend(head):
        att_ref[pl.ds(head * head_dim, head_dim), :] = dot_nn(
            proj_ref[head_rows(1, head), :], weight_ref[head]
        )

    scores = score(0)
    for head in range(HEADS):
        following = score(head + 1) if head + 1 < HEADS else None
        store_weights(head, scores)
        if head:
            attend(head - 1)
        scores = following
    attend(HEADS - 1)

    normal_mid, inverse_mid = norm_forward(att_ref[...])
    gate_rows = proj_ref[pl.ds(0, width), :].astype(F32)
    scaled = normal_mid * gain_mid_ref[...]
    mixed = (scaled * gate_rows).astype(BF16)
    valid = lax.broadcasted_iota(jnp.int32, (width, positions), 1) < length
    cotangent = jnp.where(valid, joined(1).astype(F32), 0.0)
    d_mixed = dot_nn(w_out_ref[...], cotangent.astype(BF16))
    out_ref[...] = (embedded + dot_nn(w_out_ref[...].T, mixed)).astype(BF16)
    out_copy.start()

    dproj_ref[pl.ds(0, width), :] = (d_mixed * scaled * slope_ref[pl.ds(0, width), :]).astype(BF16)
    d_att = norm_backward(d_mixed * gate_rows * gain_mid_ref[...], normal_mid, inverse_mid)
    att_ref[...] = d_att

    def d_weights(head):
        values = proj_ref[head_rows(1, head), :]
        d_head = att_ref[pl.ds(head * head_dim, head_dim), :].astype(BF16)
        return [dot_tn(values[:, start : start + half], d_head[:, start:]) for start in starts]

    def d_scores(head, products):
        low, high = (
            (block * score_slope_ref[head, pl.ds(start, half), pl.ds(start, positions - start)]).astype(
                BF16
            )
            for start, block in zip(starts, products)
        )
        empty = jnp.zeros((half, half), BF16)
        return jnp.concatenate([low, jnp.concatenate([empty, high], axis=1)], axis=0)

    def d_project(head, d_score):
        d_head = att_ref[pl.ds(head * head_dim, head_dim), :].astype(BF16)
        queries, keys = proj_ref[head_rows(2, head), :], proj_ref[head_rows(3, head), :]
        products = (
            dot_nt(d_head, weight_ref[head]),
            dot_nn(keys, d_score) * (0.5 * scale),
            dot_nt(queries, d_score) * (0.5 * scale),
        )
        for kind, product in zip((1, 2, 3), products):
            rows = head_rows(kind, head)
            dproj_ref[rows, :] = (product * slope_ref[rows, :]).astype(BF16)

    products, before = d_weights(0), None
    for head in range(HEADS):
        following = d_weights(head + 1) if head + 1 < HEADS else None
        d_score = d_scores(head, products)
        if head:
            d_project(head - 1, before)
        products, before = following, d_score
    d_project(HEADS - 1, before)

    d_normed = dot_nn(w_in_ref[...], dproj_ref[...])
    d_normal = d_normed * (0.5 * gain_in_ref[...])
    shift, slope = norm_backward_means(d_normal, normal_in)
    for peer in range(peers):
        rows = slice(peer * features, (peer + 1) * features)
        d_embedded = (d_normal[rows] - shift - normal_in[rows] * slope) * inverse_in
        grad_ref[rows, :] = (cotangent[rows] + d_embedded).astype(BF16)
        grad_copy(peer).start()
    out_copy.wait()
    for peer in range(peers):
        grad_copy(peer).wait()


def run_layer(me, lengths, received, w_in, w_out, gain_in, gain_mid):
    peers, _, positions = received.shape
    width = w_out.shape[0]
    smem, vmem = pl.BlockSpec(memory_space=pltpu.SMEM), pl.BlockSpec(memory_space=pltpu.VMEM)
    hbm = pl.BlockSpec(memory_space=pltpu.HBM)
    shape = jax.ShapeDtypeStruct((width, positions), BF16)
    return pl.pallas_call(
        layer_kernel,
        out_shape=[shape, shape],
        in_specs=[smem, smem] + [vmem] * 5,
        out_specs=[hbm, hbm],
        scratch_shapes=[
            pltpu.VMEM((width, positions), BF16),
            pltpu.VMEM((width, positions), BF16),
            pltpu.VMEM((4 * width, positions), BF16),
            pltpu.VMEM((4 * width, positions), F32),
            pltpu.VMEM((HEADS, positions, positions), BF16),
            pltpu.VMEM((HEADS, positions, positions), F32),
            pltpu.VMEM((width, positions), F32),
            pltpu.VMEM((4 * width, positions), BF16),
            pltpu.VMEM((width, positions), F32),
            pltpu.VMEM((width, positions), F32),
            pltpu.VMEM((positions, positions), F32),
            pltpu.SemaphoreType.DMA((1 + peers,)),
        ],
        compiler_params=pltpu.CompilerParams(vmem_limit_bytes=LAYER_VMEM_BYTES),
        cost_estimate=pl.CostEstimate(flops=10**10, bytes_accessed=10**7, transcendentals=10**6),
        name="layer",
    )(
        me,
        lengths,
        received,
        w_in,
        w_out,
        gain_in,
        gain_mid,
    )


LOW = 256
STACK = 16


def ranks(member, users):
    rows, positions = member.shape
    ones = jnp.where(member, 1.0, 0.0).astype(BF16)

    def iota(shape, dimension):
        return lax.broadcasted_iota(jnp.int32, shape, dimension)

    square = (positions, positions)
    before = jnp.where(iota(square, 0) < iota(square, 1), 1.0, 0.0).astype(BF16)
    row, other = iota((rows, rows), 0), iota((rows, rows), 1)
    shift = users.bit_length() - 1
    above = (other < row) & ((other >> shift) == (row >> shift))
    earlier = dot_nn(jnp.where(above, 1.0, 0.0).astype(BF16), ones)
    return (dot_nn(ones, before) + jnp.sum(earlier, axis=1, keepdims=True)).astype(jnp.int32)


def plan_kernel(own, home_ref, turn_ref, ids_ref, low_ref, high_ref, slot_ref, most_ref, *scratch):
    chosen_ref, digit_ref, wide_ref, rank_ref = scratch
    groups, users, positions = ids_ref.shape
    capacity = low_ref.shape[1]
    home = home_ref[0]
    first = turn_ref[0] * capacity
    own_bits, low_bits = own.bit_length() - 1, LOW.bit_length() - 1

    all_items = ids_ref[...].reshape(groups * users, positions)
    sent = jnp.concatenate([ids_ref[0] >> own_bits == owner for owner in range(groups)], axis=0)
    arriving = all_items >> own_bits == home
    rank_ref[...] = ranks(jnp.concatenate([arriving, sent], axis=0), users) - first
    slot = jnp.full((users, positions), -1, jnp.int32)
    for owner in range(groups):
        rank = rank_ref[pl.ds((groups + owner) * users, users), :]
        fits = (ids_ref[0] >> own_bits == owner) & (rank >= 0) & (rank < capacity)
        slot = jnp.where(fits, rank + owner * capacity, slot)
    slot_ref[...] = slot

    digit = lax.broadcasted_iota(jnp.int32, (LOW, positions), 0)
    place = lax.broadcasted_iota(jnp.int32, (capacity, positions), 0)

    def one_group(group, most):
        items = ids_ref[group]
        for owner in range(groups):
            count = jnp.sum(jnp.where(items >> own_bits == owner, 1.0, 0.0))
            most = jnp.maximum(most, count)
        mine = items >> own_bits == home
        local = items & (own - 1)
        rank = rank_ref[pl.ds(pl.multiple_of(group * users, users), users), :]
        slot = jnp.where(mine, rank, -1)
        low = local & (LOW - 1)
        high = jnp.where(mine, (local >> low_bits) + 1, 0).astype(F32)
        for user in range(users):
            columns = pl.ds(user * positions, positions)
            chosen_ref[:, columns] = jnp.where(place == slot[user : user + 1], 1.0, 0.0).astype(BF16)
            digit_ref[:, columns] = jnp.where(digit == low[user : user + 1], 1.0, 0.0).astype(BF16)
            wide_ref[:, columns] = jnp.broadcast_to(high[user : user + 1], (16, positions)).astype(BF16)
        low_ref[group] = dot_nt(chosen_ref[...], digit_ref[...]).astype(BF16)
        high_ref[pl.ds(group, 1), :] = dot_nt(wide_ref[...], chosen_ref[...])[:1]
        return most

    most_ref[0] = lax.fori_loop(0, groups, one_group, jnp.float32(0)).astype(jnp.int32)


def plan_turn(home, turn, all_ids, own, capacity):
    groups, users, positions = all_ids.shape
    smem, vmem = pl.BlockSpec(memory_space=pltpu.SMEM), pl.BlockSpec(memory_space=pltpu.VMEM)
    return pl.pallas_call(
        functools.partial(plan_kernel, own),
        out_shape=[
            jax.ShapeDtypeStruct((groups, capacity, LOW), BF16),
            jax.ShapeDtypeStruct((groups, capacity), F32),
            jax.ShapeDtypeStruct((users, positions), jnp.int32),
            jax.ShapeDtypeStruct((1,), jnp.int32),
        ],
        in_specs=[smem, smem, vmem],
        out_specs=[vmem] * 3 + [smem],
        scratch_shapes=[
            pltpu.VMEM((capacity, users * positions), BF16),
            pltpu.VMEM((LOW, users * positions), BF16),
            pltpu.VMEM((16, users * positions), BF16),
            pltpu.VMEM((2 * groups * users, positions), jnp.int32),
        ],
        compiler_params=pltpu.CompilerParams(vmem_limit_bytes=PLAN_VMEM_BYTES),
        cost_estimate=pl.CostEstimate(flops=4 * 10**9, bytes_accessed=5 * 10**6, transcendentals=0),
        name="plan_turn",
    )(home, turn, all_ids)


def pack_kernel(distances, home_ref, slot_ref, grad_ref, *refs):
    *packed_refs, wide_ref, chosen_ref = refs
    users, _, positions = grad_ref.shape
    capacity = packed_refs[0].shape[1]
    padded = jnp.concatenate(
        [slot_ref[...].astype(F32), jnp.zeros((LANES - users, positions), F32)], axis=0
    )
    slots = padded.T.astype(jnp.int32)
    place = lax.broadcasted_iota(jnp.int32, (positions, capacity), 1)
    for user in range(users):
        wide_ref[:, pl.ds(user * positions, positions)] = grad_ref[user]
    for distance, packed_ref in zip(distances, packed_refs):
        first = (home_ref[0] ^ distance) * capacity
        for user in range(users):
            chosen_ref[pl.ds(user * positions, positions), :] = jnp.where(
                place == slots[:, user : user + 1] - first, 1.0, 0.0
            ).astype(BF16)
        packed_ref[...] = dot_nn(wide_ref[...], chosen_ref[...]).astype(BF16)


def pack_lists(distances, home, slot, grads, capacity):
    users, features, positions = grads.shape
    smem, vmem = pl.BlockSpec(memory_space=pltpu.SMEM), pl.BlockSpec(memory_space=pltpu.VMEM)
    return pl.pallas_call(
        functools.partial(pack_kernel, distances),
        out_shape=[jax.ShapeDtypeStruct((features, capacity), BF16)] * len(distances),
        in_specs=[smem, vmem, vmem],
        out_specs=[vmem] * len(distances),
        scratch_shapes=[
            pltpu.VMEM((features, users * positions), BF16),
            pltpu.VMEM((users * positions, capacity), BF16),
        ],
        compiler_params=pltpu.CompilerParams(vmem_limit_bytes=LIST_VMEM_BYTES),
        cost_estimate=pl.CostEstimate(
            flops=len(distances) * 8 * 10**8, bytes_accessed=10**6, transcendentals=0
        ),
        name="pack_lists",
    )(home, slot, grads)


def scatter_kernel(groups, stack, low_ref, high_ref, *refs):
    list_refs, (*before_ref, out_ref, spread_ref) = refs[:groups], refs[groups:]
    features, capacity = list_refs[0].shape
    step = pl.program_id(0)
    for group, list_ref in enumerate(list_refs):
        high = high_ref[pl.ds(group, 1), :]
        for part in range(stack):
            wanted = (step * stack + part + 1).astype(F32)
            chosen = jnp.where(high == wanted, 1.0, 0.0).astype(BF16)
            spread_ref[pl.ds(part * features, features), pl.ds(group * capacity, capacity)] = (
                list_ref[...] * chosen
            )
    sums = dot_nn(spread_ref[...], low_ref[...])
    for part in range(stack):
        columns = pl.ds(part * LOW, LOW)
        term = sums[part * features : (part + 1) * features]
        out_ref[:, columns] = term + before_ref[0][:, columns] if before_ref else term


def scatter_slots(low, high, lists, own, before=None):
    groups = len(lists)
    features, capacity = lists[0].shape
    low = low.reshape(groups * capacity, LOW)
    stack = min(STACK, own // LOW)
    block = pl.BlockSpec((features, stack * LOW), lambda i: (0, i))
    extra = [] if before is None else [before]
    return pl.pallas_call(
        functools.partial(scatter_kernel, groups, stack),
        grid=(own // (LOW * stack),),
        out_shape=jax.ShapeDtypeStruct((features, own), F32),
        in_specs=[
            pl.BlockSpec((groups * capacity, LOW), lambda i: (0, 0)),
            pl.BlockSpec(high.shape, lambda i: (0, 0)),
        ]
        + [pl.BlockSpec((features, capacity), lambda i: (0, 0))] * groups
        + [block] * len(extra),
        out_specs=block,
        scratch_shapes=[pltpu.VMEM((stack * features, groups * capacity), BF16)],
        input_output_aliases={2 + groups: 0} if extra else {},
        compiler_params=pltpu.CompilerParams(vmem_limit_bytes=LIST_VMEM_BYTES),
        cost_estimate=pl.CostEstimate(flops=3 * 10**9, bytes_accessed=10**6, transcendentals=0),
        name="scatter_slots",
    )(low, high, *lists, *extra)


def swap(value, axis, distance):
    size = lax.axis_size(axis)
    return lax.ppermute(value, axis, [(i, i ^ distance) for i in range(size)])


def send_lists(home, slot, grads, owners, capacity):
    lists = [None] * owners
    for distances in ((owners - 1,), tuple(range(1, owners - 1)), (0,)):
        made = pack_lists(distances, home, slot, grads, capacity)
        slot, made = lax.optimization_barrier((slot, made))
        for distance, one_list in zip(distances, made):
            lists[distance] = swap(one_list, "dp", distance) if distance else one_list
    return lists


def exchange(value, axis):
    return lax.all_to_all(value, axis, split_axis=0, concat_axis=0, tiled=True)


def on_device(item_ids, user_len, emb_table, cotangent, w_uvqk, w_out, gain_in, gain_mid):
    dp_size = lax.axis_size("dp")
    table_size = lax.axis_size("table")
    users = user_len.shape[0]
    features, vocab = emb_table.shape
    rows = item_ids.shape[0]
    positions = rows // users
    own = vocab // dp_size
    capacity = -(-(rows // dp_size * 5 // 4) // LANES) * LANES
    assert users == table_size and users <= LANES and positions <= 256 and own // LOW <= 255
    assert dp_size & (dp_size - 1) == 0 and users & (users - 1) == 0 and own & (own - 1) == 0
    me = lax.axis_index("table").astype(jnp.int32).reshape(1)
    home = lax.axis_index("dp").astype(jnp.int32).reshape(1)

    send, valid_ids = gather_columns(item_ids, user_len, cotangent, emb_table)
    received = exchange(send, "table")
    all_ids = jnp.stack([valid_ids] + [swap(valid_ids, "dp", k) for k in range(1, dp_size)])
    out_cols, grad_cols = run_layer(me, user_len, received, w_uvqk, w_out, gain_in, gain_mid)
    per_peer = (table_size, features, positions)
    all_ids, grad_cols = lax.optimization_barrier((all_ids, grad_cols))
    plan = plan_turn(home, jnp.zeros((1,), jnp.int32), all_ids, own, capacity)
    grad_home = exchange(grad_cols.reshape(per_peer), "table")
    out_cols, grad_home, plan = lax.optimization_barrier((out_cols, grad_home, plan))
    out_home = exchange(out_cols.reshape(per_peer), "table")
    low, high, slot, most = plan
    lists = send_lists(home, slot, grad_home, dp_size, capacity)
    own_list, out_home = lax.optimization_barrier((lists[0], out_home))
    lists = [own_list] + lists[1:]
    layer_out = jnp.transpose(out_home, (1, 0, 2)).reshape(features, rows)
    layer_out, lists = lax.optimization_barrier((layer_out, lists))
    table_grad = scatter_slots(low, high, lists, own)

    turns = (most[0] + capacity - 1) // capacity

    def another(state):
        turn, sums = state
        more_low, more_high, more_slot, _ = plan_turn(home, turn.reshape(1), all_ids, own, capacity)
        more_lists = send_lists(home, more_slot, grad_home, dp_size, capacity)
        return turn + 1, scatter_slots(more_low, more_high, more_lists, own, sums)

    _, table_grad = lax.while_loop(
        lambda state: state[0] < turns, another, (jnp.int32(1), table_grad)
    )
    return (layer_out, table_grad)


def solution(mesh):
    return jax.shard_map(
        on_device,
        mesh=mesh,
        in_specs=(P("dp"), P("dp"), P("table", None), P("table", "dp"), P(), P(), P(), P()),
        out_specs=(P("table", "dp"), P("table", "dp")),
        check_vma=False,
    )
```
